32 devices in a mesh: seq: 8 (over z, y), batch: 4 (over x, core).
Axes of the slice: x: 2, y: 2, z: 4, core: 2. Of those that a mesh axis runs over, the one named last changes fastest.
Arguments:
- tokens: bfloat16 [2, 4, 2048, 1024], P(None, 'batch', 'seq'), may hold values from -6 to 6
- ln_gain: float32 [1024], replicated, may hold values from 0.1 to 1.9
- w_up: bfloat16 [1024, 4096], replicated, may hold values from -0.1875 to 0.1875
- conv_w: float32 [4, 2048], replicated, may hold values from -3 to 3
- conv_b: float32 [2048], replicated, may hold values from -1.2 to 1.2
- w_query: bfloat16 [4, 512, 512], replicated, may hold values from -0.25 to 0.25
- w_key: bfloat16 [4, 512, 512], replicated, may hold values from -0.25 to 0.25
- w_value: bfloat16 [4, 512, 512], replicated, may hold values from -0.25 to 0.25
- gate_w: float32 [6144, 8], replicated, may hold values from -0.0546875 to 0.0546875
- gate_b: float32 [4], replicated, may hold values from 1 to 12
- out_gain: float32 [2048], replicated, may hold values from 0.1 to 1.9
- skip_gain: float32 [2048], replicated, may hold values from 0.5 to 1.5
- w_down: bfloat16 [2048, 1024], replicated, may hold values from -0.125 to 0.125
- d_out: bfloat16 [2, 4, 2048, 1024], P(None, 'batch', 'seq'), may hold values from -6 to 6
Outputs:
- block_out: bfloat16 [2, 4, 2048, 1024], P(None, 'batch', 'seq')
- grad_tokens: bfloat16 [2, 4, 2048, 1024], P(None, 'batch', 'seq')
- grad_ln_gain: float32 [1024], replicated
- grad_w_up: float32 [1024, 4096], P('seq', 'batch')
- grad_conv_w: float32 [4, 2048], replicated
- grad_conv_b: float32 [2048], replicated
- grad_w_query: float32 [4, 512, 512], P(None, 'seq', 'batch')
- grad_w_key: float32 [4, 512, 512], P(None, 'seq', 'batch')
- grad_w_value: float32 [4, 512, 512], P(None, 'seq', 'batch')
- grad_gate_w: float32 [6144, 8], replicated
- grad_gate_b: float32 [4], replicated
- grad_out_gain: float32 [2048], replicated
- grad_skip_gain: float32 [2048], replicated
- grad_w_down: float32 [2048, 1024], P('seq', 'batch')
The draws below stay inside these ranges and needn't reach their ends.
All inputs are finite; a program needn't handle non-finite values.
Results may differ from the reference program's by a relative error of at most 0.023.
The reference program's roundings to bfloat16 on the way count: a program that leaves them out, or rounds other values in their place, can miss the bound.
Values may be sent and summed in bfloat16 or wider, within the bound.
A program may use at most 576 MiB of HBM per device.

```python
import math
import jax
import jax.numpy as jnp
from jax import lax

D = 1024
INNER = 2048
NH = 4
DH = 512
KCONV = 4
TOK_DEV = 256
MICRO = 2
LENGTH = 2048
SEQS = 4


def draw_gate_b(key, part):
    key = jax.random.fold_in(key, 7)
    second, third, fourth, fifth = jax.random.split(key, 4)
    order = jax.random.permutation(second, NH)
    slow_rate = jnp.exp(jax.random.uniform(third, (NH,), jnp.float32, math.log(0.5 / LENGTH), math.log(2.0 / LENGTH)))
    range_rate = jnp.exp(jax.random.uniform(fifth, (NH,), jnp.float32, math.log(0.5 / TOK_DEV), math.log(1.0 / TOK_DEV)))
    fast_rate = jnp.exp(jax.random.uniform(fourth, (NH,), jnp.float32, math.log(1.0 / 50.0), math.log(1.0 / 30.0)))
    rate = jnp.where(order == 0, range_rate, jnp.where(order < NH // 2, fast_rate, slow_rate))
    forget_bias = -jnp.log(jnp.expm1(rate))
    return forget_bias.astype(jnp.float32)


def shard_levels(stream_key, extent, cuts, low, largest):
    def one(position, shards_of):
        heights = jax.random.uniform(jax.random.fold_in(jax.random.fold_in(stream_key, 6), position), (shards_of,), jnp.float32, low / len(cuts), largest / len(cuts))
        return jnp.repeat(jnp.exp(heights), extent[position] // shards_of).reshape((-1,) + (1,) * (len(extent) - position - 1))

    level = one(*cuts[0])
    for cut in cuts[1:]:
        level = level * one(*cut)
    return level


def noise(own_key, shape, scale, reach, shards=(), dtype=jnp.bfloat16):
    loudness = shard_levels(own_key, shape, shards, -0.22, 0.18) if shards else 1.0
    result = jax.random.normal(own_key, shape, jnp.float32) * scale * loudness
    return jnp.minimum(jnp.maximum(result, -reach), reach).astype(dtype)


def setup_inputs(seed: int = 0) -> dict:
    splits = jax.random.split(jax.random.key(seed), 15)
    return {
        "tokens": noise(splits[0], (MICRO, SEQS, LENGTH, D), 1.0, 6.0, ((1, 4), (2, 8))),
        "ln_gain": jnp.clip(1.0 + 0.18 * jax.random.normal(splits[1], (D,), jnp.float32), 0.1, 1.9),
        "w_up": noise(splits[2], (D, 2 * INNER), D ** -0.5, 0.1875),
        "conv_w": noise(splits[3], (KCONV, INNER), KCONV ** -0.5, 3.0, (), jnp.float32),
        "conv_b": noise(splits[4], (INNER,), 0.3, 1.2, (), jnp.float32),
        "w_query": noise(splits[5], (NH, DH, DH), DH ** -0.5, 0.25),
        "w_key": noise(splits[6], (NH, DH, DH), DH ** -0.5, 0.25),
        "w_value": noise(splits[7], (NH, DH, DH), DH ** -0.5, 0.25),
        "gate_w": noise(splits[8], (3 * INNER, 2 * NH), (0.7 / (3 * INNER) ** 0.5), 0.0546875, (), jnp.float32),
        "gate_b": draw_gate_b(jax.random.fold_in(splits[14], 71), 0),
        "out_gain": jnp.clip(1.0 + 0.18 * jax.random.normal(splits[10], (INNER,), jnp.float32), 0.1, 1.9),
        "skip_gain": jnp.clip(jax.random.uniform(splits[11], (INNER,), jnp.float32, 0.5, 1.5), 0.5, 1.5),
        "w_down": noise(splits[12], (INNER, D), INNER ** -0.5, 0.125),
        "d_out": noise(splits[13], (MICRO, SEQS, LENGTH, D), 1.0, 6.0, ((1, 4), (2, 8))),
    }


highest_mode = lax.Precision.HIGHEST
norm_epsilon = 1e-05
floor_value = -1e+30

@jax.custom_vjp
def low(v):
    return lax.optimization_barrier(v.astype(jnp.bfloat16)).astype(jnp.float32)

@jax.custom_vjp
def low_back(v):
    return v

def low_keep(v):
    return (low(v), None)

def low_pass(kept, grad):
    return (grad,)

def back_keep(v):
    return (v, None)

def back_low(kept, grad):
    return (low(grad),)
low.defvjp(low_keep, low_pass)
low_back.defvjp(back_keep, back_low)

def layer_norm(row_data, gain_vec):
    centre = row_data - lax.optimization_barrier(jnp.mean(row_data, axis=-1, keepdims=True))
    spread = lax.optimization_barrier(jnp.mean(centre * centre, axis=-1, keepdims=True))
    return centre * lax.rsqrt(spread + norm_epsilon) * gain_vec

def conv_silu(extended, conv_w, conv_b):
    conv_width = conv_w.shape[0]
    out_len = extended.shape[0] - conv_width + 1
    summed = conv_b + conv_w[0] * extended[0:out_len]
    for j in range(1, conv_width):
        summed = summed + conv_w[j] * extended[j:j + out_len]
    return jax.nn.silu(summed)

def head_product(features, matrices):
    token_count = features.shape[0]
    head_count = matrices.shape[0]
    by_head = features.reshape(token_count, head_count, -1)
    return jnp.einsum('thd,hde->the', by_head, matrices, precision=highest_mode).reshape(token_count, -1)

def cell_block(queries, key_rows, value_rows, in_gate, log_forget, state_c, state_n, state_m):
    head_size = queries.shape[-1]
    length = queries.shape[1]
    scaled = queries * head_size ** (-0.5)
    running = jnp.cumsum(log_forget, axis=1)
    seg_total = running[:, -1]
    causal = jnp.arange(length)[:, None] >= jnp.arange(length)[None, :]
    decays = running[:, :, None] - running[:, None, :] + in_gate[:, None, :]
    decays = jnp.where(causal[None], decays, floor_value)
    carried = running + state_m[:, None]
    stable = jnp.maximum(carried, lax.optimization_barrier(jnp.max(decays, axis=2)))
    scores = jnp.einsum('htd,hsd->hts', scaled, key_rows, precision=highest_mode)
    weights = jnp.exp(decays - stable[:, :, None]) * scores
    from_state = jnp.exp(carried - stable)
    numerator = jnp.einsum('hts,hsd->htd', weights, value_rows, precision=highest_mode)
    numerator = numerator + from_state[:, :, None] * jnp.einsum('htd,hde->hte', scaled, state_c, precision=highest_mode)
    denominator = lax.optimization_barrier(jnp.sum(weights, axis=2)) + from_state * jnp.einsum('htd,hd->ht', scaled, state_n, precision=highest_mode)
    hidden = numerator / jnp.maximum(jnp.abs(denominator), jnp.exp(-stable))[:, :, None]
    exponent = seg_total[:, None] - running + in_gate
    local_top = lax.optimization_barrier(jnp.max(exponent, axis=1))
    new_m = jnp.maximum(seg_total + state_m, local_top)
    key_weight = jnp.exp(exponent - new_m[:, None])
    weighted = key_rows * key_weight[:, :, None]
    keep_old = jnp.exp(seg_total + state_m - new_m)
    new_c = keep_old[:, None, None] * state_c + jnp.einsum('hsd,hse->hde', weighted, value_rows, precision=highest_mode)
    new_n = keep_old[:, None] * state_n + lax.optimization_barrier(jnp.sum(weighted, axis=1))
    return (hidden, new_c, new_n, new_m)

def head_output(hidden, out_gain, skip_gain, conv_out, gate_z):
    centre = hidden - lax.optimization_barrier(jnp.mean(hidden, axis=-1, keepdims=True))
    spread = lax.optimization_barrier(jnp.mean(centre * centre, axis=-1, keepdims=True))
    normed = centre * lax.rsqrt(spread + norm_epsilon)
    flat_out = normed.transpose(1, 0, 2).reshape(hidden.shape[1], -1) * out_gain
    return (flat_out + skip_gain * conv_out) * jax.nn.silu(gate_z)

def sequence_block(row_data, weights_all):
    ln_gain, w_up, conv_w, conv_b, w_query, w_key, w_value, gate_w, gate_b, out_gain, skip_gain, w_down = weights_all
    inner = w_down.shape[0]
    head_count = w_query.shape[0]
    head_size = w_query.shape[1]
    seq_len = row_data.shape[0]
    block_count = seq_len // TOK_DEV
    normed = low(layer_norm(row_data, ln_gain))
    lifted = low_back(jnp.dot(normed, w_up, precision=highest_mode))
    mix_in = low(lifted[:, :inner])
    gate_z = lifted[:, inner:]
    halo_rows = jnp.zeros((conv_w.shape[0] - 1, inner), jnp.float32)
    conv_out = low(conv_silu(jnp.concatenate([halo_rows, mix_in], axis=0), conv_w, conv_b))
    queries = low(low_back(head_product(conv_out, w_query)))
    key_rows = low(low_back(head_product(conv_out, w_key)))
    value_rows = low(low_back(head_product(mix_in, w_value)))
    joined = jnp.concatenate([queries, key_rows, value_rows], axis=1)
    gate_pre = jnp.dot(joined, gate_w, precision=highest_mode)
    in_gate = gate_pre[:, :head_count]
    log_forget = jax.nn.log_sigmoid(gate_pre[:, head_count:] + gate_b)

    def to_blocks(features):
        return features.reshape(block_count, TOK_DEV, head_count, -1).transpose(0, 2, 1, 3)

    def gate_blocks(values):
        return values.reshape(block_count, TOK_DEV, head_count).transpose(0, 2, 1)

    def advance(state_in, block_in):
        hidden, new_c, new_n, new_m = cell_block(block_in[0], block_in[1], block_in[2], block_in[3], block_in[4], state_in[0], state_in[1], state_in[2])
        return ((new_c, new_n, new_m), hidden)
    initial = (jnp.zeros((head_count, head_size, head_size), jnp.float32), jnp.zeros((head_count, head_size), jnp.float32), jnp.full((head_count,), floor_value, jnp.float32))
    blocks_in = (to_blocks(queries), to_blocks(key_rows), to_blocks(value_rows), gate_blocks(in_gate), gate_blocks(log_forget))
    final_state, hidden = lax.scan(jax.checkpoint(advance), initial, blocks_in)
    hidden = hidden.transpose(1, 0, 2, 3).reshape(head_count, seq_len, head_size)
    gated = low(head_output(hidden, out_gain, skip_gain, conv_out, gate_z))
    return row_data + jnp.dot(gated, w_down, precision=highest_mode)

def reference(tokens, ln_gain, w_up, conv_w, conv_b, w_query, w_key, w_value, gate_w, gate_b, out_gain, skip_gain, w_down, d_out):
    weights_all = tuple((p.astype(jnp.float32) for p in (ln_gain, w_up, conv_w, conv_b, w_query, w_key, w_value, gate_w, gate_b, out_gain, skip_gain, w_down)))
    micro_count, seq_count, seq_len, model_width = tokens.shape
    flat_in = tokens.astype(jnp.float32).reshape(micro_count * seq_count, seq_len, model_width)
    flat_cot = d_out.astype(jnp.float32).reshape(micro_count * seq_count, seq_len, model_width)

    def forward(all_rows, weights_in):

        def single(one_seq):
            return sequence_block(one_seq, weights_in)
        return lax.map(jax.checkpoint(single), all_rows)
    outputs, backward = jax.vjp(forward, flat_in, weights_all)
    grad_in, grads = backward(flat_cot)
    return (outputs.reshape(tokens.shape).astype(jnp.bfloat16), grad_in.reshape(tokens.shape).astype(jnp.bfloat16), grads[0], grads[1], grads[2], grads[3], grads[4], grads[5], grads[6], grads[7], grads[8], grads[9], grads[10], grads[11])
```

```python
from functools import partial

import jax
import jax.numpy as jnp
from jax import lax
from jax.experimental import pallas as pl
from jax.experimental.pallas import tpu as pltpu
from jax.sharding import PartitionSpec as P

norm_epsilon = 1e-05
floor_value = -1e30


def shifted(value, axis, steps):
    count = lax.axis_size(axis)
    initial, last = (max(0, -steps), min(count, count - steps))
    return lax.ppermute(value, axis, [(source, source + steps) for source in range(initial, last)])


def combine_states(earlier, later):
    top = jnp.maximum(later[3] + earlier[2], later[2])
    keep_first = jnp.exp(later[3] + earlier[2] - top)
    keep_second = jnp.exp(later[2] - top)
    merged_c = keep_first[..., None, None] * earlier[0] + keep_second[..., None, None] * later[0]
    merged_n = keep_first[..., None] * earlier[1] + keep_second[..., None] * later[1]
    return (merged_c, merged_n, top, earlier[3] + later[3])


def state_identity(template):
    return (
        jnp.zeros_like(template[0]),
        jnp.zeros_like(template[1]),
        jnp.full_like(template[2], floor_value),
        jnp.zeros_like(template[3]),
    )


def head_output(hidden, out_gain, skip_gain, conv_out, gate_z):
    centre = hidden - jnp.mean(hidden, axis=-1, keepdims=True)
    spread = jnp.mean(centre * centre, axis=-1, keepdims=True)
    normed = centre * lax.rsqrt(spread + norm_epsilon)
    flat_out = normed.transpose(1, 0, 2).reshape(hidden.shape[1], -1) * out_gain
    return (flat_out + skip_gain * conv_out) * jax.nn.silu(gate_z)


def output_tail(
    query_f,
    key_f,
    value_f,
    gate_pre,
    conv_f,
    gate_z,
    out_gain,
    skip_gain,
    state_c,
    state_n,
    state_m,
):
    head_count = gate_pre.shape[1] // 2
    in_gate = gate_pre[:, :head_count].T
    log_forget = jax.nn.log_sigmoid(gate_pre[:, head_count:]).T
    hidden = cell_hidden(
        to_heads(query_f, head_count),
        to_heads(key_f, head_count),
        to_heads(value_f, head_count),
        in_gate,
        log_forget,
        state_c,
        state_n,
        state_m,
    )
    return head_output(hidden, out_gain, skip_gain, conv_f, gate_z)


def state_tail(key_f, value_f, gate_pre, state_c, state_n, state_m):
    head_count = gate_pre.shape[1] // 2
    in_gate = gate_pre[:, :head_count].T
    log_forget = jax.nn.log_sigmoid(gate_pre[:, head_count:]).T
    return cell_state(
        to_heads(key_f, head_count),
        to_heads(value_f, head_count),
        in_gate,
        log_forget,
        state_c,
        state_n,
        state_m,
    )


def to_device_blocks(grad_full, seq_count, batch_count):
    if grad_full.ndim == 2:
        rows, cols = grad_full.shape
        split = grad_full.reshape(seq_count, rows // seq_count, batch_count, cols // batch_count)
        return split.transpose(0, 2, 1, 3).reshape(
            seq_count * batch_count, rows // seq_count, cols // batch_count
        )
    heads, rows, cols = grad_full.shape
    split = grad_full.reshape(heads, seq_count, rows // seq_count, batch_count, cols // batch_count)
    return split.transpose(1, 3, 0, 2, 4).reshape(
        seq_count * batch_count, heads, rows // seq_count, cols // batch_count
    )


f32 = jnp.float32
bf16 = jnp.bfloat16
chunk_len = 256
wide_len = 512
vmem_bytes = 56 * 1024 * 1024


def mm(a, b):
    return lax.dot_general(a, b, (((1,), (0,)), ((), ())), preferred_element_type=f32)


def mm_nt(a, b):
    return lax.dot_general(a, b, (((1,), (1,)), ((), ())), preferred_element_type=f32)


def mm_tn(a, b):
    return lax.dot_general(a, b, (((0,), (0,)), ((), ())), preferred_element_type=f32)


def split_three(value):
    high = value.astype(bf16)
    rest = value - high.astype(f32)
    middle = rest.astype(bf16)
    low = (rest - middle.astype(f32)).astype(bf16)
    return high, middle, low


def conv_taps(ext, length):
    return [pltpu.roll(ext, 3 - j, 0)[8 : 8 + length] if j < 3 else ext[8 : 8 + length] for j in range(4)]


def lift_kernel(chained, head_ref, normed, w_mix, w_gate, w_q, w_k, w_v, conv_w, conv_b, gate_w, *refs):
    if chained:
        rows_before, *refs, halo_out, carry = refs
    else:
        *refs, carry = refs
    mix_out, conv_out, q_out, k_out, v_out, z_out, gate_out = refs
    length = normed.shape[0]

    @pl.when(pl.program_id(0) == 0)
    def _():
        if chained:
            mix_before = mm(rows_before[...], w_mix[...]).astype(bf16)
            halo_out[...] = mix_before
            carry[...] = mix_before[8:16].astype(f32)
        else:
            carry[...] = jnp.zeros_like(carry)

    rows = normed[...]
    mix = mm(rows, w_mix[...]).astype(bf16)
    mix_out[...] = mix
    z_out[...] = mm(rows, w_gate[...])
    mix_f = mix.astype(f32)
    taps = conv_taps(jnp.concatenate([carry[...], mix_f], axis=0), length)
    carry[...] = mix_f[length - 8 :]
    summed = conv_b[...]
    for j in range(4):
        summed = summed + conv_w[j : j + 1, :] * taps[j]
    conv = (summed * jax.nn.sigmoid(summed)).astype(bf16)
    conv_out[...] = conv
    q = mm(conv, w_q[0]).astype(bf16)
    k = mm(conv, w_k[0]).astype(bf16)
    v = mm(mix, w_v[0]).astype(bf16)
    q_out[...] = q
    k_out[...] = k
    v_out[...] = v
    parts = mm_nt(gate_w[0], q) + mm_nt(gate_w[1], k) + mm_nt(gate_w[2], v)
    gate_out[...] = parts[0:8] + parts[8:16] + parts[16:24]


def gate_rows(gates, causal, diagonal):
    in_row = gates[0:1, :]
    pre = gates[1:2, :]
    log_forget = jnp.minimum(pre, 0.0) - jnp.log1p(jnp.exp(-jnp.abs(pre)))
    run_col = jnp.sum(jnp.where(causal, log_forget, 0.0), axis=1, keepdims=True)
    run_row = jnp.sum(jnp.where(diagonal, run_col, 0.0), axis=0, keepdims=True)
    return in_row - run_row, run_col, log_forget


def masks(length):
    row = lax.broadcasted_iota(jnp.int32, (length, length), 0)
    col = lax.broadcasted_iota(jnp.int32, (length, length), 1)
    return row >= col, row == col


def cell_forward_kernel(
    chained, head_ref, gates, q_ref, k_ref, v_ref, conv_ref, z_ref, out_gain, skip_gain, w_down, *refs
):
    if chained:
        *first, part_out, normed_out, state_out, norm_out, weight_out, col_out, row_out = refs[:10]
        *final, state, norm, level = refs[10:]
    else:
        part_out, normed_out, state_out, norm_out, weight_out, col_out, row_out = refs[:7]
        state, norm, level = refs[7:]
    length = q_ref.shape[0]
    head_size = q_ref.shape[1]
    scale = head_size ** (-0.5)

    @pl.when(pl.program_id(0) == 0)
    def _():
        if chained:
            for ref, value in zip((state, norm, level), first):
                ref[...] = value[...]
        else:
            state[...] = jnp.zeros_like(state)
            norm[...] = jnp.zeros_like(norm)
            level[...] = jnp.full_like(level, floor_value)

    causal, diagonal = masks(length)
    a_row, run_col, log_forget = gate_rows(gates[...], causal, diagonal)
    before = level[0:1, 0:1]
    top = jnp.maximum(
        before, jnp.max(jnp.where(causal, a_row, floor_value), axis=1, keepdims=True)
    )
    decay = jnp.exp(jnp.where(causal, a_row - top, floor_value))
    q = q_ref[...]
    k = k_ref[...]
    v = v_ref[...]
    q_f = q.astype(f32)
    weights = decay * (mm_nt(q, k) * scale)
    weights_low = weights.astype(bf16)
    weight_out[...] = weights_low
    from_state = jnp.exp(before - top)
    state_low = state[...].astype(bf16)
    state_out[0] = state_low
    norm_row = norm[0:1, :]
    norm_out[0] = norm[...]
    numerator = mm(weights_low, v) + (from_state * scale) * mm(q, state_low)
    denominator = jnp.sum(weights, axis=1, keepdims=True) + (from_state * scale) * jnp.sum(
        q_f * norm_row, axis=1, keepdims=True
    )
    floor = jnp.exp(-(run_col + top))
    size = jnp.abs(denominator)
    inverse = 1.0 / jnp.maximum(size, floor)
    hidden = numerator * inverse
    centre = hidden - jnp.mean(hidden, axis=1, keepdims=True)
    spread = jnp.mean(centre * centre, axis=1, keepdims=True)
    rstd = lax.rsqrt(spread + norm_epsilon)
    normed = centre * rstd
    normed_out[...] = normed
    gate_z = z_ref[...]
    gated = (normed * out_gain[...] + skip_gain[...] * conv_ref[...].astype(f32)) * (
        gate_z * jax.nn.sigmoid(gate_z)
    )
    part_out[...] = mm(gated.astype(bf16), w_down[...]).astype(bf16)
    factor = jnp.where(
        size > floor,
        jnp.where(denominator > 0, 1.0, -1.0) * inverse * (norm_epsilon * rstd * rstd),
        0.0,
    )
    lane = lax.broadcasted_iota(jnp.int32, (length, 128), 1)
    packed = jnp.where(lane == 0, rstd, inverse)
    packed = jnp.where(lane == 2, from_state, packed)
    packed = jnp.where(lane == 3, top, packed)
    col_out[...] = jnp.where(lane == 4, factor, packed)
    sub = lax.broadcasted_iota(jnp.int32, (8, length), 0)
    row_out[...] = jnp.where(sub == 0, a_row, 1.0 - jnp.exp(log_forget))
    last = top[length - 1 : length, :]
    a_col = jnp.sum(jnp.where(diagonal, a_row, 0.0), axis=1, keepdims=True)
    weighted = k.astype(f32) * jnp.exp(a_col - last)
    keep = jnp.exp(before - last)
    state[...] = keep * state[...] + mm_tn(weighted.astype(bf16), v)
    norm[...] = keep * norm[...] + jnp.sum(weighted, axis=0, keepdims=True)
    level[...] = jnp.broadcast_to(run_col[length - 1 : length, :] + last, level.shape)
    if chained:
        for ref, value in zip(final, (state, norm, level)):
            ref[...] = value[...]


def cell_backward_kernel(
    chained, head_ref, rows_ref, q_ref, k_ref, v_ref, conv_ref, z_ref, normed_ref, state_ref, norm_ref,
    weight_ref, col_ref, cot_ref, out_gain, skip_gain, w_down, *refs
):
    if chained:
        *first, dq_out, dk_out, dv_out, dskip_out, dz_out, gate_out, g_down_out, g_gain_out = refs[:10]
        *final, d_state, d_norm, g_down, g_gain = refs[10:]
    else:
        dq_out, dk_out, dv_out, dskip_out, dz_out, gate_out, g_down_out, g_gain_out = refs[:8]
        d_state, d_norm, g_down, g_gain = refs[8:]
    length = q_ref.shape[0]
    head_size = q_ref.shape[1]
    scale = head_size ** (-0.5)

    @pl.when(pl.program_id(0) == 0)
    def _():
        if chained:
            d_state[...] = first[0][...]
            d_norm[...] = first[1][...]
        else:
            d_state[...] = jnp.zeros_like(d_state)
            d_norm[...] = jnp.zeros_like(d_norm)
        g_down[...] = jnp.zeros_like(g_down)
        g_gain[...] = jnp.zeros_like(g_gain)

    causal, diagonal = masks(length)
    rstd = col_ref[:, 0:1]
    inverse = col_ref[:, 1:2]
    from_state = col_ref[:, 2:3]
    top = col_ref[:, 3:4]
    factor = col_ref[:, 4:5]
    a_row = rows_ref[0:1, :]
    q = q_ref[...]
    k = k_ref[...]
    v = v_ref[...]
    q_f = q.astype(f32)
    k_f = k.astype(f32)
    conv = conv_ref[...].astype(f32)
    normed = normed_ref[...]
    gate_z = z_ref[...]
    cot = cot_ref[...]
    opened = jax.nn.sigmoid(gate_z)
    silu = gate_z * opened
    head_in = normed * out_gain[...] + skip_gain[...] * conv
    g_down[...] += mm_tn((head_in * silu).astype(bf16), cot)
    d_gated = mm_nt(cot, w_down[...])
    dz_out[...] = (d_gated * head_in * (opened * (1.0 + gate_z * (1.0 - opened)))).astype(bf16)
    d_head = d_gated * silu
    g_gain[0:1, :] += jnp.sum(d_head * normed, axis=0, keepdims=True)
    g_gain[1:2, :] += jnp.sum(d_head * conv, axis=0, keepdims=True)
    dskip_out[...] = skip_gain[...] * d_head
    d_hat = d_head * out_gain[...]
    along = jnp.sum(d_hat * normed, axis=1, keepdims=True)
    d_hidden = rstd * (
        d_hat - jnp.mean(d_hat, axis=1, keepdims=True) - normed * (along / head_size)
    )
    d_num = d_hidden * inverse
    d_den = -along * factor
    d_num_low = d_num.astype(bf16)
    decay = jnp.exp(jnp.where(causal, a_row - top, floor_value))
    d_scores = ((mm_nt(d_num_low, v) + d_den) * (decay * scale)).astype(bf16)
    through = from_state * scale
    dq_near = mm(d_scores, k)
    dq_far = (
        mm_nt((d_num * through).astype(bf16), state_ref[0])
        + (through * d_den) * norm_ref[0, 0:1, :]
    )
    last = top[length - 1 : length, :]
    keep = from_state[length - 1 : length, :]
    a_col = jnp.sum(jnp.where(diagonal, a_row, 0.0), axis=1, keepdims=True)
    key_weight = jnp.exp(a_col - last)
    d_state_low = d_state[...].astype(bf16)
    dk_near = mm_tn(d_scores, q)
    dk_far = key_weight * (mm_nt(v, d_state_low) + d_norm[0:1, :])
    dv = mm_tn(weight_ref[...], d_num_low) + mm((k_f * key_weight).astype(bf16), d_state_low)
    dq_out[...] = dq_near + dq_far
    dk_out[...] = dk_near + dk_far
    dv_out[...] = dv
    held = state_ref[0].astype(f32) * d_state[...]
    held = jnp.sum(jnp.sum(held, axis=0, keepdims=True) + norm_ref[0, 0:1, :] * d_norm[0:1, :])
    q_state = q_f * through
    d_state[...] = keep * d_state[...] + mm_tn(q_state.astype(bf16), d_num_low)
    d_norm[...] = keep * d_norm[...] + jnp.sum(q_state * d_den, axis=0, keepdims=True)
    q_dot = jnp.sum(q_f * (dq_near + dq_far), axis=1, keepdims=True)
    k_near = jnp.sum(k_f * dk_near, axis=1, keepdims=True)
    k_far = jnp.sum(k_f * dk_far, axis=1, keepdims=True)
    d_in = jnp.sum(jnp.where(diagonal, k_near + k_far, 0.0), axis=0, keepdims=True)
    d_log = jnp.sum(
        jnp.where(causal, q_dot - k_near, jnp.where(diagonal, 0.0, k_far)), axis=0, keepdims=True
    )
    d_log = d_log + keep * held
    sub = lax.broadcasted_iota(jnp.int32, (8, length), 0)
    gate_out[...] = jnp.where(sub == 0, d_in, d_log * rows_ref[1:2, :])

    @pl.when(pl.program_id(0) == pl.num_programs(0) - 1)
    def _():
        if chained:
            final[0][...] = d_state[...]
            final[1][...] = d_norm[...]
        g_down_out[...] = g_down[...].astype(bf16)
        g_gain_out[...] = g_gain[...]


def lower_kernel(
    chained, head_ref, d_gate, dq_ref, dk_ref, dv_ref, dskip_ref, dz_ref, mix_ref, mix_before, conv_ref,
    q_ref, k_ref, v_ref, normed, w_q, w_k, w_v, w_mix, w_gate, conv_w, conv_b, gate_w, *refs
):
    if chained:
        first_halo, first_later, *refs = refs
        later_out = refs.pop(7)
    part_out, gq_out, gk_out, gv_out, gm_out, gz_out, small_out = refs[:7]
    g_q, g_k, g_v, g_m, g_z, g_small, later = refs[7:]
    length = q_ref.shape[0]
    step = pl.program_id(0)

    @pl.when(step == 0)
    def _():
        for ref in (g_q, g_k, g_v, g_m, g_z, g_small, later):
            ref[...] = jnp.zeros_like(ref)
        if chained:
            later[...] = first_later[...]

    high, middle, low = split_three(d_gate[...])
    left = jnp.concatenate([high, middle, low, high, middle, high], axis=0)
    d_joined = mm_tn(left, gate_w[...])
    size = q_ref.shape[1]
    query_low = (dq_ref[...] + d_joined[:, :size]).astype(bf16)
    key_low = (dk_ref[...] + d_joined[:, size : 2 * size]).astype(bf16)
    value_low = (dv_ref[...] + d_joined[:, 2 * size :]).astype(bf16)
    conv = conv_ref[...]
    mix = mix_ref[...]
    g_q[...] += mm_tn(conv, query_low)
    g_k[...] += mm_tn(conv, key_low)
    g_v[...] += mm_tn(mix, value_low)
    three = jnp.concatenate([high, middle, low], axis=0)
    for at, ref in enumerate((q_ref, k_ref, v_ref)):
        got = mm(three, ref[...])
        g_small[8 * at : 8 * at + 8, :] += got[0:8] + got[8:16] + got[16:24]
    d_conv = dskip_ref[...] + mm_nt(query_low, w_q[0]) + mm_nt(key_low, w_k[0])
    halo = mix_before[8:16, :].astype(f32)
    edge = first_halo[8:16, :].astype(f32) if chained else 0.0
    halo = jnp.where(step == pl.num_programs(0) - 1, edge, halo)
    taps = conv_taps(jnp.concatenate([halo, mix.astype(f32)], axis=0), length)
    summed = conv_b[...]
    for j in range(4):
        summed = summed + conv_w[j : j + 1, :] * taps[j]
    opened = jax.nn.sigmoid(summed)
    d_summed = d_conv * (opened * (1.0 + summed * (1.0 - opened)))
    for j in range(4):
        g_small[24 + j : 25 + j, :] += jnp.sum(d_summed * taps[j], axis=0, keepdims=True)
    g_small[28:29, :] += jnp.sum(d_summed, axis=0, keepdims=True)
    ext = jnp.concatenate([d_summed, later[...]], axis=0)
    later[...] = d_summed[0:8]
    d_mix = conv_w[3:4, :] * d_summed
    for j in range(3):
        d_mix = d_mix + conv_w[j : j + 1, :] * pltpu.roll(ext, length + 8 - (3 - j), 0)[0:length]
    d_mix = (d_mix + mm_nt(value_low, w_v[0])).astype(bf16)
    d_z = dz_ref[...]
    rows = normed[...]
    g_m[...] += mm_tn(rows, d_mix)
    g_z[...] += mm_tn(rows, d_z)
    part_out[...] = (mm_nt(d_mix, w_mix[...]) + mm_nt(d_z, w_gate[...])).astype(bf16)

    @pl.when(step == pl.num_programs(0) - 1)
    def _():
        gq_out[...] = g_q[...].astype(bf16)
        gk_out[...] = g_k[...].astype(bf16)
        gv_out[...] = g_v[...].astype(bf16)
        gm_out[...] = g_m[...].astype(bf16)
        gz_out[...] = g_z[...].astype(bf16)
        small_out[...] = g_small[...]
        if chained:
            later_out[...] = later[...]


def struct(shape, dtype):
    return jax.ShapeDtypeStruct(shape, dtype)


def run_kernel(body, head, grid, inputs, in_specs, outs, out_specs, scratch, name, flops, nbytes):
    return pl.pallas_call(
        body,
        grid_spec=pltpu.PrefetchScalarGridSpec(
            num_scalar_prefetch=1,
            grid=(grid,),
            in_specs=in_specs,
            out_specs=out_specs,
            scratch_shapes=scratch,
        ),
        out_shape=outs,
        compiler_params=pltpu.CompilerParams(
            dimension_semantics=("arbitrary",), vmem_limit_bytes=vmem_bytes
        ),
        cost_estimate=pl.CostEstimate(flops=flops, bytes_accessed=nbytes, transcendentals=0),
        name=name,
    )(head, *inputs)


def fixed(shape, *index):
    return pl.BlockSpec(shape, lambda g, h: tuple(h[0] if i == "h" else i for i in index))


def lift(head, normed, w_up, w_query, w_key, w_value, conv_w, conv_b, gate_parts, *first):
    tokens, width = normed.shape
    heads, size, _ = w_query.shape
    length = wide_len
    by_row = lambda cols: pl.BlockSpec((length, cols), lambda g, h: (g, 0))
    weight = pl.BlockSpec((1, size, size), lambda g, h: (h[0], 0, 0))
    chained = len(first) > 0
    halo = [pl.BlockSpec((16, size), lambda g, h: (0, 0))] * chained
    return run_kernel(
        partial(lift_kernel, chained), head, tokens // length,
        (normed, w_up, w_up, w_query, w_key, w_value, conv_w, conv_b, gate_parts, *first),
        [
            by_row(width),
            pl.BlockSpec((width, size), lambda g, h: (0, h[0])),
            pl.BlockSpec((width, size), lambda g, h: (0, heads + h[0])),
            weight, weight, weight,
            pl.BlockSpec((4, size), lambda g, h: (0, h[0])),
            pl.BlockSpec((1, size), lambda g, h: (0, h[0])),
            pl.BlockSpec(gate_parts.shape, lambda g, h: (0, 0, 0)),
        ]
        + [pl.BlockSpec((16, width), lambda g, h: (0, 0))] * chained,
        [struct((tokens, size), bf16)] * 5
        + [struct((tokens, size), f32), struct((8, tokens), f32)]
        + [struct((16, size), bf16)] * chained,
        [by_row(size)] * 6 + [pl.BlockSpec((8, length), lambda g, h: (0, g))] + halo,
        [pltpu.VMEM((8, size), f32)],
        "lift", 2 * tokens * size * (2 * width + 3 * size), 24 * 2**20,
    )


def cell_forward(head, gates, q, k, v, conv, gate_z, out_gain, skip_gain, w_down, *first):
    tokens, size = q.shape
    width = w_down.shape[1]
    length = chunk_len
    steps = tokens // length
    by_row = lambda cols: pl.BlockSpec((length, cols), lambda g, h: (g, 0))
    gain = pl.BlockSpec((1, size), lambda g, h: (0, h[0]))
    carried = [struct(value.shape, f32) for value in first]
    carried_specs = [pl.BlockSpec(value.shape, lambda g, h: (0, 0)) for value in first]
    return run_kernel(
        partial(cell_forward_kernel, len(first) > 0), head, steps,
        (gates, q, k, v, conv, gate_z, out_gain, skip_gain, w_down, *first),
        [pl.BlockSpec((2, length), lambda g, h: (0, g))]
        + [by_row(size)] * 5
        + [gain, gain, pl.BlockSpec((size, width), lambda g, h: (h[0], 0))]
        + carried_specs,
        [
            struct((tokens, width), bf16),
            struct((tokens, size), f32),
            struct((steps, size, size), bf16),
            struct((steps, 8, size), f32),
            struct((tokens, length), bf16),
            struct((tokens, 128), f32),
            struct((8, tokens), f32),
        ]
        + carried,
        [
            by_row(width),
            by_row(size),
            pl.BlockSpec((1, size, size), lambda g, h: (g, 0, 0)),
            pl.BlockSpec((1, 8, size), lambda g, h: (g, 0, 0)),
            by_row(length),
            by_row(128),
            pl.BlockSpec((8, length), lambda g, h: (0, g)),
        ]
        + carried_specs,
        [pltpu.VMEM((size, size), f32), pltpu.VMEM((8, size), f32), pltpu.VMEM((8, 128), f32)],
        "cell_forward", 2 * tokens * size * (2 * length + 2 * size + width), 28 * 2**20,
    )


def cell_backward(
    head, rows, q, k, v, conv, gate_z, normed, states, norms, weights, cols, cot,
    out_gain, skip_gain, w_down, *first,
):
    tokens, size = q.shape
    width = w_down.shape[1]
    length = chunk_len
    steps = tokens // length
    end = steps - 1
    by_row = lambda n: pl.BlockSpec((length, n), lambda g, h: (end - g, 0))
    gain = pl.BlockSpec((1, size), lambda g, h: (0, h[0]))
    whole = lambda shape: pl.BlockSpec(shape, lambda g, h: (0, 0))
    carried = [struct(value.shape, f32) for value in first]
    carried_specs = [whole(value.shape) for value in first]
    return run_kernel(
        partial(cell_backward_kernel, len(first) > 0), head, steps,
        (rows, q, k, v, conv, gate_z, normed, states, norms, weights, cols, cot,
         out_gain, skip_gain, w_down, *first),
        [pl.BlockSpec((8, length), lambda g, h: (0, end - g))]
        + [by_row(size)] * 6
        + [
            pl.BlockSpec((1, size, size), lambda g, h: (end - g, 0, 0)),
            pl.BlockSpec((1, 8, size), lambda g, h: (end - g, 0, 0)),
            by_row(length),
            by_row(128),
            by_row(width),
            gain, gain,
            pl.BlockSpec((size, width), lambda g, h: (h[0], 0)),
        ]
        + carried_specs,
        [struct((tokens, size), f32)] * 4
        + [
            struct((tokens, size), bf16),
            struct((8, tokens), f32),
            struct((size, width), bf16),
            struct((8, size), f32),
        ]
        + carried,
        [by_row(size)] * 5
        + [
            pl.BlockSpec((8, length), lambda g, h: (0, end - g)),
            whole((size, width)),
            whole((8, size)),
        ]
        + carried_specs,
        [
            pltpu.VMEM((size, size), f32),
            pltpu.VMEM((8, size), f32),
            pltpu.VMEM((size, width), f32),
            pltpu.VMEM((8, size), f32),
        ],
        "cell_backward", 2 * tokens * size * (4 * length + 4 * size + 2 * width), 44 * 2**20,
    )


def lower(
    head, d_gate, dq, dk, dv, dskip, dz, mix, conv, q, k, v, normed,
    w_query, w_key, w_value, w_up, conv_w, conv_b, gate_pairs, *first,
):
    tokens, size = q.shape
    width = normed.shape[1]
    heads = w_query.shape[0]
    length = wide_len
    steps = tokens // length
    end = steps - 1
    by_row = lambda n: pl.BlockSpec((length, n), lambda g, h: (end - g, 0))
    weight = pl.BlockSpec((1, size, size), lambda g, h: (h[0], 0, 0))
    whole = lambda shape: pl.BlockSpec(shape, lambda g, h: (0, 0))
    chained = len(first) > 0
    return run_kernel(
        partial(lower_kernel, chained), head, steps,
        (d_gate, dq, dk, dv, dskip, dz, mix, mix, conv, q, k, v, normed,
         w_query, w_key, w_value, w_up, w_up, conv_w, conv_b, gate_pairs, *first),
        [pl.BlockSpec((8, length), lambda g, h: (0, end - g))]
        + [by_row(size)] * 6
        + [
            pl.BlockSpec(
                (16, size),
                lambda g, h: (jnp.maximum((end - g) * (length // 16) - 1, 0), 0),
            )
        ]
        + [by_row(size)] * 4
        + [by_row(width), weight, weight, weight]
        + [
            pl.BlockSpec((width, size), lambda g, h: (0, h[0])),
            pl.BlockSpec((width, size), lambda g, h: (0, heads + h[0])),
            pl.BlockSpec((4, size), lambda g, h: (0, h[0])),
            pl.BlockSpec((1, size), lambda g, h: (0, h[0])),
            whole(gate_pairs.shape),
        ]
        + [whole(value.shape) for value in first],
        [struct((tokens, width), bf16)]
        + [struct((size, size), bf16)] * 3
        + [struct((width, size), bf16)] * 2
        + [struct((32, size), f32)]
        + [struct((8, size), f32)] * chained,
        [by_row(width)]
        + [whole((size, size))] * 3
        + [whole((width, size))] * 2
        + [whole((32, size))]
        + [whole((8, size))] * chained,
        [pltpu.VMEM((size, size), f32)] * 3
        + [pltpu.VMEM((width, size), f32)] * 2
        + [pltpu.VMEM((32, size), f32), pltpu.VMEM((8, size), f32)],
        "lower", 2 * tokens * size * (6 * size + 4 * width), 48 * 2**20,
    )


def swap(value, axis, mask):
    count = lax.axis_size(axis)
    return lax.ppermute(value, axis, [(s, s ^ mask) for s in range(count)])


def part_of(value, at, count, axis):
    size = value.shape[axis] // count
    return lax.dynamic_slice_in_dim(value, at * size, size, axis)


def halved(value, bit, dim, axis, mask):
    kept = part_of(value, bit, 2, dim).astype(f32)
    return kept + swap(part_of(value, 1 - bit, 2, dim), axis, mask).astype(f32)


def paired(mine, other, bit, dim):
    return jnp.where(
        bit == 0, jnp.concatenate([mine, other], dim), jnp.concatenate([other, mine], dim)
    )


def place():
    at_seq, at_batch = lax.axis_index("seq"), lax.axis_index("batch")
    return (at_seq % 8) // 2, at_seq % 2, at_batch // 2, at_batch % 2


def across(blocks, z):
    got = [lax.dynamic_index_in_dim(blocks, z, 0, keepdims=False)]
    for k in range(1, 4):
        got.append(swap(lax.dynamic_index_in_dim(blocks, z ^ k, 0, keepdims=False), "seq", 2 * k))
    got = jnp.stack(got)
    return jnp.stack([lax.dynamic_index_in_dim(got, z ^ k, 0, keepdims=False) for k in range(4)])


def gather_sequence(own):
    z, y, x, c = place()
    micro, rows, width = own.shape
    slots = paired(own, swap(own, "batch", 1), c, 0)
    blocks = across(part_of(slots, c, 2, 2), z)[:, None]
    both = paired(blocks, swap(blocks, "seq", 1), y, 1)
    return paired(both, swap(both, "batch", 1), c, 3).reshape(8 * rows, width)


def scatter_sequence(parts):
    z, y, x, c = place()
    width = parts.shape[1]
    blocks = parts.reshape(4, 2, -1, width)
    blocks = halved(blocks, c, 2, "batch", 1).astype(bf16)
    blocks = halved(blocks, y, 1, "seq", 1).astype(bf16)[:, 0]
    slots = across(blocks, z)
    other = swap(part_of(slots, 1 - c, 2, 0), "batch", 1)
    return paired(part_of(slots, c, 2, 0), other, c, 1).astype(f32)


def total_over_heads(value):
    value = value + swap(value, "batch", 1)
    return value + swap(value, "seq", 1)


def reduce_up(pair):
    z, y, x, c = place()
    kept = halved(pair, x, 0, "batch", 2)[0].astype(bf16)
    kept = halved(kept, z // 2, 0, "seq", 4).astype(bf16)
    kept = halved(kept, z % 2, 0, "seq", 2).astype(bf16)
    other = swap(part_of(kept, 1 - y, 2, 0), "seq", 1)
    return paired(part_of(kept, y, 2, 0), other, y, 1).astype(f32)


def reduce_square(stack):
    z, y, x, c = place()
    kept = halved(stack, x, 2, "batch", 2).astype(bf16)
    kept = halved(kept, z // 2, 1, "seq", 4).astype(bf16)
    kept = halved(kept, z % 2, 1, "seq", 2).astype(bf16)
    other = swap(part_of(kept, 1 - y, 2, 1), "seq", 1)
    kept = paired(part_of(kept, y, 2, 1)[None], other[None], y, 0)
    other = swap(part_of(kept, 1 - c, 2, 3), "batch", 1)
    return paired(part_of(kept, c, 2, 3), other, c, 0).astype(f32)


def reduce_down(value):
    z, y, x, c = place()
    kept = halved(value, x, 1, "batch", 2).astype(bf16)
    kept = (kept.astype(f32) + swap(kept, "seq", 4).astype(f32)).astype(bf16)
    kept = kept.astype(f32) + swap(kept, "seq", 2).astype(f32)
    kept = jnp.where(z == 2 * c + y, kept, 0.0).astype(bf16)
    kept = halved(kept, y, 0, "seq", 1).astype(bf16)
    return halved(kept, c, 1, "batch", 1)


def over_ranges(value, count):
    size = lax.axis_size("seq")
    groups = [[first + 8 * k for k in range(count)] for first in range(8)]
    return lax.all_gather(value, "seq", axis_index_groups=groups) if size > 8 else value[None]


def state_before(state, norm, level, total, ranges):
    index = lax.axis_index("seq") // 8
    summary = (state, norm[0], level[0, 0], total)
    everything = jax.tree.map(lambda part: over_ranges(part, ranges), summary)
    before = state_identity(summary)
    for k in range(ranges - 1):
        new = combine_states(before, jax.tree.map(lambda part: part[k], everything))
        before = jax.tree.map(lambda a, b: jnp.where(k < index, a, b), new, before)
    return (
        before[0],
        jnp.broadcast_to(before[1], norm.shape),
        jnp.broadcast_to(before[2], level.shape),
    )


def cotangent_after(d_state, d_norm, keep, ranges):
    index = lax.axis_index("seq") // 8
    own = (d_state, d_norm)
    everything = jax.tree.map(lambda part: over_ranges(part, ranges), own)
    keeps = over_ranges(keep, ranges)
    after = jax.tree.map(jnp.zeros_like, own)
    for k in range(ranges - 1, 0, -1):
        new = jax.tree.map(lambda a, b: a[k] + keeps[k] * b, everything, after)
        after = jax.tree.map(lambda a, b: jnp.where(k > index, a, b), new, after)
    return after


def reduce_blocks(at, g_m, g_z, squares, g_down, heads):
    count, batch_count = lax.axis_size("seq"), lax.axis_size("batch")
    width, size = g_m.shape
    inner = heads * size
    up = jnp.zeros((width, 2 * inner), f32)
    up = lax.dynamic_update_slice_in_dim(up, g_m.astype(f32), at * size, 1)
    up = lax.dynamic_update_slice_in_dim(up, g_z.astype(f32), inner + at * size, 1)
    down = lax.dynamic_update_slice_in_dim(
        jnp.zeros((inner, width), f32), g_down.astype(f32), at * size, 0
    )
    full = [up, down]
    for g in squares:
        full.append(
            lax.dynamic_update_slice_in_dim(
                jnp.zeros((heads, size, size), f32), g.astype(f32)[None], at, 0
            )
        )
    blocks = tuple(to_device_blocks(g, count, batch_count) for g in full)
    pieces = lax.psum_scatter(blocks, ("seq", "batch"), scatter_dimension=0, tiled=True)
    s_up, s_down, s_query, s_key, s_value = tuple(p[0] for p in pieces)
    return s_up, jnp.stack([s_query, s_key, s_value], 1), s_down


def head_device(
    tokens, ln_gain, w_up, conv_w, conv_b, w_query, w_key, w_value, gate_w, gate_b,
    out_gain, skip_gain, w_down, d_out,
):
    z, y, x, c = place()
    at = 2 * c + y
    ranges = lax.axis_size("seq") // 8
    direct = ranges == 1 and lax.axis_size("batch") == 4
    head = jnp.reshape(at, (1,)).astype(jnp.int32)
    heads, size, _ = w_query.shape
    inner = heads * size
    conv_row = conv_b.reshape(1, inner)
    out_row = out_gain.reshape(1, inner)
    skip_row = skip_gain.reshape(1, inner)

    row_f = tokens[:, 0].astype(f32)
    centre = row_f - jnp.mean(row_f, axis=-1, keepdims=True)
    rstd = lax.rsqrt(jnp.mean(centre * centre, axis=-1, keepdims=True) + norm_epsilon)
    row_hat = centre * rstd
    normed = gather_sequence((row_hat * ln_gain).astype(bf16))
    cot = gather_sequence(d_out[:, 0])

    gate_own = lax.dynamic_index_in_dim(
        gate_w.reshape(3, heads, size, 8), at, 1, keepdims=False
    ).transpose(0, 2, 1)
    high = lax.reduce_precision(gate_own, 8, 7)
    middle = lax.reduce_precision(gate_own - high, 8, 7)
    low = lax.reduce_precision(gate_own - high - middle, 8, 7)
    gate_parts = jnp.concatenate([high, middle, low, jnp.zeros_like(high)], 1).astype(bf16)
    gate_pairs = (
        jnp.concatenate([high, high, high, middle, middle, low], 1)
        .astype(bf16)
        .transpose(1, 0, 2)
        .reshape(48, 3 * size)
    )

    first = () if ranges == 1 else (shifted(normed[-16:], "seq", 8),)
    mix, conv, q, k, v, gate_z, gates, *halo = lift(
        head, normed, w_up, w_query, w_key, w_value, conv_w, conv_row, gate_parts, *first
    )
    gates = total_over_heads(gates)
    gates = jnp.concatenate(
        [
            lax.dynamic_slice_in_dim(gates, at, 1, 0),
            lax.dynamic_slice_in_dim(gates, heads + at, 1, 0)
            + lax.dynamic_slice_in_dim(gate_b, at, 1, 0)[:, None],
        ]
    )
    first = ()
    if ranges > 1:
        first = (
            jnp.zeros((size, size), f32),
            jnp.zeros((8, size), f32),
            jnp.full((8, 128), floor_value, f32),
        )
        *_, state, norm, level = cell_forward(
            head, gates, q, k, v, conv, gate_z, out_row, skip_row, w_down, *first
        )
        total = jnp.sum(jax.nn.log_sigmoid(gates[1]))
        first = state_before(state, norm, level, total, ranges)
    part, head_normed, states, norms, weights, cols, rows, *last = cell_forward(
        head, gates, q, k, v, conv, gate_z, out_row, skip_row, w_down, *first
    )
    block_rows = (row_f + scatter_sequence(part)).astype(bf16)
    after = ()
    if ranges > 1:
        after = (jnp.zeros((size, size), f32), jnp.zeros((8, size), f32))
        *_, d_state, d_norm = cell_backward(
            head, rows, q, k, v, conv, gate_z, head_normed, states, norms, weights, cols, cot,
            out_row, skip_row, w_down, *after,
        )
        keep = jnp.exp(total + first[2][0, 0] - last[2][0, 0])
        after = cotangent_after(d_state, d_norm, keep, ranges)
    dq, dk, dv, dskip, dz, d_rows, g_down, g_gain, *_ = cell_backward(
        head, rows, q, k, v, conv, gate_z, head_normed, states, norms, weights, cols, cot,
        out_row, skip_row, w_down, *after,
    )
    if direct:
        s_down = reduce_down(g_down)
    index = jnp.arange(2 * heads)[:, None]
    d_gate = jnp.where(index == at, d_rows[0:1], jnp.where(index == heads + at, d_rows[1:2], 0.0))
    d_gate = total_over_heads(d_gate)
    first = ()
    if ranges > 1:
        *_, later = lower(
            head, d_gate, dq, dk, dv, dskip, dz, mix, conv, q, k, v, normed,
            w_query, w_key, w_value, w_up, conv_w, conv_row, gate_pairs,
            halo[0], jnp.zeros((8, size), f32),
        )
        first = (halo[0], shifted(later, "seq", -8))
    d_part, g_q, g_k, g_v, g_m, g_z, small, *_ = lower(
        head, d_gate, dq, dk, dv, dskip, dz, mix, conv, q, k, v, normed,
        w_query, w_key, w_value, w_up, conv_w, conv_row, gate_pairs, *first,
    )
    d_normed = scatter_sequence(d_part)
    scaled = d_normed * ln_gain
    d_row = rstd * (
        scaled
        - jnp.mean(scaled, axis=-1, keepdims=True)
        - row_hat * jnp.mean(scaled * row_hat, axis=-1, keepdims=True)
    )
    grad_rows = (d_out[:, 0].astype(f32) + d_row).astype(bf16)
    g_ln = jnp.sum(d_normed * row_hat, axis=(0, 1))
    if direct:
        s_up = reduce_up(jnp.stack([g_m, g_z]))
        squares = reduce_square(jnp.stack([g_q, g_k, g_v]))
    else:
        s_up, squares, s_down = reduce_blocks(at, g_m, g_z, (g_q, g_k, g_v), g_down, heads)
    bias = jnp.broadcast_to(jnp.sum(d_rows[1]), (1, size))
    small = jnp.concatenate([small[:29], g_gain[0:2], bias])[None]
    small = jnp.where(jnp.arange(heads)[:, None, None] == at, small, 0.0)
    small, s_ln = lax.psum((small, g_ln), ("seq", "batch"))
    s_gate_w = small[:, :24].reshape(heads, 3, 8, size).transpose(1, 0, 3, 2).reshape(3 * inner, 8)
    s_conv_w = small[:, 24:28].transpose(1, 0, 2).reshape(4, inner)
    return (
        block_rows[:, None],
        grad_rows[:, None],
        s_ln,
        s_up,
        s_conv_w,
        small[:, 28].reshape(inner),
        squares[:, 0],
        squares[:, 1],
        squares[:, 2],
        s_gate_w,
        small[:, 31, 0],
        small[:, 29].reshape(inner),
        small[:, 30].reshape(inner),
        s_down,
    )


def solution(mesh):
    placed = (P(None, "batch", "seq", None),) + (P(),) * 12 + (P(None, "batch", "seq", None),)
    return jax.shard_map(
        head_device,
        mesh=mesh,
        in_specs=placed,
        out_specs=(
            P(None, "batch", "seq", None),
            P(None, "batch", "seq", None),
            P(),
            P("seq", "batch"),
            P(),
            P(),
            P(None, "seq", "batch"),
            P(None, "seq", "batch"),
            P(None, "seq", "batch"),
            P(),
            P(),
            P(),
            P(),
            P("seq", "batch"),
        ),
        check_vma=False,
    )
```

```python
from functools import partial

import jax
import jax.numpy as jnp
from jax import lax
from jax.experimental import pallas as pl
from jax.experimental.pallas import tpu as pltpu
from jax.sharding import PartitionSpec as P

norm_epsilon = 1e-05
floor_value = -1e30


def shifted(value, axis, steps):
    count = lax.axis_size(axis)
    initial, last = (max(0, -steps), min(count, count - steps))
    return lax.ppermute(value, axis, [(source, source + steps) for source in range(initial, last)])


def combine_states(earlier, later):
    top = jnp.maximum(later[3] + earlier[2], later[2])
    keep_first = jnp.exp(later[3] + earlier[2] - top)
    keep_second = jnp.exp(later[2] - top)
    merged_c = keep_first[..., None, None] * earlier[0] + keep_second[..., None, None] * later[0]
    merged_n = keep_first[..., None] * earlier[1] + keep_second[..., None] * later[1]
    return (merged_c, merged_n, top, earlier[3] + later[3])


def state_identity(template):
    return (
        jnp.zeros_like(template[0]),
        jnp.zeros_like(template[1]),
        jnp.full_like(template[2], floor_value),
        jnp.zeros_like(template[3]),
    )


def head_output(hidden, out_gain, skip_gain, conv_out, gate_z):
    centre = hidden - jnp.mean(hidden, axis=-1, keepdims=True)
    spread = jnp.mean(centre * centre, axis=-1, keepdims=True)
    normed = centre * lax.rsqrt(spread + norm_epsilon)
    flat_out = normed.transpose(1, 0, 2).reshape(hidden.shape[1], -1) * out_gain
    return (flat_out + skip_gain * conv_out) * jax.nn.silu(gate_z)


def output_tail(
    query_f,
    key_f,
    value_f,
    gate_pre,
    conv_f,
    gate_z,
    out_gain,
    skip_gain,
    state_c,
    state_n,
    state_m,
):
    head_count = gate_pre.shape[1] // 2
    in_gate = gate_pre[:, :head_count].T
    log_forget = jax.nn.log_sigmoid(gate_pre[:, head_count:]).T
    hidden = cell_hidden(
        to_heads(query_f, head_count),
        to_heads(key_f, head_count),
        to_heads(value_f, head_count),
        in_gate,
        log_forget,
        state_c,
        state_n,
        state_m,
    )
    return head_output(hidden, out_gain, skip_gain, conv_f, gate_z)


def state_tail(key_f, value_f, gate_pre, state_c, state_n, state_m):
    head_count = gate_pre.shape[1] // 2
    in_gate = gate_pre[:, :head_count].T
    log_forget = jax.nn.log_sigmoid(gate_pre[:, head_count:]).T
    return cell_state(
        to_heads(key_f, head_count),
        to_heads(value_f, head_count),
        in_gate,
        log_forget,
        state_c,
        state_n,
        state_m,
    )


def to_device_blocks(grad_full, seq_count, batch_count):
    if grad_full.ndim == 2:
        rows, cols = grad_full.shape
        split = grad_full.reshape(seq_count, rows // seq_count, batch_count, cols // batch_count)
        return split.transpose(0, 2, 1, 3).reshape(
            seq_count * batch_count, rows // seq_count, cols // batch_count
        )
    heads, rows, cols = grad_full.shape
    split = grad_full.reshape(heads, seq_count, rows // seq_count, batch_count, cols // batch_count)
    return split.transpose(1, 3, 0, 2, 4).reshape(
        seq_count * batch_count, heads, rows // seq_count, cols // batch_count
    )


f32 = jnp.float32
bf16 = jnp.bfloat16
chunk_len = 256
wide_len = 512
vmem_bytes = 56 * 1024 * 1024


def mm(a, b):
    return lax.dot_general(a, b, (((1,), (0,)), ((), ())), preferred_element_type=f32)


def mm_nt(a, b):
    return lax.dot_general(a, b, (((1,), (1,)), ((), ())), preferred_element_type=f32)


def mm_tn(a, b):
    return lax.dot_general(a, b, (((0,), (0,)), ((), ())), preferred_element_type=f32)


def split_three(value):
    high = value.astype(bf16)
    rest = value - high.astype(f32)
    middle = rest.astype(bf16)
    low = (rest - middle.astype(f32)).astype(bf16)
    return high, middle, low


def conv_taps(ext, length):
    return [pltpu.roll(ext, 3 - j, 0)[8 : 8 + length] if j < 3 else ext[8 : 8 + length] for j in range(4)]


def lift_kernel(chained, head_ref, normed, w_mix, w_gate, w_q, w_k, w_v, conv_w, conv_b, gate_w, *refs):
    if chained:
        rows_before, *refs, halo_out, carry = refs
    else:
        *refs, carry = refs
    mix_out, conv_out, q_out, k_out, v_out, z_out, gate_out = refs
    length = normed.shape[0]

    @pl.when(pl.program_id(0) == 0)
    def _():
        if chained:
            mix_before = mm(rows_before[...], w_mix[...]).astype(bf16)
            halo_out[...] = mix_before
            carry[...] = mix_before[8:16].astype(f32)
        else:
            carry[...] = jnp.zeros_like(carry)

    rows = normed[...]
    mix = mm(rows, w_mix[...]).astype(bf16)
    mix_out[...] = mix
    z_out[...] = mm(rows, w_gate[...])
    mix_f = mix.astype(f32)
    taps = conv_taps(jnp.concatenate([carry[...], mix_f], axis=0), length)
    carry[...] = mix_f[length - 8 :]
    summed = conv_b[...]
    for j in range(4):
        summed = summed + conv_w[j : j + 1, :] * taps[j]
    conv = (summed * jax.nn.sigmoid(summed)).astype(bf16)
    conv_out[...] = conv
    q = mm(conv, w_q[0]).astype(bf16)
    k = mm(conv, w_k[0]).astype(bf16)
    v = mm(mix, w_v[0]).astype(bf16)
    q_out[...] = q
    k_out[...] = k
    v_out[...] = v
    parts = mm_nt(gate_w[0], q) + mm_nt(gate_w[1], k) + mm_nt(gate_w[2], v)
    gate_out[...] = parts[0:8] + parts[8:16] + parts[16:24]


def gate_rows(gates, causal, diagonal):
    in_row = gates[0:1, :]
    pre = gates[1:2, :]
    log_forget = jnp.minimum(pre, 0.0) - jnp.log1p(jnp.exp(-jnp.abs(pre)))
    run_col = jnp.sum(jnp.where(causal, log_forget, 0.0), axis=1, keepdims=True)
    run_row = jnp.sum(jnp.where(diagonal, run_col, 0.0), axis=0, keepdims=True)
    return in_row - run_row, run_col, log_forget


def masks(length):
    row = lax.broadcasted_iota(jnp.int32, (length, length), 0)
    col = lax.broadcasted_iota(jnp.int32, (length, length), 1)
    return row >= col, row == col


def cell_forward_kernel(
    chained, head_ref, gates, q_ref, k_ref, v_ref, conv_ref, z_ref, out_gain, skip_gain, w_down, *refs
):
    if chained:
        *first, part_out, normed_out, state_out, norm_out, weight_out, col_out, row_out = refs[:10]
        *final, state, norm, level = refs[10:]
    else:
        part_out, normed_out, state_out, norm_out, weight_out, col_out, row_out = refs[:7]
        state, norm, level = refs[7:]
    length = q_ref.shape[0]
    head_size = q_ref.shape[1]
    scale = head_size ** (-0.5)

    @pl.when(pl.program_id(0) == 0)
    def _():
        if chained:
            for ref, value in zip((state, norm, level), first):
                ref[...] = value[...]
        else:
            state[...] = jnp.zeros_like(state)
            norm[...] = jnp.zeros_like(norm)
            level[...] = jnp.full_like(level, floor_value)

    causal, diagonal = masks(length)
    a_row, run_col, log_forget = gate_rows(gates[...], causal, diagonal)
    before = level[0:1, 0:1]
    top = jnp.maximum(
        before, jnp.max(jnp.where(causal, a_row, floor_value), axis=1, keepdims=True)
    )
    decay = jnp.exp(jnp.where(causal, a_row - top, floor_value))
    q = q_ref[...]
    k = k_ref[...]
    v = v_ref[...]
    q_f = q.astype(f32)
    weights = decay * (mm_nt(q, k) * scale)
    weights_low = weights.astype(bf16)
    weight_out[...] = weights_low
    from_state = jnp.exp(before - top)
    state_low = state[...].astype(bf16)
    state_out[0] = state_low
    norm_row = norm[0:1, :]
    norm_out[0] = norm[...]
    numerator = mm(weights_low, v) + (from_state * scale) * mm(q, state_low)
    denominator = jnp.sum(weights, axis=1, keepdims=True) + (from_state * scale) * jnp.sum(
        q_f * norm_row, axis=1, keepdims=True
    )
    floor = jnp.exp(-(run_col + top))
    size = jnp.abs(denominator)
    inverse = 1.0 / jnp.maximum(size, floor)
    hidden = numerator * inverse
    centre = hidden - jnp.mean(hidden, axis=1, keepdims=True)
    spread = jnp.mean(centre * centre, axis=1, keepdims=True)
    rstd = lax.rsqrt(spread + norm_epsilon)
    normed = centre * rstd
    normed_out[...] = normed
    gate_z = z_ref[...]
    gated = (normed * out_gain[...] + skip_gain[...] * conv_ref[...].astype(f32)) * (
        gate_z * jax.nn.sigmoid(gate_z)
    )
    part_out[...] = mm(gated.astype(bf16), w_down[...]).astype(bf16)
    factor = jnp.where(
        size > floor,
        jnp.where(denominator > 0, 1.0, -1.0) * inverse * (norm_epsilon * rstd * rstd),
        0.0,
    )
    lane = lax.broadcasted_iota(jnp.int32, (length, 128), 1)
    packed = jnp.where(lane == 0, rstd, inverse)
    packed = jnp.where(lane == 2, from_state, packed)
    packed = jnp.where(lane == 3, top, packed)
    col_out[...] = jnp.where(lane == 4, factor, packed)
    sub = lax.broadcasted_iota(jnp.int32, (8, length), 0)
    row_out[...] = jnp.where(sub == 0, a_row, 1.0 - jnp.exp(log_forget))
    last = top[length - 1 : length, :]
    a_col = jnp.sum(jnp.where(diagonal, a_row, 0.0), axis=1, keepdims=True)
    weighted = k.astype(f32) * jnp.exp(a_col - last)
    keep = jnp.exp(before - last)
    state[...] = keep * state[...] + mm_tn(weighted.astype(bf16), v)
    norm[...] = keep * norm[...] + jnp.sum(weighted, axis=0, keepdims=True)
    level[...] = jnp.broadcast_to(run_col[length - 1 : length, :] + last, level.shape)
    if chained:
        for ref, value in zip(final, (state, norm, level)):
            ref[...] = value[...]


def cell_backward_kernel(
    chained, head_ref, rows_ref, q_ref, k_ref, v_ref, conv_ref, z_ref, normed_ref, state_ref, norm_ref,
    weight_ref, col_ref, cot_ref, out_gain, skip_gain, w_down, *refs
):
    if chained:
        *first, dq_out, dk_out, dv_out, dskip_out, dz_out, gate_out, g_down_out, g_gain_out = refs[:10]
        *final, d_state, d_norm, g_down, g_gain = refs[10:]
    else:
        dq_out, dk_out, dv_out, dskip_out, dz_out, gate_out, g_down_out, g_gain_out = refs[:8]
        d_state, d_norm, g_down, g_gain = refs[8:]
    length = q_ref.shape[0]
    head_size = q_ref.shape[1]
    scale = head_size ** (-0.5)

    @pl.when(pl.program_id(0) == 0)
    def _():
        if chained:
            d_state[...] = first[0][...]
            d_norm[...] = first[1][...]
        else:
            d_state[...] = jnp.zeros_like(d_state)
            d_norm[...] = jnp.zeros_like(d_norm)
        g_down[...] = jnp.zeros_like(g_down)
        g_gain[...] = jnp.zeros_like(g_gain)

    causal, diagonal = masks(length)
    rstd = col_ref[:, 0:1]
    inverse = col_ref[:, 1:2]
    from_state = col_ref[:, 2:3]
    top = col_ref[:, 3:4]
    factor = col_ref[:, 4:5]
    a_row = rows_ref[0:1, :]
    q = q_ref[...]
    k = k_ref[...]
    v = v_ref[...]
    q_f = q.astype(f32)
    k_f = k.astype(f32)
    conv = conv_ref[...].astype(f32)
    normed = normed_ref[...]
    gate_z = z_ref[...]
    cot = cot_ref[...]
    opened = jax.nn.sigmoid(gate_z)
    silu = gate_z * opened
    head_in = normed * out_gain[...] + skip_gain[...] * conv
    g_down[...] += mm_tn((head_in * silu).astype(bf16), cot)
    d_gated = mm_nt(cot, w_down[...])
    dz_out[...] = (d_gated * head_in * (opened * (1.0 + gate_z * (1.0 - opened)))).astype(bf16)
    d_head = d_gated * silu
    g_gain[0:1, :] += jnp.sum(d_head * normed, axis=0, keepdims=True)
    g_gain[1:2, :] += jnp.sum(d_head * conv, axis=0, keepdims=True)
    dskip_out[...] = skip_gain[...] * d_head
    d_hat = d_head * out_gain[...]
    along = jnp.sum(d_hat * normed, axis=1, keepdims=True)
    d_hidden = rstd * (
        d_hat - jnp.mean(d_hat, axis=1, keepdims=True) - normed * (along / head_size)
    )
    d_num = d_hidden * inverse
    d_den = -along * factor
    d_num_low = d_num.astype(bf16)
    decay = jnp.exp(jnp.where(causal, a_row - top, floor_value))
    d_scores = ((mm_nt(d_num_low, v) + d_den) * (decay * scale)).astype(bf16)
    through = from_state * scale
    dq_near = mm(d_scores, k)
    dq_far = (
        mm_nt((d_num * through).astype(bf16), state_ref[0])
        + (through * d_den) * norm_ref[0, 0:1, :]
    )
    last = top[length - 1 : length, :]
    keep = from_state[length - 1 : length, :]
    a_col = jnp.sum(jnp.where(diagonal, a_row, 0.0), axis=1, keepdims=True)
    key_weight = jnp.exp(a_col - last)
    d_state_low = d_state[...].astype(bf16)
    dk_near = mm_tn(d_scores, q)
    dk_far = key_weight * (mm_nt(v, d_state_low) + d_norm[0:1, :])
    dv = mm_tn(weight_ref[...], d_num_low) + mm((k_f * key_weight).astype(bf16), d_state_low)
    dq_out[...] = dq_near + dq_far
    dk_out[...] = dk_near + dk_far
    dv_out[...] = dv
    held = state_ref[0].astype(f32) * d_state[...]
    held = jnp.sum(jnp.sum(held, axis=0, keepdims=True) + norm_ref[0, 0:1, :] * d_norm[0:1, :])
    q_state = q_f * through
    d_state[...] = keep * d_state[...] + mm_tn(q_state.astype(bf16), d_num_low)
    d_norm[...] = keep * d_norm[...] + jnp.sum(q_state * d_den, axis=0, keepdims=True)
    q_dot = jnp.sum(q_f * (dq_near + dq_far), axis=1, keepdims=True)
    k_near = jnp.sum(k_f * dk_near, axis=1, keepdims=True)
    k_far = jnp.sum(k_f * dk_far, axis=1, keepdims=True)
    d_in = jnp.sum(jnp.where(diagonal, k_near + k_far, 0.0), axis=0, keepdims=True)
    d_log = jnp.sum(
        jnp.where(causal, q_dot - k_near, jnp.where(diagonal, 0.0, k_far)), axis=0, keepdims=True
    )
    d_log = d_log + keep * held
    sub = lax.broadcasted_iota(jnp.int32, (8, length), 0)
    d_pre = d_log * rows_ref[1:2, :]
    gate_out[...] = jnp.where(sub == 0, d_in, d_pre)
    g_gain[2:3, :] += jnp.broadcast_to(jnp.sum(d_pre, axis=1, keepdims=True), (1, head_size))

    @pl.when(pl.program_id(0) == pl.num_programs(0) - 1)
    def _():
        if chained:
            final[0][...] = d_state[...]
            final[1][...] = d_norm[...]
        half = g_down.shape[1] // 2
        g_down_out[0] = g_down[:, :half].astype(bf16)
        g_down_out[1] = g_down[:, half:].astype(bf16)
        g_gain_out[...] = g_gain[...]


def lower_kernel(
    chained, head_ref, d_gate, dq_ref, dk_ref, dv_ref, dskip_ref, dz_ref, mix_ref, mix_before, conv_ref,
    q_ref, k_ref, v_ref, normed, w_q, w_k, w_v, w_mix, w_gate, conv_w, conv_b, gate_w, g_gain, *refs
):
    if chained:
        first_halo, first_later, *refs = refs
        later_out = refs.pop(4)
    part_out, square_out, up_out, small_out = refs[:4]
    g_q, g_k, g_v, g_m, g_z, g_small, later = refs[4:]
    length = q_ref.shape[0]
    step = pl.program_id(0)

    @pl.when(step == 0)
    def _():
        for ref in (g_q, g_k, g_v, g_m, g_z, g_small, later):
            ref[...] = jnp.zeros_like(ref)
        if chained:
            later[...] = first_later[...]

    high, middle, low = split_three(d_gate[...])
    left = jnp.concatenate([high, middle, low, high, middle, high], axis=0)
    d_joined = mm_tn(left, gate_w[...])
    size = q_ref.shape[1]
    query_low = (dq_ref[...] + d_joined[:, :size]).astype(bf16)
    key_low = (dk_ref[...] + d_joined[:, size : 2 * size]).astype(bf16)
    value_low = (dv_ref[...] + d_joined[:, 2 * size :]).astype(bf16)
    conv = conv_ref[...]
    mix = mix_ref[...]
    g_q[...] += mm_tn(conv, query_low)
    g_k[...] += mm_tn(conv, key_low)
    g_v[...] += mm_tn(mix, value_low)
    three = jnp.concatenate([high, middle, low], axis=0)
    for at, ref in enumerate((q_ref, k_ref, v_ref)):
        got = mm(three, ref[...])
        g_small[8 * at : 8 * at + 8, :] += got[0:8] + got[8:16] + got[16:24]
    d_conv = dskip_ref[...] + mm_nt(query_low, w_q[0]) + mm_nt(key_low, w_k[0])
    halo = mix_before[8:16, :].astype(f32)
    edge = first_halo[8:16, :].astype(f32) if chained else 0.0
    halo = jnp.where(step == pl.num_programs(0) - 1, edge, halo)
    taps = conv_taps(jnp.concatenate([halo, mix.astype(f32)], axis=0), length)
    summed = conv_b[...]
    for j in range(4):
        summed = summed + conv_w[j : j + 1, :] * taps[j]
    opened = jax.nn.sigmoid(summed)
    d_summed = d_conv * (opened * (1.0 + summed * (1.0 - opened)))
    for j in range(4):
        g_small[24 + j : 25 + j, :] += jnp.sum(d_summed * taps[j], axis=0, keepdims=True)
    g_small[28:29, :] += jnp.sum(d_summed, axis=0, keepdims=True)
    ext = jnp.concatenate([d_summed, later[...]], axis=0)
    later[...] = d_summed[0:8]
    d_mix = conv_w[3:4, :] * d_summed
    for j in range(3):
        d_mix = d_mix + conv_w[j : j + 1, :] * pltpu.roll(ext, length + 8 - (3 - j), 0)[0:length]
    d_mix = (d_mix + mm_nt(value_low, w_v[0])).astype(bf16)
    d_z = dz_ref[...]
    rows = normed[...]
    g_m[...] += mm_tn(rows, d_mix)
    g_z[...] += mm_tn(rows, d_z)
    d_normed = mm_nt(d_mix, w_mix[...]) + mm_nt(d_z, w_gate[...])
    part_out[...] = d_normed.astype(bf16)
    g_ln = jnp.sum(d_normed * rows.astype(f32), axis=0, keepdims=True)
    g_small[32:33, :] += g_ln[:, :size]
    g_small[33:34, :] += g_ln[:, size:]

    @pl.when(step == pl.num_programs(0) - 1)
    def _():
        half = size // 2
        for at, ref in enumerate((g_q, g_k, g_v)):
            square_out[0, :, half * at : half * at + half] = ref[:, :half].astype(bf16)
            square_out[1, :, half * at : half * at + half] = ref[:, half:].astype(bf16)
        up_out[0] = g_m[...].astype(bf16)
        up_out[1] = g_z[...].astype(bf16)
        g_small[29:32, :] = g_gain[0:3, :]
        small_out[...] = g_small[...]
        if chained:
            later_out[...] = later[...]


def struct(shape, dtype):
    return jax.ShapeDtypeStruct(shape, dtype)


def run_kernel(body, head, grid, inputs, in_specs, outs, out_specs, scratch, name, flops, nbytes):
    return pl.pallas_call(
        body,
        grid_spec=pltpu.PrefetchScalarGridSpec(
            num_scalar_prefetch=1,
            grid=(grid,),
            in_specs=in_specs,
            out_specs=out_specs,
            scratch_shapes=scratch,
        ),
        out_shape=outs,
        compiler_params=pltpu.CompilerParams(
            dimension_semantics=("arbitrary",), vmem_limit_bytes=vmem_bytes
        ),
        cost_estimate=pl.CostEstimate(flops=flops, bytes_accessed=nbytes, transcendentals=0),
        name=name,
    )(head, *inputs)


def fixed(shape, *index):
    return pl.BlockSpec(shape, lambda g, h: tuple(h[0] if i == "h" else i for i in index))


def lift(head, normed, w_up, w_query, w_key, w_value, conv_w, conv_b, gate_parts, *first):
    tokens, width = normed.shape
    heads, size, _ = w_query.shape
    length = wide_len
    by_row = lambda cols: pl.BlockSpec((length, cols), lambda g, h: (g, 0))
    weight = pl.BlockSpec((1, size, size), lambda g, h: (h[0], 0, 0))
    chained = len(first) > 0
    halo = [pl.BlockSpec((16, size), lambda g, h: (0, 0))] * chained
    return run_kernel(
        partial(lift_kernel, chained), head, tokens // length,
        (normed, w_up, w_up, w_query, w_key, w_value, conv_w, conv_b, gate_parts, *first),
        [
            by_row(width),
            pl.BlockSpec((width, size), lambda g, h: (0, h[0])),
            pl.BlockSpec((width, size), lambda g, h: (0, heads + h[0])),
            weight, weight, weight,
            pl.BlockSpec((4, size), lambda g, h: (0, h[0])),
            pl.BlockSpec((1, size), lambda g, h: (0, h[0])),
            pl.BlockSpec(gate_parts.shape, lambda g, h: (0, 0, 0)),
        ]
        + [pl.BlockSpec((16, width), lambda g, h: (0, 0))] * chained,
        [struct((tokens, size), bf16)] * 5
        + [struct((tokens, size), f32), struct((8, tokens), f32)]
        + [struct((16, size), bf16)] * chained,
        [by_row(size)] * 6 + [pl.BlockSpec((8, length), lambda g, h: (0, g))] + halo,
        [pltpu.VMEM((8, size), f32)],
        "lift", 2 * tokens * size * (2 * width + 3 * size), 24 * 2**20,
    )


def cell_forward(head, gates, q, k, v, conv, gate_z, out_gain, skip_gain, w_down, *first):
    tokens, size = q.shape
    width = w_down.shape[1]
    length = chunk_len
    steps = tokens // length
    by_row = lambda cols: pl.BlockSpec((length, cols), lambda g, h: (g, 0))
    gain = pl.BlockSpec((1, size), lambda g, h: (0, h[0]))
    carried = [struct(value.shape, f32) for value in first]
    carried_specs = [pl.BlockSpec(value.shape, lambda g, h: (0, 0)) for value in first]
    return run_kernel(
        partial(cell_forward_kernel, len(first) > 0), head, steps,
        (gates, q, k, v, conv, gate_z, out_gain, skip_gain, w_down, *first),
        [pl.BlockSpec((2, length), lambda g, h: (0, g))]
        + [by_row(size)] * 5
        + [gain, gain, pl.BlockSpec((size, width), lambda g, h: (h[0], 0))]
        + carried_specs,
        [
            struct((tokens, width), bf16),
            struct((tokens, size), f32),
            struct((steps, size, size), bf16),
            struct((steps, 8, size), f32),
            struct((tokens, length), bf16),
            struct((tokens, 128), f32),
            struct((8, tokens), f32),
        ]
        + carried,
        [
            by_row(width),
            by_row(size),
            pl.BlockSpec((1, size, size), lambda g, h: (g, 0, 0)),
            pl.BlockSpec((1, 8, size), lambda g, h: (g, 0, 0)),
            by_row(length),
            by_row(128),
            pl.BlockSpec((8, length), lambda g, h: (0, g)),
        ]
        + carried_specs,
        [pltpu.VMEM((size, size), f32), pltpu.VMEM((8, size), f32), pltpu.VMEM((8, 128), f32)],
        "cell_forward", 2 * tokens * size * (2 * length + 2 * size + width), 28 * 2**20,
    )


def cell_backward(
    head, rows, q, k, v, conv, gate_z, normed, states, norms, weights, cols, cot,
    out_gain, skip_gain, w_down, *first,
):
    tokens, size = q.shape
    width = w_down.shape[1]
    length = chunk_len
    steps = tokens // length
    end = steps - 1
    by_row = lambda n: pl.BlockSpec((length, n), lambda g, h: (end - g, 0))
    gain = pl.BlockSpec((1, size), lambda g, h: (0, h[0]))
    whole = lambda shape: pl.BlockSpec(shape, lambda g, h: (0, 0))
    carried = [struct(value.shape, f32) for value in first]
    carried_specs = [whole(value.shape) for value in first]
    return run_kernel(
        partial(cell_backward_kernel, len(first) > 0), head, steps,
        (rows, q, k, v, conv, gate_z, normed, states, norms, weights, cols, cot,
         out_gain, skip_gain, w_down, *first),
        [pl.BlockSpec((8, length), lambda g, h: (0, end - g))]
        + [by_row(size)] * 6
        + [
            pl.BlockSpec((1, size, size), lambda g, h: (end - g, 0, 0)),
            pl.BlockSpec((1, 8, size), lambda g, h: (end - g, 0, 0)),
            by_row(length),
            by_row(128),
            by_row(width),
            gain, gain,
            pl.BlockSpec((size, width), lambda g, h: (h[0], 0)),
        ]
        + carried_specs,
        [struct((tokens, size), f32)] * 4
        + [
            struct((tokens, size), bf16),
            struct((8, tokens), f32),
            struct((2, size, width // 2), bf16),
            struct((8, size), f32),
        ]
        + carried,
        [by_row(size)] * 5
        + [
            pl.BlockSpec((8, length), lambda g, h: (0, end - g)),
            pl.BlockSpec((2, size, width // 2), lambda g, h: (0, 0, 0)),
            whole((8, size)),
        ]
        + carried_specs,
        [
            pltpu.VMEM((size, size), f32),
            pltpu.VMEM((8, size), f32),
            pltpu.VMEM((size, width), f32),
            pltpu.VMEM((8, size), f32),
        ],
        "cell_backward", 2 * tokens * size * (4 * length + 4 * size + 2 * width), 44 * 2**20,
    )


def lower(
    head, d_gate, dq, dk, dv, dskip, dz, mix, conv, q, k, v, normed,
    w_query, w_key, w_value, w_up, conv_w, conv_b, gate_pairs, g_gain, *first,
):
    tokens, size = q.shape
    width = normed.shape[1]
    heads = w_query.shape[0]
    length = wide_len
    steps = tokens // length
    end = steps - 1
    by_row = lambda n: pl.BlockSpec((length, n), lambda g, h: (end - g, 0))
    weight = pl.BlockSpec((1, size, size), lambda g, h: (h[0], 0, 0))
    whole = lambda shape: pl.BlockSpec(shape, lambda g, h: (0, 0))
    chained = len(first) > 0
    return run_kernel(
        partial(lower_kernel, chained), head, steps,
        (d_gate, dq, dk, dv, dskip, dz, mix, mix, conv, q, k, v, normed,
         w_query, w_key, w_value, w_up, w_up, conv_w, conv_b, gate_pairs, g_gain, *first),
        [pl.BlockSpec((8, length), lambda g, h: (0, end - g))]
        + [by_row(size)] * 6
        + [
            pl.BlockSpec(
                (16, size),
                lambda g, h: (jnp.maximum((end - g) * (length // 16) - 1, 0), 0),
            )
        ]
        + [by_row(size)] * 4
        + [by_row(width), weight, weight, weight]
        + [
            pl.BlockSpec((width, size), lambda g, h: (0, h[0])),
            pl.BlockSpec((width, size), lambda g, h: (0, heads + h[0])),
            pl.BlockSpec((4, size), lambda g, h: (0, h[0])),
            pl.BlockSpec((1, size), lambda g, h: (0, h[0])),
            whole(gate_pairs.shape),
            whole(g_gain.shape),
        ]
        + [whole(value.shape) for value in first],
        [struct((tokens, width), bf16)]
        + [struct((2, size, 3 * size // 2), bf16), struct((2, width, size), bf16)]
        + [struct((40, size), f32)]
        + [struct((8, size), f32)] * chained,
        [by_row(width)]
        + [
            pl.BlockSpec((2, size, 3 * size // 2), lambda g, h: (0, 0, 0)),
            pl.BlockSpec((2, width, size), lambda g, h: (0, 0, 0)),
        ]
        + [whole((40, size))]
        + [whole((8, size))] * chained,
        [pltpu.VMEM((size, size), f32)] * 3
        + [pltpu.VMEM((width, size), f32)] * 2
        + [pltpu.VMEM((40, size), f32), pltpu.VMEM((8, size), f32)],
        "lower", 2 * tokens * size * (6 * size + 4 * width), 48 * 2**20,
    )
MESH_ID = pl.DeviceIdType.MESH


def where_am_i():
    at_seq, at_batch = lax.axis_index("seq"), lax.axis_index("batch")
    within = lax.rem(at_seq, 8)
    first = at_seq - within
    return first, within // 2, lax.rem(within, 2), at_batch // 2, lax.rem(at_batch, 2)


def greet(others):
    barrier = pltpu.get_barrier_semaphore()
    for other in others:
        pl.semaphore_signal(barrier, 1, device_id=other, device_id_type=MESH_ID)
    pl.semaphore_wait(barrier, len(others))


def remote(src, dst, sent, landed, device):
    return pltpu.make_async_remote_copy(src, dst, sent, landed, device_id=device, device_id_type=MESH_ID)


def normalize(rows):
    centre = rows - jnp.mean(rows, axis=-1, keepdims=True)
    rstd = lax.rsqrt(jnp.mean(centre * centre, axis=-1, keepdims=True) + norm_epsilon)
    return centre * rstd, rstd


def gather_kernel(
    rows_ref, gain_ref, out_ref, staged, kept, z_sent, z_landed, y_sent, y_landed, c_sent, c_landed
):
    first, z, y, x, c = where_am_i()
    parts = z_landed.shape[1]
    block = rows_ref.shape[1]
    size = block // parts

    def device(zz, yy, cc):
        return (first + 2 * zz + yy, 2 * x + cc)

    def rows(zz, yy, part):
        return out_ref.at[pl.ds(pl.multiple_of((2 * zz + yy) * block + part * size, size), size)]

    others = [device(lax.rem(z + k, 4), y, c) for k in range(1, 4)]
    greet(others + [device(z, 1 - y, c), device(z, y, 1 - c)])
    enters = z // 2 == c

    def to_column(m, part):
        return remote(
            staged.at[m, pl.ds(part * size, size)], rows(z, y, part),
            z_sent.at[m, part], z_landed.at[z, part], device(2 * c + m, y, c),
        )

    def keep(m, part):
        return pltpu.make_async_copy(
            staged.at[m, pl.ds(part * size, size)], rows(z, y, part), kept.at[part]
        )

    def from_column(zz, part):
        return remote(
            rows(zz, y, part), rows(zz, y, part), z_sent.at[0, part], z_landed.at[zz, part],
            device(zz, y, c),
        )

    def to_row(zz, k, part):
        return remote(
            rows(zz, y, part), rows(zz, y, part), y_sent.at[k, part], y_landed.at[zz, part],
            device(z, 1 - y, c),
        )

    def from_row(zz, k, part):
        return remote(
            rows(zz, 1 - y, part), rows(zz, 1 - y, part), y_sent.at[k, part],
            y_landed.at[zz, part], device(z, 1 - y, c),
        )

    def to_core(zz, yy, k, part):
        return remote(
            rows(zz, yy, part), rows(zz, yy, part), c_sent.at[k, part],
            c_landed.at[2 * zz + yy, part], device(z, y, 1 - c),
        )

    for m in range(2):
        staged[m] = (normalize(rows_ref[m].astype(f32))[0] * gain_ref[...]).astype(bf16)
        away = 2 * c + m != z
        for part in range(parts):
            pl.when(away)(lambda m=m, part=part: to_column(m, part).start())
            pl.when(jnp.logical_not(away))(lambda m=m, part=part: keep(m, part).start())

    @pl.when(enters)
    def _():
        for k in range(4):
            zz = lax.rem(z + k, 4)
            for part in range(parts):
                if k == 0:
                    keep(0, part).wait()
                else:
                    from_column(zz, part).wait_recv()
                to_row(zz, k, part).start()
                to_core(zz, y, k, part).start()
        for k in range(4):
            zz = lax.rem(z + k, 4)
            for part in range(parts):
                from_row(zz, k, part).wait_recv()
                to_core(zz, 1 - y, 4 + k, part).start()
        for k in range(4):
            zz = lax.rem(z + k, 4)
            for part in range(parts):
                to_row(zz, k, part).wait_send()
                to_core(zz, y, k, part).wait_send()
                to_core(zz, 1 - y, 4 + k, part).wait_send()

    @pl.when(jnp.logical_not(enters))
    def _():
        for zz in range(4):
            for yy in range(2):
                for part in range(parts):
                    to_core(zz, yy, 0, part).wait_recv()

    for m in range(2):
        for part in range(parts):
            pl.when(2 * c + m != z)(lambda m=m, part=part: to_column(m, part).wait_send())


def gather_normed(rows, gain):
    micro, block, width = rows.shape
    parts = 2
    sems = [(parts,), (2, parts), (4, parts), (4, parts), (4, parts), (8, parts), (8, parts)]
    return pl.pallas_call(
        gather_kernel,
        out_shape=struct((8 * block, width), bf16),
        in_specs=[pl.BlockSpec(memory_space=pltpu.VMEM)] * 2,
        out_specs=pl.BlockSpec(memory_space=pl.ANY),
        scratch_shapes=[pltpu.VMEM((micro, block, width), bf16)]
        + [pltpu.SemaphoreType.DMA(shape) for shape in sems],
        compiler_params=pltpu.CompilerParams(
            collective_id=0, has_side_effects=True, vmem_limit_bytes=32 * 2**20
        ),
        name="gather_normed",
    )(rows, gain)


def finish_kernel(
    part_ref, up_ref, square_ref, down_ref, small_ref, rows_ref, cot_ref, gain_ref,
    grad_out, up_out, query_out, key_out, value_out, down_out, small_out,
    own, from_core, to_row, from_row, to_owner, owned,
    up_x, up_sum, up_send, up_left, up_right, sq_x, sq_sum, sq_send, sq_left, sq_right,
    dn_x, dn_sum, dn_send, dn_left, dn_right,
    up_go, up_got, sq_go, sq_got, dn_go, dn_got, small_x, small_sum, small_z, small_all,
    own_sem, c_sent, c_landed, y_sent, y_landed, o_sent, o_landed,
    x_sent, x_landed, r_sent, r_landed, l_sent, l_landed,
    up_sem, sq_sent, sq_landed, dn_sent, dn_landed, sx_sem, sz_sent, sz_landed, sh_sent, sh_landed,
):
    first, z, y, x, c = where_am_i()
    head = 2 * c + y

    def device(zz, yy, cc, xx=x):
        return (first + 2 * zz + yy, 2 * xx + cc)

    around = [lax.rem(z + k, 4) for k in range(1, 4)]
    group = [(1 - y, c), (y, 1 - c), (1 - y, 1 - c)]
    others = [device(z, yy, cc) for yy, cc in group] + [device(z, y, c, 1 - x)]
    for zz in around:
        others += [device(zz, yy, cc) for yy, cc in [(y, c)] + group]
    greet(others)

    sources = (up_ref, square_ref, down_ref)
    from_x = (up_x, sq_x, dn_x)
    totals = (up_sum, sq_sum, dn_sum)
    sends = (up_send, sq_send, dn_send)
    from_left = (up_left, sq_left, dn_left)
    from_right = (up_right, sq_right, dn_right)
    half = own.shape[1]

    def to_x(p, zz):
        size = totals[p].shape[1]
        here = pl.ds(zz * size, size)
        return remote(
            sources[p].at[1 - x, here], from_x[p].at[here], x_sent.at[p, zz], x_landed.at[p, zz],
            device(z, y, c, 1 - x),
        )

    def block(zz, yy, cc):
        start = ((2 * zz + yy) * 2 + cc) * half
        return part_ref.at[pl.ds(pl.multiple_of(start, half), half)]

    def load(zz, yy, k):
        return pltpu.make_async_copy(block(zz, yy, c), own.at[k], own_sem.at[k])

    def to_c(zz, yy, k):
        return remote(
            block(zz, yy, 1 - c), from_core.at[2 * zz + yy], c_sent.at[k],
            c_landed.at[2 * zz + yy], device(z, y, 1 - c),
        )

    def to_y(zz):
        return remote(
            to_row.at[zz], from_row.at[zz], y_sent.at[zz], y_landed.at[zz], device(z, 1 - y, c)
        )

    def to_o(zz):
        return remote(
            to_owner.at[zz], owned.at[lax.rem(z, 2), c], o_sent.at[zz],
            o_landed.at[lax.rem(z, 2), c], device(zz, y, z // 2),
        )

    def right(p, zz):
        return remote(
            sends[p].at[zz], from_left[p].at[zz - 1], r_sent.at[p, zz - 1],
            r_landed.at[p, zz - 1], device(lax.rem(z + 1, 4), y, c),
        )

    def left(p, zz):
        return remote(
            sends[p].at[zz], from_right[p].at[zz], l_sent.at[p, zz], l_landed.at[p, zz],
            device(lax.rem(z + 3, 4), y, c),
        )

    order = (3, 0, 2, 1)
    small_to_x = remote(
        small_ref, small_x, sx_sem.at[0], sx_sem.at[1], device(z, y, c, 1 - x)
    )
    small_to_x.start()
    for p in range(3):
        for zz in order:
            to_x(p, zz).start()
    for yy, at in ((1 - y, 0), (y, 4)):
        for zz in range(4):
            to_c(zz, yy, at + zz).start()
            load(zz, yy, at + zz).start()

    def core_sum(zz, yy, k):
        load(zz, yy, k).wait()
        to_c(zz, yy, k).wait_recv()
        return (own[k].astype(f32) + from_core[2 * zz + yy].astype(f32)).astype(bf16)

    for zz in range(4):
        to_row[zz] = core_sum(zz, 1 - y, zz)
        to_y(zz).start()
    for zz in range(4):
        own[4 + zz] = core_sum(zz, y, 4 + zz)

    def row_step(zz):
        to_y(zz).wait_recv()
        to_owner[zz] = (own[4 + zz].astype(f32) + from_row[zz].astype(f32)).astype(bf16)
        stays = jnp.logical_and(z == zz, z // 2 == c)

        @pl.when(stays)
        def _():
            owned[lax.rem(z, 2), c] = to_owner[zz]

        pl.when(jnp.logical_not(stays))(lambda: to_o(zz).start())

    def x_step(p, zz):
        size = totals[p].shape[1]
        here = pl.ds(zz * size, size)
        to_x(p, zz).wait_recv()
        totals[p][zz] = (
            sources[p][x, here].astype(f32) + from_x[p][here].astype(f32)
        ).astype(bf16)

    def chain_step(p, zz):
        if zz > 0:

            @pl.when(z == 0)
            def _():
                sends[p][zz] = totals[p][zz]
                right(p, zz).start()

        if zz > 1:

            @pl.when(jnp.logical_and(z > 0, z < zz))
            def _():
                right(p, zz).wait_recv()
                sends[p][zz] = (
                    totals[p][zz].astype(f32) + from_left[p][zz - 1].astype(f32)
                ).astype(bf16)
                right(p, zz).start()

        if zz < 3:

            @pl.when(z == 3)
            def _():
                sends[p][zz] = totals[p][zz]
                left(p, zz).start()

        if zz < 2:

            @pl.when(jnp.logical_and(z < 3, z > zz))
            def _():
                left(p, zz).wait_recv()
                sends[p][zz] = (
                    totals[p][zz].astype(f32) + from_right[p][zz].astype(f32)
                ).astype(bf16)
                left(p, zz).start()

    def end_step(p, use):
        for zz in range(4):

            @pl.when(z == zz)
            def _():
                value = totals[p][zz].astype(f32)
                if zz > 0:
                    right(p, zz).wait_recv()
                    value = value + from_left[p][zz - 1].astype(f32)
                if zz < 3:
                    left(p, zz).wait_recv()
                    value = value + from_right[p][zz].astype(f32)
                use(value)

    def passed(p):
        for zz in range(4):
            if zz > 0:
                pl.when(z < zz)(lambda: right(p, zz).wait_send())
            if zz < 3:
                pl.when(z > zz)(lambda: left(p, zz).wait_send())

    for p in range(3):
        row_step(p)
        for zz in order:
            x_step(p, zz)
            chain_step(p, zz)
    row_step(3)

    small_to_x.wait_recv()
    small_sum[...] = small_ref[...] + small_x[...]
    small_z[z] = small_sum[...]

    def small_to_z(k):
        return remote(
            small_sum, small_z.at[z], sz_sent.at[k], sz_landed.at[z], device(around[k], y, c)
        )

    def small_from_z(k):
        return remote(
            small_sum, small_z.at[around[k]], sz_sent.at[k], sz_landed.at[around[k]],
            device(around[k], y, c),
        )

    for k in range(3):
        small_to_z(k).start()

    rows = up_go.shape[0]
    cols = up_go.shape[1]

    def use_up(value):
        mine = jnp.where(y == 0, value[:rows], value[rows:])
        up_go[...] = jnp.where(y == 0, value[rows:], value[:rows]).astype(bf16)
        for yy in range(2):

            @pl.when(y == yy)
            def _():
                up_out[:, cols * yy : cols * yy + cols] = mine

    end_step(0, use_up)
    up_to_y = remote(up_go, up_got, up_sem.at[0], up_sem.at[1], device(z, 1 - y, c))
    up_to_y.start()

    for k in range(3):
        small_from_z(k).wait_recv()
    total = small_z[0]
    for zz in range(1, 4):
        total = total + small_z[zz]
    small_all[head] = total

    def to_group(k, src, dst, sent, landed):
        yy, cc = group[k]
        return remote(src, dst, sent.at[k], landed, device(z, yy, cc))

    def small_to_head(k):
        return to_group(k, small_all.at[head], small_all.at[head], sh_sent, sh_landed.at[head])

    def small_from_head(k):
        at = 2 * group[k][1] + group[k][0]
        return to_group(k, small_all.at[at], small_all.at[at], sh_sent, sh_landed.at[at])

    for k in range(3):
        small_to_head(k).start()

    tall, wide = sq_got.shape[1], sq_got.shape[2] // 3

    def use_square(value):
        for yy in range(2):
            for cc in range(2):
                for a in range(3):
                    sq_go[yy, cc, :, wide * a : wide * a + wide] = value[
                        tall * yy : tall * yy + tall,
                        (2 * a + cc) * wide : (2 * a + cc) * wide + wide,
                    ].astype(bf16)

    end_step(1, use_square)
    sq_got[head] = sq_go[y, c]

    def square_to(k):
        yy, cc = group[k]
        return to_group(k, sq_go.at[yy, cc], sq_got.at[head], sq_sent, sq_landed.at[head])

    def square_from(k):
        at = 2 * group[k][1] + group[k][0]
        return to_group(k, sq_go.at[0, 0], sq_got.at[at], sq_sent, sq_landed.at[at])

    for k in range(3):
        square_to(k).start()

    span = dn_go.shape[2]

    def use_down(value):
        for cc in range(2):
            dn_go[cc] = value[:, span * cc : span * cc + span].astype(bf16)

    end_step(2, use_down)

    def down_to(cc):
        return remote(
            dn_go.at[cc], dn_got.at[lax.rem(z, 2)], dn_sent.at[cc], dn_landed.at[lax.rem(z, 2)],
            device(head, z // 2, cc),
        )

    def down_from(k):
        return remote(
            dn_go.at[0], dn_got.at[k], dn_sent.at[0], dn_landed.at[k],
            device(2 * y + k, lax.rem(z, 2), z // 2),
        )

    home = jnp.logical_and(head == z, z // 2 == y)
    for cc in range(2):
        stays = jnp.logical_and(home, c == cc)

        @pl.when(stays)
        def _():
            dn_got[lax.rem(z, 2)] = dn_go[cc]

        pl.when(jnp.logical_not(stays))(lambda: down_to(cc).start())

    for m in range(2):
        for cc in range(2):
            own_part = jnp.logical_and(2 * c + m == z, c == cc)
            landed = remote(
                to_owner.at[0], owned.at[m, cc], o_sent.at[0], o_landed.at[m, cc],
                device(2 * c + m, y, cc),
            )
            pl.when(jnp.logical_not(own_part))(lambda landed=landed: landed.wait_recv())
        for cc in range(2):
            here = pl.ds(cc * half, half)
            row_hat, rstd = normalize(rows_ref[m, here].astype(f32))
            scaled = owned[m, cc].astype(f32) * gain_ref[...]
            d_row = rstd * (
                scaled
                - jnp.mean(scaled, axis=-1, keepdims=True)
                - row_hat * jnp.mean(scaled * row_hat, axis=-1, keepdims=True)
            )
            grad_out[m, here] = (cot_ref[m, here].astype(f32) + d_row).astype(bf16)

    up_to_y.wait_recv()
    for yy in range(2):

        @pl.when(y == yy)
        def _():
            up_out[:, cols * (1 - yy) : cols * (1 - yy) + cols] = up_got[...].astype(f32)

    for k in range(3):
        small_from_head(k).wait_recv()
    small_out[...] = small_all[...]
    for k in range(3):
        square_from(k).wait_recv()
    for a, ref in enumerate((query_out, key_out, value_out)):
        ref[...] = sq_got[:, :, wide * a : wide * a + wide].astype(f32)
    for k in range(2):
        mine = jnp.logical_and(home, jnp.logical_and(lax.rem(z, 2) == k, z // 2 == c))
        pl.when(jnp.logical_not(mine))(lambda: down_from(k).wait_recv())
        tall = dn_got.shape[1]
        down_out[tall * k : tall * k + tall] = dn_got[k].astype(f32)

    small_to_x.wait_send()
    up_to_y.wait_send()
    for p in range(3):
        for zz in range(4):
            to_x(p, zz).wait_send()
        passed(p)
    for yy, at in ((1 - y, 0), (y, 4)):
        for zz in range(4):
            to_c(zz, yy, at + zz).wait_send()
    for zz in range(4):
        to_y(zz).wait_send()
        stays = jnp.logical_and(z == zz, z // 2 == c)
        pl.when(jnp.logical_not(stays))(lambda: to_o(zz).wait_send())
    for k in range(3):
        small_to_z(k).wait_send()
        small_to_head(k).wait_send()
        square_to(k).wait_send()
    for cc in range(2):
        stays = jnp.logical_and(home, c == cc)
        pl.when(jnp.logical_not(stays))(lambda: down_to(cc).wait_send())


def finish(part, up, square, down, small, rows, cot, gain):
    micro, block, width = rows.shape
    half = block // 2
    size = down.shape[1]
    lines = small.shape[0]
    scratch = [
        ((8, half, width), bf16), ((8, half, width), bf16), ((4, half, width), bf16),
        ((4, half, width), bf16), ((4, half, width), bf16), ((2, 2, half, width), bf16),
    ]
    for piece in (up, square, down):
        _, tall, wide = piece.shape
        scratch += [((tall, wide), bf16), ((4, tall // 4, wide), bf16), ((4, tall // 4, wide), bf16)]
        scratch += [((3, tall // 4, wide), bf16)] * 2
    scratch += [
        ((width // 8, size), bf16), ((width // 8, size), bf16),
        ((2, 2, size // 8, 3 * size // 4), bf16), ((4, size // 8, 3 * size // 4), bf16),
        ((2, size // 4, width // 4), bf16), ((2, size // 4, width // 4), bf16),
        ((lines, size), f32), ((lines, size), f32), ((4, lines, size), f32), ((4, lines, size), f32),
    ]
    sems = [
        (8,), (8,), (8,), (4,), (4,), (4,), (2, 2), (3, 4), (3, 4), (3, 3), (3, 3), (3, 3), (3, 3),
        (2,), (3,), (4,), (2,), (2,), (2,), (3,), (4,), (3,), (4,),
    ]
    vmem = pl.BlockSpec(memory_space=pltpu.VMEM)
    square_shape = struct((4, size // 8, size // 4), f32)
    return pl.pallas_call(
        finish_kernel,
        out_shape=[
            struct(rows.shape, bf16), struct((width // 8, 2 * size), f32),
            square_shape, square_shape, square_shape,
            struct((size // 2, width // 4), f32), struct((4, lines, size), f32),
        ],
        in_specs=[pl.BlockSpec(memory_space=pl.ANY)] + [vmem] * 7,
        out_specs=[vmem] * 7,
        scratch_shapes=[pltpu.VMEM(shape, dtype) for shape, dtype in scratch]
        + [pltpu.SemaphoreType.DMA(shape) for shape in sems],
        compiler_params=pltpu.CompilerParams(
            collective_id=1, has_side_effects=True, vmem_limit_bytes=vmem_bytes
        ),
        name="finish",
    )(part, up, square, down, small, rows, cot, gain)


def swap(value, axis, mask):
    count = lax.axis_size(axis)
    return lax.ppermute(value, axis, [(s, s ^ mask) for s in range(count)])


def part_of(value, at, count, axis):
    size = value.shape[axis] // count
    return lax.dynamic_slice_in_dim(value, at * size, size, axis)


def halved(value, bit, dim, axis, mask):
    kept = part_of(value, bit, 2, dim).astype(f32)
    return kept + swap(part_of(value, 1 - bit, 2, dim), axis, mask).astype(f32)


def paired(mine, other, bit, dim):
    return jnp.where(
        bit == 0, jnp.concatenate([mine, other], dim), jnp.concatenate([other, mine], dim)
    )


def place():
    at_seq, at_batch = lax.axis_index("seq"), lax.axis_index("batch")
    return (at_seq % 8) // 2, at_seq % 2, at_batch // 2, at_batch % 2


def across(blocks, z):
    got = [lax.dynamic_index_in_dim(blocks, z, 0, keepdims=False)]
    for k in range(1, 4):
        got.append(swap(lax.dynamic_index_in_dim(blocks, z ^ k, 0, keepdims=False), "seq", 2 * k))
    got = jnp.stack(got)
    return jnp.stack([lax.dynamic_index_in_dim(got, z ^ k, 0, keepdims=False) for k in range(4)])


def gather_sequence(own):
    z, y, x, c = place()
    micro, rows, width = own.shape
    slots = paired(own, swap(own, "batch", 1), c, 0)
    blocks = across(part_of(slots, c, 2, 2), z)[:, None]
    both = paired(blocks, swap(blocks, "seq", 1), y, 1)
    return paired(both, swap(both, "batch", 1), c, 3).reshape(8 * rows, width)


def scatter_sequence(parts):
    z, y, x, c = place()
    width = parts.shape[1]
    blocks = parts.reshape(4, 2, -1, width)
    blocks = halved(blocks, c, 2, "batch", 1).astype(bf16)
    blocks = halved(blocks, y, 1, "seq", 1).astype(bf16)[:, 0]
    slots = across(blocks, z)
    other = swap(part_of(slots, 1 - c, 2, 0), "batch", 1)
    return paired(part_of(slots, c, 2, 0), other, c, 1).astype(f32)


def total_over_heads(value):
    value = value + swap(value, "batch", 1)
    return value + swap(value, "seq", 1)


def over_ranges(value, count):
    size = lax.axis_size("seq")
    groups = [[first + 8 * k for k in range(count)] for first in range(8)]
    return lax.all_gather(value, "seq", axis_index_groups=groups) if size > 8 else value[None]


def state_before(state, norm, level, total, ranges):
    index = lax.axis_index("seq") // 8
    summary = (state, norm[0], level[0, 0], total)
    everything = jax.tree.map(lambda part: over_ranges(part, ranges), summary)
    before = state_identity(summary)
    for k in range(ranges - 1):
        new = combine_states(before, jax.tree.map(lambda part: part[k], everything))
        before = jax.tree.map(lambda a, b: jnp.where(k < index, a, b), new, before)
    return (
        before[0],
        jnp.broadcast_to(before[1], norm.shape),
        jnp.broadcast_to(before[2], level.shape),
    )


def cotangent_after(d_state, d_norm, keep, ranges):
    index = lax.axis_index("seq") // 8
    own = (d_state, d_norm)
    everything = jax.tree.map(lambda part: over_ranges(part, ranges), own)
    keeps = over_ranges(keep, ranges)
    after = jax.tree.map(jnp.zeros_like, own)
    for k in range(ranges - 1, 0, -1):
        new = jax.tree.map(lambda a, b: a[k] + keeps[k] * b, everything, after)
        after = jax.tree.map(lambda a, b: jnp.where(k > index, a, b), new, after)
    return after


def reduce_blocks(at, up, square, down, heads):
    count, batch_count = lax.axis_size("seq"), lax.axis_size("batch")
    g_m, g_z = up
    width, size = g_m.shape
    half = size // 2
    squares = [
        jnp.concatenate([square[0, :, k : k + half], square[1, :, k : k + half]], 1)
        for k in range(0, 3 * half, half)
    ]
    g_down = jnp.concatenate([down[0], down[1]], 1)
    inner = heads * size
    up = jnp.zeros((width, 2 * inner), f32)
    up = lax.dynamic_update_slice_in_dim(up, g_m.astype(f32), at * size, 1)
    up = lax.dynamic_update_slice_in_dim(up, g_z.astype(f32), inner + at * size, 1)
    down = lax.dynamic_update_slice_in_dim(
        jnp.zeros((inner, width), f32), g_down.astype(f32), at * size, 0
    )
    full = [up, down]
    for g in squares:
        full.append(
            lax.dynamic_update_slice_in_dim(
                jnp.zeros((heads, size, size), f32), g.astype(f32)[None], at, 0
            )
        )
    blocks = tuple(to_device_blocks(g, count, batch_count) for g in full)
    pieces = lax.psum_scatter(blocks, ("seq", "batch"), scatter_dimension=0, tiled=True)
    s_up, s_down, s_query, s_key, s_value = tuple(p[0] for p in pieces)
    return s_up, jnp.stack([s_query, s_key, s_value], 1), s_down


def head_device(
    tokens, ln_gain, w_up, conv_w, conv_b, w_query, w_key, w_value, gate_w, gate_b,
    out_gain, skip_gain, w_down, d_out,
):
    z, y, x, c = place()
    at = 2 * c + y
    ranges = lax.axis_size("seq") // 8
    direct = ranges == 1 and lax.axis_size("batch") == 4
    head = jnp.reshape(at, (1,)).astype(jnp.int32)
    heads, size, _ = w_query.shape
    inner = heads * size
    conv_row = conv_b.reshape(1, inner)
    out_row = out_gain.reshape(1, inner)
    skip_row = skip_gain.reshape(1, inner)

    normed = gather_normed(tokens[:, 0], ln_gain[None])
    cot = gather_sequence(d_out[:, 0])

    gate_own = lax.dynamic_index_in_dim(
        gate_w.reshape(3, heads, size, 8), at, 1, keepdims=False
    ).transpose(0, 2, 1)
    high = lax.reduce_precision(gate_own, 8, 7)
    middle = lax.reduce_precision(gate_own - high, 8, 7)
    low = lax.reduce_precision(gate_own - high - middle, 8, 7)
    gate_parts = jnp.concatenate([high, middle, low, jnp.zeros_like(high)], 1).astype(bf16)
    gate_pairs = (
        jnp.concatenate([high, high, high, middle, middle, low], 1)
        .astype(bf16)
        .transpose(1, 0, 2)
        .reshape(48, 3 * size)
    )

    first = () if ranges == 1 else (shifted(normed[-16:], "seq", 8),)
    mix, conv, q, k, v, gate_z, gates, *halo = lift(
        head, normed, w_up, w_query, w_key, w_value, conv_w, conv_row, gate_parts, *first
    )
    gates = total_over_heads(gates)
    gates = jnp.concatenate(
        [
            lax.dynamic_slice_in_dim(gates, at, 1, 0),
            lax.dynamic_slice_in_dim(gates, heads + at, 1, 0)
            + lax.dynamic_slice_in_dim(gate_b, at, 1, 0)[:, None],
        ]
    )
    first = ()
    if ranges > 1:
        first = (
            jnp.zeros((size, size), f32),
            jnp.zeros((8, size), f32),
            jnp.full((8, 128), floor_value, f32),
        )
        *_, state, norm, level = cell_forward(
            head, gates, q, k, v, conv, gate_z, out_row, skip_row, w_down, *first
        )
        total = jnp.sum(jax.nn.log_sigmoid(gates[1]))
        first = state_before(state, norm, level, total, ranges)
    part, head_normed, states, norms, weights, cols, rows, *last = cell_forward(
        head, gates, q, k, v, conv, gate_z, out_row, skip_row, w_down, *first
    )
    block_rows = (tokens[:, 0].astype(f32) + scatter_sequence(part)).astype(bf16)
    after = ()
    if ranges > 1:
        after = (jnp.zeros((size, size), f32), jnp.zeros((8, size), f32))
        *_, d_state, d_norm = cell_backward(
            head, rows, q, k, v, conv, gate_z, head_normed, states, norms, weights, cols, cot,
            out_row, skip_row, w_down, *after,
        )
        keep = jnp.exp(total + first[2][0, 0] - last[2][0, 0])
        after = cotangent_after(d_state, d_norm, keep, ranges)
    dq, dk, dv, dskip, dz, d_rows, g_down, g_gain, *_ = cell_backward(
        head, rows, q, k, v, conv, gate_z, head_normed, states, norms, weights, cols, cot,
        out_row, skip_row, w_down, *after,
    )
    index = jnp.arange(2 * heads)[:, None]
    d_gate = jnp.where(index == at, d_rows[0:1], jnp.where(index == heads + at, d_rows[1:2], 0.0))
    d_gate = total_over_heads(d_gate)
    first = ()
    if ranges > 1:
        *_, later = lower(
            head, d_gate, dq, dk, dv, dskip, dz, mix, conv, q, k, v, normed,
            w_query, w_key, w_value, w_up, conv_w, conv_row, gate_pairs, g_gain,
            halo[0], jnp.zeros((8, size), f32),
        )
        first = (halo[0], shifted(later, "seq", -8))
    d_part, square, up, small, *_ = lower(
        head, d_gate, dq, dk, dv, dskip, dz, mix, conv, q, k, v, normed,
        w_query, w_key, w_value, w_up, conv_w, conv_row, gate_pairs, g_gain, *first,
    )
    if direct:
        grad_rows, s_up, s_query, s_key, s_value, s_down, small = finish(
            d_part, up, square, g_down, small, tokens[:, 0], d_out[:, 0], ln_gain[None]
        )
    else:
        d_normed = scatter_sequence(d_part)
        row_f = tokens[:, 0].astype(f32)
        centre = row_f - jnp.mean(row_f, axis=-1, keepdims=True)
        rstd = lax.rsqrt(jnp.mean(centre * centre, axis=-1, keepdims=True) + norm_epsilon)
        row_hat = centre * rstd
        scaled = d_normed * ln_gain
        d_row = rstd * (
            scaled
            - jnp.mean(scaled, axis=-1, keepdims=True)
            - row_hat * jnp.mean(scaled * row_hat, axis=-1, keepdims=True)
        )
        grad_rows = (d_out[:, 0].astype(f32) + d_row).astype(bf16)
        s_up, squares, s_down = reduce_blocks(at, up, square, g_down, heads)
        s_query, s_key, s_value = squares[:, 0], squares[:, 1], squares[:, 2]
        small = jnp.where(jnp.arange(heads)[:, None, None] == at, small, 0.0)
        small = lax.psum(small, ("seq", "batch"))
    s_ln = jnp.sum(small[:, 32:34], 0).reshape(-1) / ln_gain
    s_gate_w = small[:, :24].reshape(heads, 3, 8, size).transpose(1, 0, 3, 2).reshape(3 * inner, 8)
    s_conv_w = small[:, 24:28].transpose(1, 0, 2).reshape(4, inner)
    return (
        block_rows[:, None],
        grad_rows[:, None],
        s_ln,
        s_up,
        s_conv_w,
        small[:, 28].reshape(inner),
        s_query,
        s_key,
        s_value,
        s_gate_w,
        small[:, 31, 0],
        small[:, 29].reshape(inner),
        small[:, 30].reshape(inner),
        s_down,
    )


def solution(mesh):
    placed = (P(None, "batch", "seq", None),) + (P(),) * 12 + (P(None, "batch", "seq", None),)
    return jax.shard_map(
        head_device,
        mesh=mesh,
        in_specs=placed,
        out_specs=(
            P(None, "batch", "seq", None),
            P(None, "batch", "seq", None),
            P(),
            P("seq", "batch"),
            P(),
            P(),
            P(None, "seq", "batch"),
            P(None, "seq", "batch"),
            P(None, "seq", "batch"),
            P(),
            P(),
            P(),
            P(),
            P("seq", "batch"),
        ),
        check_vma=False,
    )
```

```python
from functools import partial

import jax
import jax.numpy as jnp
from jax import lax
from jax.experimental import pallas as pl
from jax.experimental.pallas import tpu as pltpu
from jax.sharding import PartitionSpec as P

norm_epsilon = 1e-05
floor_value = -1e30


def shifted(value, axis, steps):
    count = lax.axis_size(axis)
    initial, last = (max(0, -steps), min(count, count - steps))
    return lax.ppermute(value, axis, [(source, source + steps) for source in range(initial, last)])


def combine_states(earlier, later):
    top = jnp.maximum(later[3] + earlier[2], later[2])
    keep_first = jnp.exp(later[3] + earlier[2] - top)
    keep_second = jnp.exp(later[2] - top)
    merged_c = keep_first[..., None, None] * earlier[0] + keep_second[..., None, None] * later[0]
    merged_n = keep_first[..., None] * earlier[1] + keep_second[..., None] * later[1]
    return (merged_c, merged_n, top, earlier[3] + later[3])


def state_identity(template):
    return (
        jnp.zeros_like(template[0]),
        jnp.zeros_like(template[1]),
        jnp.full_like(template[2], floor_value),
        jnp.zeros_like(template[3]),
    )


def head_output(hidden, out_gain, skip_gain, conv_out, gate_z):
    centre = hidden - jnp.mean(hidden, axis=-1, keepdims=True)
    spread = jnp.mean(centre * centre, axis=-1, keepdims=True)
    normed = centre * lax.rsqrt(spread + norm_epsilon)
    flat_out = normed.transpose(1, 0, 2).reshape(hidden.shape[1], -1) * out_gain
    return (flat_out + skip_gain * conv_out) * jax.nn.silu(gate_z)


def output_tail(
    query_f,
    key_f,
    value_f,
    gate_pre,
    conv_f,
    gate_z,
    out_gain,
    skip_gain,
    state_c,
    state_n,
    state_m,
):
    head_count = gate_pre.shape[1] // 2
    in_gate = gate_pre[:, :head_count].T
    log_forget = jax.nn.log_sigmoid(gate_pre[:, head_count:]).T
    hidden = cell_hidden(
        to_heads(query_f, head_count),
        to_heads(key_f, head_count),
        to_heads(value_f, head_count),
        in_gate,
        log_forget,
        state_c,
        state_n,
        state_m,
    )
    return head_output(hidden, out_gain, skip_gain, conv_f, gate_z)


def state_tail(key_f, value_f, gate_pre, state_c, state_n, state_m):
    head_count = gate_pre.shape[1] // 2
    in_gate = gate_pre[:, :head_count].T
    log_forget = jax.nn.log_sigmoid(gate_pre[:, head_count:]).T
    return cell_state(
        to_heads(key_f, head_count),
        to_heads(value_f, head_count),
        in_gate,
        log_forget,
        state_c,
        state_n,
        state_m,
    )


def to_device_blocks(grad_full, seq_count, batch_count):
    if grad_full.ndim == 2:
        rows, cols = grad_full.shape
        split = grad_full.reshape(seq_count, rows // seq_count, batch_count, cols // batch_count)
        return split.transpose(0, 2, 1, 3).reshape(
            seq_count * batch_count, rows // seq_count, cols // batch_count
        )
    heads, rows, cols = grad_full.shape
    split = grad_full.reshape(heads, seq_count, rows // seq_count, batch_count, cols // batch_count)
    return split.transpose(1, 3, 0, 2, 4).reshape(
        seq_count * batch_count, heads, rows // seq_count, cols // batch_count
    )


f32 = jnp.float32
bf16 = jnp.bfloat16
chunk_len = 256
wide_len = 512
vmem_bytes = 56 * 1024 * 1024


def mm(a, b):
    return lax.dot_general(a, b, (((1,), (0,)), ((), ())), preferred_element_type=f32)


def mm_nt(a, b):
    return lax.dot_general(a, b, (((1,), (1,)), ((), ())), preferred_element_type=f32)


def mm_tn(a, b):
    return lax.dot_general(a, b, (((0,), (0,)), ((), ())), preferred_element_type=f32)


def split_three(value):
    high = value.astype(bf16)
    rest = value - high.astype(f32)
    middle = rest.astype(bf16)
    low = (rest - middle.astype(f32)).astype(bf16)
    return high, middle, low


def conv_taps(ext, length):
    return [pltpu.roll(ext, 3 - j, 0)[8 : 8 + length] if j < 3 else ext[8 : 8 + length] for j in range(4)]


def lift_kernel(chained, head_ref, normed, w_mix, w_gate, w_q, w_k, w_v, conv_w, conv_b, gate_w, *refs):
    if chained:
        rows_before, *refs, halo_out, carry = refs
    else:
        *refs, carry = refs
    mix_out, conv_out, q_out, k_out, v_out, z_out, gate_out = refs
    length = normed.shape[0]

    @pl.when(pl.program_id(0) == 0)
    def _():
        if chained:
            mix_before = mm(rows_before[...], w_mix[...]).astype(bf16)
            halo_out[...] = mix_before
            carry[...] = mix_before[8:16].astype(f32)
        else:
            carry[...] = jnp.zeros_like(carry)

    rows = normed[...]
    mix = mm(rows, w_mix[...]).astype(bf16)
    mix_out[...] = mix
    z_out[...] = mm(rows, w_gate[...])
    mix_f = mix.astype(f32)
    taps = conv_taps(jnp.concatenate([carry[...], mix_f], axis=0), length)
    carry[...] = mix_f[length - 8 :]
    summed = conv_b[...]
    for j in range(4):
        summed = summed + conv_w[j : j + 1, :] * taps[j]
    conv = (summed * jax.nn.sigmoid(summed)).astype(bf16)
    conv_out[...] = conv
    q = mm(conv, w_q[0]).astype(bf16)
    k = mm(conv, w_k[0]).astype(bf16)
    v = mm(mix, w_v[0]).astype(bf16)
    q_out[...] = q
    k_out[...] = k
    v_out[...] = v
    parts = mm_nt(gate_w[0], q) + mm_nt(gate_w[1], k) + mm_nt(gate_w[2], v)
    gate_out[...] = parts[0:8] + parts[8:16] + parts[16:24]


def gate_rows(gates, causal, diagonal):
    in_row = gates[0:1, :]
    pre = gates[1:2, :]
    log_forget = jnp.minimum(pre, 0.0) - jnp.log1p(jnp.exp(-jnp.abs(pre)))
    run_col = jnp.sum(jnp.where(causal, log_forget, 0.0), axis=1, keepdims=True)
    run_row = jnp.sum(jnp.where(diagonal, run_col, 0.0), axis=0, keepdims=True)
    return in_row - run_row, run_col, log_forget


def masks(length):
    row = lax.broadcasted_iota(jnp.int32, (length, length), 0)
    col = lax.broadcasted_iota(jnp.int32, (length, length), 1)
    return row >= col, row == col


def cell_forward_kernel(
    chained, head_ref, gates, q_ref, k_ref, v_ref, conv_ref, z_ref, out_gain, skip_gain, w_down, *refs
):
    if chained:
        *first, part_out, normed_out, state_out, norm_out, weight_out, col_out, row_out = refs[:10]
        *final, state, norm, level = refs[10:]
    else:
        part_out, normed_out, state_out, norm_out, weight_out, col_out, row_out = refs[:7]
        state, norm, level = refs[7:]
    length = q_ref.shape[0]
    head_size = q_ref.shape[1]
    scale = head_size ** (-0.5)

    @pl.when(pl.program_id(0) == 0)
    def _():
        if chained:
            for ref, value in zip((state, norm, level), first):
                ref[...] = value[...]
        else:
            state[...] = jnp.zeros_like(state)
            norm[...] = jnp.zeros_like(norm)
            level[...] = jnp.full_like(level, floor_value)

    causal, diagonal = masks(length)
    a_row, run_col, log_forget = gate_rows(gates[...], causal, diagonal)
    before = level[0:1, 0:1]
    top = jnp.maximum(
        before, jnp.max(jnp.where(causal, a_row, floor_value), axis=1, keepdims=True)
    )
    decay = jnp.exp(jnp.where(causal, a_row - top, floor_value))
    q = q_ref[...]
    k = k_ref[...]
    v = v_ref[...]
    q_f = q.astype(f32)
    weights = decay * (mm_nt(q, k) * scale)
    weights_low = weights.astype(bf16)
    weight_out[...] = weights_low
    from_state = jnp.exp(before - top)
    state_low = state[...].astype(bf16)
    state_out[0] = state_low
    norm_row = norm[0:1, :]
    norm_out[0] = norm[...]
    numerator = mm(weights_low, v) + (from_state * scale) * mm(q, state_low)
    denominator = jnp.sum(weights, axis=1, keepdims=True) + (from_state * scale) * jnp.sum(
        q_f * norm_row, axis=1, keepdims=True
    )
    floor = jnp.exp(-(run_col + top))
    size = jnp.abs(denominator)
    inverse = 1.0 / jnp.maximum(size, floor)
    hidden = numerator * inverse
    centre = hidden - jnp.mean(hidden, axis=1, keepdims=True)
    spread = jnp.mean(centre * centre, axis=1, keepdims=True)
    rstd = lax.rsqrt(spread + norm_epsilon)
    normed = centre * rstd
    normed_out[...] = normed
    gate_z = z_ref[...]
    gated = (normed * out_gain[...] + skip_gain[...] * conv_ref[...].astype(f32)) * (
        gate_z * jax.nn.sigmoid(gate_z)
    )
    part_out[...] = mm(gated.astype(bf16), w_down[...]).astype(bf16)
    factor = jnp.where(
        size > floor,
        jnp.where(denominator > 0, 1.0, -1.0) * inverse * (norm_epsilon * rstd * rstd),
        0.0,
    )
    lane = lax.broadcasted_iota(jnp.int32, (length, 128), 1)
    packed = jnp.where(lane == 0, rstd, inverse)
    packed = jnp.where(lane == 2, from_state, packed)
    packed = jnp.where(lane == 3, top, packed)
    col_out[...] = jnp.where(lane == 4, factor, packed)
    sub = lax.broadcasted_iota(jnp.int32, (8, length), 0)
    row_out[...] = jnp.where(sub == 0, a_row, 1.0 - jnp.exp(log_forget))
    last = top[length - 1 : length, :]
    a_col = jnp.sum(jnp.where(diagonal, a_row, 0.0), axis=1, keepdims=True)
    weighted = k.astype(f32) * jnp.exp(a_col - last)
    keep = jnp.exp(before - last)
    state[...] = keep * state[...] + mm_tn(weighted.astype(bf16), v)
    norm[...] = keep * norm[...] + jnp.sum(weighted, axis=0, keepdims=True)
    level[...] = jnp.broadcast_to(run_col[length - 1 : length, :] + last, level.shape)
    if chained:
        for ref, value in zip(final, (state, norm, level)):
            ref[...] = value[...]


def cell_backward_kernel(
    chained, head_ref, rows_ref, q_ref, k_ref, v_ref, conv_ref, z_ref, normed_ref, state_ref, norm_ref,
    weight_ref, col_ref, cot_ref, out_gain, skip_gain, w_down, *refs
):
    if chained:
        *first, dq_out, dk_out, dv_out, dskip_out, dz_out, gate_out, g_down_out, g_gain_out = refs[:10]
        *final, d_state, d_norm, g_down, g_gain = refs[10:]
    else:
        dq_out, dk_out, dv_out, dskip_out, dz_out, gate_out, g_down_out, g_gain_out = refs[:8]
        d_state, d_norm, g_down, g_gain = refs[8:]
    length = q_ref.shape[0]
    head_size = q_ref.shape[1]
    scale = head_size ** (-0.5)

    @pl.when(pl.program_id(0) == 0)
    def _():
        if chained:
            d_state[...] = first[0][...]
            d_norm[...] = first[1][...]
        else:
            d_state[...] = jnp.zeros_like(d_state)
            d_norm[...] = jnp.zeros_like(d_norm)
        g_down[...] = jnp.zeros_like(g_down)
        g_gain[...] = jnp.zeros_like(g_gain)

    causal, diagonal = masks(length)
    rstd = col_ref[:, 0:1]
    inverse = col_ref[:, 1:2]
    from_state = col_ref[:, 2:3]
    top = col_ref[:, 3:4]
    factor = col_ref[:, 4:5]
    a_row = rows_ref[0:1, :]
    q = q_ref[...]
    k = k_ref[...]
    v = v_ref[...]
    q_f = q.astype(f32)
    k_f = k.astype(f32)
    conv = conv_ref[...].astype(f32)
    normed = normed_ref[...]
    gate_z = z_ref[...]
    cot = cot_ref[...]
    opened = jax.nn.sigmoid(gate_z)
    silu = gate_z * opened
    head_in = normed * out_gain[...] + skip_gain[...] * conv
    g_down[...] += mm_tn((head_in * silu).astype(bf16), cot)
    d_gated = mm_nt(cot, w_down[...])
    dz_out[...] = (d_gated * head_in * (opened * (1.0 + gate_z * (1.0 - opened)))).astype(bf16)
    d_head = d_gated * silu
    g_gain[0:1, :] += jnp.sum(d_head * normed, axis=0, keepdims=True)
    g_gain[1:2, :] += jnp.sum(d_head * conv, axis=0, keepdims=True)
    dskip_out[...] = skip_gain[...] * d_head
    d_hat = d_head * out_gain[...]
    along = jnp.sum(d_hat * normed, axis=1, keepdims=True)
    d_hidden = rstd * (
        d_hat - jnp.mean(d_hat, axis=1, keepdims=True) - normed * (along / head_size)
    )
    d_num = d_hidden * inverse
    d_den = -along * factor
    d_num_low = d_num.astype(bf16)
    decay = jnp.exp(jnp.where(causal, a_row - top, floor_value))
    d_scores = ((mm_nt(d_num_low, v) + d_den) * (decay * scale)).astype(bf16)
    through = from_state * scale
    dq_near = mm(d_scores, k)
    dq_far = (
        mm_nt((d_num * through).astype(bf16), state_ref[0])
        + (through * d_den) * norm_ref[0, 0:1, :]
    )
    last = top[length - 1 : length, :]
    keep = from_state[length - 1 : length, :]
    a_col = jnp.sum(jnp.where(diagonal, a_row, 0.0), axis=1, keepdims=True)
    key_weight = jnp.exp(a_col - last)
    d_state_low = d_state[...].astype(bf16)
    dk_near = mm_tn(d_scores, q)
    dk_far = key_weight * (mm_nt(v, d_state_low) + d_norm[0:1, :])
    dv = mm_tn(weight_ref[...], d_num_low) + mm((k_f * key_weight).astype(bf16), d_state_low)
    dq_out[...] = dq_near + dq_far
    dk_out[...] = dk_near + dk_far
    dv_out[...] = dv
    held = state_ref[0].astype(f32) * d_state[...]
    held = jnp.sum(jnp.sum(held, axis=0, keepdims=True) + norm_ref[0, 0:1, :] * d_norm[0:1, :])
    q_state = q_f * through
    d_state[...] = keep * d_state[...] + mm_tn(q_state.astype(bf16), d_num_low)
    d_norm[...] = keep * d_norm[...] + jnp.sum(q_state * d_den, axis=0, keepdims=True)
    q_dot = jnp.sum(q_f * (dq_near + dq_far), axis=1, keepdims=True)
    k_near = jnp.sum(k_f * dk_near, axis=1, keepdims=True)
    k_far = jnp.sum(k_f * dk_far, axis=1, keepdims=True)
    d_in = jnp.sum(jnp.where(diagonal, k_near + k_far, 0.0), axis=0, keepdims=True)
    d_log = jnp.sum(
        jnp.where(causal, q_dot - k_near, jnp.where(diagonal, 0.0, k_far)), axis=0, keepdims=True
    )
    d_log = d_log + keep * held
    sub = lax.broadcasted_iota(jnp.int32, (8, length), 0)
    d_pre = d_log * rows_ref[1:2, :]
    gate_out[...] = jnp.where(sub == 0, d_in, d_pre)
    g_gain[2:3, :] += jnp.broadcast_to(jnp.sum(d_pre, axis=1, keepdims=True), (1, head_size))

    @pl.when(pl.program_id(0) == pl.num_programs(0) - 1)
    def _():
        if chained:
            final[0][...] = d_state[...]
            final[1][...] = d_norm[...]
        half = g_down.shape[1] // 2
        g_down_out[0] = g_down[:, :half].astype(bf16)
        g_down_out[1] = g_down[:, half:].astype(bf16)
        g_gain_out[...] = g_gain[...]


def lower_kernel(
    chained, head_ref, d_gate, dq_ref, dk_ref, dv_ref, dskip_ref, dz_ref, mix_ref, mix_before, conv_ref,
    q_ref, k_ref, v_ref, normed, w_q, w_k, w_v, w_mix, w_gate, conv_w, conv_b, gate_w, g_gain, *refs
):
    if chained:
        first_halo, first_later, *refs = refs
        later_out = refs.pop(4)
    part_out, square_out, up_out, small_out = refs[:4]
    g_q, g_k, g_v, g_m, g_z, g_small, later = refs[4:]
    length = q_ref.shape[0]
    step = pl.program_id(0)

    @pl.when(step == 0)
    def _():
        for ref in (g_q, g_k, g_v, g_m, g_z, g_small, later):
            ref[...] = jnp.zeros_like(ref)
        if chained:
            later[...] = first_later[...]

    high, middle, low = split_three(d_gate[...])
    left = jnp.concatenate([high, middle, low, high, middle, high], axis=0)
    d_joined = mm_tn(left, gate_w[...])
    size = q_ref.shape[1]
    query_low = (dq_ref[...] + d_joined[:, :size]).astype(bf16)
    key_low = (dk_ref[...] + d_joined[:, size : 2 * size]).astype(bf16)
    value_low = (dv_ref[...] + d_joined[:, 2 * size :]).astype(bf16)
    conv = conv_ref[...]
    mix = mix_ref[...]
    g_q[...] += mm_tn(conv, query_low)
    g_k[...] += mm_tn(conv, key_low)
    g_v[...] += mm_tn(mix, value_low)
    three = jnp.concatenate([high, middle, low], axis=0)
    for at, ref in enumerate((q_ref, k_ref, v_ref)):
        got = mm(three, ref[...])
        g_small[8 * at : 8 * at + 8, :] += got[0:8] + got[8:16] + got[16:24]
    d_conv = dskip_ref[...] + mm_nt(query_low, w_q[0]) + mm_nt(key_low, w_k[0])
    halo = mix_before[8:16, :].astype(f32)
    edge = first_halo[8:16, :].astype(f32) if chained else 0.0
    halo = jnp.where(step == pl.num_programs(0) - 1, edge, halo)
    taps = conv_taps(jnp.concatenate([halo, mix.astype(f32)], axis=0), length)
    summed = conv_b[...]
    for j in range(4):
        summed = summed + conv_w[j : j + 1, :] * taps[j]
    opened = jax.nn.sigmoid(summed)
    d_summed = d_conv * (opened * (1.0 + summed * (1.0 - opened)))
    for j in range(4):
        g_small[24 + j : 25 + j, :] += jnp.sum(d_summed * taps[j], axis=0, keepdims=True)
    g_small[28:29, :] += jnp.sum(d_summed, axis=0, keepdims=True)
    ext = jnp.concatenate([d_summed, later[...]], axis=0)
    later[...] = d_summed[0:8]
    d_mix = conv_w[3:4, :] * d_summed
    for j in range(3):
        d_mix = d_mix + conv_w[j : j + 1, :] * pltpu.roll(ext, length + 8 - (3 - j), 0)[0:length]
    d_mix = (d_mix + mm_nt(value_low, w_v[0])).astype(bf16)
    d_z = dz_ref[...]
    rows = normed[...]
    g_m[...] += mm_tn(rows, d_mix)
    g_z[...] += mm_tn(rows, d_z)
    d_normed = mm_nt(d_mix, w_mix[...]) + mm_nt(d_z, w_gate[...])
    part_out[...] = d_normed.astype(bf16)
    g_ln = jnp.sum(d_normed * rows.astype(f32), axis=0, keepdims=True)
    g_small[32:33, :] += g_ln[:, :size]
    g_small[33:34, :] += g_ln[:, size:]

    @pl.when(step == pl.num_programs(0) - 1)
    def _():
        half = size // 2
        for at, ref in enumerate((g_q, g_k, g_v)):
            square_out[0, :, half * at : half * at + half] = ref[:, :half].astype(bf16)
            square_out[1, :, half * at : half * at + half] = ref[:, half:].astype(bf16)
        up_out[0] = g_m[...].astype(bf16)
        up_out[1] = g_z[...].astype(bf16)
        g_small[29:32, :] = g_gain[0:3, :]
        small_out[...] = g_small[...]
        if chained:
            later_out[...] = later[...]


def struct(shape, dtype):
    return jax.ShapeDtypeStruct(shape, dtype)


def run_kernel(body, head, grid, inputs, in_specs, outs, out_specs, scratch, name, flops, nbytes):
    return pl.pallas_call(
        body,
        grid_spec=pltpu.PrefetchScalarGridSpec(
            num_scalar_prefetch=1,
            grid=(grid,),
            in_specs=in_specs,
            out_specs=out_specs,
            scratch_shapes=scratch,
        ),
        out_shape=outs,
        compiler_params=pltpu.CompilerParams(
            dimension_semantics=("arbitrary",), vmem_limit_bytes=vmem_bytes
        ),
        cost_estimate=pl.CostEstimate(flops=flops, bytes_accessed=nbytes, transcendentals=0),
        name=name,
    )(head, *inputs)


def fixed(shape, *index):
    return pl.BlockSpec(shape, lambda g, h: tuple(h[0] if i == "h" else i for i in index))


def lift(head, normed, w_up, w_query, w_key, w_value, conv_w, conv_b, gate_parts, *first):
    tokens, width = normed.shape
    heads, size, _ = w_query.shape
    length = wide_len
    by_row = lambda cols: pl.BlockSpec((length, cols), lambda g, h: (g, 0))
    weight = pl.BlockSpec((1, size, size), lambda g, h: (h[0], 0, 0))
    chained = len(first) > 0
    halo = [pl.BlockSpec((16, size), lambda g, h: (0, 0))] * chained
    return run_kernel(
        partial(lift_kernel, chained), head, tokens // length,
        (normed, w_up, w_up, w_query, w_key, w_value, conv_w, conv_b, gate_parts, *first),
        [
            by_row(width),
            pl.BlockSpec((width, size), lambda g, h: (0, h[0])),
            pl.BlockSpec((width, size), lambda g, h: (0, heads + h[0])),
            weight, weight, weight,
            pl.BlockSpec((4, size), lambda g, h: (0, h[0])),
            pl.BlockSpec((1, size), lambda g, h: (0, h[0])),
            pl.BlockSpec(gate_parts.shape, lambda g, h: (0, 0, 0)),
        ]
        + [pl.BlockSpec((16, width), lambda g, h: (0, 0))] * chained,
        [struct((tokens, size), bf16)] * 5
        + [struct((tokens, size), f32), struct((8, tokens), f32)]
        + [struct((16, size), bf16)] * chained,
        [by_row(size)] * 6 + [pl.BlockSpec((8, length), lambda g, h: (0, g))] + halo,
        [pltpu.VMEM((8, size), f32)],
        "lift", 2 * tokens * size * (2 * width + 3 * size), 24 * 2**20,
    )


def cell_forward(head, gates, q, k, v, conv, gate_z, out_gain, skip_gain, w_down, *first):
    tokens, size = q.shape
    width = w_down.shape[1]
    length = chunk_len
    steps = tokens // length
    by_row = lambda cols: pl.BlockSpec((length, cols), lambda g, h: (g, 0))
    gain = pl.BlockSpec((1, size), lambda g, h: (0, h[0]))
    carried = [struct(value.shape, f32) for value in first]
    carried_specs = [pl.BlockSpec(value.shape, lambda g, h: (0, 0)) for value in first]
    return run_kernel(
        partial(cell_forward_kernel, len(first) > 0), head, steps,
        (gates, q, k, v, conv, gate_z, out_gain, skip_gain, w_down, *first),
        [pl.BlockSpec((2, length), lambda g, h: (0, g))]
        + [by_row(size)] * 5
        + [gain, gain, pl.BlockSpec((size, width), lambda g, h: (h[0], 0))]
        + carried_specs,
        [
            struct((tokens, width), bf16),
            struct((tokens, size), f32),
            struct((steps, size, size), bf16),
            struct((steps, 8, size), f32),
            struct((tokens, length), bf16),
            struct((tokens, 128), f32),
            struct((8, tokens), f32),
        ]
        + carried,
        [
            by_row(width),
            by_row(size),
            pl.BlockSpec((1, size, size), lambda g, h: (g, 0, 0)),
            pl.BlockSpec((1, 8, size), lambda g, h: (g, 0, 0)),
            by_row(length),
            by_row(128),
            pl.BlockSpec((8, length), lambda g, h: (0, g)),
        ]
        + carried_specs,
        [pltpu.VMEM((size, size), f32), pltpu.VMEM((8, size), f32), pltpu.VMEM((8, 128), f32)],
        "cell_forward", 2 * tokens * size * (2 * length + 2 * size + width), 28 * 2**20,
    )


def cell_backward(
    head, rows, q, k, v, conv, gate_z, normed, states, norms, weights, cols, cot,
    out_gain, skip_gain, w_down, *first,
):
    tokens, size = q.shape
    width = w_down.shape[1]
    length = chunk_len
    steps = tokens // length
    end = steps - 1
    by_row = lambda n: pl.BlockSpec((length, n), lambda g, h: (end - g, 0))
    gain = pl.BlockSpec((1, size), lambda g, h: (0, h[0]))
    whole = lambda shape: pl.BlockSpec(shape, lambda g, h: (0, 0))
    carried = [struct(value.shape, f32) for value in first]
    carried_specs = [whole(value.shape) for value in first]
    return run_kernel(
        partial(cell_backward_kernel, len(first) > 0), head, steps,
        (rows, q, k, v, conv, gate_z, normed, states, norms, weights, cols, cot,
         out_gain, skip_gain, w_down, *first),
        [pl.BlockSpec((8, length), lambda g, h: (0, end - g))]
        + [by_row(size)] * 6
        + [
            pl.BlockSpec((1, size, size), lambda g, h: (end - g, 0, 0)),
            pl.BlockSpec((1, 8, size), lambda g, h: (end - g, 0, 0)),
            by_row(length),
            by_row(128),
            by_row(width),
            gain, gain,
            pl.BlockSpec((size, width), lambda g, h: (h[0], 0)),
        ]
        + carried_specs,
        [struct((tokens, size), f32)] * 4
        + [
            struct((tokens, size), bf16),
            struct((8, tokens), f32),
            struct((2, size, width // 2), bf16),
            struct((8, size), f32),
        ]
        + carried,
        [by_row(size)] * 5
        + [
            pl.BlockSpec((8, length), lambda g, h: (0, end - g)),
            pl.BlockSpec((2, size, width // 2), lambda g, h: (0, 0, 0)),
            whole((8, size)),
        ]
        + carried_specs,
        [
            pltpu.VMEM((size, size), f32),
            pltpu.VMEM((8, size), f32),
            pltpu.VMEM((size, width), f32),
            pltpu.VMEM((8, size), f32),
        ],
        "cell_backward", 2 * tokens * size * (4 * length + 4 * size + 2 * width), 44 * 2**20,
    )


def lower(
    head, d_gate, dq, dk, dv, dskip, dz, mix, conv, q, k, v, normed,
    w_query, w_key, w_value, w_up, conv_w, conv_b, gate_pairs, g_gain, *first,
):
    tokens, size = q.shape
    width = normed.shape[1]
    heads = w_query.shape[0]
    length = wide_len
    steps = tokens // length
    end = steps - 1
    by_row = lambda n: pl.BlockSpec((length, n), lambda g, h: (end - g, 0))
    weight = pl.BlockSpec((1, size, size), lambda g, h: (h[0], 0, 0))
    whole = lambda shape: pl.BlockSpec(shape, lambda g, h: (0, 0))
    chained = len(first) > 0
    return run_kernel(
        partial(lower_kernel, chained), head, steps,
        (d_gate, dq, dk, dv, dskip, dz, mix, mix, conv, q, k, v, normed,
         w_query, w_key, w_value, w_up, w_up, conv_w, conv_b, gate_pairs, g_gain, *first),
        [pl.BlockSpec((8, length), lambda g, h: (0, end - g))]
        + [by_row(size)] * 6
        + [
            pl.BlockSpec(
                (16, size),
                lambda g, h: (jnp.maximum((end - g) * (length // 16) - 1, 0), 0),
            )
        ]
        + [by_row(size)] * 4
        + [by_row(width), weight, weight, weight]
        + [
            pl.BlockSpec((width, size), lambda g, h: (0, h[0])),
            pl.BlockSpec((width, size), lambda g, h: (0, heads + h[0])),
            pl.BlockSpec((4, size), lambda g, h: (0, h[0])),
            pl.BlockSpec((1, size), lambda g, h: (0, h[0])),
            whole(gate_pairs.shape),
            whole(g_gain.shape),
        ]
        + [whole(value.shape) for value in first],
        [struct((tokens, width), bf16)]
        + [struct((2, size, 3 * size // 2), bf16), struct((2, width, size), bf16)]
        + [struct((40, size), f32)]
        + [struct((8, size), f32)] * chained,
        [by_row(width)]
        + [
            pl.BlockSpec((2, size, 3 * size // 2), lambda g, h: (0, 0, 0)),
            pl.BlockSpec((2, width, size), lambda g, h: (0, 0, 0)),
        ]
        + [whole((40, size))]
        + [whole((8, size))] * chained,
        [pltpu.VMEM((size, size), f32)] * 3
        + [pltpu.VMEM((width, size), f32)] * 2
        + [pltpu.VMEM((40, size), f32), pltpu.VMEM((8, size), f32)],
        "lower", 2 * tokens * size * (6 * size + 4 * width), 48 * 2**20,
    )
MESH_ID = pl.DeviceIdType.MESH


def where_am_i():
    at_seq, at_batch = lax.axis_index("seq"), lax.axis_index("batch")
    within = lax.rem(at_seq, 8)
    first = at_seq - within
    return first, within // 2, lax.rem(within, 2), at_batch // 2, lax.rem(at_batch, 2)


def greet(others):
    barrier = pltpu.get_barrier_semaphore()
    for other in others:
        pl.semaphore_signal(barrier, 1, device_id=other, device_id_type=MESH_ID)
    pl.semaphore_wait(barrier, len(others))


def remote(src, dst, sent, landed, device):
    return pltpu.make_async_remote_copy(src, dst, sent, landed, device_id=device, device_id_type=MESH_ID)


def normalize(rows):
    centre = rows - jnp.mean(rows, axis=-1, keepdims=True)
    rstd = lax.rsqrt(jnp.mean(centre * centre, axis=-1, keepdims=True) + norm_epsilon)
    return centre * rstd, rstd


def gather_kernel(
    rows_ref, gain_ref, out_ref, staged, kept, z_sent, z_landed, y_sent, y_landed, c_sent, c_landed
):
    first, z, y, x, c = where_am_i()
    parts = z_landed.shape[1]
    block = rows_ref.shape[1]
    size = block // parts

    def device(zz, yy, cc):
        return (first + 2 * zz + yy, 2 * x + cc)

    def rows(zz, yy, part):
        return out_ref.at[pl.ds(pl.multiple_of((2 * zz + yy) * block + part * size, size), size)]

    others = [device(lax.rem(z + k, 4), y, c) for k in range(1, 4)]
    greet(others + [device(z, 1 - y, c), device(z, y, 1 - c)])
    enters = z // 2 == c

    def to_column(m, part):
        return remote(
            staged.at[m, pl.ds(part * size, size)], rows(z, y, part),
            z_sent.at[m, part], z_landed.at[z, part], device(2 * c + m, y, c),
        )

    def keep(m, part):
        return pltpu.make_async_copy(
            staged.at[m, pl.ds(part * size, size)], rows(z, y, part), kept.at[part]
        )

    def from_column(zz, part):
        return remote(
            rows(zz, y, part), rows(zz, y, part), z_sent.at[0, part], z_landed.at[zz, part],
            device(zz, y, c),
        )

    def to_row(zz, k, part):
        return remote(
            rows(zz, y, part), rows(zz, y, part), y_sent.at[k, part], y_landed.at[zz, part],
            device(z, 1 - y, c),
        )

    def from_row(zz, k, part):
        return remote(
            rows(zz, 1 - y, part), rows(zz, 1 - y, part), y_sent.at[k, part],
            y_landed.at[zz, part], device(z, 1 - y, c),
        )

    def to_core(zz, yy, k, part):
        return remote(
            rows(zz, yy, part), rows(zz, yy, part), c_sent.at[k, part],
            c_landed.at[2 * zz + yy, part], device(z, y, 1 - c),
        )

    for part in range(parts):
        here = pl.ds(part * size, size)
        for m in range(2):
            staged[m, here] = (
                normalize(rows_ref[m, here].astype(f32))[0] * gain_ref[...]
            ).astype(bf16)
            away = 2 * c + m != z
            pl.when(away)(lambda m=m, part=part: to_column(m, part).start())
            pl.when(jnp.logical_not(away))(lambda m=m, part=part: keep(m, part).start())

    @pl.when(enters)
    def _():
        for part in range(parts):
            for k in range(4):
                zz = lax.rem(z + k, 4)
                if k == 0:
                    keep(0, part).wait()
                else:
                    from_column(zz, part).wait_recv()
                to_row(zz, k, part).start()
                to_core(zz, y, k, part).start()
            if part > 0:
                for k in range(4):
                    zz = lax.rem(z + k, 4)
                    from_row(zz, k, part - 1).wait_recv()
                    to_core(zz, 1 - y, 4 + k, part - 1).start()
        for k in range(4):
            zz = lax.rem(z + k, 4)
            from_row(zz, k, parts - 1).wait_recv()
            to_core(zz, 1 - y, 4 + k, parts - 1).start()
        for k in range(4):
            zz = lax.rem(z + k, 4)
            for part in range(parts):
                to_row(zz, k, part).wait_send()
                to_core(zz, y, k, part).wait_send()
                to_core(zz, 1 - y, 4 + k, part).wait_send()

    @pl.when(jnp.logical_not(enters))
    def _():
        for zz in range(4):
            for yy in range(2):
                for part in range(parts):
                    to_core(zz, yy, 0, part).wait_recv()

    for m in range(2):
        for part in range(parts):
            pl.when(2 * c + m != z)(lambda m=m, part=part: to_column(m, part).wait_send())


def gather_normed(rows, gain):
    micro, block, width = rows.shape
    parts = 4
    sems = [(parts,), (2, parts), (4, parts), (4, parts), (4, parts), (8, parts), (8, parts)]
    return pl.pallas_call(
        gather_kernel,
        out_shape=struct((8 * block, width), bf16),
        in_specs=[pl.BlockSpec(memory_space=pltpu.VMEM)] * 2,
        out_specs=pl.BlockSpec(memory_space=pl.ANY),
        scratch_shapes=[pltpu.VMEM((micro, block, width), bf16)]
        + [pltpu.SemaphoreType.DMA(shape) for shape in sems],
        compiler_params=pltpu.CompilerParams(
            collective_id=0, has_side_effects=True, vmem_limit_bytes=32 * 2**20
        ),
        name="gather_normed",
    )(rows, gain)


def finish_kernel(
    part_ref, up_ref, square_ref, down_ref, small_ref, rows_ref, cot_ref, gain_ref,
    grad_out, up_out, query_out, key_out, value_out, down_out, small_out,
    own, from_core, to_row, from_row, to_owner, owned,
    up_x, up_sum, up_near, up_pair, up_far, up_end, sq_x, sq_sum, sq_near, sq_pair, sq_far, sq_end,
    dn_x, dn_sum, dn_near, dn_pair, dn_far, dn_end,
    up_go, up_got, sq_go, sq_got, dn_go, dn_got, small_x, small_sum, small_z, small_all,
    own_sem, c_sent, c_landed, y_sent, y_landed, o_sent, o_landed,
    x_sent, x_landed, near_sent, near_landed, far_sent, far_landed,
    up_sem, sq_sent, sq_landed, dn_sent, dn_landed, sx_sem, sz_sent, sz_landed, sh_sent, sh_landed,
):
    first, z, y, x, c = where_am_i()
    head = 2 * c + y

    def device(zz, yy, cc, xx=x):
        return (first + 2 * zz + yy, 2 * xx + cc)

    around = [lax.rem(z + k, 4) for k in range(1, 4)]
    group = [(1 - y, c), (y, 1 - c), (1 - y, 1 - c)]
    others = [device(z, yy, cc) for yy, cc in group] + [device(z, y, c, 1 - x)]
    for zz in around:
        others += [device(zz, yy, cc) for yy, cc in [(y, c)] + group]
    greet(others)

    sources = (up_ref, square_ref, down_ref)
    from_x = (up_x, sq_x, dn_x)
    totals = (up_sum, sq_sum, dn_sum)
    from_near = (up_near, sq_near, dn_near)
    pairs = (up_pair, sq_pair, dn_pair)
    from_far = (up_far, sq_far, dn_far)
    ends = (up_end, sq_end, dn_end)
    high, low = z // 2, lax.rem(z, 2)
    cut = up_sum.shape[2] // 2
    items = [(0, k, pl.ds(m * cut, cut)) for m in range(2) for k in range(2)]
    items += [(p, k, slice(None)) for p in (2, 1) for k in range(2)]
    count = len(items)
    half = own.shape[1]

    def to_x(n):
        p, k, lanes = items[n]
        size = 2 * totals[p].shape[1]
        here = (pl.ds(k * size, size), lanes)
        return remote(
            sources[p].at[(1 - x, *here)], from_x[p].at[here], x_sent.at[n], x_landed.at[n],
            device(z, y, c, 1 - x),
        )

    def to_near(n):
        p, k, lanes = items[n]
        return remote(
            totals[p].at[2 * k + 1 - low, :, lanes], from_near[p].at[k, :, lanes],
            near_sent.at[n], near_landed.at[n], device(z + 1 - 2 * low, y, c),
        )

    def to_far(n):
        p, k, lanes = items[n]
        return remote(
            pairs[p].at[k, :, lanes], from_far[p].at[:, lanes], far_sent.at[n], far_landed.at[n],
            device(z + 2 - 4 * high, y, c),
        )

    def block(zz, yy, cc):
        start = ((2 * zz + yy) * 2 + cc) * half
        return part_ref.at[pl.ds(pl.multiple_of(start, half), half)]

    def load(zz, yy, k):
        return pltpu.make_async_copy(block(zz, yy, c), own.at[k], own_sem.at[k])

    def to_c(zz, yy, k):
        return remote(
            block(zz, yy, 1 - c), from_core.at[2 * zz + yy], c_sent.at[k],
            c_landed.at[2 * zz + yy], device(z, y, 1 - c),
        )

    def to_y(zz):
        return remote(
            to_row.at[zz], from_row.at[zz], y_sent.at[zz], y_landed.at[zz], device(z, 1 - y, c)
        )

    def to_o(zz):
        return remote(
            to_owner.at[zz], owned.at[lax.rem(z, 2), c], o_sent.at[zz],
            o_landed.at[lax.rem(z, 2), c], device(zz, y, z // 2),
        )

    ahead = 2
    small_to_x = remote(
        small_ref, small_x, sx_sem.at[0], sx_sem.at[1], device(z, y, c, 1 - x)
    )
    small_to_x.start()
    for n in range(ahead):
        to_x(n).start()
    for yy, at in ((1 - y, 0), (y, 4)):
        for zz in range(4):
            to_c(zz, yy, at + zz).start()
            load(zz, yy, at + zz).start()

    def core_sum(zz, yy, k):
        load(zz, yy, k).wait()
        to_c(zz, yy, k).wait_recv()
        return (own[k].astype(f32) + from_core[2 * zz + yy].astype(f32)).astype(bf16)

    for zz in range(4):
        to_row[zz] = core_sum(zz, 1 - y, zz)
        if zz < ahead:
            to_y(zz).start()
    for zz in range(4):
        own[4 + zz] = core_sum(zz, y, 4 + zz)

    def row_step(zz):
        to_y(zz).wait_recv()
        if zz + ahead < 4:
            to_y(zz + ahead).start()
        to_owner[zz] = (own[4 + zz].astype(f32) + from_row[zz].astype(f32)).astype(bf16)
        stays = jnp.logical_and(z == zz, z // 2 == c)

        @pl.when(stays)
        def _():
            owned[lax.rem(z, 2), c] = to_owner[zz]

        pl.when(jnp.logical_not(stays))(lambda: to_o(zz).start())

    def x_step(n):
        p, k, lanes = items[n]
        size = totals[p].shape[1]
        to_x(n).wait_recv()
        if n + ahead < count:
            to_x(n + ahead).start()
        for at in (2 * k, 2 * k + 1):
            here = (pl.ds(at * size, size), lanes)
            totals[p][at, :, lanes] = (
                sources[p][(x, *here)].astype(f32) + from_x[p][here].astype(f32)
            ).astype(bf16)
        to_near(n).start()

    def near_step(n):
        p, k, lanes = items[n]
        to_near(n).wait_recv()
        pairs[p][k, :, lanes] = (
            totals[p][2 * k + low, :, lanes].astype(f32) + from_near[p][k, :, lanes].astype(f32)
        ).astype(bf16)
        pl.when(high != k)(lambda: to_far(n).start())

    def far_step(n):
        p, k, lanes = items[n]

        @pl.when(high == k)
        def _():
            to_far(n).wait_recv()
            ends[p][:, lanes] = pairs[p][k, :, lanes].astype(f32) + from_far[p][:, lanes].astype(f32)

    def small_to_z(k):
        return remote(
            small_sum, small_z.at[z], sz_sent.at[k], sz_landed.at[z], device(around[k], y, c)
        )

    def small_from_z(k):
        return remote(
            small_sum, small_z.at[around[k]], sz_sent.at[k], sz_landed.at[around[k]],
            device(around[k], y, c),
        )

    def to_group(k, src, dst, sent, landed):
        yy, cc = group[k]
        return remote(src, dst, sent.at[k], landed, device(z, yy, cc))

    def small_to_head(k):
        return to_group(k, small_all.at[head], small_all.at[head], sh_sent, sh_landed.at[head])

    def small_from_head(k):
        at = 2 * group[k][1] + group[k][0]
        return to_group(k, small_all.at[at], small_all.at[at], sh_sent, sh_landed.at[at])

    for n in range(count + 3):
        if n < 4:
            row_step(n)
        if n < count:
            x_step(n)
        if 1 <= n <= count:
            near_step(n - 1)
        if n >= 3:
            far_step(n - 3)
        if n == 2:
            small_to_x.wait_recv()
            small_sum[...] = small_ref[...] + small_x[...]
            small_z[z] = small_sum[...]
            for k in range(3):
                small_to_z(k).start()
        if n == 5:
            for k in range(3):
                small_from_z(k).wait_recv()
            total = small_z[0]
            for zz in range(1, 4):
                total = total + small_z[zz]
            small_all[head] = total
            for k in range(3):
                small_to_head(k).start()

    rows = up_go.shape[0]
    cols = up_go.shape[1]

    def use_up(value):
        mine = jnp.where(y == 0, value[:rows], value[rows:])
        up_go[...] = jnp.where(y == 0, value[rows:], value[:rows]).astype(bf16)
        for yy in range(2):

            @pl.when(y == yy)
            def _():
                up_out[:, cols * yy : cols * yy + cols] = mine

    use_up(up_end[...])
    up_to_y = remote(up_go, up_got, up_sem.at[0], up_sem.at[1], device(z, 1 - y, c))
    up_to_y.start()

    tall, wide = sq_got.shape[1], sq_got.shape[2] // 3

    def use_square(value):
        for yy in range(2):
            for cc in range(2):
                for a in range(3):
                    sq_go[yy, cc, :, wide * a : wide * a + wide] = value[
                        tall * yy : tall * yy + tall,
                        (2 * a + cc) * wide : (2 * a + cc) * wide + wide,
                    ].astype(bf16)

    use_square(sq_end[...])
    sq_got[head] = sq_go[y, c]

    def square_to(k):
        yy, cc = group[k]
        return to_group(k, sq_go.at[yy, cc], sq_got.at[head], sq_sent, sq_landed.at[head])

    def square_from(k):
        at = 2 * group[k][1] + group[k][0]
        return to_group(k, sq_go.at[0, 0], sq_got.at[at], sq_sent, sq_landed.at[at])

    for k in range(3):
        square_to(k).start()

    span = dn_go.shape[2]

    def use_down(value):
        for cc in range(2):
            dn_go[cc] = value[:, span * cc : span * cc + span].astype(bf16)

    use_down(dn_end[...])

    def down_to(cc):
        return remote(
            dn_go.at[cc], dn_got.at[lax.rem(z, 2)], dn_sent.at[cc], dn_landed.at[lax.rem(z, 2)],
            device(head, z // 2, cc),
        )

    def down_from(k):
        return remote(
            dn_go.at[0], dn_got.at[k], dn_sent.at[0], dn_landed.at[k],
            device(2 * y + k, lax.rem(z, 2), z // 2),
        )

    home = jnp.logical_and(head == z, z // 2 == y)
    for cc in range(2):
        stays = jnp.logical_and(home, c == cc)

        @pl.when(stays)
        def _():
            dn_got[lax.rem(z, 2)] = dn_go[cc]

        pl.when(jnp.logical_not(stays))(lambda: down_to(cc).start())

    for m in range(2):
        for cc in range(2):
            own_part = jnp.logical_and(2 * c + m == z, c == cc)
            landed = remote(
                to_owner.at[0], owned.at[m, cc], o_sent.at[0], o_landed.at[m, cc],
                device(2 * c + m, y, cc),
            )
            pl.when(jnp.logical_not(own_part))(lambda landed=landed: landed.wait_recv())
        for cc in range(2):
            here = pl.ds(cc * half, half)
            row_hat, rstd = normalize(rows_ref[m, here].astype(f32))
            scaled = owned[m, cc].astype(f32) * gain_ref[...]
            d_row = rstd * (
                scaled
                - jnp.mean(scaled, axis=-1, keepdims=True)
                - row_hat * jnp.mean(scaled * row_hat, axis=-1, keepdims=True)
            )
            grad_out[m, here] = (cot_ref[m, here].astype(f32) + d_row).astype(bf16)

    up_to_y.wait_recv()
    for yy in range(2):

        @pl.when(y == yy)
        def _():
            up_out[:, cols * (1 - yy) : cols * (1 - yy) + cols] = up_got[...].astype(f32)

    for k in range(3):
        small_from_head(k).wait_recv()
    small_out[...] = small_all[...]
    for k in range(3):
        square_from(k).wait_recv()
    for a, ref in enumerate((query_out, key_out, value_out)):
        ref[...] = sq_got[:, :, wide * a : wide * a + wide].astype(f32)
    for k in range(2):
        mine = jnp.logical_and(home, jnp.logical_and(lax.rem(z, 2) == k, z // 2 == c))
        pl.when(jnp.logical_not(mine))(lambda: down_from(k).wait_recv())
        tall = dn_got.shape[1]
        down_out[tall * k : tall * k + tall] = dn_got[k].astype(f32)

    small_to_x.wait_send()
    up_to_y.wait_send()
    for n in range(count):
        to_x(n).wait_send()
        to_near(n).wait_send()
        pl.when(high != items[n][1])(lambda: to_far(n).wait_send())
    for yy, at in ((1 - y, 0), (y, 4)):
        for zz in range(4):
            to_c(zz, yy, at + zz).wait_send()
    for zz in range(4):
        to_y(zz).wait_send()
        stays = jnp.logical_and(z == zz, z // 2 == c)
        pl.when(jnp.logical_not(stays))(lambda: to_o(zz).wait_send())
    for k in range(3):
        small_to_z(k).wait_send()
        small_to_head(k).wait_send()
        square_to(k).wait_send()
    for cc in range(2):
        stays = jnp.logical_and(home, c == cc)
        pl.when(jnp.logical_not(stays))(lambda: down_to(cc).wait_send())


def finish(part, up, square, down, small, rows, cot, gain):
    micro, block, width = rows.shape
    half = block // 2
    size = down.shape[1]
    lines = small.shape[0]
    scratch = [
        ((8, half, width), bf16), ((8, half, width), bf16), ((4, half, width), bf16),
        ((4, half, width), bf16), ((4, half, width), bf16), ((2, 2, half, width), bf16),
    ]
    for piece in (up, square, down):
        _, tall, wide = piece.shape
        scratch += [((tall, wide), bf16), ((4, tall // 4, wide), bf16)]
        scratch += [((2, tall // 4, wide), bf16)] * 2
        scratch += [((tall // 4, wide), bf16), ((tall // 4, wide), f32)]
    scratch += [
        ((width // 8, size), bf16), ((width // 8, size), bf16),
        ((2, 2, size // 8, 3 * size // 4), bf16), ((4, size // 8, 3 * size // 4), bf16),
        ((2, size // 4, width // 4), bf16), ((2, size // 4, width // 4), bf16),
        ((lines, size), f32), ((lines, size), f32), ((4, lines, size), f32), ((4, lines, size), f32),
    ]
    sems = [
        (8,), (8,), (8,), (4,), (4,), (4,), (2, 2), (8,), (8,), (8,), (8,), (8,), (8,),
        (2,), (3,), (4,), (2,), (2,), (2,), (3,), (4,), (3,), (4,),
    ]
    vmem = pl.BlockSpec(memory_space=pltpu.VMEM)
    square_shape = struct((4, size // 8, size // 4), f32)
    return pl.pallas_call(
        finish_kernel,
        out_shape=[
            struct(rows.shape, bf16), struct((width // 8, 2 * size), f32),
            square_shape, square_shape, square_shape,
            struct((size // 2, width // 4), f32), struct((4, lines, size), f32),
        ],
        in_specs=[pl.BlockSpec(memory_space=pl.ANY)] + [vmem] * 7,
        out_specs=[vmem] * 7,
        scratch_shapes=[pltpu.VMEM(shape, dtype) for shape, dtype in scratch]
        + [pltpu.SemaphoreType.DMA(shape) for shape in sems],
        compiler_params=pltpu.CompilerParams(
            collective_id=1, has_side_effects=True, vmem_limit_bytes=vmem_bytes
        ),
        name="finish",
    )(part, up, square, down, small, rows, cot, gain)


def swap(value, axis, mask):
    count = lax.axis_size(axis)
    return lax.ppermute(value, axis, [(s, s ^ mask) for s in range(count)])


def part_of(value, at, count, axis):
    size = value.shape[axis] // count
    return lax.dynamic_slice_in_dim(value, at * size, size, axis)


def halved(value, bit, dim, axis, mask):
    kept = part_of(value, bit, 2, dim).astype(f32)
    return kept + swap(part_of(value, 1 - bit, 2, dim), axis, mask).astype(f32)


def paired(mine, other, bit, dim):
    return jnp.where(
        bit == 0, jnp.concatenate([mine, other], dim), jnp.concatenate([other, mine], dim)
    )


def place():
    at_seq, at_batch = lax.axis_index("seq"), lax.axis_index("batch")
    return (at_seq % 8) // 2, at_seq % 2, at_batch // 2, at_batch % 2


def sent_across(blocks, z):
    got = [lax.dynamic_index_in_dim(blocks, z, 0, keepdims=False)]
    for k in range(1, 4):
        got.append(swap(lax.dynamic_index_in_dim(blocks, z ^ k, 0, keepdims=False), "seq", 2 * k))
    return got


def in_order(got, z):
    got = jnp.stack(got)
    return jnp.stack([lax.dynamic_index_in_dim(got, z ^ k, 0, keepdims=False) for k in range(4)])


def hold(value, *done):
    return lax.optimization_barrier((value, *done))


def gather_first(own):
    z, y, x, c = place()
    slots = paired(own, swap(own, "batch", 1), c, 0)
    return part_of(slots, c, 2, 2)


def gather_last(blocks, other):
    z, y, x, c = place()
    rows, width = blocks.shape[2:]
    both = paired(blocks, other, y, 1)
    return paired(both, swap(both, "batch", 1), c, 3).reshape(8 * rows, 2 * width)


def scatter_first(parts):
    z, y, x, c = place()
    blocks = parts.reshape(4, 2, -1, parts.shape[1])
    return halved(blocks, c, 2, "batch", 1).astype(bf16)


def scatter_last(slots):
    z, y, x, c = place()
    other = swap(part_of(slots, 1 - c, 2, 0), "batch", 1)
    return paired(part_of(slots, c, 2, 0), other, c, 1).astype(f32)


def scatter_sequence(parts):
    z, y, x, c = place()
    blocks = scatter_first(parts)
    blocks = halved(blocks, y, 1, "seq", 1).astype(bf16)[:, 0]
    return scatter_last(in_order(sent_across(blocks, z), z))


def total_over_heads(value):
    value = value + swap(value, "batch", 1)
    return value + swap(value, "seq", 1)


def over_ranges(value, count):
    size = lax.axis_size("seq")
    groups = [[first + 8 * k for k in range(count)] for first in range(8)]
    return lax.all_gather(value, "seq", axis_index_groups=groups) if size > 8 else value[None]


def state_before(state, norm, level, total, ranges):
    index = lax.axis_index("seq") // 8
    summary = (state, norm[0], level[0, 0], total)
    everything = jax.tree.map(lambda part: over_ranges(part, ranges), summary)
    before = state_identity(summary)
    for k in range(ranges - 1):
        new = combine_states(before, jax.tree.map(lambda part: part[k], everything))
        before = jax.tree.map(lambda a, b: jnp.where(k < index, a, b), new, before)
    return (
        before[0],
        jnp.broadcast_to(before[1], norm.shape),
        jnp.broadcast_to(before[2], level.shape),
    )


def cotangent_after(d_state, d_norm, keep, ranges):
    index = lax.axis_index("seq") // 8
    own = (d_state, d_norm)
    everything = jax.tree.map(lambda part: over_ranges(part, ranges), own)
    keeps = over_ranges(keep, ranges)
    after = jax.tree.map(jnp.zeros_like, own)
    for k in range(ranges - 1, 0, -1):
        new = jax.tree.map(lambda a, b: a[k] + keeps[k] * b, everything, after)
        after = jax.tree.map(lambda a, b: jnp.where(k > index, a, b), new, after)
    return after


def reduce_blocks(at, up, square, down, heads):
    count, batch_count = lax.axis_size("seq"), lax.axis_size("batch")
    g_m, g_z = up
    width, size = g_m.shape
    half = size // 2
    squares = [
        jnp.concatenate([square[0, :, k : k + half], square[1, :, k : k + half]], 1)
        for k in range(0, 3 * half, half)
    ]
    g_down = jnp.concatenate([down[0], down[1]], 1)
    inner = heads * size
    up = jnp.zeros((width, 2 * inner), f32)
    up = lax.dynamic_update_slice_in_dim(up, g_m.astype(f32), at * size, 1)
    up = lax.dynamic_update_slice_in_dim(up, g_z.astype(f32), inner + at * size, 1)
    down = lax.dynamic_update_slice_in_dim(
        jnp.zeros((inner, width), f32), g_down.astype(f32), at * size, 0
    )
    full = [up, down]
    for g in squares:
        full.append(
            lax.dynamic_update_slice_in_dim(
                jnp.zeros((heads, size, size), f32), g.astype(f32)[None], at, 0
            )
        )
    blocks = tuple(to_device_blocks(g, count, batch_count) for g in full)
    pieces = lax.psum_scatter(blocks, ("seq", "batch"), scatter_dimension=0, tiled=True)
    s_up, s_down, s_query, s_key, s_value = tuple(p[0] for p in pieces)
    return s_up, jnp.stack([s_query, s_key, s_value], 1), s_down


def head_device(
    tokens, ln_gain, w_up, conv_w, conv_b, w_query, w_key, w_value, gate_w, gate_b,
    out_gain, skip_gain, w_down, d_out,
):
    z, y, x, c = place()
    at = 2 * c + y
    ranges = lax.axis_size("seq") // 8
    direct = ranges == 1 and lax.axis_size("batch") == 4
    head = jnp.reshape(at, (1,)).astype(jnp.int32)
    heads, size, _ = w_query.shape
    inner = heads * size
    conv_row = conv_b.reshape(1, inner)
    out_row = out_gain.reshape(1, inner)
    skip_row = skip_gain.reshape(1, inner)

    normed = gather_normed(tokens[:, 0], ln_gain[None])
    cot_half, normed = hold(gather_first(d_out[:, 0]), normed)
    cot_across = sent_across(cot_half, z)

    gate_own = lax.dynamic_index_in_dim(
        gate_w.reshape(3, heads, size, 8), at, 1, keepdims=False
    ).transpose(0, 2, 1)
    high = lax.reduce_precision(gate_own, 8, 7)
    middle = lax.reduce_precision(gate_own - high, 8, 7)
    low = lax.reduce_precision(gate_own - high - middle, 8, 7)
    gate_parts = jnp.concatenate([high, middle, low, jnp.zeros_like(high)], 1).astype(bf16)
    gate_pairs = (
        jnp.concatenate([high, high, high, middle, middle, low], 1)
        .astype(bf16)
        .transpose(1, 0, 2)
        .reshape(48, 3 * size)
    )

    first = () if ranges == 1 else (shifted(normed[-16:], "seq", 8),)
    mix, conv, q, k, v, gate_z, gates, *halo = lift(
        head, normed, w_up, w_query, w_key, w_value, conv_w, conv_row, gate_parts, *first
    )
    cot_across, gates = hold(cot_across, gates)
    cot_blocks = in_order(cot_across, z)[:, None]
    gates = total_over_heads(gates)
    cot_blocks, gates = hold(cot_blocks, gates)
    cot_row = swap(cot_blocks, "seq", 1)
    gates = jnp.concatenate(
        [
            lax.dynamic_slice_in_dim(gates, at, 1, 0),
            lax.dynamic_slice_in_dim(gates, heads + at, 1, 0)
            + lax.dynamic_slice_in_dim(gate_b, at, 1, 0)[:, None],
        ]
    )
    first = ()
    if ranges > 1:
        first = (
            jnp.zeros((size, size), f32),
            jnp.zeros((8, size), f32),
            jnp.full((8, 128), floor_value, f32),
        )
        *_, state, norm, level = cell_forward(
            head, gates, q, k, v, conv, gate_z, out_row, skip_row, w_down, *first
        )
        total = jnp.sum(jax.nn.log_sigmoid(gates[1]))
        first = state_before(state, norm, level, total, ranges)
    part, head_normed, states, norms, weights, cols, rows, *last = cell_forward(
        head, gates, q, k, v, conv, gate_z, out_row, skip_row, w_down, *first
    )
    cot_row, part = hold(cot_row, part)
    cot = gather_last(cot_blocks, cot_row)
    part = scatter_first(part)
    part, cot = hold(part, cot)
    part_row = swap(part_of(part, 1 - y, 2, 1), "seq", 1)
    after = ()
    if ranges > 1:
        after = (jnp.zeros((size, size), f32), jnp.zeros((8, size), f32))
        *_, d_state, d_norm = cell_backward(
            head, rows, q, k, v, conv, gate_z, head_normed, states, norms, weights, cols, cot,
            out_row, skip_row, w_down, *after,
        )
        keep = jnp.exp(total + first[2][0, 0] - last[2][0, 0])
        after = cotangent_after(d_state, d_norm, keep, ranges)
    dq, dk, dv, dskip, dz, d_rows, g_down, g_gain, *_ = cell_backward(
        head, rows, q, k, v, conv, gate_z, head_normed, states, norms, weights, cols, cot,
        out_row, skip_row, w_down, *after,
    )
    part_row, d_rows = hold(part_row, d_rows)
    part = (part_of(part, y, 2, 1).astype(f32) + part_row.astype(f32)).astype(bf16)[:, 0]
    index = jnp.arange(2 * heads)[:, None]
    d_gate = jnp.where(index == at, d_rows[0:1], jnp.where(index == heads + at, d_rows[1:2], 0.0))
    d_gate = total_over_heads(d_gate)
    part, d_gate = hold(part, d_gate)
    part_across = sent_across(part, z)
    first = ()
    if ranges > 1:
        *_, later = lower(
            head, d_gate, dq, dk, dv, dskip, dz, mix, conv, q, k, v, normed,
            w_query, w_key, w_value, w_up, conv_w, conv_row, gate_pairs, g_gain,
            halo[0], jnp.zeros((8, size), f32),
        )
        first = (halo[0], shifted(later, "seq", -8))
    d_part, square, up, small, *_ = lower(
        head, d_gate, dq, dk, dv, dskip, dz, mix, conv, q, k, v, normed,
        w_query, w_key, w_value, w_up, conv_w, conv_row, gate_pairs, g_gain, *first,
    )
    part_across, small = hold(part_across, small)
    block_rows = scatter_last(in_order(part_across, z))
    block_rows = (tokens[:, 0].astype(f32) + block_rows).astype(bf16)
    if direct:
        grad_rows, s_up, s_query, s_key, s_value, s_down, small = finish(
            d_part, up, square, g_down, small, tokens[:, 0], d_out[:, 0], ln_gain[None]
        )
    else:
        d_normed = scatter_sequence(d_part)
        row_f = tokens[:, 0].astype(f32)
        centre = row_f - jnp.mean(row_f, axis=-1, keepdims=True)
        rstd = lax.rsqrt(jnp.mean(centre * centre, axis=-1, keepdims=True) + norm_epsilon)
        row_hat = centre * rstd
        scaled = d_normed * ln_gain
        d_row = rstd * (
            scaled
            - jnp.mean(scaled, axis=-1, keepdims=True)
            - row_hat * jnp.mean(scaled * row_hat, axis=-1, keepdims=True)
        )
        grad_rows = (d_out[:, 0].astype(f32) + d_row).astype(bf16)
        s_up, squares, s_down = reduce_blocks(at, up, square, g_down, heads)
        s_query, s_key, s_value = squares[:, 0], squares[:, 1], squares[:, 2]
        small = jnp.where(jnp.arange(heads)[:, None, None] == at, small, 0.0)
        small = lax.psum(small, ("seq", "batch"))
    s_ln = jnp.sum(small[:, 32:34], 0).reshape(-1) / ln_gain
    s_gate_w = small[:, :24].reshape(heads, 3, 8, size).transpose(1, 0, 3, 2).reshape(3 * inner, 8)
    s_conv_w = small[:, 24:28].transpose(1, 0, 2).reshape(4, inner)
    return (
        block_rows[:, None],
        grad_rows[:, None],
        s_ln,
        s_up,
        s_conv_w,
        small[:, 28].reshape(inner),
        s_query,
        s_key,
        s_value,
        s_gate_w,
        small[:, 31, 0],
        small[:, 29].reshape(inner),
        small[:, 30].reshape(inner),
        s_down,
    )


def solution(mesh):
    placed = (P(None, "batch", "seq", None),) + (P(),) * 12 + (P(None, "batch", "seq", None),)
    return jax.shard_map(
        head_device,
        mesh=mesh,
        in_specs=placed,
        out_specs=(
            P(None, "batch", "seq", None),
            P(None, "batch", "seq", None),
            P(),
            P("seq", "batch"),
            P(),
            P(),
            P(None, "seq", "batch"),
            P(None, "seq", "batch"),
            P(None, "seq", "batch"),
            P(),
            P(),
            P(),
            P(),
            P("seq", "batch"),
        ),
        check_vma=False,
    )
```

```python
from functools import partial

import jax
import jax.numpy as jnp
from jax import lax
from jax.experimental import pallas as pl
from jax.experimental.pallas import tpu as pltpu
from jax.sharding import PartitionSpec as P

norm_epsilon = 1e-05
floor_value = -1e30


def shifted(value, axis, steps):
    count = lax.axis_size(axis)
    initial, last = (max(0, -steps), min(count, count - steps))
    return lax.ppermute(value, axis, [(source, source + steps) for source in range(initial, last)])


def combine_states(earlier, later):
    top = jnp.maximum(later[3] + earlier[2], later[2])
    keep_first = jnp.exp(later[3] + earlier[2] - top)
    keep_second = jnp.exp(later[2] - top)
    merged_c = keep_first[..., None, None] * earlier[0] + keep_second[..., None, None] * later[0]
    merged_n = keep_first[..., None] * earlier[1] + keep_second[..., None] * later[1]
    return (merged_c, merged_n, top, earlier[3] + later[3])


def state_identity(template):
    return (
        jnp.zeros_like(template[0]),
        jnp.zeros_like(template[1]),
        jnp.full_like(template[2], floor_value),
        jnp.zeros_like(template[3]),
    )


def head_output(hidden, out_gain, skip_gain, conv_out, gate_z):
    centre = hidden - jnp.mean(hidden, axis=-1, keepdims=True)
    spread = jnp.mean(centre * centre, axis=-1, keepdims=True)
    normed = centre * lax.rsqrt(spread + norm_epsilon)
    flat_out = normed.transpose(1, 0, 2).reshape(hidden.shape[1], -1) * out_gain
    return (flat_out + skip_gain * conv_out) * jax.nn.silu(gate_z)


def output_tail(
    query_f,
    key_f,
    value_f,
    gate_pre,
    conv_f,
    gate_z,
    out_gain,
    skip_gain,
    state_c,
    state_n,
    state_m,
):
    head_count = gate_pre.shape[1] // 2
    in_gate = gate_pre[:, :head_count].T
    log_forget = jax.nn.log_sigmoid(gate_pre[:, head_count:]).T
    hidden = cell_hidden(
        to_heads(query_f, head_count),
        to_heads(key_f, head_count),
        to_heads(value_f, head_count),
        in_gate,
        log_forget,
        state_c,
        state_n,
        state_m,
    )
    return head_output(hidden, out_gain, skip_gain, conv_f, gate_z)


def state_tail(key_f, value_f, gate_pre, state_c, state_n, state_m):
    head_count = gate_pre.shape[1] // 2
    in_gate = gate_pre[:, :head_count].T
    log_forget = jax.nn.log_sigmoid(gate_pre[:, head_count:]).T
    return cell_state(
        to_heads(key_f, head_count),
        to_heads(value_f, head_count),
        in_gate,
        log_forget,
        state_c,
        state_n,
        state_m,
    )


def to_device_blocks(grad_full, seq_count, batch_count):
    if grad_full.ndim == 2:
        rows, cols = grad_full.shape
        split = grad_full.reshape(seq_count, rows // seq_count, batch_count, cols // batch_count)
        return split.transpose(0, 2, 1, 3).reshape(
            seq_count * batch_count, rows // seq_count, cols // batch_count
        )
    heads, rows, cols = grad_full.shape
    split = grad_full.reshape(heads, seq_count, rows // seq_count, batch_count, cols // batch_count)
    return split.transpose(1, 3, 0, 2, 4).reshape(
        seq_count * batch_count, heads, rows // seq_count, cols // batch_count
    )


f32 = jnp.float32
bf16 = jnp.bfloat16
chunk_len = 256
wide_len = 512
vmem_bytes = 56 * 1024 * 1024


def mm(a, b):
    return lax.dot_general(a, b, (((1,), (0,)), ((), ())), preferred_element_type=f32)


def mm_nt(a, b):
    return lax.dot_general(a, b, (((1,), (1,)), ((), ())), preferred_element_type=f32)


def mm_tn(a, b):
    return lax.dot_general(a, b, (((0,), (0,)), ((), ())), preferred_element_type=f32)


def split_three(value):
    high = value.astype(bf16)
    rest = value - high.astype(f32)
    middle = rest.astype(bf16)
    low = (rest - middle.astype(f32)).astype(bf16)
    return high, middle, low


def conv_taps(ext, length):
    return [pltpu.roll(ext, 3 - j, 0)[8 : 8 + length] if j < 3 else ext[8 : 8 + length] for j in range(4)]


def lift_kernel(chained, head_ref, normed, w_mix, w_gate, w_q, w_k, w_v, conv_w, conv_b, gate_w, *refs):
    if chained:
        rows_before, *refs, halo_out, carry = refs
    else:
        *refs, carry = refs
    mix_out, conv_out, q_out, k_out, v_out, z_out, gate_out = refs
    length = normed.shape[0]

    @pl.when(pl.program_id(0) == 0)
    def _():
        if chained:
            mix_before = mm(rows_before[...], w_mix[...]).astype(bf16)
            halo_out[...] = mix_before
            carry[...] = mix_before[8:16].astype(f32)
        else:
            carry[...] = jnp.zeros_like(carry)

    rows = normed[...]
    mix = mm(rows, w_mix[...]).astype(bf16)
    mix_out[...] = mix
    z_out[...] = mm(rows, w_gate[...])
    mix_f = mix.astype(f32)
    taps = conv_taps(jnp.concatenate([carry[...], mix_f], axis=0), length)
    carry[...] = mix_f[length - 8 :]
    summed = conv_b[...]
    for j in range(4):
        summed = summed + conv_w[j : j + 1, :] * taps[j]
    conv = (summed * jax.nn.sigmoid(summed)).astype(bf16)
    conv_out[...] = conv
    q = mm(conv, w_q[0]).astype(bf16)
    k = mm(conv, w_k[0]).astype(bf16)
    v = mm(mix, w_v[0]).astype(bf16)
    q_out[...] = q
    k_out[...] = k
    v_out[...] = v
    parts = mm_nt(gate_w[0], q) + mm_nt(gate_w[1], k) + mm_nt(gate_w[2], v)
    gate_out[...] = parts[0:8] + parts[8:16] + parts[16:24]


def gate_rows(gates, causal, diagonal):
    in_row = gates[0:1, :]
    pre = gates[1:2, :]
    log_forget = jnp.minimum(pre, 0.0) - jnp.log1p(jnp.exp(-jnp.abs(pre)))
    run_col = jnp.sum(jnp.where(causal, log_forget, 0.0), axis=1, keepdims=True)
    run_row = jnp.sum(jnp.where(diagonal, run_col, 0.0), axis=0, keepdims=True)
    return in_row - run_row, run_col, log_forget


def masks(length):
    row = lax.broadcasted_iota(jnp.int32, (length, length), 0)
    col = lax.broadcasted_iota(jnp.int32, (length, length), 1)
    return row >= col, row == col


def cell_forward_kernel(
    chained, head_ref, gates, q_ref, k_ref, v_ref, conv_ref, z_ref, out_gain, skip_gain, w_down, *refs
):
    if chained:
        *first, part_out, normed_out, state_out, norm_out, weight_out, col_out, row_out = refs[:10]
        *final, state, norm, level = refs[10:]
    else:
        part_out, normed_out, state_out, norm_out, weight_out, col_out, row_out = refs[:7]
        state, norm, level = refs[7:]
    length = q_ref.shape[0]
    head_size = q_ref.shape[1]
    scale = head_size ** (-0.5)

    @pl.when(pl.program_id(0) == 0)
    def _():
        if chained:
            for ref, value in zip((state, norm, level), first):
                ref[...] = value[...]
        else:
            state[...] = jnp.zeros_like(state)
            norm[...] = jnp.zeros_like(norm)
            level[...] = jnp.full_like(level, floor_value)

    causal, diagonal = masks(length)
    a_row, run_col, log_forget = gate_rows(gates[...], causal, diagonal)
    before = level[0:1, 0:1]
    top = jnp.maximum(
        before, jnp.max(jnp.where(causal, a_row, floor_value), axis=1, keepdims=True)
    )
    decay = jnp.exp(jnp.where(causal, a_row - top, floor_value))
    q = q_ref[...]
    k = k_ref[...]
    v = v_ref[...]
    q_f = q.astype(f32)
    weights = decay * (mm_nt(q, k) * scale)
    weights_low = weights.astype(bf16)
    weight_out[...] = weights_low
    from_state = jnp.exp(before - top)
    state_low = state[...].astype(bf16)
    state_out[0] = state_low
    norm_row = norm[0:1, :]
    norm_out[0] = norm[...]
    numerator = mm(weights_low, v) + (from_state * scale) * mm(q, state_low)
    denominator = jnp.sum(weights, axis=1, keepdims=True) + (from_state * scale) * jnp.sum(
        q_f * norm_row, axis=1, keepdims=True
    )
    floor = jnp.exp(-(run_col + top))
    size = jnp.abs(denominator)
    inverse = 1.0 / jnp.maximum(size, floor)
    hidden = numerator * inverse
    centre = hidden - jnp.mean(hidden, axis=1, keepdims=True)
    spread = jnp.mean(centre * centre, axis=1, keepdims=True)
    rstd = lax.rsqrt(spread + norm_epsilon)
    normed = centre * rstd
    normed_out[...] = normed
    gate_z = z_ref[...]
    gated = (normed * out_gain[...] + skip_gain[...] * conv_ref[...].astype(f32)) * (
        gate_z * jax.nn.sigmoid(gate_z)
    )
    part_out[...] = mm(gated.astype(bf16), w_down[...]).astype(bf16)
    factor = jnp.where(
        size > floor,
        jnp.where(denominator > 0, 1.0, -1.0) * inverse * (norm_epsilon * rstd * rstd),
        0.0,
    )
    lane = lax.broadcasted_iota(jnp.int32, (length, 128), 1)
    packed = jnp.where(lane == 0, rstd, inverse)
    packed = jnp.where(lane == 2, from_state, packed)
    packed = jnp.where(lane == 3, top, packed)
    col_out[...] = jnp.where(lane == 4, factor, packed)
    sub = lax.broadcasted_iota(jnp.int32, (8, length), 0)
    row_out[...] = jnp.where(sub == 0, a_row, 1.0 - jnp.exp(log_forget))
    last = top[length - 1 : length, :]
    a_col = jnp.sum(jnp.where(diagonal, a_row, 0.0), axis=1, keepdims=True)
    weighted = k.astype(f32) * jnp.exp(a_col - last)
    keep = jnp.exp(before - last)
    state[...] = keep * state[...] + mm_tn(weighted.astype(bf16), v)
    norm[...] = keep * norm[...] + jnp.sum(weighted, axis=0, keepdims=True)
    level[...] = jnp.broadcast_to(run_col[length - 1 : length, :] + last, level.shape)
    if chained:
        for ref, value in zip(final, (state, norm, level)):
            ref[...] = value[...]


def cell_backward_kernel(
    chained, head_ref, rows_ref, q_ref, k_ref, v_ref, conv_ref, z_ref, normed_ref, state_ref, norm_ref,
    weight_ref, col_ref, cot_ref, rows_in, out_gain, skip_gain, w_down, *refs
):
    if chained:
        first, refs = refs[:2], refs[2:]
    dq_out, dk_out, dv_out, dskip_out, dz_out, gate_out, g_down_out, g_z_out, g_gain_out, *refs = refs
    *final, d_state, d_norm, g_down, g_z, g_gain = refs
    length = q_ref.shape[0]
    head_size = q_ref.shape[1]
    scale = head_size ** (-0.5)

    @pl.when(pl.program_id(0) == 0)
    def _():
        if chained:
            d_state[...] = first[0][...]
            d_norm[...] = first[1][...]
        else:
            d_state[...] = jnp.zeros_like(d_state)
            d_norm[...] = jnp.zeros_like(d_norm)
        g_down[...] = jnp.zeros_like(g_down)
        g_z[...] = jnp.zeros_like(g_z)
        g_gain[...] = jnp.zeros_like(g_gain)

    causal, diagonal = masks(length)
    rstd = col_ref[:, 0:1]
    inverse = col_ref[:, 1:2]
    from_state = col_ref[:, 2:3]
    top = col_ref[:, 3:4]
    factor = col_ref[:, 4:5]
    a_row = rows_ref[0:1, :]
    q = q_ref[...]
    k = k_ref[...]
    v = v_ref[...]
    q_f = q.astype(f32)
    k_f = k.astype(f32)
    conv = conv_ref[...].astype(f32)
    normed = normed_ref[...]
    gate_z = z_ref[...]
    cot = cot_ref[...]
    opened = jax.nn.sigmoid(gate_z)
    silu = gate_z * opened
    head_in = normed * out_gain[...] + skip_gain[...] * conv
    g_down[...] += mm_tn((head_in * silu).astype(bf16), cot)
    d_gated = mm_nt(cot, w_down[...])
    d_z = (d_gated * head_in * (opened * (1.0 + gate_z * (1.0 - opened)))).astype(bf16)
    dz_out[...] = d_z
    g_z[...] += mm_tn(rows_in[...], d_z)
    d_head = d_gated * silu
    g_gain[0:1, :] += jnp.sum(d_head * normed, axis=0, keepdims=True)
    g_gain[1:2, :] += jnp.sum(d_head * conv, axis=0, keepdims=True)
    dskip_out[...] = skip_gain[...] * d_head
    d_hat = d_head * out_gain[...]
    along = jnp.sum(d_hat * normed, axis=1, keepdims=True)
    d_hidden = rstd * (
        d_hat - jnp.mean(d_hat, axis=1, keepdims=True) - normed * (along / head_size)
    )
    d_num = d_hidden * inverse
    d_den = -along * factor
    d_num_low = d_num.astype(bf16)
    decay = jnp.exp(jnp.where(causal, a_row - top, floor_value))
    d_scores = ((mm_nt(d_num_low, v) + d_den) * (decay * scale)).astype(bf16)
    through = from_state * scale
    dq_near = mm(d_scores, k)
    dq_far = (
        mm_nt((d_num * through).astype(bf16), state_ref[0])
        + (through * d_den) * norm_ref[0, 0:1, :]
    )
    last = top[length - 1 : length, :]
    keep = from_state[length - 1 : length, :]
    a_col = jnp.sum(jnp.where(diagonal, a_row, 0.0), axis=1, keepdims=True)
    key_weight = jnp.exp(a_col - last)
    d_state_low = d_state[...].astype(bf16)
    dk_near = mm_tn(d_scores, q)
    dk_far = key_weight * (mm_nt(v, d_state_low) + d_norm[0:1, :])
    dv = mm_tn(weight_ref[...], d_num_low) + mm((k_f * key_weight).astype(bf16), d_state_low)
    dq_out[...] = dq_near + dq_far
    dk_out[...] = dk_near + dk_far
    dv_out[...] = dv
    held = state_ref[0].astype(f32) * d_state[...]
    held = jnp.sum(jnp.sum(held, axis=0, keepdims=True) + norm_ref[0, 0:1, :] * d_norm[0:1, :])
    q_state = q_f * through
    d_state[...] = keep * d_state[...] + mm_tn(q_state.astype(bf16), d_num_low)
    d_norm[...] = keep * d_norm[...] + jnp.sum(q_state * d_den, axis=0, keepdims=True)
    q_dot = jnp.sum(q_f * (dq_near + dq_far), axis=1, keepdims=True)
    k_near = jnp.sum(k_f * dk_near, axis=1, keepdims=True)
    k_far = jnp.sum(k_f * dk_far, axis=1, keepdims=True)
    d_in = jnp.sum(jnp.where(diagonal, k_near + k_far, 0.0), axis=0, keepdims=True)
    d_log = jnp.sum(
        jnp.where(causal, q_dot - k_near, jnp.where(diagonal, 0.0, k_far)), axis=0, keepdims=True
    )
    d_log = d_log + keep * held
    sub = lax.broadcasted_iota(jnp.int32, (8, length), 0)
    d_pre = d_log * rows_ref[1:2, :]
    gate_out[...] = jnp.where(sub == 0, d_in, d_pre)
    g_gain[2:3, :] += jnp.broadcast_to(jnp.sum(d_pre, axis=1, keepdims=True), (1, head_size))

    @pl.when(pl.program_id(0) == pl.num_programs(0) - 1)
    def _():
        if chained:
            final[0][...] = d_state[...]
            final[1][...] = d_norm[...]
        half = g_down.shape[1] // 2
        g_down_out[0] = g_down[:, :half].astype(bf16)
        g_down_out[1] = g_down[:, half:].astype(bf16)
        g_z_out[...] = g_z[...].astype(bf16)
        g_gain_out[...] = g_gain[...]


def lower_first(d_gate, dq_ref, dk_ref, dv_ref, mix_ref, conv_ref, q_ref, k_ref, v_ref, gate_w,
                g_q, g_k, g_v, g_small):
    high, middle, low = split_three(d_gate[...])
    left = jnp.concatenate([high, middle, low, high, middle, high], axis=0)
    d_joined = mm_tn(left, gate_w[...])
    size = q_ref.shape[1]
    query_low = (dq_ref[...] + d_joined[:, :size]).astype(bf16)
    key_low = (dk_ref[...] + d_joined[:, size : 2 * size]).astype(bf16)
    value_low = (dv_ref[...] + d_joined[:, 2 * size :]).astype(bf16)
    conv = conv_ref[...]
    g_q[...] += mm_tn(conv, query_low)
    g_k[...] += mm_tn(conv, key_low)
    g_v[...] += mm_tn(mix_ref[...], value_low)
    three = jnp.concatenate([high, middle, low], axis=0)
    for at, ref in enumerate((q_ref, k_ref, v_ref)):
        got = mm(three, ref[...])
        g_small[8 * at : 8 * at + 8, :] += got[0:8] + got[8:16] + got[16:24]
    return query_low, key_low, value_low


def lower_second(
    edge, last, lows, dskip_ref, dz_ref, mix_ref, mix_before, normed, w_q, w_k, w_v, w_mix, w_gate,
    conv_w, conv_b, g_gain, g_small, later,
):
    query_low, key_low, value_low = lows
    length, size = mix_ref.shape
    mix = mix_ref[...]
    d_conv = dskip_ref[...] + mm_nt(query_low, w_q[...]) + mm_nt(key_low, w_k[...])
    halo = jnp.where(last, edge, mix_before[8:16, :].astype(f32))
    taps = conv_taps(jnp.concatenate([halo, mix.astype(f32)], axis=0), length)
    summed = conv_b[...]
    for j in range(4):
        summed = summed + conv_w[j : j + 1, :] * taps[j]
    opened = jax.nn.sigmoid(summed)
    d_summed = d_conv * (opened * (1.0 + summed * (1.0 - opened)))
    for j in range(4):
        g_small[24 + j : 25 + j, :] += jnp.sum(d_summed * taps[j], axis=0, keepdims=True)
    g_small[28:29, :] += jnp.sum(d_summed, axis=0, keepdims=True)
    ext = jnp.concatenate([d_summed, later[...]], axis=0)
    later[...] = d_summed[0:8]
    d_mix = conv_w[3:4, :] * d_summed
    for j in range(3):
        d_mix = d_mix + conv_w[j : j + 1, :] * pltpu.roll(ext, length + 8 - (3 - j), 0)[0:length]
    d_mix = (d_mix + mm_nt(value_low, w_v[...])).astype(bf16)
    d_z = dz_ref[...]
    rows = normed[...]
    d_normed = mm_nt(d_mix, w_mix[...]) + mm_nt(d_z, w_gate[...])
    g_ln = jnp.sum(d_normed * rows.astype(f32), axis=0, keepdims=True)
    g_small[32:33, :] += g_ln[:, :size]
    g_small[33:34, :] += g_ln[:, size:]

    @pl.when(last)
    def _():
        g_small[29:32, :] = g_gain[0:3, :]

    return rows, d_mix, d_z, d_normed


def lower_kernel(chained, head_ref, *refs):
    ins, refs = refs[:22], list(refs[22:])
    edge = 0.0
    if chained:
        first_halo, first_later, *refs = refs
        edge = first_halo[8:16, :].astype(f32)
        later_out = refs.pop(4)
    part_out, square_out, up_out, small_out = refs[:4]
    g_q, g_k, g_v, g_m, g_z, g_small, later = refs[4:]
    step = pl.program_id(0)
    size = g_q.shape[0]

    @pl.when(step == 0)
    def _():
        for ref in (g_q, g_k, g_v, g_m, g_z, g_small, later):
            ref[...] = jnp.zeros_like(ref)
        if chained:
            later[...] = first_later[...]

    (d_gate, dq, dk, dv, dskip, dz, mix, mix_before, conv, q, k, v, normed,
     w_q, w_k, w_v, w_mix, w_gate, conv_w, conv_b, gate_w, g_gain) = ins
    lows = lower_first(d_gate, dq, dk, dv, mix, conv, q, k, v, gate_w, g_q, g_k, g_v, g_small)
    rows, d_mix, d_z, d_normed = lower_second(
        edge, step == pl.num_programs(0) - 1, lows, dskip, dz, mix, mix_before, normed,
        w_q.at[0], w_k.at[0], w_v.at[0], w_mix, w_gate, conv_w, conv_b, g_gain, g_small, later,
    )
    g_m[...] += mm_tn(rows, d_mix)
    g_z[...] += mm_tn(rows, d_z)
    part_out[...] = d_normed.astype(bf16)

    @pl.when(step == pl.num_programs(0) - 1)
    def _():
        half = size // 2
        for at, ref in enumerate((g_q, g_k, g_v)):
            square_out[0, :, half * at : half * at + half] = ref[:, :half].astype(bf16)
            square_out[1, :, half * at : half * at + half] = ref[:, half:].astype(bf16)
        up_out[0] = g_m[...].astype(bf16)
        up_out[1] = g_z[...].astype(bf16)
        small_out[...] = g_small[...]
        if chained:
            later_out[...] = later[...]


def struct(shape, dtype):
    return jax.ShapeDtypeStruct(shape, dtype)


def run_kernel(body, head, grid, inputs, in_specs, outs, out_specs, scratch, name, flops, nbytes):
    return pl.pallas_call(
        body,
        grid_spec=pltpu.PrefetchScalarGridSpec(
            num_scalar_prefetch=1,
            grid=(grid,),
            in_specs=in_specs,
            out_specs=out_specs,
            scratch_shapes=scratch,
        ),
        out_shape=outs,
        compiler_params=pltpu.CompilerParams(
            dimension_semantics=("arbitrary",), vmem_limit_bytes=vmem_bytes
        ),
        cost_estimate=pl.CostEstimate(flops=flops, bytes_accessed=nbytes, transcendentals=0),
        name=name,
    )(head, *inputs)


def fixed(shape, *index):
    return pl.BlockSpec(shape, lambda g, h: tuple(h[0] if i == "h" else i for i in index))


def lift(head, normed, w_up, w_query, w_key, w_value, conv_w, conv_b, gate_parts, *first):
    tokens, width = normed.shape
    heads, size, _ = w_query.shape
    length = wide_len
    by_row = lambda cols: pl.BlockSpec((length, cols), lambda g, h: (g, 0))
    weight = pl.BlockSpec((1, size, size), lambda g, h: (h[0], 0, 0))
    chained = len(first) > 0
    halo = [pl.BlockSpec((16, size), lambda g, h: (0, 0))] * chained
    return run_kernel(
        partial(lift_kernel, chained), head, tokens // length,
        (normed, w_up, w_up, w_query, w_key, w_value, conv_w, conv_b, gate_parts, *first),
        [
            by_row(width),
            pl.BlockSpec((width, size), lambda g, h: (0, h[0])),
            pl.BlockSpec((width, size), lambda g, h: (0, heads + h[0])),
            weight, weight, weight,
            pl.BlockSpec((4, size), lambda g, h: (0, h[0])),
            pl.BlockSpec((1, size), lambda g, h: (0, h[0])),
            pl.BlockSpec(gate_parts.shape, lambda g, h: (0, 0, 0)),
        ]
        + [pl.BlockSpec((16, width), lambda g, h: (0, 0))] * chained,
        [struct((tokens, size), bf16)] * 5
        + [struct((tokens, size), f32), struct((8, tokens), f32)]
        + [struct((16, size), bf16)] * chained,
        [by_row(size)] * 6 + [pl.BlockSpec((8, length), lambda g, h: (0, g))] + halo,
        [pltpu.VMEM((8, size), f32)],
        "lift", 2 * tokens * size * (2 * width + 3 * size), 24 * 2**20,
    )


def cell_forward(head, gates, q, k, v, conv, gate_z, out_gain, skip_gain, w_down, *first):
    tokens, size = q.shape
    width = w_down.shape[1]
    length = chunk_len
    steps = tokens // length
    by_row = lambda cols: pl.BlockSpec((length, cols), lambda g, h: (g, 0))
    gain = pl.BlockSpec((1, size), lambda g, h: (0, h[0]))
    carried = [struct(value.shape, f32) for value in first]
    carried_specs = [pl.BlockSpec(value.shape, lambda g, h: (0, 0)) for value in first]
    return run_kernel(
        partial(cell_forward_kernel, len(first) > 0), head, steps,
        (gates, q, k, v, conv, gate_z, out_gain, skip_gain, w_down, *first),
        [pl.BlockSpec((2, length), lambda g, h: (0, g))]
        + [by_row(size)] * 5
        + [gain, gain, pl.BlockSpec((size, width), lambda g, h: (h[0], 0))]
        + carried_specs,
        [
            struct((tokens, width), bf16),
            struct((tokens, size), f32),
            struct((steps, size, size), bf16),
            struct((steps, 8, size), f32),
            struct((tokens, length), bf16),
            struct((tokens, 128), f32),
            struct((8, tokens), f32),
        ]
        + carried,
        [
            by_row(width),
            by_row(size),
            pl.BlockSpec((1, size, size), lambda g, h: (g, 0, 0)),
            pl.BlockSpec((1, 8, size), lambda g, h: (g, 0, 0)),
            by_row(length),
            by_row(128),
            pl.BlockSpec((8, length), lambda g, h: (0, g)),
        ]
        + carried_specs,
        [pltpu.VMEM((size, size), f32), pltpu.VMEM((8, size), f32), pltpu.VMEM((8, 128), f32)],
        "cell_forward", 2 * tokens * size * (2 * length + 2 * size + width), 28 * 2**20,
    )


def cell_backward(
    head, rows, q, k, v, conv, gate_z, normed, states, norms, weights, cols, cot, rows_in,
    out_gain, skip_gain, w_down, *first,
):
    tokens, size = q.shape
    width = w_down.shape[1]
    length = chunk_len
    steps = tokens // length
    end = steps - 1
    by_row = lambda n: pl.BlockSpec((length, n), lambda g, h: (end - g, 0))
    gain = pl.BlockSpec((1, size), lambda g, h: (0, h[0]))
    whole = lambda shape: pl.BlockSpec(shape, lambda g, h: (0, 0))
    carried = [struct(value.shape, f32) for value in first]
    carried_specs = [whole(value.shape) for value in first]
    return run_kernel(
        partial(cell_backward_kernel, len(first) > 0), head, steps,
        (rows, q, k, v, conv, gate_z, normed, states, norms, weights, cols, cot, rows_in,
         out_gain, skip_gain, w_down, *first),
        [pl.BlockSpec((8, length), lambda g, h: (0, end - g))]
        + [by_row(size)] * 6
        + [
            pl.BlockSpec((1, size, size), lambda g, h: (end - g, 0, 0)),
            pl.BlockSpec((1, 8, size), lambda g, h: (end - g, 0, 0)),
            by_row(length),
            by_row(128),
            by_row(width),
            by_row(width),
            gain, gain,
            pl.BlockSpec((size, width), lambda g, h: (h[0], 0)),
        ]
        + carried_specs,
        [struct((tokens, size), f32)] * 4
        + [
            struct((tokens, size), bf16),
            struct((8, tokens), f32),
            struct((2, size, width // 2), bf16),
            struct((width, size), bf16),
            struct((8, size), f32),
        ]
        + carried,
        [by_row(size)] * 5
        + [
            pl.BlockSpec((8, length), lambda g, h: (0, end - g)),
            pl.BlockSpec((2, size, width // 2), lambda g, h: (0, 0, 0)),
            whole((width, size)),
            whole((8, size)),
        ]
        + carried_specs,
        [
            pltpu.VMEM((size, size), f32),
            pltpu.VMEM((8, size), f32),
            pltpu.VMEM((size, width), f32),
            pltpu.VMEM((width, size), f32),
            pltpu.VMEM((8, size), f32),
        ],
        "cell_backward", 2 * tokens * size * (4 * length + 4 * size + 2 * width), 44 * 2**20,
    )


def lower_inputs(
    length, d_gate, dq, dk, dv, dskip, dz, mix, conv, q, k, v, normed,
    w_query, w_key, w_value, w_up, conv_w, conv_b, gate_pairs, g_gain,
):
    tokens, size = q.shape
    width = normed.shape[1]
    heads = w_query.shape[0]
    end = tokens // length - 1
    by_row = lambda n: pl.BlockSpec((length, n), lambda g, h: (end - g, 0))
    kept = lambda shape, index: pl.BlockSpec(shape, index, pipeline_mode=pl.Buffered(1))
    weight = kept((1, size, size), lambda g, h: (h[0], 0, 0))
    inputs = (
        d_gate, dq, dk, dv, dskip, dz, mix, mix, conv, q, k, v, normed,
        w_query, w_key, w_value, w_up, w_up, conv_w, conv_b, gate_pairs, g_gain,
    )
    specs = [pl.BlockSpec((8, length), lambda g, h: (0, end - g))]
    specs += [by_row(size)] * 6
    specs += [
        pl.BlockSpec(
            (16, size), lambda g, h: (jnp.maximum((end - g) * (length // 16) - 1, 0), 0)
        )
    ]
    specs += [by_row(size)] * 4
    specs += [by_row(width), weight, weight, weight]
    specs += [
        kept((width, size), lambda g, h: (0, h[0])),
        kept((width, size), lambda g, h: (0, heads + h[0])),
        kept((4, size), lambda g, h: (0, h[0])),
        kept((1, size), lambda g, h: (0, h[0])),
        kept(gate_pairs.shape, lambda g, h: (0, 0)),
        kept(g_gain.shape, lambda g, h: (0, 0)),
    ]
    return inputs, specs


def lower(head, *inputs):
    inputs, first = inputs[:20], inputs[20:]
    tokens, size = inputs[1].shape
    width = inputs[11].shape[1]
    length = wide_len
    end = tokens // length - 1
    by_row = lambda n: pl.BlockSpec((length, n), lambda g, h: (end - g, 0))
    whole = lambda shape: pl.BlockSpec(shape, lambda g, h: (0, 0))
    chained = len(first) > 0
    inputs, specs = lower_inputs(length, *inputs)
    return run_kernel(
        partial(lower_kernel, chained), head, tokens // length,
        (*inputs, *first),
        specs + [whole(value.shape) for value in first],
        [struct((tokens, width), bf16)]
        + [struct((2, size, 3 * size // 2), bf16), struct((2, width, size), bf16)]
        + [struct((40, size), f32)]
        + [struct((8, size), f32)] * chained,
        [by_row(width)]
        + [
            pl.BlockSpec((2, size, 3 * size // 2), lambda g, h: (0, 0, 0)),
            pl.BlockSpec((2, width, size), lambda g, h: (0, 0, 0)),
        ]
        + [whole((40, size))]
        + [whole((8, size))] * chained,
        [pltpu.VMEM((size, size), f32)] * 3
        + [pltpu.VMEM((width, size), f32)] * 2
        + [pltpu.VMEM((40, size), f32), pltpu.VMEM((8, size), f32)],
        "lower", 2 * tokens * size * (6 * size + 4 * width), 48 * 2**20,
    )
MESH_ID = pl.DeviceIdType.MESH


def where_am_i():
    at_seq, at_batch = lax.axis_index("seq"), lax.axis_index("batch")
    within = lax.rem(at_seq, 8)
    first = at_seq - within
    return first, within // 2, lax.rem(within, 2), at_batch // 2, lax.rem(at_batch, 2)


def greet(others):
    barrier = pltpu.get_barrier_semaphore()
    for other in others:
        pl.semaphore_signal(barrier, 1, device_id=other, device_id_type=MESH_ID)
    pl.semaphore_wait(barrier, len(others))


def remote(src, dst, sent, landed, device):
    return pltpu.make_async_remote_copy(src, dst, sent, landed, device_id=device, device_id_type=MESH_ID)


def normalize(rows):
    centre = rows - jnp.mean(rows, axis=-1, keepdims=True)
    rstd = lax.rsqrt(jnp.mean(centre * centre, axis=-1, keepdims=True) + norm_epsilon)
    return centre * rstd, rstd


def gather_kernel(
    rows_ref, gain_ref, out_ref, staged, kept, z_sent, z_landed, y_sent, y_landed, c_sent, c_landed
):
    first, z, y, x, c = where_am_i()
    parts = z_landed.shape[1]
    block = rows_ref.shape[1]
    size = block // parts

    def device(zz, yy, cc):
        return (first + 2 * zz + yy, 2 * x + cc)

    def rows(zz, yy, part):
        return out_ref.at[pl.ds(pl.multiple_of((2 * zz + yy) * block + part * size, size), size)]

    others = [device(lax.rem(z + k, 4), y, c) for k in range(1, 4)]
    greet(others + [device(z, 1 - y, c), device(z, y, 1 - c)])
    enters = z // 2 == c

    def to_column(m, part):
        return remote(
            staged.at[m, pl.ds(part * size, size)], rows(z, y, part),
            z_sent.at[m, part], z_landed.at[z, part], device(2 * c + m, y, c),
        )

    def keep(m, part):
        return pltpu.make_async_copy(
            staged.at[m, pl.ds(part * size, size)], rows(z, y, part), kept.at[part]
        )

    def from_column(zz, part):
        return remote(
            rows(zz, y, part), rows(zz, y, part), z_sent.at[0, part], z_landed.at[zz, part],
            device(zz, y, c),
        )

    def to_row(zz, k, part):
        return remote(
            rows(zz, y, part), rows(zz, y, part), y_sent.at[k, part], y_landed.at[zz, part],
            device(z, 1 - y, c),
        )

    def from_row(zz, k, part):
        return remote(
            rows(zz, 1 - y, part), rows(zz, 1 - y, part), y_sent.at[k, part],
            y_landed.at[zz, part], device(z, 1 - y, c),
        )

    def to_core(zz, yy, k, part):
        return remote(
            rows(zz, yy, part), rows(zz, yy, part), c_sent.at[k, part],
            c_landed.at[2 * zz + yy, part], device(z, y, 1 - c),
        )

    for part in range(parts):
        here = pl.ds(part * size, size)
        for m in range(2):
            staged[m, here] = (
                normalize(rows_ref[m, here].astype(f32))[0] * gain_ref[...]
            ).astype(bf16)
            away = 2 * c + m != z
            pl.when(away)(lambda m=m, part=part: to_column(m, part).start())
            pl.when(jnp.logical_not(away))(lambda m=m, part=part: keep(m, part).start())

    @pl.when(enters)
    def _():
        for part in range(parts):
            for k in range(4):
                zz = lax.rem(z + k, 4)
                if k == 0:
                    keep(0, part).wait()
                else:
                    from_column(zz, part).wait_recv()
                to_row(zz, k, part).start()
                to_core(zz, y, k, part).start()
            if part > 0:
                for k in range(4):
                    zz = lax.rem(z + k, 4)
                    from_row(zz, k, part - 1).wait_recv()
                    to_core(zz, 1 - y, 4 + k, part - 1).start()
        for k in range(4):
            zz = lax.rem(z + k, 4)
            from_row(zz, k, parts - 1).wait_recv()
            to_core(zz, 1 - y, 4 + k, parts - 1).start()
        for k in range(4):
            zz = lax.rem(z + k, 4)
            for part in range(parts):
                to_row(zz, k, part).wait_send()
                to_core(zz, y, k, part).wait_send()
                to_core(zz, 1 - y, 4 + k, part).wait_send()

    @pl.when(jnp.logical_not(enters))
    def _():
        for zz in range(4):
            for yy in range(2):
                for part in range(parts):
                    to_core(zz, yy, 0, part).wait_recv()

    for m in range(2):
        for part in range(parts):
            pl.when(2 * c + m != z)(lambda m=m, part=part: to_column(m, part).wait_send())


def gather_normed(rows, gain):
    micro, block, width = rows.shape
    parts = 4
    sems = [(parts,), (2, parts), (4, parts), (4, parts), (4, parts), (8, parts), (8, parts)]
    return pl.pallas_call(
        gather_kernel,
        out_shape=struct((8 * block, width), bf16),
        in_specs=[pl.BlockSpec(memory_space=pltpu.VMEM)] * 2,
        out_specs=pl.BlockSpec(memory_space=pl.ANY),
        scratch_shapes=[pltpu.VMEM((micro, block, width), bf16)]
        + [pltpu.SemaphoreType.DMA(shape) for shape in sems],
        compiler_params=pltpu.CompilerParams(
            collective_id=0, has_side_effects=True, vmem_limit_bytes=32 * 2**20
        ),
        name="gather_normed",
    )(rows, gain)


def drain_kernel(
    d_gate, dq, dk, dv, mix_ref, conv, q_ref, k_ref, v_ref, dskip, dz, mix_before, normed,
    gate_pairs, g_gain, w_query, w_key, w_value, w_up, conv_w, conv_b,
    down_ref, lifted_ref, rows_ref, cot_ref, gain_ref, *refs
):
    grad_out, up_out, query_out, key_out, value_out, down_out, small_out, *refs = refs
    w_q, w_k, w_v, w_mix, w_gate, taps_w, taps_b, q_all, k_all, v_all, *refs = refs
    g_q, g_k, g_v, g_small, later, rows_all, lifted_all, part_all, *refs = refs
    from_core, kept, to_row, from_row, to_owner, owned, *refs = refs
    give_up, give_square, *refs = refs
    from_x, totals, from_near, pairs, from_far, ends = (refs[k : 18 : 6] for k in range(6))
    refs = refs[18:]
    up_go, up_got, sq_go, sq_got, dn_go, dn_got, small_x, small_sum, small_z, small_all, *refs = refs
    c_sent, c_landed, y_sent, y_landed, o_sent, o_landed, *refs = refs
    x_sent, x_landed, near_sent, near_landed, far_sent, far_landed, *refs = refs
    w_sem, up_sem, sq_sent, sq_landed, dn_sent, dn_landed, sx_sem, sz_sent, sz_landed, *refs = refs
    sh_sent, sh_landed = refs
    step = pl.program_id(0)
    blocks, block, width = part_all.shape
    half = block // 2
    size = g_q.shape[0]
    first, z, y, x, c = where_am_i()
    head = 2 * c + y
    high, low = z // 2, lax.rem(z, 2)

    def device(zz, yy, cc, xx=x):
        return (first + 2 * zz + yy, 2 * xx + cc)

    around = [lax.rem(z + k, 4) for k in range(1, 4)]
    group = [(1 - y, c), (y, 1 - c), (1 - y, 1 - c)]

    def down_rows(q):
        tall = down_ref.shape[1] // 4
        return pl.ds(q * tall, tall)

    def up_rows(q):
        tall = lifted_ref.shape[0] // 4
        return pl.ds(q * tall, tall)

    def to_x(p, q):
        give = (give_up, give_square)[p].at[q] if p < 2 else down_ref.at[1 - x, down_rows(q)]
        return remote(
            give, from_x[p].at[q], x_sent.at[p, q], x_landed.at[p, q], device(z, y, c, 1 - x)
        )

    def to_near(p, q):
        return remote(
            totals[p].at[q], from_near[p].at[q // 2], near_sent.at[p, q], near_landed.at[p, q],
            device(z + 1 - 2 * low, y, c),
        )

    def to_far(p, q):
        return remote(
            pairs[p].at[q // 2], from_far[p], far_sent.at[p, q], far_landed.at[p, q],
            device(z + 2 - 4 * high, y, c),
        )

    def x_step(p, q):
        to_x(p, q).wait_recv()
        own = totals[p][q] if p < 2 else down_ref[x, down_rows(q)]
        totals[p][q] = (own.astype(f32) + from_x[p][q].astype(f32)).astype(bf16)
        pl.when(low != q % 2)(lambda: to_near(p, q).start())

    def near_step(p, q):
        @pl.when(low == q % 2)
        def _():
            to_near(p, q).wait_recv()
            pairs[p][q // 2] = (
                totals[p][q].astype(f32) + from_near[p][q // 2].astype(f32)
            ).astype(bf16)
            pl.when(high != q // 2)(lambda: to_far(p, q).start())

    def far_step(p, q):
        @pl.when(z == q)
        def _():
            to_far(p, q).wait_recv()
            ends[p][...] = pairs[p][q // 2].astype(f32) + from_far[p][...].astype(f32)

    def weight_copies():
        lanes = pl.ds(pl.multiple_of(head * size, size), size)
        gate_lanes = pl.ds(pl.multiple_of((w_query.shape[0] + head) * size, size), size)
        pairs_of = [
            (w_query.at[head], w_q), (w_key.at[head], w_k), (w_value.at[head], w_v),
            (w_up.at[:, lanes], w_mix), (w_up.at[:, gate_lanes], w_gate),
            (conv_w.at[:, lanes], taps_w), (conv_b.at[:, lanes], taps_b),
        ]
        return [
            pltpu.make_async_copy(src, dst, w_sem.at[k]) for k, (src, dst) in enumerate(pairs_of)
        ]

    def to_c(at):
        there = pl.ds(pl.multiple_of((1 - c) * half, half), half)
        return remote(
            part_all.at[at, there], from_core.at[at], c_sent.at[at], c_landed.at[at],
            device(z, y, 1 - c),
        )

    def to_y(zz):
        return remote(
            to_row.at[zz], from_row.at[zz], y_sent.at[zz], y_landed.at[zz], device(z, 1 - y, c)
        )

    def to_o(zz):
        return remote(
            to_owner.at[zz], owned.at[low, c], o_sent.at[zz], o_landed.at[low, c],
            device(zz, y, z // 2),
        )

    def stays(zz):
        return jnp.logical_and(z == zz, z // 2 == c)

    def core_step(at):
        zz, yy = at // 2, lax.rem(at, 2)
        to_c(at).wait_recv()
        here = pl.ds(pl.multiple_of(c * half, half), half)
        value = (part_all[at, here].astype(f32) + from_core[at].astype(f32)).astype(bf16)

        @pl.when(yy == y)
        def _():
            kept[zz] = value

        @pl.when(yy != y)
        def _():
            to_row[zz] = value
            to_y(zz).start()

    def row_step(zz):
        to_y(zz).wait_recv()
        to_owner[zz] = (kept[zz].astype(f32) + from_row[zz].astype(f32)).astype(bf16)

        @pl.when(stays(zz))
        def _():
            owned[low, c] = to_owner[zz]

        pl.when(jnp.logical_not(stays(zz)))(lambda: to_o(zz).start())

    def to_group(k, src, dst, sent, landed):
        yy, cc = group[k]
        return remote(src, dst, sent.at[k], landed, device(z, yy, cc))

    def small_to_x():
        return remote(g_small, small_x, sx_sem.at[0], sx_sem.at[1], device(z, y, c, 1 - x))

    def small_to_z(k):
        return remote(
            small_sum, small_z.at[z], sz_sent.at[k], sz_landed.at[z], device(around[k], y, c)
        )

    def small_from_z(k):
        return remote(
            small_sum, small_z.at[around[k]], sz_sent.at[k], sz_landed.at[around[k]],
            device(around[k], y, c),
        )

    def small_to_head(k):
        return to_group(k, small_all.at[head], small_all.at[head], sh_sent, sh_landed.at[head])

    def small_from_head(k):
        at = 2 * group[k][1] + group[k][0]
        return to_group(k, small_all.at[at], small_all.at[at], sh_sent, sh_landed.at[at])

    def up_to_y():
        return remote(up_go, up_got, up_sem.at[0], up_sem.at[1], device(z, 1 - y, c))

    def square_to(k):
        yy, cc = group[k]
        return to_group(k, sq_go.at[yy, cc], sq_got.at[head], sq_sent, sq_landed.at[head])

    def square_from(k):
        at = 2 * group[k][1] + group[k][0]
        return to_group(k, sq_go.at[0, 0], sq_got.at[at], sq_sent, sq_landed.at[at])

    def down_to(cc):
        return remote(
            dn_go.at[cc], dn_got.at[low], dn_sent.at[cc], dn_landed.at[low],
            device(head, z // 2, cc),
        )

    def down_from(k):
        return remote(
            dn_go.at[0], dn_got.at[k], dn_sent.at[0], dn_landed.at[k],
            device(2 * y + k, low, z // 2),
        )

    home = jnp.logical_and(head == z, z // 2 == y)

    @pl.when(step == 0)
    def _():
        others = [device(z, yy, cc) for yy, cc in group] + [device(z, y, c, 1 - x)]
        for zz in around:
            others += [device(zz, yy, cc) for yy, cc in [(y, c)] + group]
        greet(others)
        for q in range(4):
            to_x(2, q).start()
        for copy in weight_copies():
            copy.start()
        for ref in (g_q, g_k, g_v, g_small, later):
            ref[...] = jnp.zeros_like(ref)

    tall, wide = size // 4, size // 2

    @pl.when(step < blocks)
    def _():
        lows = lower_first(
            d_gate, dq, dk, dv, mix_ref, conv, q_ref, k_ref, v_ref, gate_pairs, g_q, g_k, g_v, g_small
        )
        here = pl.ds(pl.multiple_of(step * block, block), block)
        for ref, value in zip((q_all, k_all, v_all), lows):
            ref[here] = value

    @pl.when(step == blocks - 1)
    def _():
        for q in range(4):
            rows_q = slice(tall * q, tall * q + tall)
            for at, ref in enumerate((g_q, g_k, g_v)):
                lanes = slice(wide * at, wide * at + wide)
                left, right = ref[rows_q, :wide], ref[rows_q, wide:]
                totals[1][q, :, lanes] = jnp.where(x == 0, left, right).astype(bf16)
                give_square[q, :, lanes] = jnp.where(x == 0, right, left).astype(bf16)
            to_x(1, q).start()
        for copy in weight_copies():
            copy.wait()

    @pl.when(step >= blocks)
    def _():
        now = 2 * blocks - 1 - step
        here = pl.ds(pl.multiple_of(now * block, block), block)
        lows = (q_all[here], k_all[here], v_all[here])
        rows, d_mix, d_z, d_normed = lower_second(
            0.0, now == 0, lows, dskip, dz, mix_ref, mix_before, normed,
            w_q, w_k, w_v, w_mix, w_gate, taps_w, taps_b, g_gain, g_small, later,
        )
        rows_all[here] = rows
        lifted_all[here] = d_mix
        part_all[now] = d_normed.astype(bf16)
        to_c(now).start()
        pl.when(now < blocks - 1)(lambda: core_step(now + 1))

    def at_end(when, *work):
        @pl.when(step == blocks + when)
        def _():
            for do in work:
                do()

    def spread_down():
        span = dn_go.shape[2]
        for cc in range(2):
            dn_go[cc] = ends[2][:, span * cc : span * cc + span].astype(bf16)
            left_here = jnp.logical_and(home, c == cc)

            @pl.when(left_here)
            def _():
                dn_got[low] = dn_go[cc]

            pl.when(jnp.logical_not(left_here))(lambda: down_to(cc).start())

    def every(do, p):
        return [partial(do, p, q) for q in range(4)]

    at_end(1, *every(x_step, 2))
    at_end(3, partial(x_step, 1, 0))
    at_end(4, *every(near_step, 2))
    at_end(5, partial(x_step, 1, 1), partial(near_step, 1, 0))
    at_end(6, partial(row_step, 3))
    at_end(7, partial(x_step, 1, 2), partial(near_step, 1, 1), *every(far_step, 2), spread_down)

    @pl.when(step == 2 * blocks - 1)
    def _():
        small_to_x().start()
        for q in range(4):
            got = mm_tn(rows_all[:, block * q : block * q + block], lifted_all[...]).astype(bf16)
            given = lifted_ref[up_rows(q)]
            totals[0][q] = jnp.where(x == 0, got, given)
            give_up[q] = jnp.where(x == 0, given, got)
            if q < 2:
                to_x(0, q).start()
            if q == 0:
                core_step(0)
        row_step(2)
        x_step(1, 3)
        near_step(1, 2)
        row_step(1)
        x_step(0, 0)
        to_x(0, 2).start()
        near_step(1, 3)
        far_step(1, 0)
        far_step(1, 1)
        small_to_x().wait_recv()
        small_sum[...] = g_small[...] + small_x[...]
        small_z[z] = small_sum[...]
        for k in range(3):
            small_to_z(k).start()
        row_step(0)
        x_step(0, 1)
        to_x(0, 3).start()
        near_step(0, 0)
        far_step(1, 2)
        far_step(1, 3)
        for yy in range(2):
            for cc in range(2):
                for a in range(3):
                    sq_go[yy, cc, :, tall * a : tall * a + tall] = ends[1][
                        tall // 2 * yy : tall // 2 * yy + tall // 2,
                        (2 * a + cc) * tall : (2 * a + cc) * tall + tall,
                    ].astype(bf16)
        sq_got[head] = sq_go[y, c]
        for k in range(3):
            square_to(k).start()
        for k in range(3):
            small_from_z(k).wait_recv()
        total = small_z[0]
        for zz in range(1, 4):
            total = total + small_z[zz]
        small_all[head] = total
        for k in range(3):
            small_to_head(k).start()
        x_step(0, 2)
        near_step(0, 1)
        far_step(0, 0)
        x_step(0, 3)
        near_step(0, 2)
        far_step(0, 1)
        near_step(0, 3)
        far_step(0, 2)
        far_step(0, 3)
        value = ends[0][...]
        mine = jnp.where(y == 0, value[:half], value[half:])
        up_go[...] = jnp.where(y == 0, value[half:], value[:half]).astype(bf16)
        up_to_y().start()
        for yy in range(2):

            @pl.when(y == yy)
            def _():
                up_out[:, size * yy : size * yy + size] = mine

        for m in range(2):
            for cc in range(2):
                own_part = jnp.logical_and(2 * c + m == z, c == cc)
                landed = remote(
                    to_owner.at[0], owned.at[m, cc], o_sent.at[0], o_landed.at[m, cc],
                    device(2 * c + m, y, cc),
                )
                pl.when(jnp.logical_not(own_part))(lambda: landed.wait_recv())
                rows_here = pl.ds(cc * half, half)
                row_hat, rstd = normalize(rows_ref[m, rows_here].astype(f32))
                scaled = owned[m, cc].astype(f32) * gain_ref[...]
                d_row = rstd * (
                    scaled
                    - jnp.mean(scaled, axis=-1, keepdims=True)
                    - row_hat * jnp.mean(scaled * row_hat, axis=-1, keepdims=True)
                )
                grad_out[m, rows_here] = (cot_ref[m, rows_here].astype(f32) + d_row).astype(bf16)

        for k in range(3):
            small_from_head(k).wait_recv()
        small_out[...] = small_all[...]
        for k in range(3):
            square_from(k).wait_recv()
        for a, ref in enumerate((query_out, key_out, value_out)):
            ref[...] = sq_got[:, :, tall * a : tall * a + tall].astype(f32)
        for k in range(2):
            mine = jnp.logical_and(home, jnp.logical_and(low == k, z // 2 == c))
            pl.when(jnp.logical_not(mine))(lambda: down_from(k).wait_recv())
            deep = dn_got.shape[1]
            down_out[deep * k : deep * k + deep] = dn_got[k].astype(f32)
        up_to_y().wait_recv()
        for yy in range(2):

            @pl.when(y == yy)
            def _():
                up_out[:, size * (1 - yy) : size * (1 - yy) + size] = up_got[...].astype(f32)

        small_to_x().wait_send()
        up_to_y().wait_send()
        for p in range(3):
            for q in range(4):
                to_x(p, q).wait_send()
                pl.when(low != q % 2)(lambda: to_near(p, q).wait_send())
                passes = jnp.logical_and(low == q % 2, high != q // 2)
                pl.when(passes)(lambda: to_far(p, q).wait_send())
        for at in range(blocks):
            to_c(at).wait_send()
        for zz in range(4):
            to_y(zz).wait_send()
            pl.when(jnp.logical_not(stays(zz)))(lambda: to_o(zz).wait_send())
        for k in range(3):
            small_to_z(k).wait_send()
            small_to_head(k).wait_send()
            square_to(k).wait_send()
        for cc in range(2):
            left_here = jnp.logical_and(home, c == cc)
            pl.when(jnp.logical_not(left_here))(lambda: down_to(cc).wait_send())


def drain(inputs, down, lifted, rows, cot, gain):
    (d_gate, dq, dk, dv, dskip, dz, mix, conv, q, k, v, normed,
     w_query, w_key, w_value, w_up, conv_w, conv_b, gate_pairs, g_gain) = inputs
    tokens, size = q.shape
    micro, block, width = rows.shape
    half = block // 2
    lines = 40
    steps = tokens // block
    early = lambda g: jnp.minimum(g, steps - 1)
    late = lambda g: jnp.minimum(2 * steps - 1 - g, steps - 1)
    both = lambda g: jnp.where(g < steps, g, 2 * steps - 1 - g)
    by_row = lambda n, at: pl.BlockSpec((block, n), lambda g: (at(g), 0))
    kept = lambda value: pl.BlockSpec(
        value.shape, lambda g: (0,) * value.ndim, pipeline_mode=pl.Buffered(1)
    )
    anywhere = pl.BlockSpec(memory_space=pl.ANY)
    arguments = (
        d_gate, dq, dk, dv, mix, conv, q, k, v, dskip, dz, mix, normed, gate_pairs, g_gain,
        w_query, w_key, w_value, w_up, conv_w, conv_b, down, lifted, rows, cot, gain,
    )
    specs = [pl.BlockSpec((8, block), lambda g: (0, early(g)))] + [by_row(size, early)] * 3
    specs += [by_row(size, both)] + [by_row(size, early)] * 4 + [by_row(size, late)] * 2
    specs += [
        pl.BlockSpec((16, size), lambda g: (jnp.maximum(late(g) * (block // 16) - 1, 0), 0)),
        by_row(width, late), kept(gate_pairs), kept(g_gain),
    ]
    specs += [anywhere] * 6 + [kept(value) for value in (down, lifted, rows, cot, gain)]
    scratch = [((size, size), bf16)] * 3 + [((width, size), bf16)] * 2
    scratch += [((4, size), f32), ((1, size), f32)] + [((tokens, size), bf16)] * 3
    scratch += [((size, size), f32)] * 3 + [((lines, size), f32), ((8, size), f32)]
    scratch += [((tokens, width), bf16), ((tokens, size), bf16), ((8, block, width), bf16)]
    scratch += [
        ((8, half, width), bf16), ((4, half, width), bf16), ((4, half, width), bf16),
        ((4, half, width), bf16), ((4, half, width), bf16), ((2, 2, half, width), bf16),
    ]
    pieces = [(width // 4, size), (size // 4, 3 * size // 2), (size // 4, width // 2)]
    scratch += [((4, *piece), bf16) for piece in pieces[:2]]
    for piece in pieces:
        scratch += [((4, *piece), bf16)] * 2 + [((2, *piece), bf16)] * 2
        scratch += [(piece, bf16), (piece, f32)]
    scratch += [
        ((width // 8, size), bf16), ((width // 8, size), bf16),
        ((2, 2, size // 8, 3 * size // 4), bf16), ((4, size // 8, 3 * size // 4), bf16),
        ((2, size // 4, width // 4), bf16), ((2, size // 4, width // 4), bf16),
        ((lines, size), f32), ((lines, size), f32), ((4, lines, size), f32), ((4, lines, size), f32),
    ]
    sems = [(8,), (8,), (4,), (4,), (4,), (2, 2)] + [(3, 4)] * 6
    sems += [(7,), (2,), (3,), (4,), (2,), (2,), (2,), (3,), (4,), (3,), (4,)]
    square = struct((4, size // 8, size // 4), f32)
    outs = [
        struct(rows.shape, bf16), struct((width // 8, 2 * size), f32), square, square, square,
        struct((size // 2, width // 4), f32), struct((4, lines, size), f32),
    ]
    return pl.pallas_call(
        drain_kernel,
        grid=(2 * steps,),
        in_specs=specs,
        out_specs=[kept(value) for value in outs],
        scratch_shapes=[pltpu.VMEM(shape, dtype) for shape, dtype in scratch]
        + [pltpu.SemaphoreType.DMA(shape) for shape in sems],
        out_shape=outs,
        compiler_params=pltpu.CompilerParams(
            dimension_semantics=("arbitrary",), collective_id=1, has_side_effects=True,
            vmem_limit_bytes=60 * 2**20,
        ),
        cost_estimate=pl.CostEstimate(
            flops=2 * tokens * size * (6 * size + 4 * width), bytes_accessed=48 * 2**20,
            transcendentals=0,
        ),
        name="drain",
    )(*arguments)


def swap(value, axis, mask):
    count = lax.axis_size(axis)
    return lax.ppermute(value, axis, [(s, s ^ mask) for s in range(count)])


def part_of(value, at, count, axis):
    size = value.shape[axis] // count
    return lax.dynamic_slice_in_dim(value, at * size, size, axis)


def halved(value, bit, dim, axis, mask):
    kept = part_of(value, bit, 2, dim).astype(f32)
    return kept + swap(part_of(value, 1 - bit, 2, dim), axis, mask).astype(f32)


def paired(mine, other, bit, dim):
    return jnp.where(
        bit == 0, jnp.concatenate([mine, other], dim), jnp.concatenate([other, mine], dim)
    )


def place():
    at_seq, at_batch = lax.axis_index("seq"), lax.axis_index("batch")
    return (at_seq % 8) // 2, at_seq % 2, at_batch // 2, at_batch % 2


def sent_across(blocks, z):
    got = [lax.dynamic_index_in_dim(blocks, z, 0, keepdims=False)]
    for k in range(1, 4):
        got.append(swap(lax.dynamic_index_in_dim(blocks, z ^ k, 0, keepdims=False), "seq", 2 * k))
    return got


def in_order(got, z):
    got = jnp.stack(got)
    return jnp.stack([lax.dynamic_index_in_dim(got, z ^ k, 0, keepdims=False) for k in range(4)])


def hold(value, *done):
    return lax.optimization_barrier((value, *done))


def gather_first(own):
    z, y, x, c = place()
    slots = paired(own, swap(own, "batch", 1), c, 0)
    return part_of(slots, c, 2, 2)


def gather_last(blocks, other):
    z, y, x, c = place()
    rows, width = blocks.shape[2:]
    both = paired(blocks, other, y, 1)
    return paired(both, swap(both, "batch", 1), c, 3).reshape(8 * rows, 2 * width)


def scatter_first(parts):
    z, y, x, c = place()
    blocks = parts.reshape(4, 2, -1, parts.shape[1])
    return halved(blocks, c, 2, "batch", 1).astype(bf16)


def scatter_last(slots):
    z, y, x, c = place()
    other = swap(part_of(slots, 1 - c, 2, 0), "batch", 1)
    return paired(part_of(slots, c, 2, 0), other, c, 1).astype(f32)


def scatter_sequence(parts):
    z, y, x, c = place()
    blocks = scatter_first(parts)
    blocks = halved(blocks, y, 1, "seq", 1).astype(bf16)[:, 0]
    return scatter_last(in_order(sent_across(blocks, z), z))


def total_over_heads(value):
    value = value + swap(value, "batch", 1)
    return value + swap(value, "seq", 1)


def over_ranges(value, count):
    size = lax.axis_size("seq")
    groups = [[first + 8 * k for k in range(count)] for first in range(8)]
    return lax.all_gather(value, "seq", axis_index_groups=groups) if size > 8 else value[None]


def state_before(state, norm, level, total, ranges):
    index = lax.axis_index("seq") // 8
    summary = (state, norm[0], level[0, 0], total)
    everything = jax.tree.map(lambda part: over_ranges(part, ranges), summary)
    before = state_identity(summary)
    for k in range(ranges - 1):
        new = combine_states(before, jax.tree.map(lambda part: part[k], everything))
        before = jax.tree.map(lambda a, b: jnp.where(k < index, a, b), new, before)
    return (
        before[0],
        jnp.broadcast_to(before[1], norm.shape),
        jnp.broadcast_to(before[2], level.shape),
    )


def cotangent_after(d_state, d_norm, keep, ranges):
    index = lax.axis_index("seq") // 8
    own = (d_state, d_norm)
    everything = jax.tree.map(lambda part: over_ranges(part, ranges), own)
    keeps = over_ranges(keep, ranges)
    after = jax.tree.map(jnp.zeros_like, own)
    for k in range(ranges - 1, 0, -1):
        new = jax.tree.map(lambda a, b: a[k] + keeps[k] * b, everything, after)
        after = jax.tree.map(lambda a, b: jnp.where(k > index, a, b), new, after)
    return after


def reduce_blocks(at, up, square, down, heads):
    count, batch_count = lax.axis_size("seq"), lax.axis_size("batch")
    g_m, g_z = up
    width, size = g_m.shape
    half = size // 2
    squares = [
        jnp.concatenate([square[0, :, k : k + half], square[1, :, k : k + half]], 1)
        for k in range(0, 3 * half, half)
    ]
    g_down = jnp.concatenate([down[0], down[1]], 1)
    inner = heads * size
    up = jnp.zeros((width, 2 * inner), f32)
    up = lax.dynamic_update_slice_in_dim(up, g_m.astype(f32), at * size, 1)
    up = lax.dynamic_update_slice_in_dim(up, g_z.astype(f32), inner + at * size, 1)
    down = lax.dynamic_update_slice_in_dim(
        jnp.zeros((inner, width), f32), g_down.astype(f32), at * size, 0
    )
    full = [up, down]
    for g in squares:
        full.append(
            lax.dynamic_update_slice_in_dim(
                jnp.zeros((heads, size, size), f32), g.astype(f32)[None], at, 0
            )
        )
    blocks = tuple(to_device_blocks(g, count, batch_count) for g in full)
    pieces = lax.psum_scatter(blocks, ("seq", "batch"), scatter_dimension=0, tiled=True)
    s_up, s_down, s_query, s_key, s_value = tuple(p[0] for p in pieces)
    return s_up, jnp.stack([s_query, s_key, s_value], 1), s_down


def head_device(
    tokens, ln_gain, w_up, conv_w, conv_b, w_query, w_key, w_value, gate_w, gate_b,
    out_gain, skip_gain, w_down, d_out,
):
    z, y, x, c = place()
    at = 2 * c + y
    ranges = lax.axis_size("seq") // 8
    direct = ranges == 1 and lax.axis_size("batch") == 4
    head = jnp.reshape(at, (1,)).astype(jnp.int32)
    heads, size, _ = w_query.shape
    inner = heads * size
    conv_row = conv_b.reshape(1, inner)
    out_row = out_gain.reshape(1, inner)
    skip_row = skip_gain.reshape(1, inner)

    normed = gather_normed(tokens[:, 0], ln_gain[None])
    cot_half, normed = hold(gather_first(d_out[:, 0]), normed)
    cot_across = sent_across(cot_half, z)

    gate_own = lax.dynamic_index_in_dim(
        gate_w.reshape(3, heads, size, 8), at, 1, keepdims=False
    ).transpose(0, 2, 1)
    high = lax.reduce_precision(gate_own, 8, 7)
    middle = lax.reduce_precision(gate_own - high, 8, 7)
    low = lax.reduce_precision(gate_own - high - middle, 8, 7)
    gate_parts = jnp.concatenate([high, middle, low, jnp.zeros_like(high)], 1).astype(bf16)
    gate_pairs = (
        jnp.concatenate([high, high, high, middle, middle, low], 1)
        .astype(bf16)
        .transpose(1, 0, 2)
        .reshape(48, 3 * size)
    )

    first = () if ranges == 1 else (shifted(normed[-16:], "seq", 8),)
    mix, conv, q, k, v, gate_z, gates, *halo = lift(
        head, normed, w_up, w_query, w_key, w_value, conv_w, conv_row, gate_parts, *first
    )
    cot_across, gates = hold(cot_across, gates)
    cot_blocks = in_order(cot_across, z)[:, None]
    gates = total_over_heads(gates)
    cot_blocks, gates = hold(cot_blocks, gates)
    cot_row = swap(cot_blocks, "seq", 1)
    gates = jnp.concatenate(
        [
            lax.dynamic_slice_in_dim(gates, at, 1, 0),
            lax.dynamic_slice_in_dim(gates, heads + at, 1, 0)
            + lax.dynamic_slice_in_dim(gate_b, at, 1, 0)[:, None],
        ]
    )
    first = ()
    if ranges > 1:
        first = (
            jnp.zeros((size, size), f32),
            jnp.zeros((8, size), f32),
            jnp.full((8, 128), floor_value, f32),
        )
        *_, state, norm, level = cell_forward(
            head, gates, q, k, v, conv, gate_z, out_row, skip_row, w_down, *first
        )
        total = jnp.sum(jax.nn.log_sigmoid(gates[1]))
        first = state_before(state, norm, level, total, ranges)
    part, head_normed, states, norms, weights, cols, rows, *last = cell_forward(
        head, gates, q, k, v, conv, gate_z, out_row, skip_row, w_down, *first
    )
    cot_row, part = hold(cot_row, part)
    cot = gather_last(cot_blocks, cot_row)
    part = scatter_first(part)
    part, cot = hold(part, cot)
    part_row = swap(part_of(part, 1 - y, 2, 1), "seq", 1)
    after = ()
    if ranges > 1:
        after = (jnp.zeros((size, size), f32), jnp.zeros((8, size), f32))
        *_, d_state, d_norm = cell_backward(
            head, rows, q, k, v, conv, gate_z, head_normed, states, norms, weights, cols, cot, normed,
            out_row, skip_row, w_down, *after,
        )
        keep = jnp.exp(total + first[2][0, 0] - last[2][0, 0])
        after = cotangent_after(d_state, d_norm, keep, ranges)
    dq, dk, dv, dskip, dz, d_rows, g_down, g_z, g_gain, *_ = cell_backward(
        head, rows, q, k, v, conv, gate_z, head_normed, states, norms, weights, cols, cot, normed,
        out_row, skip_row, w_down, *after,
    )
    part_row, d_rows = hold(part_row, d_rows)
    part = (part_of(part, y, 2, 1).astype(f32) + part_row.astype(f32)).astype(bf16)[:, 0]
    index = jnp.arange(2 * heads)[:, None]
    d_gate = jnp.where(index == at, d_rows[0:1], jnp.where(index == heads + at, d_rows[1:2], 0.0))
    d_gate = total_over_heads(d_gate)
    part, d_gate = hold(part, d_gate)
    part_across = sent_across(part, z)
    lower_args = (
        d_gate, dq, dk, dv, dskip, dz, mix, conv, q, k, v, normed,
        w_query, w_key, w_value, w_up, conv_w, conv_row, gate_pairs, g_gain,
    )
    if direct:
        grad_rows, s_up, s_query, s_key, s_value, s_down, small = drain(
            lower_args, g_down, g_z, tokens[:, 0], d_out[:, 0], ln_gain[None]
        )
    else:
        first = ()
        if ranges > 1:
            *_, later = lower(head, *lower_args, halo[0], jnp.zeros((8, size), f32))
            first = (halo[0], shifted(later, "seq", -8))
        d_part, square, up, small, *_ = lower(head, *lower_args, *first)
    part_across, small = hold(part_across, small)
    block_rows = scatter_last(in_order(part_across, z))
    block_rows = (tokens[:, 0].astype(f32) + block_rows).astype(bf16)
    if not direct:
        d_normed = scatter_sequence(d_part)
        row_f = tokens[:, 0].astype(f32)
        centre = row_f - jnp.mean(row_f, axis=-1, keepdims=True)
        rstd = lax.rsqrt(jnp.mean(centre * centre, axis=-1, keepdims=True) + norm_epsilon)
        row_hat = centre * rstd
        scaled = d_normed * ln_gain
        d_row = rstd * (
            scaled
            - jnp.mean(scaled, axis=-1, keepdims=True)
            - row_hat * jnp.mean(scaled * row_hat, axis=-1, keepdims=True)
        )
        grad_rows = (d_out[:, 0].astype(f32) + d_row).astype(bf16)
        s_up, squares, s_down = reduce_blocks(at, up, square, g_down, heads)
        s_query, s_key, s_value = squares[:, 0], squares[:, 1], squares[:, 2]
        small = jnp.where(jnp.arange(heads)[:, None, None] == at, small, 0.0)
        small = lax.psum(small, ("seq", "batch"))
    s_ln = jnp.sum(small[:, 32:34], 0).reshape(-1) / ln_gain
    s_gate_w = small[:, :24].reshape(heads, 3, 8, size).transpose(1, 0, 3, 2).reshape(3 * inner, 8)
    s_conv_w = small[:, 24:28].transpose(1, 0, 2).reshape(4, inner)
    return (
        block_rows[:, None],
        grad_rows[:, None],
        s_ln,
        s_up,
        s_conv_w,
        small[:, 28].reshape(inner),
        s_query,
        s_key,
        s_value,
        s_gate_w,
        small[:, 31, 0],
        small[:, 29].reshape(inner),
        small[:, 30].reshape(inner),
        s_down,
    )


def solution(mesh):
    placed = (P(None, "batch", "seq", None),) + (P(),) * 12 + (P(None, "batch", "seq", None),)
    return jax.shard_map(
        head_device,
        mesh=mesh,
        in_specs=placed,
        out_specs=(
            P(None, "batch", "seq", None),
            P(None, "batch", "seq", None),
            P(),
            P("seq", "batch"),
            P(),
            P(),
            P(None, "seq", "batch"),
            P(None, "seq", "batch"),
            P(None, "seq", "batch"),
            P(),
            P(),
            P(),
            P(),
            P("seq", "batch"),
        ),
        check_vma=False,
    )
```

```python
from functools import partial

import jax
import jax.numpy as jnp
from jax import lax
from jax.experimental import pallas as pl
from jax.experimental.pallas import tpu as pltpu
from jax.sharding import PartitionSpec as P

norm_epsilon = 1e-05
floor_value = -1e30


def shifted(value, axis, steps):
    count = lax.axis_size(axis)
    initial, last = (max(0, -steps), min(count, count - steps))
    return lax.ppermute(value, axis, [(source, source + steps) for source in range(initial, last)])


def combine_states(earlier, later):
    top = jnp.maximum(later[3] + earlier[2], later[2])
    keep_first = jnp.exp(later[3] + earlier[2] - top)
    keep_second = jnp.exp(later[2] - top)
    merged_c = keep_first[..., None, None] * earlier[0] + keep_second[..., None, None] * later[0]
    merged_n = keep_first[..., None] * earlier[1] + keep_second[..., None] * later[1]
    return (merged_c, merged_n, top, earlier[3] + later[3])


def state_identity(template):
    return (
        jnp.zeros_like(template[0]),
        jnp.zeros_like(template[1]),
        jnp.full_like(template[2], floor_value),
        jnp.zeros_like(template[3]),
    )


def head_output(hidden, out_gain, skip_gain, conv_out, gate_z):
    centre = hidden - jnp.mean(hidden, axis=-1, keepdims=True)
    spread = jnp.mean(centre * centre, axis=-1, keepdims=True)
    normed = centre * lax.rsqrt(spread + norm_epsilon)
    flat_out = normed.transpose(1, 0, 2).reshape(hidden.shape[1], -1) * out_gain
    return (flat_out + skip_gain * conv_out) * jax.nn.silu(gate_z)


def output_tail(
    query_f,
    key_f,
    value_f,
    gate_pre,
    conv_f,
    gate_z,
    out_gain,
    skip_gain,
    state_c,
    state_n,
    state_m,
):
    head_count = gate_pre.shape[1] // 2
    in_gate = gate_pre[:, :head_count].T
    log_forget = jax.nn.log_sigmoid(gate_pre[:, head_count:]).T
    hidden = cell_hidden(
        to_heads(query_f, head_count),
        to_heads(key_f, head_count),
        to_heads(value_f, head_count),
        in_gate,
        log_forget,
        state_c,
        state_n,
        state_m,
    )
    return head_output(hidden, out_gain, skip_gain, conv_f, gate_z)


def state_tail(key_f, value_f, gate_pre, state_c, state_n, state_m):
    head_count = gate_pre.shape[1] // 2
    in_gate = gate_pre[:, :head_count].T
    log_forget = jax.nn.log_sigmoid(gate_pre[:, head_count:]).T
    return cell_state(
        to_heads(key_f, head_count),
        to_heads(value_f, head_count),
        in_gate,
        log_forget,
        state_c,
        state_n,
        state_m,
    )


def to_device_blocks(grad_full, seq_count, batch_count):
    if grad_full.ndim == 2:
        rows, cols = grad_full.shape
        split = grad_full.reshape(seq_count, rows // seq_count, batch_count, cols // batch_count)
        return split.transpose(0, 2, 1, 3).reshape(
            seq_count * batch_count, rows // seq_count, cols // batch_count
        )
    heads, rows, cols = grad_full.shape
    split = grad_full.reshape(heads, seq_count, rows // seq_count, batch_count, cols // batch_count)
    return split.transpose(1, 3, 0, 2, 4).reshape(
        seq_count * batch_count, heads, rows // seq_count, cols // batch_count
    )


f32 = jnp.float32
bf16 = jnp.bfloat16
chunk_len = 256
wide_len = 512
vmem_bytes = 56 * 1024 * 1024


def mm(a, b):
    return lax.dot_general(a, b, (((1,), (0,)), ((), ())), preferred_element_type=f32)


def mm_nt(a, b):
    return lax.dot_general(a, b, (((1,), (1,)), ((), ())), preferred_element_type=f32)


def mm_tn(a, b):
    return lax.dot_general(a, b, (((0,), (0,)), ((), ())), preferred_element_type=f32)


def split_three(value):
    high = value.astype(bf16)
    rest = value - high.astype(f32)
    middle = rest.astype(bf16)
    low = (rest - middle.astype(f32)).astype(bf16)
    return high, middle, low


def conv_taps(ext, length):
    return [pltpu.roll(ext, 3 - j, 0)[8 : 8 + length] if j < 3 else ext[8 : 8 + length] for j in range(4)]


def lift_kernel(chained, head_ref, normed, w_mix, w_gate, w_q, w_k, w_v, conv_w, conv_b, gate_w, *refs):
    if chained:
        rows_before, *refs, halo_out, carry = refs
    else:
        *refs, carry = refs
    mix_out, conv_out, q_out, k_out, v_out, z_out, gate_out = refs
    length = normed.shape[0]

    @pl.when(pl.program_id(0) == 0)
    def _():
        if chained:
            mix_before = mm(rows_before[...], w_mix[...]).astype(bf16)
            halo_out[...] = mix_before
            carry[...] = mix_before[8:16].astype(f32)
        else:
            carry[...] = jnp.zeros_like(carry)

    rows = normed[...]
    mix = mm(rows, w_mix[...]).astype(bf16)
    mix_out[...] = mix
    z_out[...] = mm(rows, w_gate[...])
    mix_f = mix.astype(f32)
    taps = conv_taps(jnp.concatenate([carry[...], mix_f], axis=0), length)
    carry[...] = mix_f[length - 8 :]
    summed = conv_b[...]
    for j in range(4):
        summed = summed + conv_w[j : j + 1, :] * taps[j]
    conv = (summed * jax.nn.sigmoid(summed)).astype(bf16)
    conv_out[...] = conv
    q = mm(conv, w_q[0]).astype(bf16)
    k = mm(conv, w_k[0]).astype(bf16)
    v = mm(mix, w_v[0]).astype(bf16)
    q_out[...] = q
    k_out[...] = k
    v_out[...] = v
    parts = mm_nt(gate_w[0], q) + mm_nt(gate_w[1], k) + mm_nt(gate_w[2], v)
    gate_out[...] = parts[0:8] + parts[8:16] + parts[16:24]


def gate_rows(gates, causal, diagonal):
    in_row = gates[0:1, :]
    pre = gates[1:2, :]
    log_forget = jnp.minimum(pre, 0.0) - jnp.log1p(jnp.exp(-jnp.abs(pre)))
    run_col = jnp.sum(jnp.where(causal, log_forget, 0.0), axis=1, keepdims=True)
    run_row = jnp.sum(jnp.where(diagonal, run_col, 0.0), axis=0, keepdims=True)
    return in_row - run_row, run_col, log_forget


def masks(length):
    row = lax.broadcasted_iota(jnp.int32, (length, length), 0)
    col = lax.broadcasted_iota(jnp.int32, (length, length), 1)
    return row >= col, row == col


def cell_forward_kernel(
    chained, head_ref, gates, q_ref, k_ref, v_ref, conv_ref, z_ref, out_gain, skip_gain, w_down, *refs,
    start=0,
):
    if chained:
        *first, part_out, normed_out, state_out, norm_out, weight_out, col_out, row_out = refs[:10]
        *final, state, norm, level = refs[10:]
    else:
        part_out, normed_out, state_out, norm_out, weight_out, col_out, row_out = refs[:7]
        state, norm, level = refs[7:]
    length = q_ref.shape[0]
    head_size = q_ref.shape[1]
    scale = head_size ** (-0.5)

    @pl.when(pl.program_id(0) == start)
    def _():
        if chained:
            for ref, value in zip((state, norm, level), first):
                ref[...] = value[...]
        else:
            state[...] = jnp.zeros_like(state)
            norm[...] = jnp.zeros_like(norm)
            level[...] = jnp.full_like(level, floor_value)

    causal, diagonal = masks(length)
    a_row, run_col, log_forget = gate_rows(gates[...], causal, diagonal)
    before = level[0:1, 0:1]
    top = jnp.maximum(
        before, jnp.max(jnp.where(causal, a_row, floor_value), axis=1, keepdims=True)
    )
    decay = jnp.exp(jnp.where(causal, a_row - top, floor_value))
    q = q_ref[...]
    k = k_ref[...]
    v = v_ref[...]
    q_f = q.astype(f32)
    weights = decay * (mm_nt(q, k) * scale)
    weights_low = weights.astype(bf16)
    weight_out[...] = weights_low
    from_state = jnp.exp(before - top)
    state_low = state[...].astype(bf16)
    state_out[0] = state_low
    norm_row = norm[0:1, :]
    norm_out[0] = norm[...]
    numerator = mm(weights_low, v) + (from_state * scale) * mm(q, state_low)
    denominator = jnp.sum(weights, axis=1, keepdims=True) + (from_state * scale) * jnp.sum(
        q_f * norm_row, axis=1, keepdims=True
    )
    floor = jnp.exp(-(run_col + top))
    size = jnp.abs(denominator)
    inverse = 1.0 / jnp.maximum(size, floor)
    hidden = numerator * inverse
    centre = hidden - jnp.mean(hidden, axis=1, keepdims=True)
    spread = jnp.mean(centre * centre, axis=1, keepdims=True)
    rstd = lax.rsqrt(spread + norm_epsilon)
    normed = centre * rstd
    normed_out[...] = normed
    gate_z = z_ref[...]
    gated = (normed * out_gain[...] + skip_gain[...] * conv_ref[...].astype(f32)) * (
        gate_z * jax.nn.sigmoid(gate_z)
    )
    part_out[...] = mm(gated.astype(bf16), w_down[...]).astype(bf16)
    factor = jnp.where(
        size > floor,
        jnp.where(denominator > 0, 1.0, -1.0) * inverse * (norm_epsilon * rstd * rstd),
        0.0,
    )
    lane = lax.broadcasted_iota(jnp.int32, (length, 128), 1)
    packed = jnp.where(lane == 0, rstd, inverse)
    packed = jnp.where(lane == 2, from_state, packed)
    packed = jnp.where(lane == 3, top, packed)
    col_out[...] = jnp.where(lane == 4, factor, packed)
    sub = lax.broadcasted_iota(jnp.int32, (8, length), 0)
    row_out[...] = jnp.where(sub == 0, a_row, 1.0 - jnp.exp(log_forget))
    last = top[length - 1 : length, :]
    a_col = jnp.sum(jnp.where(diagonal, a_row, 0.0), axis=1, keepdims=True)
    weighted = k.astype(f32) * jnp.exp(a_col - last)
    keep = jnp.exp(before - last)
    state[...] = keep * state[...] + mm_tn(weighted.astype(bf16), v)
    norm[...] = keep * norm[...] + jnp.sum(weighted, axis=0, keepdims=True)
    level[...] = jnp.broadcast_to(run_col[length - 1 : length, :] + last, level.shape)
    if chained:
        for ref, value in zip(final, (state, norm, level)):
            ref[...] = value[...]


def cell_backward_kernel(
    chained, head_ref, rows_ref, q_ref, k_ref, v_ref, conv_ref, z_ref, normed_ref, state_ref, norm_ref,
    weight_ref, col_ref, cot_ref, rows_in, out_gain, skip_gain, w_down, *refs
):
    if chained:
        first, refs = refs[:2], refs[2:]
    dq_out, dk_out, dv_out, dskip_out, dz_out, gate_out, g_down_out, g_z_out, g_gain_out, *refs = refs
    *final, d_state, d_norm, g_down, g_z, g_gain = refs
    length = q_ref.shape[0]
    head_size = q_ref.shape[1]
    scale = head_size ** (-0.5)

    @pl.when(pl.program_id(0) == 0)
    def _():
        if chained:
            d_state[...] = first[0][...]
            d_norm[...] = first[1][...]
        else:
            d_state[...] = jnp.zeros_like(d_state)
            d_norm[...] = jnp.zeros_like(d_norm)
        g_down[...] = jnp.zeros_like(g_down)
        g_z[...] = jnp.zeros_like(g_z)
        g_gain[...] = jnp.zeros_like(g_gain)

    causal, diagonal = masks(length)
    rstd = col_ref[:, 0:1]
    inverse = col_ref[:, 1:2]
    from_state = col_ref[:, 2:3]
    top = col_ref[:, 3:4]
    factor = col_ref[:, 4:5]
    a_row = rows_ref[0:1, :]
    q = q_ref[...]
    k = k_ref[...]
    v = v_ref[...]
    q_f = q.astype(f32)
    k_f = k.astype(f32)
    conv = conv_ref[...].astype(f32)
    normed = normed_ref[...]
    gate_z = z_ref[...]
    cot = cot_ref[...]
    opened = jax.nn.sigmoid(gate_z)
    silu = gate_z * opened
    head_in = normed * out_gain[...] + skip_gain[...] * conv
    g_down[...] += mm_tn((head_in * silu).astype(bf16), cot)
    d_gated = mm_nt(cot, w_down[...])
    d_z = (d_gated * head_in * (opened * (1.0 + gate_z * (1.0 - opened)))).astype(bf16)
    dz_out[...] = d_z
    g_z[...] += mm_tn(rows_in[...], d_z)
    d_head = d_gated * silu
    g_gain[0:1, :] += jnp.sum(d_head * normed, axis=0, keepdims=True)
    g_gain[1:2, :] += jnp.sum(d_head * conv, axis=0, keepdims=True)
    dskip_out[...] = skip_gain[...] * d_head
    d_hat = d_head * out_gain[...]
    along = jnp.sum(d_hat * normed, axis=1, keepdims=True)
    d_hidden = rstd * (
        d_hat - jnp.mean(d_hat, axis=1, keepdims=True) - normed * (along / head_size)
    )
    d_num = d_hidden * inverse
    d_den = -along * factor
    d_num_low = d_num.astype(bf16)
    decay = jnp.exp(jnp.where(causal, a_row - top, floor_value))
    d_scores = ((mm_nt(d_num_low, v) + d_den) * (decay * scale)).astype(bf16)
    through = from_state * scale
    dq_near = mm(d_scores, k)
    dq_far = (
        mm_nt((d_num * through).astype(bf16), state_ref[0])
        + (through * d_den) * norm_ref[0, 0:1, :]
    )
    last = top[length - 1 : length, :]
    keep = from_state[length - 1 : length, :]
    a_col = jnp.sum(jnp.where(diagonal, a_row, 0.0), axis=1, keepdims=True)
    key_weight = jnp.exp(a_col - last)
    d_state_low = d_state[...].astype(bf16)
    dk_near = mm_tn(d_scores, q)
    dk_far = key_weight * (mm_nt(v, d_state_low) + d_norm[0:1, :])
    dv = mm_tn(weight_ref[...], d_num_low) + mm((k_f * key_weight).astype(bf16), d_state_low)
    dq_out[...] = dq_near + dq_far
    dk_out[...] = dk_near + dk_far
    dv_out[...] = dv
    held = state_ref[0].astype(f32) * d_state[...]
    held = jnp.sum(jnp.sum(held, axis=0, keepdims=True) + norm_ref[0, 0:1, :] * d_norm[0:1, :])
    q_state = q_f * through
    d_state[...] = keep * d_state[...] + mm_tn(q_state.astype(bf16), d_num_low)
    d_norm[...] = keep * d_norm[...] + jnp.sum(q_state * d_den, axis=0, keepdims=True)
    q_dot = jnp.sum(q_f * (dq_near + dq_far), axis=1, keepdims=True)
    k_near = jnp.sum(k_f * dk_near, axis=1, keepdims=True)
    k_far = jnp.sum(k_f * dk_far, axis=1, keepdims=True)
    d_in = jnp.sum(jnp.where(diagonal, k_near + k_far, 0.0), axis=0, keepdims=True)
    d_log = jnp.sum(
        jnp.where(causal, q_dot - k_near, jnp.where(diagonal, 0.0, k_far)), axis=0, keepdims=True
    )
    d_log = d_log + keep * held
    sub = lax.broadcasted_iota(jnp.int32, (8, length), 0)
    d_pre = d_log * rows_ref[1:2, :]
    gate_out[...] = jnp.where(sub == 0, d_in, d_pre)
    g_gain[2:3, :] += jnp.broadcast_to(jnp.sum(d_pre, axis=1, keepdims=True), (1, head_size))

    @pl.when(pl.program_id(0) == pl.num_programs(0) - 1)
    def _():
        if chained:
            final[0][...] = d_state[...]
            final[1][...] = d_norm[...]
        half = g_down.shape[1] // 2
        g_down_out[0] = g_down[:, :half].astype(bf16)
        g_down_out[1] = g_down[:, half:].astype(bf16)
        g_z_out[...] = g_z[...].astype(bf16)
        g_gain_out[...] = g_gain[...]


def lower_first(d_gate, dq_ref, dk_ref, dv_ref, mix_ref, conv_ref, q_ref, k_ref, v_ref, gate_w,
                g_q, g_k, g_v, g_small):
    high, middle, low = split_three(d_gate[...])
    left = jnp.concatenate([high, middle, low, high, middle, high], axis=0)
    d_joined = mm_tn(left, gate_w[...])
    size = q_ref.shape[1]
    query_low = (dq_ref[...] + d_joined[:, :size]).astype(bf16)
    key_low = (dk_ref[...] + d_joined[:, size : 2 * size]).astype(bf16)
    value_low = (dv_ref[...] + d_joined[:, 2 * size :]).astype(bf16)
    conv = conv_ref[...]
    g_q[...] += mm_tn(conv, query_low)
    g_k[...] += mm_tn(conv, key_low)
    g_v[...] += mm_tn(mix_ref[...], value_low)
    three = jnp.concatenate([high, middle, low], axis=0)
    for at, ref in enumerate((q_ref, k_ref, v_ref)):
        got = mm(three, ref[...])
        g_small[8 * at : 8 * at + 8, :] += got[0:8] + got[8:16] + got[16:24]
    return query_low, key_low, value_low


def lower_second(
    edge, last, lows, dskip_ref, dz_ref, mix_ref, mix_before, normed, w_q, w_k, w_v, w_mix, w_gate,
    conv_w, conv_b, g_gain, g_small, later,
):
    query_low, key_low, value_low = lows
    length, size = mix_ref.shape
    mix = mix_ref[...]
    d_conv = dskip_ref[...] + mm_nt(query_low, w_q[...]) + mm_nt(key_low, w_k[...])
    halo = jnp.where(last, edge, mix_before[8:16, :].astype(f32))
    taps = conv_taps(jnp.concatenate([halo, mix.astype(f32)], axis=0), length)
    summed = conv_b[...]
    for j in range(4):
        summed = summed + conv_w[j : j + 1, :] * taps[j]
    opened = jax.nn.sigmoid(summed)
    d_summed = d_conv * (opened * (1.0 + summed * (1.0 - opened)))
    for j in range(4):
        g_small[24 + j : 25 + j, :] += jnp.sum(d_summed * taps[j], axis=0, keepdims=True)
    g_small[28:29, :] += jnp.sum(d_summed, axis=0, keepdims=True)
    ext = jnp.concatenate([d_summed, later[...]], axis=0)
    later[...] = d_summed[0:8]
    d_mix = conv_w[3:4, :] * d_summed
    for j in range(3):
        d_mix = d_mix + conv_w[j : j + 1, :] * pltpu.roll(ext, length + 8 - (3 - j), 0)[0:length]
    d_mix = (d_mix + mm_nt(value_low, w_v[...])).astype(bf16)
    d_z = dz_ref[...]
    rows = normed[...]
    d_normed = mm_nt(d_mix, w_mix[...]) + mm_nt(d_z, w_gate[...])
    g_ln = jnp.sum(d_normed * rows.astype(f32), axis=0, keepdims=True)
    g_small[32:33, :] += g_ln[:, :size]
    g_small[33:34, :] += g_ln[:, size:]

    @pl.when(last)
    def _():
        g_small[29:32, :] = g_gain[0:3, :]

    return rows, d_mix, d_z, d_normed


def lower_block(
    at_start, at_end, lows, dskip_ref, dskip_next, dz_ref, mix_ref, mix_before, mix_next, normed,
    w_q, w_k, w_v, w_mix, w_gate, conv_w, conv_b, g_small,
):
    query_low, key_low, value_low = lows
    length, size = mix_ref.shape
    extra = mix_next.shape[0]
    halo = jnp.where(at_start, 0.0, mix_before[8:16, :].astype(f32))
    ext = jnp.concatenate(
        [halo, mix_ref[...].astype(f32), mix_next[...].astype(f32)], axis=0
    )
    taps = conv_taps(ext, length + extra)
    summed = conv_b[...]
    for j in range(4):
        summed = summed + conv_w[j : j + 1, :] * taps[j]
    opened = jax.nn.sigmoid(summed)
    d_conv = jnp.concatenate([dskip_ref[...], dskip_next[...]], axis=0)
    d_conv = d_conv + mm_nt(query_low, w_q[...]) + mm_nt(key_low, w_k[...])
    d_summed = d_conv * (opened * (1.0 + summed * (1.0 - opened)))
    for j in range(4):
        g_small[24 + j : 25 + j, :] += jnp.sum(
            d_summed[:length] * taps[j][:length], axis=0, keepdims=True
        )
    g_small[28:29, :] += jnp.sum(d_summed[:length], axis=0, keepdims=True)
    row = lax.broadcasted_iota(jnp.int32, d_summed.shape, 0)
    d_summed = jnp.where(jnp.logical_and(at_end, row >= length), 0.0, d_summed)
    d_mix = conv_w[3:4, :] * d_summed[:length]
    for j in range(3):
        ahead = pltpu.roll(d_summed, length + extra - (3 - j), 0)[0:length]
        d_mix = d_mix + conv_w[j : j + 1, :] * ahead
    d_mix = (d_mix + mm_nt(value_low, w_v[...])).astype(bf16)
    rows = normed[...]
    d_normed = mm_nt(d_mix, w_mix[...]) + mm_nt(dz_ref[...], w_gate[...])
    g_ln = jnp.sum(d_normed * rows.astype(f32), axis=0, keepdims=True)
    g_small[32:33, :] += g_ln[:, :size]
    g_small[33:34, :] += g_ln[:, size:]
    return rows, d_mix, d_normed


def lower_kernel(chained, head_ref, *refs):
    ins, refs = refs[:22], list(refs[22:])
    edge = 0.0
    if chained:
        first_halo, first_later, *refs = refs
        edge = first_halo[8:16, :].astype(f32)
        later_out = refs.pop(4)
    part_out, square_out, up_out, small_out = refs[:4]
    g_q, g_k, g_v, g_m, g_z, g_small, later = refs[4:]
    step = pl.program_id(0)
    size = g_q.shape[0]

    @pl.when(step == 0)
    def _():
        for ref in (g_q, g_k, g_v, g_m, g_z, g_small, later):
            ref[...] = jnp.zeros_like(ref)
        if chained:
            later[...] = first_later[...]

    (d_gate, dq, dk, dv, dskip, dz, mix, mix_before, conv, q, k, v, normed,
     w_q, w_k, w_v, w_mix, w_gate, conv_w, conv_b, gate_w, g_gain) = ins
    lows = lower_first(d_gate, dq, dk, dv, mix, conv, q, k, v, gate_w, g_q, g_k, g_v, g_small)
    rows, d_mix, d_z, d_normed = lower_second(
        edge, step == pl.num_programs(0) - 1, lows, dskip, dz, mix, mix_before, normed,
        w_q.at[0], w_k.at[0], w_v.at[0], w_mix, w_gate, conv_w, conv_b, g_gain, g_small, later,
    )
    g_m[...] += mm_tn(rows, d_mix)
    g_z[...] += mm_tn(rows, d_z)
    part_out[...] = d_normed.astype(bf16)

    @pl.when(step == pl.num_programs(0) - 1)
    def _():
        half = size // 2
        for at, ref in enumerate((g_q, g_k, g_v)):
            square_out[0, :, half * at : half * at + half] = ref[:, :half].astype(bf16)
            square_out[1, :, half * at : half * at + half] = ref[:, half:].astype(bf16)
        up_out[0] = g_m[...].astype(bf16)
        up_out[1] = g_z[...].astype(bf16)
        small_out[...] = g_small[...]
        if chained:
            later_out[...] = later[...]


def struct(shape, dtype):
    return jax.ShapeDtypeStruct(shape, dtype)


def run_kernel(body, head, grid, inputs, in_specs, outs, out_specs, scratch, name, flops, nbytes):
    return pl.pallas_call(
        body,
        grid_spec=pltpu.PrefetchScalarGridSpec(
            num_scalar_prefetch=1,
            grid=(grid,),
            in_specs=in_specs,
            out_specs=out_specs,
            scratch_shapes=scratch,
        ),
        out_shape=outs,
        compiler_params=pltpu.CompilerParams(
            dimension_semantics=("arbitrary",), vmem_limit_bytes=vmem_bytes
        ),
        cost_estimate=pl.CostEstimate(flops=flops, bytes_accessed=nbytes, transcendentals=0),
        name=name,
    )(head, *inputs)


def fixed(shape, *index):
    return pl.BlockSpec(shape, lambda g, h: tuple(h[0] if i == "h" else i for i in index))


def lift(head, normed, w_up, w_query, w_key, w_value, conv_w, conv_b, gate_parts, *first):
    tokens, width = normed.shape
    heads, size, _ = w_query.shape
    length = wide_len
    by_row = lambda cols: pl.BlockSpec((length, cols), lambda g, h: (g, 0))
    weight = pl.BlockSpec((1, size, size), lambda g, h: (h[0], 0, 0))
    chained = len(first) > 0
    halo = [pl.BlockSpec((16, size), lambda g, h: (0, 0))] * chained
    return run_kernel(
        partial(lift_kernel, chained), head, tokens // length,
        (normed, w_up, w_up, w_query, w_key, w_value, conv_w, conv_b, gate_parts, *first),
        [
            by_row(width),
            pl.BlockSpec((width, size), lambda g, h: (0, h[0])),
            pl.BlockSpec((width, size), lambda g, h: (0, heads + h[0])),
            weight, weight, weight,
            pl.BlockSpec((4, size), lambda g, h: (0, h[0])),
            pl.BlockSpec((1, size), lambda g, h: (0, h[0])),
            pl.BlockSpec(gate_parts.shape, lambda g, h: (0, 0, 0)),
        ]
        + [pl.BlockSpec((16, width), lambda g, h: (0, 0))] * chained,
        [struct((tokens, size), bf16)] * 5
        + [struct((tokens, size), f32), struct((8, tokens), f32)]
        + [struct((16, size), bf16)] * chained,
        [by_row(size)] * 6 + [pl.BlockSpec((8, length), lambda g, h: (0, g))] + halo,
        [pltpu.VMEM((8, size), f32)],
        "lift", 2 * tokens * size * (2 * width + 3 * size), 24 * 2**20,
    )


def cell_forward(head, gates, q, k, v, conv, gate_z, out_gain, skip_gain, w_down, *first):
    tokens, size = q.shape
    width = w_down.shape[1]
    length = chunk_len
    steps = tokens // length
    by_row = lambda cols: pl.BlockSpec((length, cols), lambda g, h: (g, 0))
    gain = pl.BlockSpec((1, size), lambda g, h: (0, h[0]))
    carried = [struct(value.shape, f32) for value in first]
    carried_specs = [pl.BlockSpec(value.shape, lambda g, h: (0, 0)) for value in first]
    return run_kernel(
        partial(cell_forward_kernel, len(first) > 0), head, steps,
        (gates, q, k, v, conv, gate_z, out_gain, skip_gain, w_down, *first),
        [pl.BlockSpec((2, length), lambda g, h: (0, g))]
        + [by_row(size)] * 5
        + [gain, gain, pl.BlockSpec((size, width), lambda g, h: (h[0], 0))]
        + carried_specs,
        [
            struct((tokens, width), bf16),
            struct((tokens, size), f32),
            struct((steps, size, size), bf16),
            struct((steps, 8, size), f32),
            struct((tokens, length), bf16),
            struct((tokens, 128), f32),
            struct((8, tokens), f32),
        ]
        + carried,
        [
            by_row(width),
            by_row(size),
            pl.BlockSpec((1, size, size), lambda g, h: (g, 0, 0)),
            pl.BlockSpec((1, 8, size), lambda g, h: (g, 0, 0)),
            by_row(length),
            by_row(128),
            pl.BlockSpec((8, length), lambda g, h: (0, g)),
        ]
        + carried_specs,
        [pltpu.VMEM((size, size), f32), pltpu.VMEM((8, size), f32), pltpu.VMEM((8, 128), f32)],
        "cell_forward", 2 * tokens * size * (2 * length + 2 * size + width), 28 * 2**20,
    )


def cell_backward(
    head, rows, q, k, v, conv, gate_z, normed, states, norms, weights, cols, cot, rows_in,
    out_gain, skip_gain, w_down, *first,
):
    tokens, size = q.shape
    width = w_down.shape[1]
    length = chunk_len
    steps = tokens // length
    end = steps - 1
    by_row = lambda n: pl.BlockSpec((length, n), lambda g, h: (end - g, 0))
    gain = pl.BlockSpec((1, size), lambda g, h: (0, h[0]))
    whole = lambda shape: pl.BlockSpec(shape, lambda g, h: (0, 0))
    carried = [struct(value.shape, f32) for value in first]
    carried_specs = [whole(value.shape) for value in first]
    return run_kernel(
        partial(cell_backward_kernel, len(first) > 0), head, steps,
        (rows, q, k, v, conv, gate_z, normed, states, norms, weights, cols, cot, rows_in,
         out_gain, skip_gain, w_down, *first),
        [pl.BlockSpec((8, length), lambda g, h: (0, end - g))]
        + [by_row(size)] * 6
        + [
            pl.BlockSpec((1, size, size), lambda g, h: (end - g, 0, 0)),
            pl.BlockSpec((1, 8, size), lambda g, h: (end - g, 0, 0)),
            by_row(length),
            by_row(128),
            by_row(width),
            by_row(width),
            gain, gain,
            pl.BlockSpec((size, width), lambda g, h: (h[0], 0)),
        ]
        + carried_specs,
        [struct((tokens, size), f32)] * 4
        + [
            struct((tokens, size), bf16),
            struct((8, tokens), f32),
            struct((2, size, width // 2), bf16),
            struct((width, size), bf16),
            struct((8, size), f32),
        ]
        + carried,
        [by_row(size)] * 5
        + [
            pl.BlockSpec((8, length), lambda g, h: (0, end - g)),
            pl.BlockSpec((2, size, width // 2), lambda g, h: (0, 0, 0)),
            whole((width, size)),
            whole((8, size)),
        ]
        + carried_specs,
        [
            pltpu.VMEM((size, size), f32),
            pltpu.VMEM((8, size), f32),
            pltpu.VMEM((size, width), f32),
            pltpu.VMEM((width, size), f32),
            pltpu.VMEM((8, size), f32),
        ],
        "cell_backward", 2 * tokens * size * (4 * length + 4 * size + 2 * width), 44 * 2**20,
    )


def lower_inputs(
    length, d_gate, dq, dk, dv, dskip, dz, mix, conv, q, k, v, normed,
    w_query, w_key, w_value, w_up, conv_w, conv_b, gate_pairs, g_gain,
):
    tokens, size = q.shape
    width = normed.shape[1]
    heads = w_query.shape[0]
    end = tokens // length - 1
    by_row = lambda n: pl.BlockSpec((length, n), lambda g, h: (end - g, 0))
    kept = lambda shape, index: pl.BlockSpec(shape, index, pipeline_mode=pl.Buffered(1))
    weight = kept((1, size, size), lambda g, h: (h[0], 0, 0))
    inputs = (
        d_gate, dq, dk, dv, dskip, dz, mix, mix, conv, q, k, v, normed,
        w_query, w_key, w_value, w_up, w_up, conv_w, conv_b, gate_pairs, g_gain,
    )
    specs = [pl.BlockSpec((8, length), lambda g, h: (0, end - g))]
    specs += [by_row(size)] * 6
    specs += [
        pl.BlockSpec(
            (16, size), lambda g, h: (jnp.maximum((end - g) * (length // 16) - 1, 0), 0)
        )
    ]
    specs += [by_row(size)] * 4
    specs += [by_row(width), weight, weight, weight]
    specs += [
        kept((width, size), lambda g, h: (0, h[0])),
        kept((width, size), lambda g, h: (0, heads + h[0])),
        kept((4, size), lambda g, h: (0, h[0])),
        kept((1, size), lambda g, h: (0, h[0])),
        kept(gate_pairs.shape, lambda g, h: (0, 0)),
        kept(g_gain.shape, lambda g, h: (0, 0)),
    ]
    return inputs, specs


def lower(head, *inputs):
    inputs, first = inputs[:20], inputs[20:]
    tokens, size = inputs[1].shape
    width = inputs[11].shape[1]
    length = wide_len
    end = tokens // length - 1
    by_row = lambda n: pl.BlockSpec((length, n), lambda g, h: (end - g, 0))
    whole = lambda shape: pl.BlockSpec(shape, lambda g, h: (0, 0))
    chained = len(first) > 0
    inputs, specs = lower_inputs(length, *inputs)
    return run_kernel(
        partial(lower_kernel, chained), head, tokens // length,
        (*inputs, *first),
        specs + [whole(value.shape) for value in first],
        [struct((tokens, width), bf16)]
        + [struct((2, size, 3 * size // 2), bf16), struct((2, width, size), bf16)]
        + [struct((40, size), f32)]
        + [struct((8, size), f32)] * chained,
        [by_row(width)]
        + [
            pl.BlockSpec((2, size, 3 * size // 2), lambda g, h: (0, 0, 0)),
            pl.BlockSpec((2, width, size), lambda g, h: (0, 0, 0)),
        ]
        + [whole((40, size))]
        + [whole((8, size))] * chained,
        [pltpu.VMEM((size, size), f32)] * 3
        + [pltpu.VMEM((width, size), f32)] * 2
        + [pltpu.VMEM((40, size), f32), pltpu.VMEM((8, size), f32)],
        "lower", 2 * tokens * size * (6 * size + 4 * width), 48 * 2**20,
    )
MESH_ID = pl.DeviceIdType.MESH


def halves_of(value, count):
    whole = jnp.int32(0)
    for bound in range(2, count, 2):
        whole = whole + jnp.where(value >= bound, 1, 0)
    return whole, value - 2 * whole


def where_am_i():
    at_seq, at_batch = lax.axis_index("seq"), lax.axis_index("batch")
    first = jnp.int32(0)
    for bound in range(8, lax.axis_size("seq"), 8):
        first = first + jnp.where(at_seq >= bound, 8, 0)
    z, y = halves_of(at_seq - first, 8)
    x, c = halves_of(at_batch, lax.axis_size("batch"))
    return first, z, y, x, c


def turn(value, count):
    return jnp.where(value >= count, value - count, value)


def greet(others):
    barrier = pltpu.get_barrier_semaphore()
    for other in others:
        pl.semaphore_signal(barrier, 1, device_id=other, device_id_type=MESH_ID)
    pl.semaphore_wait(barrier, len(others))


def remote(src, dst, sent, landed, device):
    return pltpu.make_async_remote_copy(src, dst, sent, landed, device_id=device, device_id_type=MESH_ID)


def normalize(rows):
    centre = rows - jnp.mean(rows, axis=-1, keepdims=True)
    rstd = lax.rsqrt(jnp.mean(centre * centre, axis=-1, keepdims=True) + norm_epsilon)
    return centre * rstd, rstd


class Gather:
    def __init__(self, source, out_ref, block, parts, sems):
        self.source, self.out_ref, self.block, self.parts = source, out_ref, block, parts
        self.kept, self.z_sent, self.z_landed, self.y_sent, self.y_landed, *sems = sems
        self.c_sent, self.c_landed = sems
        self.first, self.z, self.y, self.x, self.c = where_am_i()
        self.size = block // parts
        self.enters = halves_of(self.z, 4)[0] == self.c

    def device(self, zz, yy, cc):
        return (self.first + 2 * zz + yy, 2 * self.x + cc)

    def others(self):
        others = [self.device(turn(self.z + k, 4), self.y, self.c) for k in range(1, 4)]
        return others + [self.device(self.z, 1 - self.y, self.c), self.device(self.z, self.y, 1 - self.c)]

    def rows(self, zz, yy, part):
        start = (2 * zz + yy) * self.block + part * self.size
        return self.out_ref.at[pl.ds(pl.multiple_of(start, self.size), self.size)]

    def away(self, m):
        return 2 * self.c + m != self.z

    def to_column(self, m, part):
        return remote(
            self.source(m, part), self.rows(self.z, self.y, part), self.z_sent.at[m, part],
            self.z_landed.at[self.z, part], self.device(2 * self.c + m, self.y, self.c),
        )

    def keep(self, m, part):
        return pltpu.make_async_copy(
            self.source(m, part), self.rows(self.z, self.y, part), self.kept.at[part]
        )

    def from_column(self, zz, part):
        here = self.rows(zz, self.y, part)
        return remote(
            here, here, self.z_sent.at[0, part], self.z_landed.at[zz, part],
            self.device(zz, self.y, self.c),
        )

    def to_row(self, zz, k, part):
        here = self.rows(zz, self.y, part)
        return remote(
            here, here, self.y_sent.at[k, part], self.y_landed.at[zz, part],
            self.device(self.z, 1 - self.y, self.c),
        )

    def from_row(self, zz, k, part):
        here = self.rows(zz, 1 - self.y, part)
        return remote(
            here, here, self.y_sent.at[k, part], self.y_landed.at[zz, part],
            self.device(self.z, 1 - self.y, self.c),
        )

    def to_core(self, zz, yy, k, part):
        here = self.rows(zz, yy, part)
        return remote(
            here, here, self.c_sent.at[k, part], self.c_landed.at[2 * zz + yy, part],
            self.device(self.z, self.y, 1 - self.c),
        )

    def start(self, part):
        for m in range(2):
            pl.when(self.away(m))(lambda: self.to_column(m, part).start())
            pl.when(jnp.logical_not(self.away(m)))(lambda: self.keep(m, part).start())

    def at(self, k):
        high, low = halves_of(self.z, 4)
        far = 2 * high if k < 2 else 2 - 2 * high
        return far + (low if k % 2 == 0 else 1 - low)

    def pass_column(self, k, part):
        @pl.when(self.enters)
        def _():
            if k == 0:
                self.keep(0, part).wait()
            else:
                self.from_column(self.at(k), part).wait_recv()
            self.to_row(self.at(k), k, part).start()
            self.to_core(self.at(k), self.y, k, part).start()

    def pass_row(self, k, part):
        @pl.when(self.enters)
        def _():
            self.from_row(self.at(k), k, part).wait_recv()
            self.to_core(self.at(k), 1 - self.y, 4 + k, part).start()

    def finish(self):
        @pl.when(self.enters)
        def _():
            for k in range(4):
                for part in range(self.parts):
                    self.to_row(self.at(k), k, part).wait_send()
                    self.to_core(self.at(k), self.y, k, part).wait_send()
                    self.to_core(self.at(k), 1 - self.y, 4 + k, part).wait_send()

        @pl.when(jnp.logical_not(self.enters))
        def _():
            for zz in range(4):
                for yy in range(2):
                    for part in range(self.parts):
                        self.to_core(zz, yy, 0, part).wait_recv()

        for m in range(2):
            for part in range(self.parts):
                pl.when(self.away(m))(lambda: self.to_column(m, part).wait_send())


def gather_sems(parts):
    shapes = [(parts,), (2, parts), (4, parts), (4, parts), (4, parts), (8, parts), (8, parts)]
    return [pltpu.SemaphoreType.DMA(shape) for shape in shapes]


def gather_kernel(rows_ref, gain_ref, out_ref, staged, *sems):
    parts = sems[0].shape[0]
    block = rows_ref.shape[1]
    size = block // parts
    gather = Gather(
        lambda m, part: staged.at[m, pl.ds(part * size, size)], out_ref, block, parts, sems
    )
    greet(gather.others())
    for part in range(parts):
        here = pl.ds(part * size, size)
        for m in range(2):
            staged[m, here] = (
                normalize(rows_ref[m, here].astype(f32))[0] * gain_ref[...]
            ).astype(bf16)
        gather.start(part)
    for part in range(parts):
        for k in range(4):
            gather.pass_column(k, part)
        if part > 0:
            for k in range(4):
                gather.pass_row(k, part - 1)
    for k in range(4):
        gather.pass_row(k, parts - 1)
    gather.finish()


def gather_normed(rows, gain):
    micro, block, width = rows.shape
    return pl.pallas_call(
        gather_kernel,
        out_shape=struct((8 * block, width), bf16),
        in_specs=[pl.BlockSpec(memory_space=pltpu.VMEM)] * 2,
        out_specs=pl.BlockSpec(memory_space=pl.ANY),
        scratch_shapes=[pltpu.VMEM((micro, block, width), bf16)] + gather_sems(4),
        compiler_params=pltpu.CompilerParams(
            collective_id=0, has_side_effects=True, vmem_limit_bytes=32 * 2**20
        ),
        name="gather_normed",
    )(rows, gain)


def rise_kernel(
    normed, w_mix, w_gate, w_q, w_k, w_v, conv_w, conv_b, gate_parts, gate_b, out_gain, skip_gain,
    w_down, cot_ref, *refs
):
    lift_outs, cell_outs, (cot_out, *refs) = refs[:6], refs[6:13], refs[13:]
    q_all, k_all, v_all, conv_all, z_all, carry, gate_mine, gate_all, gates, *refs = refs
    state, h_sent, h_landed, *sems = refs[:3], *refs[3:]
    parts = sems[0].shape[0]
    step = pl.program_id(0)
    blocks = pl.num_programs(0) // 2
    block = normed.shape[0]
    size = cot_ref.shape[1] // parts
    gather = Gather(
        lambda m, part: cot_ref.at[m, pl.ds(part * size, size)], cot_out, cot_ref.shape[1], parts,
        sems,
    )
    z, y, c = gather.z, gather.y, gather.c
    head = 2 * c + y
    heads = gate_all.shape[0]
    group = [(1 - y, c), (y, 1 - c), (1 - y, 1 - c)]
    span = gate_mine.shape[1] // 2

    def gate_to(k, part):
        lanes = pl.ds(part * span, span)
        return remote(
            gate_mine.at[:, lanes], gate_all.at[head, :, lanes], h_sent.at[k, part],
            h_landed.at[head, part], gather.device(z, *group[k]),
        )

    def gate_from(k, part):
        lanes = pl.ds(part * span, span)
        at = 2 * group[k][1] + group[k][0]
        return remote(
            gate_mine.at[:, lanes], gate_all.at[at, :, lanes], h_sent.at[k, part],
            h_landed.at[at, part], gather.device(z, *group[k]),
        )

    @pl.when(step == 0)
    def _():
        greet(gather.others() + [gather.device(z, 1 - y, 1 - c)])
        for part in range(parts):
            gather.start(part)

    @pl.when(step < blocks)
    def _():
        here = pl.ds(pl.multiple_of(step * block, block), block)
        lift_kernel(
            False, None, normed, w_mix, w_gate, w_q, w_k, w_v, conv_w, conv_b, gate_parts,
            *lift_outs, gate_mine.at[:, here], carry,
        )
        for ref, made in zip((conv_all, q_all, k_all, v_all, z_all), lift_outs[1:]):
            ref[here] = made[...]
        gate_all[head, :, here] = gate_mine[:, here]

    for part in range(2):

        @pl.when(step == (blocks // 2) * (part + 1) - 1)
        def _():
            for k in range(3):
                gate_to(k, part).start()

        @pl.when(step == blocks + (blocks // 2) * part)
        def _():
            for k in range(3):
                gate_from(k, part).wait_recv()

    @pl.when(step >= blocks)
    def _():
        here = pl.ds(pl.multiple_of((step - blocks) * block, block), block)
        for row, at in enumerate((head, heads + head)):
            total = gate_all[0, pl.ds(at, 1), here]
            for h in range(1, heads):
                total = total + gate_all[h, pl.ds(at, 1), here]
            if row == 1:
                total = total + gate_b[pl.ds(head, 1), :]
            gates[row : row + 1, :] = total
        cell_forward_kernel(
            False, None, gates, q_all.at[here], k_all.at[here], v_all.at[here], conv_all.at[here],
            z_all.at[here], out_gain, skip_gain, w_down, *cell_outs, *state, start=blocks,
        )

    def columns(part, ks=(1, 2, 3)):
        return [partial(gather.pass_column, k, part) for k in ks]

    def rows(part, ks=(0, 1, 2, 3)):
        return [partial(gather.pass_row, k, part) for k in ks]

    plan = {
        0: [do for part in range(parts) for do in columns(part, (0,))],
        4: columns(0) + [do for part in range(parts) for do in rows(part, (0,))],
        7: columns(1),
        8: rows(0, (1, 2, 3)),
        10: columns(2),
        11: rows(1, (1, 2, 3)),
        13: columns(3),
        14: rows(2, (1, 2, 3)),
        15: rows(3, (1, 2, 3)),
    }
    for when, work in plan.items():

        @pl.when(step == when)
        def _():
            for do in work:
                do()

    @pl.when(step == 2 * blocks - 1)
    def _():
        gather.finish()
        for k in range(3):
            for part in range(2):
                gate_to(k, part).wait_send()


def rise(
    normed, w_up, w_query, w_key, w_value, conv_w, conv_b, gate_parts, gate_b, out_gain, skip_gain,
    w_down, cot,
):
    tokens, width = normed.shape
    heads, size, _ = w_query.shape
    micro, block, _ = cot.shape
    steps = tokens // block
    early = lambda g: jnp.minimum(g, steps - 1)
    late = lambda g: jnp.maximum(g - steps, 0)
    by_row = lambda n, at: pl.BlockSpec((block, n), lambda g: (at(g), 0))
    kept = lambda shape, index: pl.BlockSpec(shape, index, pipeline_mode=pl.Buffered(1))
    weight = kept((1, size, size), lambda g: (own_head(), 0, 0))
    lanes = lambda rows: kept((rows, size), lambda g: (0, own_head()))
    anywhere = pl.BlockSpec(memory_space=pl.ANY)
    specs = [
        by_row(width, early), lanes(width), kept((width, size), lambda g: (0, heads + own_head())),
        weight, weight, weight, lanes(4), lanes(1), kept(gate_parts.shape, lambda g: (0, 0, 0)),
        kept(gate_b.shape, lambda g: (0, 0)), lanes(1), lanes(1),
        kept((size, width), lambda g: (own_head(), 0)), kept(cot.shape, lambda g: (0, 0, 0)),
    ]
    outs = [struct((tokens, size), bf16)] * 5 + [struct((tokens, size), f32)]
    out_specs = [by_row(size, early)] * 6
    outs += [
        struct((tokens, width), bf16), struct((tokens, size), f32),
        struct((steps, size, size), bf16), struct((steps, 8, size), f32),
        struct((tokens, block), bf16), struct((tokens, 128), f32), struct((8, tokens), f32),
        struct((tokens, width), bf16),
    ]
    out_specs += [
        by_row(width, late), by_row(size, late),
        pl.BlockSpec((1, size, size), lambda g: (late(g), 0, 0)),
        pl.BlockSpec((1, 8, size), lambda g: (late(g), 0, 0)),
        by_row(block, late), by_row(128, late),
        pl.BlockSpec((8, block), lambda g: (0, late(g))), anywhere,
    ]
    scratch = [((tokens, size), bf16)] * 4 + [((tokens, size), f32), ((8, size), f32)]
    scratch += [((8, tokens), f32), ((heads, 8, tokens), f32), ((8, block), f32)]
    scratch += [((size, size), f32), ((8, size), f32), ((8, 128), f32)]
    return pl.pallas_call(
        rise_kernel,
        grid=(2 * steps,),
        in_specs=specs,
        out_specs=out_specs,
        out_shape=outs,
        scratch_shapes=[pltpu.VMEM(shape, dtype) for shape, dtype in scratch]
        + [pltpu.SemaphoreType.DMA((3, 2)), pltpu.SemaphoreType.DMA((4, 2))] + gather_sems(4),
        compiler_params=pltpu.CompilerParams(
            dimension_semantics=("arbitrary",), collective_id=3, has_side_effects=True,
            vmem_limit_bytes=vmem_bytes,
        ),
        name="rise",
    )(
        normed, w_up, w_up, w_query, w_key, w_value, conv_w, conv_b, gate_parts, gate_b, out_gain,
        skip_gain, w_down, cot,
    )


def own_head():
    first, z, y, x, c = where_am_i()
    return 2 * c + y


def settle_kernel(*refs):
    ins, refs = refs[:16], refs[16:]
    part_ref, tokens_ref, *refs = refs
    (dq_out, dk_out, dv_out, dskip_out, dz_out, g_down_out, g_z_out, g_gain_out,
     block_out, gate_out, *refs) = refs
    state, (gate_rows, gate_all, own, from_core, kept, to_row, from_row, to_owner, owned, *sems) = (
        refs[:5], refs[5:],
    )
    own_sem, c_sent, c_landed, y_sent, y_landed, o_sent, o_landed, h_sent, h_landed = sems
    step = pl.program_id(0)
    first, z, y, x, c = where_am_i()
    head = 2 * c + y
    high, low = halves_of(z, 4)
    half = own.shape[1]
    block = ins[1].shape[0]

    def device(zz, yy, cc):
        return (first + 2 * zz + yy, 2 * x + cc)

    around = [turn(z + k, 4) for k in range(1, 4)]
    order = around + [z]
    group = [(1 - y, c), (y, 1 - c), (1 - y, 1 - c)]

    def rows_of(at, cc):
        return part_ref.at[pl.ds(pl.multiple_of((2 * at + cc) * half, half), half)]

    def load(at):
        return pltpu.make_async_copy(rows_of(at, c), own.at[at], own_sem.at[at])

    def to_c(at):
        return remote(
            rows_of(at, 1 - c), from_core.at[at], c_sent.at[at], c_landed.at[at],
            device(z, y, 1 - c),
        )

    def to_y(zz):
        return remote(
            to_row.at[zz], from_row.at[zz], y_sent.at[zz], y_landed.at[zz], device(z, 1 - y, c)
        )

    def to_o(zz):
        return remote(
            to_owner.at[zz], owned.at[low, c], o_sent.at[zz], o_landed.at[low, c],
            device(zz, y, high),
        )

    def core_sum(at):
        load(at).wait()
        to_c(at).wait_recv()
        return (own[at].astype(f32) + from_core[at].astype(f32)).astype(bf16)

    def core_step(zz):
        to_row[zz] = core_sum(2 * zz + 1 - y)
        to_y(zz).start()
        kept[zz] = core_sum(2 * zz + y)

    def row_sum(zz):
        to_y(zz).wait_recv()
        return (kept[zz].astype(f32) + from_row[zz].astype(f32)).astype(bf16)

    enters = high == c

    def row_step(zz):
        to_owner[zz] = row_sum(zz)
        to_o(zz).start()

    def gate_to(k):
        yy, cc = group[k]
        return remote(
            gate_rows, gate_all.at[head], h_sent.at[k], h_landed.at[head], device(z, yy, cc)
        )

    def gate_from(k):
        at = 2 * group[k][1] + group[k][0]
        return remote(
            gate_rows, gate_all.at[at], h_sent.at[k], h_landed.at[at], device(z, *group[k])
        )

    @pl.when(step == 0)
    def _():
        others = [device(z, yy, cc) for yy, cc in group]
        for zz in around:
            others += [device(zz, y, c), device(zz, y, 1 - c)]
        greet(others)
        for zz in order:
            for yy in (1 - y, y):
                to_c(2 * zz + yy).start()
                load(2 * zz + yy).start()

    now = pl.num_programs(0) - 1 - step
    lanes = pl.ds(pl.multiple_of(now * block, block), block)
    cell_backward_kernel(
        False, None, *ins, dq_out, dk_out, dv_out, dskip_out, dz_out, gate_rows.at[:, lanes],
        g_down_out, g_z_out, g_gain_out, *state,
    )

    for k in range(4):
        pl.when(step == k)(lambda: core_step(order[k]))
    for k, when in enumerate((2, 4, 5)):
        pl.when(step == when)(lambda: row_step(order[k]))

    @pl.when(step == pl.num_programs(0) - 1)
    def _():
        for k in range(3):
            gate_to(k).start()
        gate_all[head] = gate_rows[...]

        @pl.when(enters)
        def _():
            owned[low, c] = row_sum(z)

        @pl.when(jnp.logical_not(enters))
        def _():
            row_step(z)

        for m in range(2):
            for cc in range(2):
                own_part = jnp.logical_and(2 * c + m == z, c == cc)
                landed = remote(
                    to_owner.at[0], owned.at[m, cc], o_sent.at[0], o_landed.at[m, cc],
                    device(2 * c + m, y, cc),
                )
                pl.when(jnp.logical_not(own_part))(lambda: landed.wait_recv())
                here = pl.ds(cc * half, half)
                block_out[m, here] = (
                    tokens_ref[m, here].astype(f32) + owned[m, cc].astype(f32)
                ).astype(bf16)
        for k in range(3):
            gate_from(k).wait_recv()
        heads = gate_all.shape[0]
        for h in range(heads):
            gate_out[h : h + 1, :] = gate_all[h, 0:1, :]
            gate_out[heads + h : heads + h + 1, :] = gate_all[h, 1:2, :]
        for k in range(3):
            gate_to(k).wait_send()
            to_o(order[k]).wait_send()
        pl.when(jnp.logical_not(enters))(lambda: to_o(z).wait_send())
        for zz in range(4):
            to_y(zz).wait_send()
        for at in range(8):
            to_c(at).wait_send()


def settle(
    part, tokens, rows, q, k, v, conv, gate_z, normed, states, norms, weights, cols, cot, rows_in,
    out_gain, skip_gain, w_down,
):
    count, size = q.shape
    width = w_down.shape[1]
    micro, block, _ = tokens.shape
    half = block // 2
    length = chunk_len
    end = count // length - 1
    by_row = lambda n: pl.BlockSpec((length, n), lambda g: (end - g, 0))
    gain = pl.BlockSpec((1, size), lambda g: (0, own_head()), pipeline_mode=pl.Buffered(1))
    kept = lambda value: pl.BlockSpec(
        value.shape, lambda g: (0,) * len(value.shape), pipeline_mode=pl.Buffered(1)
    )
    specs = [pl.BlockSpec((8, length), lambda g: (0, end - g))] + [by_row(size)] * 6
    specs += [
        pl.BlockSpec((1, size, size), lambda g: (end - g, 0, 0)),
        pl.BlockSpec((1, 8, size), lambda g: (end - g, 0, 0)),
        by_row(length), by_row(128), by_row(width), by_row(width), gain, gain,
        pl.BlockSpec((size, width), lambda g: (own_head(), 0), pipeline_mode=pl.Buffered(1)),
        pl.BlockSpec(memory_space=pl.ANY), kept(tokens),
    ]
    whole = [
        struct((2, size, width // 2), bf16), struct((width, size), bf16), struct((8, size), f32),
        struct(tokens.shape, bf16), struct((8, count), f32),
    ]
    outs = [struct((count, size), f32)] * 4 + [struct((count, size), bf16)] + whole
    scratch = [
        ((size, size), f32), ((8, size), f32), ((size, width), f32), ((width, size), f32),
        ((8, size), f32), ((8, count), f32), ((4, 8, count), f32),
        ((8, half, width), bf16), ((8, half, width), bf16), ((4, half, width), bf16),
        ((4, half, width), bf16), ((4, half, width), bf16), ((4, half, width), bf16),
        ((2, 2, half, width), bf16),
    ]
    sems = [(8,), (8,), (8,), (4,), (4,), (4,), (2, 2), (3,), (4,)]
    return pl.pallas_call(
        settle_kernel,
        grid=(count // length,),
        in_specs=specs,
        out_specs=[by_row(size)] * 5 + [kept(value) for value in whole],
        out_shape=outs,
        scratch_shapes=[pltpu.VMEM(shape, dtype) for shape, dtype in scratch]
        + [pltpu.SemaphoreType.DMA(shape) for shape in sems],
        compiler_params=pltpu.CompilerParams(
            dimension_semantics=("arbitrary",), collective_id=2, has_side_effects=True,
            vmem_limit_bytes=60 * 2**20,
        ),
        cost_estimate=pl.CostEstimate(
            flops=2 * count * size * (4 * length + 4 * size + 3 * width),
            bytes_accessed=48 * 2**20, transcendentals=0,
        ),
        name="settle",
    )(
        rows, q, k, v, conv, gate_z, normed, states, norms, weights, cols, cot, rows_in,
        out_gain, skip_gain, w_down, part, tokens,
    )


def drain_kernel(
    d_gate, dq, dk, dv, mix_ref, conv, q_ref, k_ref, v_ref,
    dskip, dskip_next, dz, mix_before, mix_next, normed,
    gate_pairs, g_gain, w_query, w_key, w_value, w_up, conv_w, conv_b,
    down_ref, lifted_ref, rows_ref, cot_ref, gain_ref, *refs
):
    grad_out, up_out, query_out, key_out, value_out, down_out, small_out, *refs = refs
    w_q, w_k, w_v, w_mix, w_gate, taps_w, taps_b, q_all, k_all, v_all, *refs = refs
    g_q, g_k, g_v, g_small, rows_all, lifted_all, part_all, *refs = refs
    from_core, kept, to_row, from_row, to_owner, owned, *refs = refs
    give_up, give_square, *refs = refs
    cross_go, cross_got, *refs = refs
    from_x, totals, refs = refs[:3], (*refs[3:6], None, refs[6]), refs[7:]
    from_near, pairs, from_far, ends = (refs[k : 20 : 4] for k in range(4))
    refs = refs[20:]
    up_go, up_got, sq_go, sq_got, dn_go, dn_got, small_x, small_sum, small_z, small_all, *refs = refs
    c_sent, c_landed, y_sent, y_landed, o_sent, o_landed, *refs = refs
    x_sent, x_landed, near_sent, near_landed, far_sent, far_landed, *refs = refs
    cross_sem, w_sem, up_sem, sq_sent, sq_landed, dn_sent, dn_landed, sx_sem, sz_sent, sz_landed, *refs = refs
    sh_sent, sh_landed = refs
    step = pl.program_id(0)
    blocks, block, width = part_all.shape
    half = block // 2
    size = g_q.shape[0]
    first, z, y, x, c = where_am_i()
    head = 2 * c + y
    high, low = halves_of(z, 4)

    def device(zz, yy, cc, xx=x):
        return (first + 2 * zz + yy, 2 * xx + cc)

    around = [turn(z + k, 4) for k in range(1, 4)]
    group = [(1 - y, c), (y, 1 - c), (1 - y, 1 - c)]

    def down_rows(q):
        tall = down_ref.shape[1] // 4
        return pl.ds(q * tall, tall)

    def up_rows(q):
        tall = lifted_ref.shape[0] // 4
        return pl.ds(q * tall, tall)

    def to_x(p, q):
        give = (give_up, give_square)[p].at[q] if p < 2 else down_ref.at[1 - x, down_rows(q)]
        return remote(
            give, from_x[p].at[q], x_sent.at[p, q], x_landed.at[p, q], device(z, y, c, 1 - x)
        )

    def before_near(p, q):
        if p == 3:
            return lifted_ref.at[up_rows(q), pl.ds(size // 2, size // 2)]
        return totals[p].at[q]

    def to_near(p, q):
        return remote(
            before_near(p, q), from_near[p].at[q // 2], near_sent.at[p, q], near_landed.at[p, q],
            device(z + 1 - 2 * low, y, c),
        )

    def start_near(p, q):
        pl.when(low != q % 2)(lambda: to_near(p, q).start())

    def to_far(p, q):
        return remote(
            pairs[p].at[q // 2], from_far[p], far_sent.at[p, q], far_landed.at[p, q],
            device(z + 2 - 4 * high, y, c),
        )

    def x_step(p, q):
        to_x(p, q).wait_recv()
        own = totals[p][q] if p < 2 else down_ref[x, down_rows(q)]
        totals[p][q] = (own.astype(f32) + from_x[p][q].astype(f32)).astype(bf16)
        start_near(p, q)

    def near_step(p, q):
        @pl.when(low == q % 2)
        def _():
            to_near(p, q).wait_recv()
            pairs[p][q // 2] = (
                before_near(p, q)[...].astype(f32) + from_near[p][q // 2].astype(f32)
            ).astype(bf16)
            pl.when(high != q // 2)(lambda: to_far(p, q).start())

    def far_step(p, q):
        @pl.when(z == q)
        def _():
            to_far(p, q).wait_recv()
            total = pairs[p][q // 2].astype(f32) + from_far[p][...].astype(f32)
            ends[p][:, : total.shape[1]] = total

    def to_cross():
        return remote(cross_go, cross_got, cross_sem.at[0], cross_sem.at[1], device(z, y, c, 1 - x))

    def cross(p):
        cross_go[...] = ends[p][...].astype(bf16)
        to_cross().start()

    def weight_copies():
        lanes = pl.ds(pl.multiple_of(head * size, size), size)
        gate_lanes = pl.ds(pl.multiple_of((w_query.shape[0] + head) * size, size), size)
        pairs_of = [
            (w_query.at[head], w_q), (w_key.at[head], w_k), (w_value.at[head], w_v),
            (w_up.at[:, lanes], w_mix), (w_up.at[:, gate_lanes], w_gate),
            (conv_w.at[:, lanes], taps_w), (conv_b.at[:, lanes], taps_b),
        ]
        return [
            pltpu.make_async_copy(src, dst, w_sem.at[k]) for k, (src, dst) in enumerate(pairs_of)
        ]

    def to_c(at):
        there = pl.ds(pl.multiple_of((1 - c) * half, half), half)
        return remote(
            part_all.at[at, there], from_core.at[at], c_sent.at[at], c_landed.at[at],
            device(z, y, 1 - c),
        )

    def to_y(zz):
        return remote(
            to_row.at[zz], from_row.at[zz], y_sent.at[zz], y_landed.at[zz], device(z, 1 - y, c)
        )

    def to_o(zz):
        return remote(
            to_owner.at[zz], owned.at[low, c], o_sent.at[zz], o_landed.at[low, c],
            device(zz, y, high),
        )

    def stays(zz):
        return jnp.logical_and(z == zz, high == c)

    def core_step(at):
        zz, yy = halves_of(at, 8)
        to_c(at).wait_recv()
        here = pl.ds(pl.multiple_of(c * half, half), half)
        value = (part_all[at, here].astype(f32) + from_core[at].astype(f32)).astype(bf16)

        @pl.when(yy == y)
        def _():
            kept[zz] = value

        @pl.when(yy != y)
        def _():
            to_row[zz] = value
            to_y(zz).start()

    def row_step(zz):
        to_y(zz).wait_recv()
        to_owner[zz] = (kept[zz].astype(f32) + from_row[zz].astype(f32)).astype(bf16)

        @pl.when(stays(zz))
        def _():
            owned[low, c] = to_owner[zz]

        pl.when(jnp.logical_not(stays(zz)))(lambda: to_o(zz).start())

    def to_group(k, src, dst, sent, landed):
        yy, cc = group[k]
        return remote(src, dst, sent.at[k], landed, device(z, yy, cc))

    def small_to_x():
        return remote(g_small, small_x, sx_sem.at[0], sx_sem.at[1], device(z, y, c, 1 - x))

    def small_to_z(k):
        return remote(
            small_sum, small_z.at[z], sz_sent.at[k], sz_landed.at[z], device(around[k], y, c)
        )

    def small_from_z(k):
        return remote(
            small_sum, small_z.at[around[k]], sz_sent.at[k], sz_landed.at[around[k]],
            device(around[k], y, c),
        )

    def small_to_head(k):
        return to_group(k, small_all.at[head], small_all.at[head], sh_sent, sh_landed.at[head])

    def small_from_head(k):
        at = 2 * group[k][1] + group[k][0]
        return to_group(k, small_all.at[at], small_all.at[at], sh_sent, sh_landed.at[at])

    def up_to_y():
        return remote(up_go, up_got, up_sem.at[0], up_sem.at[1], device(z, 1 - y, c))

    def square_to(k):
        yy, cc = group[k]
        return to_group(k, sq_go.at[yy, cc], sq_got.at[head], sq_sent, sq_landed.at[head])

    def square_from(k):
        at = 2 * group[k][1] + group[k][0]
        return to_group(k, sq_go.at[0, 0], sq_got.at[at], sq_sent, sq_landed.at[at])

    def down_to(cc):
        return remote(
            dn_go.at[cc], dn_got.at[low], dn_sent.at[cc], dn_landed.at[low],
            device(head, high, cc),
        )

    def down_from(k):
        return remote(
            dn_go.at[0], dn_got.at[k], dn_sent.at[0], dn_landed.at[k],
            device(2 * y + k, low, high),
        )

    home = jnp.logical_and(head == z, high == y)

    @pl.when(step == 0)
    def _():
        others = [device(z, yy, cc) for yy, cc in group] + [device(z, y, c, 1 - x)]
        for zz in around:
            others += [device(zz, yy, cc) for yy, cc in [(y, c)] + group]
        greet(others)
        for q in range(4):
            to_x(2, q).start()
        for q in range(4):
            start_near(3, q)
        for copy in weight_copies():
            copy.start()
        for ref in (g_q, g_k, g_v, g_small):
            ref[...] = jnp.zeros_like(ref)
        for ref in (q_all, k_all, v_all):
            ref[blocks * block :] = jnp.zeros_like(ref[blocks * block :])

    order = around + [z]
    tall, wide = size // 4, size // 2

    @pl.when(step < blocks)
    def _():
        lows = lower_first(
            d_gate, dq, dk, dv, mix_ref, conv, q_ref, k_ref, v_ref, gate_pairs, g_q, g_k, g_v, g_small
        )
        here = pl.ds(pl.multiple_of(step * block, block), block)
        for ref, value in zip((q_all, k_all, v_all), lows):
            ref[here] = value

    @pl.when(step == blocks - 1)
    def _():
        for q in range(4):
            rows_q = slice(tall * q, tall * q + tall)
            for at, ref in enumerate((g_q, g_k, g_v)):
                lanes = slice(wide * at, wide * at + wide)
                left, right = ref[rows_q, :wide], ref[rows_q, wide:]
                totals[1][q, :, lanes] = jnp.where(x == 0, left, right).astype(bf16)
                give_square[q, :, lanes] = jnp.where(x == 0, right, left).astype(bf16)
            to_x(1, q).start()
        for copy in weight_copies():
            copy.wait()

    @pl.when(step >= blocks)
    def _():
        now = drain_order(step, blocks)
        here = pl.ds(pl.multiple_of(now * block, block), block)
        more = pl.ds(pl.multiple_of(now * block, block), block + mix_next.shape[0])
        rows, d_mix, d_normed = lower_block(
            now == 0, now == blocks - 1, (q_all[more], k_all[more], v_all[here]),
            dskip, dskip_next, dz, mix_ref, mix_before, mix_next, normed,
            w_q, w_k, w_v, w_mix, w_gate, taps_w, taps_b, g_small,
        )
        rows_all[here] = rows
        lifted_all[here] = d_mix
        part_all[now] = d_normed.astype(bf16)
        to_c(now).start()
        pl.when(step > blocks)(lambda: core_step(drain_order(step - 1, blocks)))

    def at_end(when, *work):
        @pl.when(step == blocks + when)
        def _():
            for do in work:
                do()

    def spread_down():
        span = dn_go.shape[2]
        for cc in range(2):
            dn_go[cc] = ends[2][:, span * cc : span * cc + span].astype(bf16)
            left_here = jnp.logical_and(home, c == cc)

            @pl.when(left_here)
            def _():
                dn_got[low] = dn_go[cc]

            pl.when(jnp.logical_not(left_here))(lambda: down_to(cc).start())

    def every(do, p):
        return [partial(do, p, q) for q in range(4)]

    def early_cross():
        pl.when(x == 0)(lambda: cross(3))

    at_end(0, *every(near_step, 3))
    at_end(1, *every(x_step, 2))
    at_end(3, partial(x_step, 1, 0))
    at_end(4, *every(far_step, 3), early_cross)
    at_end(5, *every(near_step, 2), partial(x_step, 1, 1), partial(near_step, 1, 0))
    at_end(7, partial(row_step, order[0]), partial(x_step, 1, 2), partial(near_step, 1, 1))

    @pl.when(step == 2 * blocks - 1)
    def _():
        g_small[29:32, :] = g_gain[0:3, :]
        small_to_x().start()
        for q in range(4):
            got = mm_tn(rows_all[:, block * q : block * q + block], lifted_all[...]).astype(bf16)
            given = lifted_ref[up_rows(q), :wide]
            totals[0][q] = jnp.where(x == 0, got[:, :wide], given)
            give_up[q] = jnp.where(x == 0, given, got[:, :wide])
            totals[4][q] = got[:, wide:]
            to_x(0, q).start()
            start_near(4, q)
            if q == 0:
                core_step(2 * z + y)
        for q in range(4):
            far_step(2, q)
        spread_down()
        row_step(order[1])
        x_step(1, 3)
        near_step(1, 2)
        x_step(0, 0)
        row_step(order[2])
        near_step(4, 0)
        near_step(4, 1)
        near_step(1, 3)
        x_step(0, 1)
        near_step(0, 0)
        small_to_x().wait_recv()
        small_sum[...] = g_small[...] + small_x[...]
        small_z[z] = small_sum[...]
        for k in range(3):
            small_to_z(k).start()
        near_step(4, 2)
        near_step(4, 3)
        x_step(0, 2)
        near_step(0, 1)
        row_step(z)
        for q in range(4):
            far_step(1, q)
        for yy in range(2):
            for cc in range(2):
                for a in range(3):
                    sq_go[yy, cc, :, tall * a : tall * a + tall] = ends[1][
                        tall // 2 * yy : tall // 2 * yy + tall // 2,
                        (2 * a + cc) * tall : (2 * a + cc) * tall + tall,
                    ].astype(bf16)
        sq_got[head] = sq_go[y, c]
        for k in range(3):
            square_to(k).start()
        x_step(0, 3)
        near_step(0, 2)
        for q in range(4):
            far_step(4, q)
        pl.when(x == 1)(lambda: cross(4))
        near_step(0, 3)
        for k in range(3):
            small_from_z(k).wait_recv()
        total = small_z[0]
        for zz in range(1, 4):
            total = total + small_z[zz]
        small_all[head] = total
        for k in range(3):
            small_to_head(k).start()
        for q in range(4):
            far_step(0, q)
        to_cross().wait_recv()
        kept_half = jnp.where(x == 0, ends[4][...], ends[3][...])
        ends[0][:, wide:] = kept_half + cross_got[...].astype(f32)
        value = ends[0][...]
        mine = jnp.where(y == 0, value[:half], value[half:])
        up_go[...] = jnp.where(y == 0, value[half:], value[:half]).astype(bf16)
        up_to_y().start()
        for yy in range(2):

            @pl.when(y == yy)
            def _():
                up_out[:, size * yy : size * yy + size] = mine

        for m in range(2):
            for cc in range(2):
                own_part = jnp.logical_and(2 * c + m == z, c == cc)
                landed = remote(
                    to_owner.at[0], owned.at[m, cc], o_sent.at[0], o_landed.at[m, cc],
                    device(2 * c + m, y, cc),
                )
                pl.when(jnp.logical_not(own_part))(lambda: landed.wait_recv())
                rows_here = pl.ds(cc * half, half)
                row_hat, rstd = normalize(rows_ref[m, rows_here].astype(f32))
                scaled = owned[m, cc].astype(f32) * gain_ref[...]
                d_row = rstd * (
                    scaled
                    - jnp.mean(scaled, axis=-1, keepdims=True)
                    - row_hat * jnp.mean(scaled * row_hat, axis=-1, keepdims=True)
                )
                grad_out[m, rows_here] = (cot_ref[m, rows_here].astype(f32) + d_row).astype(bf16)

        for k in range(3):
            small_from_head(k).wait_recv()
        small_out[...] = small_all[...]
        for k in range(3):
            square_from(k).wait_recv()
        for a, ref in enumerate((query_out, key_out, value_out)):
            ref[...] = sq_got[:, :, tall * a : tall * a + tall].astype(f32)
        for k in range(2):
            mine = jnp.logical_and(home, jnp.logical_and(low == k, high == c))
            pl.when(jnp.logical_not(mine))(lambda: down_from(k).wait_recv())
            deep = dn_got.shape[1]
            down_out[deep * k : deep * k + deep] = dn_got[k].astype(f32)
        up_to_y().wait_recv()
        for yy in range(2):

            @pl.when(y == yy)
            def _():
                up_out[:, size * (1 - yy) : size * (1 - yy) + size] = up_got[...].astype(f32)

        small_to_x().wait_send()
        up_to_y().wait_send()
        to_cross().wait_send()
        for p in range(5):
            for q in range(4):
                if p < 3:
                    to_x(p, q).wait_send()
                pl.when(low != q % 2)(lambda: to_near(p, q).wait_send())
                passes = jnp.logical_and(low == q % 2, high != q // 2)
                pl.when(passes)(lambda: to_far(p, q).wait_send())
        for at in range(blocks):
            to_c(at).wait_send()
        for zz in range(4):
            to_y(zz).wait_send()
            pl.when(jnp.logical_not(stays(zz)))(lambda: to_o(zz).wait_send())
        for k in range(3):
            small_to_z(k).wait_send()
            small_to_head(k).wait_send()
            square_to(k).wait_send()
        for cc in range(2):
            left_here = jnp.logical_and(home, c == cc)
            pl.when(jnp.logical_not(left_here))(lambda: down_to(cc).wait_send())


def drain_order(step, blocks):
    first, z, y, x, c = where_am_i()
    k, odd = halves_of(jnp.maximum(step - blocks, 0), blocks)
    return 2 * turn(z + 1 + k, 4) + jnp.where(odd == 0, 1 - y, y)


def drain(inputs, down, lifted, rows, cot, gain):
    (d_gate, dq, dk, dv, dskip, dz, mix, conv, q, k, v, normed,
     w_query, w_key, w_value, w_up, conv_w, conv_b, gate_pairs, g_gain) = inputs
    tokens, size = q.shape
    micro, block, width = rows.shape
    half = block // 2
    lines = 40
    steps = tokens // block
    early = lambda g: jnp.minimum(g, steps - 1)
    late = lambda g: drain_order(g, steps)
    both = lambda g: jnp.where(g < steps, g, drain_order(g, steps))
    edge = lambda at: pl.BlockSpec(
        (16, size), lambda g: (jnp.clip(at(g), 0, tokens // 16 - 1), 0)
    )
    before = edge(lambda g: late(g) * (block // 16) - 1)
    behind = edge(lambda g: (late(g) + 1) * (block // 16))
    by_row = lambda n, at: pl.BlockSpec((block, n), lambda g: (at(g), 0))
    kept = lambda value: pl.BlockSpec(
        value.shape, lambda g: (0,) * value.ndim, pipeline_mode=pl.Buffered(1)
    )
    anywhere = pl.BlockSpec(memory_space=pl.ANY)
    arguments = (
        d_gate, dq, dk, dv, mix, conv, q, k, v, dskip, dskip, dz, mix, mix, normed, gate_pairs, g_gain,
        w_query, w_key, w_value, w_up, conv_w, conv_b, down, lifted, rows, cot, gain,
    )
    specs = [pl.BlockSpec((8, block), lambda g: (0, early(g)))] + [by_row(size, early)] * 3
    specs += [by_row(size, both)] + [by_row(size, early)] * 4
    specs += [by_row(size, late), behind, by_row(size, late), before, behind, by_row(width, late)]
    specs += [kept(gate_pairs), kept(g_gain)]
    specs += [anywhere] * 6 + [kept(value) for value in (down, lifted, rows, cot, gain)]
    scratch = [((size, size), bf16)] * 3 + [((width, size), bf16)] * 2
    scratch += [((4, size), f32), ((1, size), f32)] + [((tokens + 16, size), bf16)] * 3
    scratch += [((size, size), f32)] * 3 + [((lines, size), f32)]
    scratch += [((tokens, width), bf16), ((tokens, size), bf16), ((8, block, width), bf16)]
    scratch += [
        ((8, half, width), bf16), ((4, half, width), bf16), ((4, half, width), bf16),
        ((4, half, width), bf16), ((4, half, width), bf16), ((2, 2, half, width), bf16),
    ]
    up = (width // 4, size // 2)
    pieces = [up, (size // 4, 3 * size // 2), (size // 4, width // 2), up, up]
    scratch += [((4, *piece), bf16) for piece in pieces[:2]] + [(up, bf16)] * 2
    scratch += [((4, *piece), bf16) for piece in pieces[:3] + pieces[:3] + pieces[4:]]
    for piece in pieces:
        scratch += [((2, *piece), bf16)] * 2 + [(piece, bf16), (piece, f32)]
    scratch[-17] = ((up[0], size), f32)
    scratch += [
        ((width // 8, size), bf16), ((width // 8, size), bf16),
        ((2, 2, size // 8, 3 * size // 4), bf16), ((4, size // 8, 3 * size // 4), bf16),
        ((2, size // 4, width // 4), bf16), ((2, size // 4, width // 4), bf16),
        ((lines, size), f32), ((lines, size), f32), ((4, lines, size), f32), ((4, lines, size), f32),
    ]
    sems = [(8,), (8,), (4,), (4,), (4,), (2, 2)] + [(5, 4)] * 6
    sems += [(2,), (7,), (2,), (3,), (4,), (2,), (2,), (2,), (3,), (4,), (3,), (4,)]
    square = struct((4, size // 8, size // 4), f32)
    outs = [
        struct(rows.shape, bf16), struct((width // 8, 2 * size), f32), square, square, square,
        struct((size // 2, width // 4), f32), struct((4, lines, size), f32),
    ]
    return pl.pallas_call(
        drain_kernel,
        grid=(2 * steps,),
        in_specs=specs,
        out_specs=[kept(value) for value in outs],
        scratch_shapes=[pltpu.VMEM(shape, dtype) for shape, dtype in scratch]
        + [pltpu.SemaphoreType.DMA(shape) for shape in sems],
        out_shape=outs,
        compiler_params=pltpu.CompilerParams(
            dimension_semantics=("arbitrary",), collective_id=1, has_side_effects=True,
            vmem_limit_bytes=60 * 2**20,
        ),
        cost_estimate=pl.CostEstimate(
            flops=2 * tokens * size * (6 * size + 4 * width), bytes_accessed=48 * 2**20,
            transcendentals=0,
        ),
        name="drain",
    )(*arguments)


def swap(value, axis, mask):
    count = lax.axis_size(axis)
    return lax.ppermute(value, axis, [(s, s ^ mask) for s in range(count)])


def part_of(value, at, count, axis):
    size = value.shape[axis] // count
    return lax.dynamic_slice_in_dim(value, at * size, size, axis)


def halved(value, bit, dim, axis, mask):
    kept = part_of(value, bit, 2, dim).astype(f32)
    return kept + swap(part_of(value, 1 - bit, 2, dim), axis, mask).astype(f32)


def paired(mine, other, bit, dim):
    return jnp.where(
        bit == 0, jnp.concatenate([mine, other], dim), jnp.concatenate([other, mine], dim)
    )


def place():
    at_seq, at_batch = lax.axis_index("seq"), lax.axis_index("batch")
    return (at_seq % 8) // 2, at_seq % 2, at_batch // 2, at_batch % 2


def sent_across(blocks, z):
    got = [lax.dynamic_index_in_dim(blocks, z, 0, keepdims=False)]
    for k in range(1, 4):
        got.append(swap(lax.dynamic_index_in_dim(blocks, z ^ k, 0, keepdims=False), "seq", 2 * k))
    return got


def in_order(got, z):
    got = jnp.stack(got)
    return jnp.stack([lax.dynamic_index_in_dim(got, z ^ k, 0, keepdims=False) for k in range(4)])


def gather_sequence(own):
    z, y, x, c = place()
    micro, rows, width = own.shape
    slots = paired(own, swap(own, "batch", 1), c, 0)
    blocks = in_order(sent_across(part_of(slots, c, 2, 2), z), z)[:, None]
    both = paired(blocks, swap(blocks, "seq", 1), y, 1)
    return paired(both, swap(both, "batch", 1), c, 3).reshape(8 * rows, width)


def scatter_first(parts):
    z, y, x, c = place()
    blocks = parts.reshape(4, 2, -1, parts.shape[1])
    return halved(blocks, c, 2, "batch", 1).astype(bf16)


def scatter_last(slots):
    z, y, x, c = place()
    other = swap(part_of(slots, 1 - c, 2, 0), "batch", 1)
    return paired(part_of(slots, c, 2, 0), other, c, 1).astype(f32)


def scatter_sequence(parts):
    z, y, x, c = place()
    blocks = scatter_first(parts)
    blocks = halved(blocks, y, 1, "seq", 1).astype(bf16)[:, 0]
    return scatter_last(in_order(sent_across(blocks, z), z))


def total_over_heads(value):
    value = value + swap(value, "batch", 1)
    return value + swap(value, "seq", 1)


def over_ranges(value, count):
    size = lax.axis_size("seq")
    groups = [[first + 8 * k for k in range(count)] for first in range(8)]
    return lax.all_gather(value, "seq", axis_index_groups=groups) if size > 8 else value[None]


def state_before(state, norm, level, total, ranges):
    index = lax.axis_index("seq") // 8
    summary = (state, norm[0], level[0, 0], total)
    everything = jax.tree.map(lambda part: over_ranges(part, ranges), summary)
    before = state_identity(summary)
    for k in range(ranges - 1):
        new = combine_states(before, jax.tree.map(lambda part: part[k], everything))
        before = jax.tree.map(lambda a, b: jnp.where(k < index, a, b), new, before)
    return (
        before[0],
        jnp.broadcast_to(before[1], norm.shape),
        jnp.broadcast_to(before[2], level.shape),
    )


def cotangent_after(d_state, d_norm, keep, ranges):
    index = lax.axis_index("seq") // 8
    own = (d_state, d_norm)
    everything = jax.tree.map(lambda part: over_ranges(part, ranges), own)
    keeps = over_ranges(keep, ranges)
    after = jax.tree.map(jnp.zeros_like, own)
    for k in range(ranges - 1, 0, -1):
        new = jax.tree.map(lambda a, b: a[k] + keeps[k] * b, everything, after)
        after = jax.tree.map(lambda a, b: jnp.where(k > index, a, b), new, after)
    return after


def reduce_blocks(at, up, square, down, heads):
    count, batch_count = lax.axis_size("seq"), lax.axis_size("batch")
    g_m, g_z = up
    width, size = g_m.shape
    half = size // 2
    squares = [
        jnp.concatenate([square[0, :, k : k + half], square[1, :, k : k + half]], 1)
        for k in range(0, 3 * half, half)
    ]
    g_down = jnp.concatenate([down[0], down[1]], 1)
    inner = heads * size
    up = jnp.zeros((width, 2 * inner), f32)
    up = lax.dynamic_update_slice_in_dim(up, g_m.astype(f32), at * size, 1)
    up = lax.dynamic_update_slice_in_dim(up, g_z.astype(f32), inner + at * size, 1)
    down = lax.dynamic_update_slice_in_dim(
        jnp.zeros((inner, width), f32), g_down.astype(f32), at * size, 0
    )
    full = [up, down]
    for g in squares:
        full.append(
            lax.dynamic_update_slice_in_dim(
                jnp.zeros((heads, size, size), f32), g.astype(f32)[None], at, 0
            )
        )
    blocks = tuple(to_device_blocks(g, count, batch_count) for g in full)
    pieces = lax.psum_scatter(blocks, ("seq", "batch"), scatter_dimension=0, tiled=True)
    s_up, s_down, s_query, s_key, s_value = tuple(p[0] for p in pieces)
    return s_up, jnp.stack([s_query, s_key, s_value], 1), s_down


def head_device(
    tokens, ln_gain, w_up, conv_w, conv_b, w_query, w_key, w_value, gate_w, gate_b,
    out_gain, skip_gain, w_down, d_out,
):
    z, y, x, c = place()
    at = 2 * c + y
    ranges = lax.axis_size("seq") // 8
    direct = ranges == 1 and lax.axis_size("batch") == 4
    head = jnp.reshape(at, (1,)).astype(jnp.int32)
    heads, size, _ = w_query.shape
    inner = heads * size
    conv_row = conv_b.reshape(1, inner)
    out_row = out_gain.reshape(1, inner)
    skip_row = skip_gain.reshape(1, inner)

    normed = gather_normed(tokens[:, 0], ln_gain[None])
    gate_own = lax.dynamic_index_in_dim(
        gate_w.reshape(3, heads, size, 8), at, 1, keepdims=False
    ).transpose(0, 2, 1)
    high = lax.reduce_precision(gate_own, 8, 7)
    middle = lax.reduce_precision(gate_own - high, 8, 7)
    low = lax.reduce_precision(gate_own - high - middle, 8, 7)
    gate_parts = jnp.concatenate([high, middle, low, jnp.zeros_like(high)], 1).astype(bf16)
    gate_pairs = (
        jnp.concatenate([high, high, high, middle, middle, low], 1)
        .astype(bf16)
        .transpose(1, 0, 2)
        .reshape(48, 3 * size)
    )

    if direct:
        (mix, conv, q, k, v, gate_z, part, head_normed, states, norms, weights, cols, rows, cot) = rise(
            normed, w_up, w_query, w_key, w_value, conv_w, conv_row, gate_parts, gate_b[:, None],
            out_row, skip_row, w_down, d_out[:, 0],
        )
    else:
        cot = gather_sequence(d_out[:, 0])
        first = () if ranges == 1 else (shifted(normed[-16:], "seq", 8),)
        mix, conv, q, k, v, gate_z, gates, *halo = lift(
            head, normed, w_up, w_query, w_key, w_value, conv_w, conv_row, gate_parts, *first
        )
        gates = total_over_heads(gates)
        gates = jnp.concatenate(
            [
                lax.dynamic_slice_in_dim(gates, at, 1, 0),
                lax.dynamic_slice_in_dim(gates, heads + at, 1, 0)
                + lax.dynamic_slice_in_dim(gate_b, at, 1, 0)[:, None],
            ]
        )
        first = ()
        if ranges > 1:
            first = (
                jnp.zeros((size, size), f32),
                jnp.zeros((8, size), f32),
                jnp.full((8, 128), floor_value, f32),
            )
            *_, state, norm, level = cell_forward(
                head, gates, q, k, v, conv, gate_z, out_row, skip_row, w_down, *first
            )
            total = jnp.sum(jax.nn.log_sigmoid(gates[1]))
            first = state_before(state, norm, level, total, ranges)
        part, head_normed, states, norms, weights, cols, rows, *last = cell_forward(
            head, gates, q, k, v, conv, gate_z, out_row, skip_row, w_down, *first
        )
    cell_args = (
        rows, q, k, v, conv, gate_z, head_normed, states, norms, weights, cols, cot, normed,
        out_row, skip_row, w_down,
    )
    if direct:
        dq, dk, dv, dskip, dz, g_down, g_z, g_gain, block_rows, d_gate = settle(
            part, tokens[:, 0], *cell_args
        )
    else:
        block_rows = (tokens[:, 0].astype(f32) + scatter_sequence(part)).astype(bf16)
        after = ()
        if ranges > 1:
            after = (jnp.zeros((size, size), f32), jnp.zeros((8, size), f32))
            *_, d_state, d_norm = cell_backward(head, *cell_args, *after)
            keep = jnp.exp(total + first[2][0, 0] - last[2][0, 0])
            after = cotangent_after(d_state, d_norm, keep, ranges)
        dq, dk, dv, dskip, dz, d_rows, g_down, g_z, g_gain, *_ = cell_backward(
            head, *cell_args, *after
        )
        index = jnp.arange(2 * heads)[:, None]
        d_gate = jnp.where(
            index == at, d_rows[0:1], jnp.where(index == heads + at, d_rows[1:2], 0.0)
        )
        d_gate = total_over_heads(d_gate)
    lower_args = (
        d_gate, dq, dk, dv, dskip, dz, mix, conv, q, k, v, normed,
        w_query, w_key, w_value, w_up, conv_w, conv_row, gate_pairs, g_gain,
    )
    if direct:
        grad_rows, s_up, s_query, s_key, s_value, s_down, small = drain(
            lower_args, g_down, g_z, tokens[:, 0], d_out[:, 0], ln_gain[None]
        )
    else:
        first = ()
        if ranges > 1:
            *_, later = lower(head, *lower_args, halo[0], jnp.zeros((8, size), f32))
            first = (halo[0], shifted(later, "seq", -8))
        d_part, square, up, small, *_ = lower(head, *lower_args, *first)
    if not direct:
        d_normed = scatter_sequence(d_part)
        row_f = tokens[:, 0].astype(f32)
        centre = row_f - jnp.mean(row_f, axis=-1, keepdims=True)
        rstd = lax.rsqrt(jnp.mean(centre * centre, axis=-1, keepdims=True) + norm_epsilon)
        row_hat = centre * rstd
        scaled = d_normed * ln_gain
        d_row = rstd * (
            scaled
            - jnp.mean(scaled, axis=-1, keepdims=True)
            - row_hat * jnp.mean(scaled * row_hat, axis=-1, keepdims=True)
        )
        grad_rows = (d_out[:, 0].astype(f32) + d_row).astype(bf16)
        s_up, squares, s_down = reduce_blocks(at, up, square, g_down, heads)
        s_query, s_key, s_value = squares[:, 0], squares[:, 1], squares[:, 2]
        small = jnp.where(jnp.arange(heads)[:, None, None] == at, small, 0.0)
        small = lax.psum(small, ("seq", "batch"))
    s_ln = jnp.sum(small[:, 32:34], 0).reshape(-1) / ln_gain
    s_gate_w = small[:, :24].reshape(heads, 3, 8, size).transpose(1, 0, 3, 2).reshape(3 * inner, 8)
    s_conv_w = small[:, 24:28].transpose(1, 0, 2).reshape(4, inner)
    return (
        block_rows[:, None],
        grad_rows[:, None],
        s_ln,
        s_up,
        s_conv_w,
        small[:, 28].reshape(inner),
        s_query,
        s_key,
        s_value,
        s_gate_w,
        small[:, 31, 0],
        small[:, 29].reshape(inner),
        small[:, 30].reshape(inner),
        s_down,
    )


def solution(mesh):
    placed = (P(None, "batch", "seq", None),) + (P(),) * 12 + (P(None, "batch", "seq", None),)
    return jax.shard_map(
        head_device,
        mesh=mesh,
        in_specs=placed,
        out_specs=(
            P(None, "batch", "seq", None),
            P(None, "batch", "seq", None),
            P(),
            P("seq", "batch"),
            P(),
            P(),
            P(None, "seq", "batch"),
            P(None, "seq", "batch"),
            P(None, "seq", "batch"),
            P(),
            P(),
            P(),
            P(),
            P("seq", "batch"),
        ),
        check_vma=False,
    )
```

```python
from functools import partial

import jax
import jax.numpy as jnp
from jax import lax
from jax.experimental import pallas as pl
from jax.experimental.pallas import tpu as pltpu
from jax.sharding import PartitionSpec as P

norm_epsilon = 1e-05
floor_value = -1e30


def shifted(value, axis, steps):
    count = lax.axis_size(axis)
    initial, last = (max(0, -steps), min(count, count - steps))
    return lax.ppermute(value, axis, [(source, source + steps) for source in range(initial, last)])


def combine_states(earlier, later):
    top = jnp.maximum(later[3] + earlier[2], later[2])
    keep_first = jnp.exp(later[3] + earlier[2] - top)
    keep_second = jnp.exp(later[2] - top)
    merged_c = keep_first[..., None, None] * earlier[0] + keep_second[..., None, None] * later[0]
    merged_n = keep_first[..., None] * earlier[1] + keep_second[..., None] * later[1]
    return (merged_c, merged_n, top, earlier[3] + later[3])


def state_identity(template):
    return (
        jnp.zeros_like(template[0]),
        jnp.zeros_like(template[1]),
        jnp.full_like(template[2], floor_value),
        jnp.zeros_like(template[3]),
    )


def head_output(hidden, out_gain, skip_gain, conv_out, gate_z):
    centre = hidden - jnp.mean(hidden, axis=-1, keepdims=True)
    spread = jnp.mean(centre * centre, axis=-1, keepdims=True)
    normed = centre * lax.rsqrt(spread + norm_epsilon)
    flat_out = normed.transpose(1, 0, 2).reshape(hidden.shape[1], -1) * out_gain
    return (flat_out + skip_gain * conv_out) * jax.nn.silu(gate_z)


def output_tail(
    query_f,
    key_f,
    value_f,
    gate_pre,
    conv_f,
    gate_z,
    out_gain,
    skip_gain,
    state_c,
    state_n,
    state_m,
):
    head_count = gate_pre.shape[1] // 2
    in_gate = gate_pre[:, :head_count].T
    log_forget = jax.nn.log_sigmoid(gate_pre[:, head_count:]).T
    hidden = cell_hidden(
        to_heads(query_f, head_count),
        to_heads(key_f, head_count),
        to_heads(value_f, head_count),
        in_gate,
        log_forget,
        state_c,
        state_n,
        state_m,
    )
    return head_output(hidden, out_gain, skip_gain, conv_f, gate_z)


def state_tail(key_f, value_f, gate_pre, state_c, state_n, state_m):
    head_count = gate_pre.shape[1] // 2
    in_gate = gate_pre[:, :head_count].T
    log_forget = jax.nn.log_sigmoid(gate_pre[:, head_count:]).T
    return cell_state(
        to_heads(key_f, head_count),
        to_heads(value_f, head_count),
        in_gate,
        log_forget,
        state_c,
        state_n,
        state_m,
    )


def to_device_blocks(grad_full, seq_count, batch_count):
    if grad_full.ndim == 2:
        rows, cols = grad_full.shape
        split = grad_full.reshape(seq_count, rows // seq_count, batch_count, cols // batch_count)
        return split.transpose(0, 2, 1, 3).reshape(
            seq_count * batch_count, rows // seq_count, cols // batch_count
        )
    heads, rows, cols = grad_full.shape
    split = grad_full.reshape(heads, seq_count, rows // seq_count, batch_count, cols // batch_count)
    return split.transpose(1, 3, 0, 2, 4).reshape(
        seq_count * batch_count, heads, rows // seq_count, cols // batch_count
    )


f32 = jnp.float32
bf16 = jnp.bfloat16
chunk_len = 256
wide_len = 512
vmem_bytes = 56 * 1024 * 1024


def mm(a, b):
    return lax.dot_general(a, b, (((1,), (0,)), ((), ())), preferred_element_type=f32)


def mm_nt(a, b):
    return lax.dot_general(a, b, (((1,), (1,)), ((), ())), preferred_element_type=f32)


def mm_tn(a, b):
    return lax.dot_general(a, b, (((0,), (0,)), ((), ())), preferred_element_type=f32)


def split_three(value):
    high = value.astype(bf16)
    rest = value - high.astype(f32)
    middle = rest.astype(bf16)
    low = (rest - middle.astype(f32)).astype(bf16)
    return high, middle, low


def conv_taps(ext, length):
    return [pltpu.roll(ext, 3 - j, 0)[8 : 8 + length] if j < 3 else ext[8 : 8 + length] for j in range(4)]


def lift_kernel(chained, head_ref, normed, w_mix, w_gate, w_q, w_k, w_v, conv_w, conv_b, gate_w, *refs):
    if chained:
        rows_before, *refs, halo_out, carry = refs
    else:
        *refs, carry = refs
    mix_out, conv_out, q_out, k_out, v_out, z_out, gate_out = refs
    length = normed.shape[0]

    @pl.when(pl.program_id(0) == 0)
    def _():
        if chained:
            mix_before = mm(rows_before[...], w_mix[...]).astype(bf16)
            halo_out[...] = mix_before
            carry[...] = mix_before[8:16].astype(f32)
        else:
            carry[...] = jnp.zeros_like(carry)

    rows = normed[...]
    mix = mm(rows, w_mix[...]).astype(bf16)
    mix_out[...] = mix
    z_out[...] = mm(rows, w_gate[...])
    mix_f = mix.astype(f32)
    taps = conv_taps(jnp.concatenate([carry[...], mix_f], axis=0), length)
    carry[...] = mix_f[length - 8 :]
    summed = conv_b[...]
    for j in range(4):
        summed = summed + conv_w[j : j + 1, :] * taps[j]
    conv = (summed * jax.nn.sigmoid(summed)).astype(bf16)
    conv_out[...] = conv
    q = mm(conv, w_q[0]).astype(bf16)
    k = mm(conv, w_k[0]).astype(bf16)
    v = mm(mix, w_v[0]).astype(bf16)
    q_out[...] = q
    k_out[...] = k
    v_out[...] = v
    parts = mm_nt(gate_w[0], q) + mm_nt(gate_w[1], k) + mm_nt(gate_w[2], v)
    gate_out[...] = parts[0:8] + parts[8:16] + parts[16:24]


def gate_rows(gates, causal, diagonal):
    in_row = gates[0:1, :]
    pre = gates[1:2, :]
    log_forget = jnp.minimum(pre, 0.0) - jnp.log1p(jnp.exp(-jnp.abs(pre)))
    run_col = jnp.sum(jnp.where(causal, log_forget, 0.0), axis=1, keepdims=True)
    run_row = jnp.sum(jnp.where(diagonal, run_col, 0.0), axis=0, keepdims=True)
    return in_row - run_row, run_col, log_forget


def masks(length):
    row = lax.broadcasted_iota(jnp.int32, (length, length), 0)
    col = lax.broadcasted_iota(jnp.int32, (length, length), 1)
    return row >= col, row == col


def cell_forward_kernel(
    chained, head_ref, gates, q_ref, k_ref, v_ref, conv_ref, z_ref, out_gain, skip_gain, w_down, *refs,
    start=0,
):
    if chained:
        *first, part_out, normed_out, state_out, norm_out, weight_out, col_out, row_out = refs[:10]
        *final, state, norm, level = refs[10:]
    else:
        part_out, normed_out, state_out, norm_out, weight_out, col_out, row_out = refs[:7]
        state, norm, level = refs[7:]
    length = q_ref.shape[0]
    head_size = q_ref.shape[1]
    scale = head_size ** (-0.5)

    @pl.when(pl.program_id(0) == start)
    def _():
        if chained:
            for ref, value in zip((state, norm, level), first):
                ref[...] = value[...]
        else:
            state[...] = jnp.zeros_like(state)
            norm[...] = jnp.zeros_like(norm)
            level[...] = jnp.full_like(level, floor_value)

    causal, diagonal = masks(length)
    a_row, run_col, log_forget = gate_rows(gates[...], causal, diagonal)
    before = level[0:1, 0:1]
    top = jnp.maximum(
        before, jnp.max(jnp.where(causal, a_row, floor_value), axis=1, keepdims=True)
    )
    decay = jnp.exp(jnp.where(causal, a_row - top, floor_value))
    q = q_ref[...]
    k = k_ref[...]
    v = v_ref[...]
    q_f = q.astype(f32)
    weights = decay * (mm_nt(q, k) * scale)
    weights_low = weights.astype(bf16)
    weight_out[...] = weights_low
    from_state = jnp.exp(before - top)
    state_low = state[...].astype(bf16)
    state_out[0] = state_low
    norm_row = norm[0:1, :]
    norm_out[0] = norm[...]
    numerator = mm(weights_low, v) + (from_state * scale) * mm(q, state_low)
    denominator = jnp.sum(weights, axis=1, keepdims=True) + (from_state * scale) * jnp.sum(
        q_f * norm_row, axis=1, keepdims=True
    )
    floor = jnp.exp(-(run_col + top))
    size = jnp.abs(denominator)
    inverse = 1.0 / jnp.maximum(size, floor)
    hidden = numerator * inverse
    centre = hidden - jnp.mean(hidden, axis=1, keepdims=True)
    spread = jnp.mean(centre * centre, axis=1, keepdims=True)
    rstd = lax.rsqrt(spread + norm_epsilon)
    normed = centre * rstd
    normed_out[...] = normed
    gate_z = z_ref[...]
    gated = (normed * out_gain[...] + skip_gain[...] * conv_ref[...].astype(f32)) * (
        gate_z * jax.nn.sigmoid(gate_z)
    )
    part_out[...] = mm(gated.astype(bf16), w_down[...]).astype(bf16)
    factor = jnp.where(
        size > floor,
        jnp.where(denominator > 0, 1.0, -1.0) * inverse * (norm_epsilon * rstd * rstd),
        0.0,
    )
    lane = lax.broadcasted_iota(jnp.int32, (length, 128), 1)
    packed = jnp.where(lane == 0, rstd, inverse)
    packed = jnp.where(lane == 2, from_state, packed)
    packed = jnp.where(lane == 3, top, packed)
    col_out[...] = jnp.where(lane == 4, factor, packed)
    sub = lax.broadcasted_iota(jnp.int32, (8, length), 0)
    row_out[...] = jnp.where(sub == 0, a_row, 1.0 - jnp.exp(log_forget))
    last = top[length - 1 : length, :]
    a_col = jnp.sum(jnp.where(diagonal, a_row, 0.0), axis=1, keepdims=True)
    weighted = k.astype(f32) * jnp.exp(a_col - last)
    keep = jnp.exp(before - last)
    state[...] = keep * state[...] + mm_tn(weighted.astype(bf16), v)
    norm[...] = keep * norm[...] + jnp.sum(weighted, axis=0, keepdims=True)
    level[...] = jnp.broadcast_to(run_col[length - 1 : length, :] + last, level.shape)
    if chained:
        for ref, value in zip(final, (state, norm, level)):
            ref[...] = value[...]


def cell_backward_kernel(
    chained, head_ref, rows_ref, q_ref, k_ref, v_ref, conv_ref, z_ref, normed_ref, state_ref, norm_ref,
    weight_ref, col_ref, cot_ref, rows_in, out_gain, skip_gain, w_down, *refs
):
    if chained:
        first, refs = refs[:2], refs[2:]
    dq_out, dk_out, dv_out, dskip_out, dz_out, gate_out, g_down_out, g_z_out, g_gain_out, *refs = refs
    *final, d_state, d_norm, g_down, g_z, g_gain = refs
    length = q_ref.shape[0]
    head_size = q_ref.shape[1]
    scale = head_size ** (-0.5)

    @pl.when(pl.program_id(0) == 0)
    def _():
        if chained:
            d_state[...] = first[0][...]
            d_norm[...] = first[1][...]
        else:
            d_state[...] = jnp.zeros_like(d_state)
            d_norm[...] = jnp.zeros_like(d_norm)
        g_down[...] = jnp.zeros_like(g_down)
        g_z[...] = jnp.zeros_like(g_z)
        g_gain[...] = jnp.zeros_like(g_gain)

    causal, diagonal = masks(length)
    rstd = col_ref[:, 0:1]
    inverse = col_ref[:, 1:2]
    from_state = col_ref[:, 2:3]
    top = col_ref[:, 3:4]
    factor = col_ref[:, 4:5]
    a_row = rows_ref[0:1, :]
    q = q_ref[...]
    k = k_ref[...]
    v = v_ref[...]
    q_f = q.astype(f32)
    k_f = k.astype(f32)
    conv = conv_ref[...].astype(f32)
    normed = normed_ref[...]
    gate_z = z_ref[...]
    cot = cot_ref[...]
    opened = jax.nn.sigmoid(gate_z)
    silu = gate_z * opened
    head_in = normed * out_gain[...] + skip_gain[...] * conv
    g_down[...] += mm_tn((head_in * silu).astype(bf16), cot)
    d_gated = mm_nt(cot, w_down[...])
    d_z = (d_gated * head_in * (opened * (1.0 + gate_z * (1.0 - opened)))).astype(bf16)
    dz_out[...] = d_z
    g_z[...] += mm_tn(rows_in[...], d_z)
    d_head = d_gated * silu
    g_gain[0:1, :] += jnp.sum(d_head * normed, axis=0, keepdims=True)
    g_gain[1:2, :] += jnp.sum(d_head * conv, axis=0, keepdims=True)
    dskip_out[...] = skip_gain[...] * d_head
    d_hat = d_head * out_gain[...]
    along = jnp.sum(d_hat * normed, axis=1, keepdims=True)
    d_hidden = rstd * (
        d_hat - jnp.mean(d_hat, axis=1, keepdims=True) - normed * (along / head_size)
    )
    d_num = d_hidden * inverse
    d_den = -along * factor
    d_num_low = d_num.astype(bf16)
    decay = jnp.exp(jnp.where(causal, a_row - top, floor_value))
    d_scores = ((mm_nt(d_num_low, v) + d_den) * (decay * scale)).astype(bf16)
    through = from_state * scale
    dq_near = mm(d_scores, k)
    dq_far = (
        mm_nt((d_num * through).astype(bf16), state_ref[0])
        + (through * d_den) * norm_ref[0, 0:1, :]
    )
    last = top[length - 1 : length, :]
    keep = from_state[length - 1 : length, :]
    a_col = jnp.sum(jnp.where(diagonal, a_row, 0.0), axis=1, keepdims=True)
    key_weight = jnp.exp(a_col - last)
    d_state_low = d_state[...].astype(bf16)
    dk_near = mm_tn(d_scores, q)
    dk_far = key_weight * (mm_nt(v, d_state_low) + d_norm[0:1, :])
    dv = mm_tn(weight_ref[...], d_num_low) + mm((k_f * key_weight).astype(bf16), d_state_low)
    dq_out[...] = dq_near + dq_far
    dk_out[...] = dk_near + dk_far
    dv_out[...] = dv
    held = state_ref[0].astype(f32) * d_state[...]
    held = jnp.sum(jnp.sum(held, axis=0, keepdims=True) + norm_ref[0, 0:1, :] * d_norm[0:1, :])
    q_state = q_f * through
    d_state[...] = keep * d_state[...] + mm_tn(q_state.astype(bf16), d_num_low)
    d_norm[...] = keep * d_norm[...] + jnp.sum(q_state * d_den, axis=0, keepdims=True)
    q_dot = jnp.sum(q_f * (dq_near + dq_far), axis=1, keepdims=True)
    k_near = jnp.sum(k_f * dk_near, axis=1, keepdims=True)
    k_far = jnp.sum(k_f * dk_far, axis=1, keepdims=True)
    d_in = jnp.sum(jnp.where(diagonal, k_near + k_far, 0.0), axis=0, keepdims=True)
    d_log = jnp.sum(
        jnp.where(causal, q_dot - k_near, jnp.where(diagonal, 0.0, k_far)), axis=0, keepdims=True
    )
    d_log = d_log + keep * held
    sub = lax.broadcasted_iota(jnp.int32, (8, length), 0)
    d_pre = d_log * rows_ref[1:2, :]
    gate_out[...] = jnp.where(sub == 0, d_in, d_pre)
    g_gain[2:3, :] += jnp.broadcast_to(jnp.sum(d_pre, axis=1, keepdims=True), (1, head_size))

    @pl.when(pl.program_id(0) == pl.num_programs(0) - 1)
    def _():
        if chained:
            final[0][...] = d_state[...]
            final[1][...] = d_norm[...]
        half = g_down.shape[1] // 2
        g_down_out[0] = g_down[:, :half].astype(bf16)
        g_down_out[1] = g_down[:, half:].astype(bf16)
        g_z_out[...] = g_z[...].astype(bf16)
        g_gain_out[...] = g_gain[...]


def lower_first(d_gate, dq_ref, dk_ref, dv_ref, mix_ref, conv_ref, q_ref, k_ref, v_ref, gate_w,
                g_q, g_k, g_v, g_small):
    high, middle, low = split_three(d_gate[...])
    left = jnp.concatenate([high, middle, low, high, middle, high], axis=0)
    d_joined = mm_tn(left, gate_w[...])
    size = q_ref.shape[1]
    query_low = (dq_ref[...] + d_joined[:, :size]).astype(bf16)
    key_low = (dk_ref[...] + d_joined[:, size : 2 * size]).astype(bf16)
    value_low = (dv_ref[...] + d_joined[:, 2 * size :]).astype(bf16)
    conv = conv_ref[...]
    g_q[...] += mm_tn(conv, query_low)
    g_k[...] += mm_tn(conv, key_low)
    g_v[...] += mm_tn(mix_ref[...], value_low)
    three = jnp.concatenate([high, middle, low], axis=0)
    for at, ref in enumerate((q_ref, k_ref, v_ref)):
        got = mm(three, ref[...])
        g_small[8 * at : 8 * at + 8, :] += got[0:8] + got[8:16] + got[16:24]
    return query_low, key_low, value_low


def lower_second(
    edge, last, lows, dskip_ref, dz_ref, mix_ref, mix_before, normed, w_q, w_k, w_v, w_mix, w_gate,
    conv_w, conv_b, g_gain, g_small, later,
):
    query_low, key_low, value_low = lows
    length, size = mix_ref.shape
    mix = mix_ref[...]
    d_conv = dskip_ref[...] + mm_nt(query_low, w_q[...]) + mm_nt(key_low, w_k[...])
    halo = jnp.where(last, edge, mix_before[8:16, :].astype(f32))
    taps = conv_taps(jnp.concatenate([halo, mix.astype(f32)], axis=0), length)
    summed = conv_b[...]
    for j in range(4):
        summed = summed + conv_w[j : j + 1, :] * taps[j]
    opened = jax.nn.sigmoid(summed)
    d_summed = d_conv * (opened * (1.0 + summed * (1.0 - opened)))
    for j in range(4):
        g_small[24 + j : 25 + j, :] += jnp.sum(d_summed * taps[j], axis=0, keepdims=True)
    g_small[28:29, :] += jnp.sum(d_summed, axis=0, keepdims=True)
    ext = jnp.concatenate([d_summed, later[...]], axis=0)
    later[...] = d_summed[0:8]
    d_mix = conv_w[3:4, :] * d_summed
    for j in range(3):
        d_mix = d_mix + conv_w[j : j + 1, :] * pltpu.roll(ext, length + 8 - (3 - j), 0)[0:length]
    d_mix = (d_mix + mm_nt(value_low, w_v[...])).astype(bf16)
    d_z = dz_ref[...]
    rows = normed[...]
    d_normed = mm_nt(d_mix, w_mix[...]) + mm_nt(d_z, w_gate[...])
    g_ln = jnp.sum(d_normed * rows.astype(f32), axis=0, keepdims=True)
    g_small[32:33, :] += g_ln[:, :size]
    g_small[33:34, :] += g_ln[:, size:]

    @pl.when(last)
    def _():
        g_small[29:32, :] = g_gain[0:3, :]

    return rows, d_mix, d_z, d_normed


def lower_block(
    at_start, at_end, lows, dskip_ref, dskip_next, dz_ref, mix_ref, mix_before, mix_next, normed,
    w_q, w_k, w_v, w_mix, w_gate, conv_w, conv_b, g_small,
):
    query_low, key_low, value_low = lows
    length, size = mix_ref.shape
    extra = mix_next.shape[0]
    halo = jnp.where(at_start, 0.0, mix_before[8:16, :].astype(f32))
    ext = jnp.concatenate(
        [halo, mix_ref[...].astype(f32), mix_next[...].astype(f32)], axis=0
    )
    taps = conv_taps(ext, length + extra)
    summed = conv_b[...]
    for j in range(4):
        summed = summed + conv_w[j : j + 1, :] * taps[j]
    opened = jax.nn.sigmoid(summed)
    d_conv = jnp.concatenate([dskip_ref[...], dskip_next[...]], axis=0)
    d_conv = d_conv + mm_nt(query_low, w_q[...]) + mm_nt(key_low, w_k[...])
    d_summed = d_conv * (opened * (1.0 + summed * (1.0 - opened)))
    for j in range(4):
        g_small[24 + j : 25 + j, :] += jnp.sum(
            d_summed[:length] * taps[j][:length], axis=0, keepdims=True
        )
    g_small[28:29, :] += jnp.sum(d_summed[:length], axis=0, keepdims=True)
    row = lax.broadcasted_iota(jnp.int32, d_summed.shape, 0)
    d_summed = jnp.where(jnp.logical_and(at_end, row >= length), 0.0, d_summed)
    d_mix = conv_w[3:4, :] * d_summed[:length]
    for j in range(3):
        ahead = pltpu.roll(d_summed, length + extra - (3 - j), 0)[0:length]
        d_mix = d_mix + conv_w[j : j + 1, :] * ahead
    d_mix = (d_mix + mm_nt(value_low, w_v[...])).astype(bf16)
    rows = normed[...]
    d_normed = mm_nt(d_mix, w_mix[...]) + mm_nt(dz_ref[...], w_gate[...])
    g_ln = jnp.sum(d_normed * rows.astype(f32), axis=0, keepdims=True)
    g_small[32:33, :] += g_ln[:, :size]
    g_small[33:34, :] += g_ln[:, size:]
    return rows, d_mix, d_normed


def lower_kernel(chained, head_ref, *refs):
    ins, refs = refs[:22], list(refs[22:])
    edge = 0.0
    if chained:
        first_halo, first_later, *refs = refs
        edge = first_halo[8:16, :].astype(f32)
        later_out = refs.pop(4)
    part_out, square_out, up_out, small_out = refs[:4]
    g_q, g_k, g_v, g_m, g_z, g_small, later = refs[4:]
    step = pl.program_id(0)
    size = g_q.shape[0]

    @pl.when(step == 0)
    def _():
        for ref in (g_q, g_k, g_v, g_m, g_z, g_small, later):
            ref[...] = jnp.zeros_like(ref)
        if chained:
            later[...] = first_later[...]

    (d_gate, dq, dk, dv, dskip, dz, mix, mix_before, conv, q, k, v, normed,
     w_q, w_k, w_v, w_mix, w_gate, conv_w, conv_b, gate_w, g_gain) = ins
    lows = lower_first(d_gate, dq, dk, dv, mix, conv, q, k, v, gate_w, g_q, g_k, g_v, g_small)
    rows, d_mix, d_z, d_normed = lower_second(
        edge, step == pl.num_programs(0) - 1, lows, dskip, dz, mix, mix_before, normed,
        w_q.at[0], w_k.at[0], w_v.at[0], w_mix, w_gate, conv_w, conv_b, g_gain, g_small, later,
    )
    g_m[...] += mm_tn(rows, d_mix)
    g_z[...] += mm_tn(rows, d_z)
    part_out[...] = d_normed.astype(bf16)

    @pl.when(step == pl.num_programs(0) - 1)
    def _():
        half = size // 2
        for at, ref in enumerate((g_q, g_k, g_v)):
            square_out[0, :, half * at : half * at + half] = ref[:, :half].astype(bf16)
            square_out[1, :, half * at : half * at + half] = ref[:, half:].astype(bf16)
        up_out[0] = g_m[...].astype(bf16)
        up_out[1] = g_z[...].astype(bf16)
        small_out[...] = g_small[...]
        if chained:
            later_out[...] = later[...]


def struct(shape, dtype):
    return jax.ShapeDtypeStruct(shape, dtype)


def run_kernel(body, head, grid, inputs, in_specs, outs, out_specs, scratch, name, flops, nbytes):
    return pl.pallas_call(
        body,
        grid_spec=pltpu.PrefetchScalarGridSpec(
            num_scalar_prefetch=1,
            grid=(grid,),
            in_specs=in_specs,
            out_specs=out_specs,
            scratch_shapes=scratch,
        ),
        out_shape=outs,
        compiler_params=pltpu.CompilerParams(
            dimension_semantics=("arbitrary",), vmem_limit_bytes=vmem_bytes
        ),
        cost_estimate=pl.CostEstimate(flops=flops, bytes_accessed=nbytes, transcendentals=0),
        name=name,
    )(head, *inputs)


def fixed(shape, *index):
    return pl.BlockSpec(shape, lambda g, h: tuple(h[0] if i == "h" else i for i in index))


def lift(head, normed, w_up, w_query, w_key, w_value, conv_w, conv_b, gate_parts, *first):
    tokens, width = normed.shape
    heads, size, _ = w_query.shape
    length = wide_len
    by_row = lambda cols: pl.BlockSpec((length, cols), lambda g, h: (g, 0))
    weight = pl.BlockSpec((1, size, size), lambda g, h: (h[0], 0, 0))
    chained = len(first) > 0
    halo = [pl.BlockSpec((16, size), lambda g, h: (0, 0))] * chained
    return run_kernel(
        partial(lift_kernel, chained), head, tokens // length,
        (normed, w_up, w_up, w_query, w_key, w_value, conv_w, conv_b, gate_parts, *first),
        [
            by_row(width),
            pl.BlockSpec((width, size), lambda g, h: (0, h[0])),
            pl.BlockSpec((width, size), lambda g, h: (0, heads + h[0])),
            weight, weight, weight,
            pl.BlockSpec((4, size), lambda g, h: (0, h[0])),
            pl.BlockSpec((1, size), lambda g, h: (0, h[0])),
            pl.BlockSpec(gate_parts.shape, lambda g, h: (0, 0, 0)),
        ]
        + [pl.BlockSpec((16, width), lambda g, h: (0, 0))] * chained,
        [struct((tokens, size), bf16)] * 5
        + [struct((tokens, size), f32), struct((8, tokens), f32)]
        + [struct((16, size), bf16)] * chained,
        [by_row(size)] * 6 + [pl.BlockSpec((8, length), lambda g, h: (0, g))] + halo,
        [pltpu.VMEM((8, size), f32)],
        "lift", 2 * tokens * size * (2 * width + 3 * size), 24 * 2**20,
    )


def cell_forward(head, gates, q, k, v, conv, gate_z, out_gain, skip_gain, w_down, *first):
    tokens, size = q.shape
    width = w_down.shape[1]
    length = chunk_len
    steps = tokens // length
    by_row = lambda cols: pl.BlockSpec((length, cols), lambda g, h: (g, 0))
    gain = pl.BlockSpec((1, size), lambda g, h: (0, h[0]))
    carried = [struct(value.shape, f32) for value in first]
    carried_specs = [pl.BlockSpec(value.shape, lambda g, h: (0, 0)) for value in first]
    return run_kernel(
        partial(cell_forward_kernel, len(first) > 0), head, steps,
        (gates, q, k, v, conv, gate_z, out_gain, skip_gain, w_down, *first),
        [pl.BlockSpec((2, length), lambda g, h: (0, g))]
        + [by_row(size)] * 5
        + [gain, gain, pl.BlockSpec((size, width), lambda g, h: (h[0], 0))]
        + carried_specs,
        [
            struct((tokens, width), bf16),
            struct((tokens, size), f32),
            struct((steps, size, size), bf16),
            struct((steps, 8, size), f32),
            struct((tokens, length), bf16),
            struct((tokens, 128), f32),
            struct((8, tokens), f32),
        ]
        + carried,
        [
            by_row(width),
            by_row(size),
            pl.BlockSpec((1, size, size), lambda g, h: (g, 0, 0)),
            pl.BlockSpec((1, 8, size), lambda g, h: (g, 0, 0)),
            by_row(length),
            by_row(128),
            pl.BlockSpec((8, length), lambda g, h: (0, g)),
        ]
        + carried_specs,
        [pltpu.VMEM((size, size), f32), pltpu.VMEM((8, size), f32), pltpu.VMEM((8, 128), f32)],
        "cell_forward", 2 * tokens * size * (2 * length + 2 * size + width), 28 * 2**20,
    )


def cell_backward(
    head, rows, q, k, v, conv, gate_z, normed, states, norms, weights, cols, cot, rows_in,
    out_gain, skip_gain, w_down, *first,
):
    tokens, size = q.shape
    width = w_down.shape[1]
    length = chunk_len
    steps = tokens // length
    end = steps - 1
    by_row = lambda n: pl.BlockSpec((length, n), lambda g, h: (end - g, 0))
    gain = pl.BlockSpec((1, size), lambda g, h: (0, h[0]))
    whole = lambda shape: pl.BlockSpec(shape, lambda g, h: (0, 0))
    carried = [struct(value.shape, f32) for value in first]
    carried_specs = [whole(value.shape) for value in first]
    return run_kernel(
        partial(cell_backward_kernel, len(first) > 0), head, steps,
        (rows, q, k, v, conv, gate_z, normed, states, norms, weights, cols, cot, rows_in,
         out_gain, skip_gain, w_down, *first),
        [pl.BlockSpec((8, length), lambda g, h: (0, end - g))]
        + [by_row(size)] * 6
        + [
            pl.BlockSpec((1, size, size), lambda g, h: (end - g, 0, 0)),
            pl.BlockSpec((1, 8, size), lambda g, h: (end - g, 0, 0)),
            by_row(length),
            by_row(128),
            by_row(width),
            by_row(width),
            gain, gain,
            pl.BlockSpec((size, width), lambda g, h: (h[0], 0)),
        ]
        + carried_specs,
        [struct((tokens, size), f32)] * 4
        + [
            struct((tokens, size), bf16),
            struct((8, tokens), f32),
            struct((2, size, width // 2), bf16),
            struct((width, size), bf16),
            struct((8, size), f32),
        ]
        + carried,
        [by_row(size)] * 5
        + [
            pl.BlockSpec((8, length), lambda g, h: (0, end - g)),
            pl.BlockSpec((2, size, width // 2), lambda g, h: (0, 0, 0)),
            whole((width, size)),
            whole((8, size)),
        ]
        + carried_specs,
        [
            pltpu.VMEM((size, size), f32),
            pltpu.VMEM((8, size), f32),
            pltpu.VMEM((size, width), f32),
            pltpu.VMEM((width, size), f32),
            pltpu.VMEM((8, size), f32),
        ],
        "cell_backward", 2 * tokens * size * (4 * length + 4 * size + 2 * width), 44 * 2**20,
    )


def lower_inputs(
    length, d_gate, dq, dk, dv, dskip, dz, mix, conv, q, k, v, normed,
    w_query, w_key, w_value, w_up, conv_w, conv_b, gate_pairs, g_gain,
):
    tokens, size = q.shape
    width = normed.shape[1]
    heads = w_query.shape[0]
    end = tokens // length - 1
    by_row = lambda n: pl.BlockSpec((length, n), lambda g, h: (end - g, 0))
    kept = lambda shape, index: pl.BlockSpec(shape, index, pipeline_mode=pl.Buffered(1))
    weight = kept((1, size, size), lambda g, h: (h[0], 0, 0))
    inputs = (
        d_gate, dq, dk, dv, dskip, dz, mix, mix, conv, q, k, v, normed,
        w_query, w_key, w_value, w_up, w_up, conv_w, conv_b, gate_pairs, g_gain,
    )
    specs = [pl.BlockSpec((8, length), lambda g, h: (0, end - g))]
    specs += [by_row(size)] * 6
    specs += [
        pl.BlockSpec(
            (16, size), lambda g, h: (jnp.maximum((end - g) * (length // 16) - 1, 0), 0)
        )
    ]
    specs += [by_row(size)] * 4
    specs += [by_row(width), weight, weight, weight]
    specs += [
        kept((width, size), lambda g, h: (0, h[0])),
        kept((width, size), lambda g, h: (0, heads + h[0])),
        kept((4, size), lambda g, h: (0, h[0])),
        kept((1, size), lambda g, h: (0, h[0])),
        kept(gate_pairs.shape, lambda g, h: (0, 0)),
        kept(g_gain.shape, lambda g, h: (0, 0)),
    ]
    return inputs, specs


def lower(head, *inputs):
    inputs, first = inputs[:20], inputs[20:]
    tokens, size = inputs[1].shape
    width = inputs[11].shape[1]
    length = wide_len
    end = tokens // length - 1
    by_row = lambda n: pl.BlockSpec((length, n), lambda g, h: (end - g, 0))
    whole = lambda shape: pl.BlockSpec(shape, lambda g, h: (0, 0))
    chained = len(first) > 0
    inputs, specs = lower_inputs(length, *inputs)
    return run_kernel(
        partial(lower_kernel, chained), head, tokens // length,
        (*inputs, *first),
        specs + [whole(value.shape) for value in first],
        [struct((tokens, width), bf16)]
        + [struct((2, size, 3 * size // 2), bf16), struct((2, width, size), bf16)]
        + [struct((40, size), f32)]
        + [struct((8, size), f32)] * chained,
        [by_row(width)]
        + [
            pl.BlockSpec((2, size, 3 * size // 2), lambda g, h: (0, 0, 0)),
            pl.BlockSpec((2, width, size), lambda g, h: (0, 0, 0)),
        ]
        + [whole((40, size))]
        + [whole((8, size))] * chained,
        [pltpu.VMEM((size, size), f32)] * 3
        + [pltpu.VMEM((width, size), f32)] * 2
        + [pltpu.VMEM((40, size), f32), pltpu.VMEM((8, size), f32)],
        "lower", 2 * tokens * size * (6 * size + 4 * width), 48 * 2**20,
    )
MESH_ID = pl.DeviceIdType.MESH


def halves_of(value, count):
    whole = jnp.int32(0)
    for bound in range(2, count, 2):
        whole = whole + jnp.where(value >= bound, 1, 0)
    return whole, value - 2 * whole


def where_am_i():
    at_seq, at_batch = lax.axis_index("seq"), lax.axis_index("batch")
    first = jnp.int32(0)
    for bound in range(8, lax.axis_size("seq"), 8):
        first = first + jnp.where(at_seq >= bound, 8, 0)
    z, y = halves_of(at_seq - first, 8)
    x, c = halves_of(at_batch, lax.axis_size("batch"))
    return first, z, y, x, c


def turn(value, count):
    return jnp.where(value >= count, value - count, value)


def greet(others):
    barrier = pltpu.get_barrier_semaphore()
    for other in others:
        pl.semaphore_signal(barrier, 1, device_id=other, device_id_type=MESH_ID)
    pl.semaphore_wait(barrier, len(others))


def remote(src, dst, sent, landed, device):
    return pltpu.make_async_remote_copy(src, dst, sent, landed, device_id=device, device_id_type=MESH_ID)


def normalize(rows):
    centre = rows - jnp.mean(rows, axis=-1, keepdims=True)
    rstd = lax.rsqrt(jnp.mean(centre * centre, axis=-1, keepdims=True) + norm_epsilon)
    return centre * rstd, rstd


class Gather:
    def __init__(self, source, out_ref, block, parts, sems):
        self.source, self.out_ref, self.block, self.parts = source, out_ref, block, parts
        self.kept, self.z_sent, self.z_landed, self.y_sent, self.y_landed, *sems = sems
        self.c_sent, self.c_landed = sems
        self.first, self.z, self.y, self.x, self.c = where_am_i()
        self.size = block // parts
        self.enters = halves_of(self.z, 4)[0] == self.c

    def device(self, zz, yy, cc):
        return (self.first + 2 * zz + yy, 2 * self.x + cc)

    def others(self):
        others = [self.device(turn(self.z + k, 4), self.y, self.c) for k in range(1, 4)]
        return others + [self.device(self.z, 1 - self.y, self.c), self.device(self.z, self.y, 1 - self.c)]

    def rows(self, zz, yy, part):
        start = (2 * zz + yy) * self.block + part * self.size
        return self.out_ref.at[pl.ds(pl.multiple_of(start, self.size), self.size)]

    def away(self, m):
        return 2 * self.c + m != self.z

    def to_column(self, m, part):
        return remote(
            self.source(m, part), self.rows(self.z, self.y, part), self.z_sent.at[m, part],
            self.z_landed.at[self.z, part], self.device(2 * self.c + m, self.y, self.c),
        )

    def keep(self, m, part):
        return pltpu.make_async_copy(
            self.source(m, part), self.rows(self.z, self.y, part), self.kept.at[part]
        )

    def from_column(self, zz, part):
        here = self.rows(zz, self.y, part)
        return remote(
            here, here, self.z_sent.at[0, part], self.z_landed.at[zz, part],
            self.device(zz, self.y, self.c),
        )

    def to_row(self, zz, k, part):
        here = self.rows(zz, self.y, part)
        return remote(
            here, here, self.y_sent.at[k, part], self.y_landed.at[zz, part],
            self.device(self.z, 1 - self.y, self.c),
        )

    def from_row(self, zz, k, part):
        here = self.rows(zz, 1 - self.y, part)
        return remote(
            here, here, self.y_sent.at[k, part], self.y_landed.at[zz, part],
            self.device(self.z, 1 - self.y, self.c),
        )

    def to_core(self, zz, yy, k, part):
        here = self.rows(zz, yy, part)
        return remote(
            here, here, self.c_sent.at[k, part], self.c_landed.at[2 * zz + yy, part],
            self.device(self.z, self.y, 1 - self.c),
        )

    def start(self, part):
        for m in range(2):
            pl.when(self.away(m))(lambda: self.to_column(m, part).start())
            pl.when(jnp.logical_not(self.away(m)))(lambda: self.keep(m, part).start())

    def at(self, k):
        high, low = halves_of(self.z, 4)
        far = 2 * high if k < 2 else 2 - 2 * high
        return far + (low if k % 2 == 0 else 1 - low)

    def pass_column(self, k, part):
        @pl.when(self.enters)
        def _():
            if k == 0:
                self.keep(0, part).wait()
            else:
                self.from_column(self.at(k), part).wait_recv()
            self.to_row(self.at(k), k, part).start()
            self.to_core(self.at(k), self.y, k, part).start()

    def pass_row(self, k, part):
        @pl.when(self.enters)
        def _():
            self.from_row(self.at(k), k, part).wait_recv()
            self.to_core(self.at(k), 1 - self.y, 4 + k, part).start()

    def finish(self, wait_core):
        @pl.when(self.enters)
        def _():
            for k in range(4):
                for part in range(self.parts):
                    self.to_row(self.at(k), k, part).wait_send()
                    self.to_core(self.at(k), self.y, k, part).wait_send()
                    self.to_core(self.at(k), 1 - self.y, 4 + k, part).wait_send()

        if wait_core:

            @pl.when(jnp.logical_not(self.enters))
            def _():
                for zz in range(4):
                    for yy in range(2):
                        for part in range(self.parts):
                            self.to_core(zz, yy, 0, part).wait_recv()

        for m in range(2):
            for part in range(self.parts):
                pl.when(self.away(m))(lambda: self.to_column(m, part).wait_send())


def gather_sems(parts):
    shapes = [(parts,), (2, parts), (4, parts), (4, parts), (4, parts), (8, parts), (8, parts)]
    return [pltpu.SemaphoreType.DMA(shape) for shape in shapes]


def gather_kernel(rows_ref, gain_ref, out_ref, staged, *sems):
    parts = sems[0].shape[0]
    block = rows_ref.shape[1]
    size = block // parts
    gather = Gather(
        lambda m, part: staged.at[m, pl.ds(part * size, size)], out_ref, block, parts, sems
    )
    greet(gather.others())
    for part in range(parts):
        here = pl.ds(part * size, size)
        for m in range(2):
            staged[m, here] = (
                normalize(rows_ref[m, here].astype(f32))[0] * gain_ref[...]
            ).astype(bf16)
        gather.start(part)
    for part in range(parts):
        for k in range(4):
            gather.pass_column(k, part)
        if part > 0:
            for k in range(4):
                gather.pass_row(k, part - 1)
    for k in range(4):
        gather.pass_row(k, parts - 1)
    gather.finish(True)


def gather_normed(rows, gain):
    micro, block, width = rows.shape
    return pl.pallas_call(
        gather_kernel,
        out_shape=struct((8 * block, width), bf16),
        in_specs=[pl.BlockSpec(memory_space=pltpu.VMEM)] * 2,
        out_specs=pl.BlockSpec(memory_space=pl.ANY),
        scratch_shapes=[pltpu.VMEM((micro, block, width), bf16)] + gather_sems(4),
        compiler_params=pltpu.CompilerParams(
            collective_id=0, has_side_effects=True, vmem_limit_bytes=32 * 2**20
        ),
        name="gather_normed",
    )(rows, gain)


def lift_rest(rows, before, w_q, w_k, w_v, conv_w, conv_b, gate_parts):
    length = rows.shape[0]
    taps = conv_taps(jnp.concatenate([before, rows.astype(f32)], axis=0), length)
    summed = conv_b[...]
    for j in range(4):
        summed = summed + conv_w[j : j + 1, :] * taps[j]
    conv = (summed * jax.nn.sigmoid(summed)).astype(bf16)
    q = mm(conv, w_q[0]).astype(bf16)
    k = mm(conv, w_k[0]).astype(bf16)
    v = mm(rows, w_v[0]).astype(bf16)
    parts = mm_nt(gate_parts[0], q) + mm_nt(gate_parts[1], k) + mm_nt(gate_parts[2], v)
    return conv, q, k, v, parts[0:8] + parts[8:16] + parts[16:24]


def rise_kernel(
    tokens, ln_gain, w_mix, w_gate, w_q, w_k, w_v, conv_w, conv_b, gate_own, gate_b, out_gain,
    skip_gain, w_down, cot_ref, *refs
):
    kept_outs, cell_outs, (cot_out, *refs) = refs[:7], refs[7:14], refs[14:]
    rows_all, mix_all, conv_all, q_all, k_all, v_all, z_all, *refs = refs
    staged, gate_mine, gate_all, gates, gate_parts, *refs = refs
    state, h_sent, h_landed, out_sem, *sems = refs[:3], *refs[3:]
    parts = sems[0].shape[0]
    step = pl.program_id(0)
    blocks = pl.num_programs(0) // 2
    micro, block, width = cot_ref.shape
    size = block // parts
    normed = Gather(
        lambda m, part: staged.at[m, pl.ds(part * size, size)], rows_all, block, parts, sems[:7]
    )
    gather = Gather(
        lambda m, part: cot_ref.at[m, pl.ds(part * size, size)], cot_out, block, parts, sems[7:]
    )
    z, y, c = gather.z, gather.y, gather.c
    head = 2 * c + y
    heads = gate_all.shape[0]
    group = [(1 - y, c), (y, 1 - c), (1 - y, 1 - c)]
    span = gate_mine.shape[1] // 2

    def gate_to(k, part):
        lanes = pl.ds(part * span, span)
        return remote(
            gate_mine.at[:, lanes], gate_all.at[head, :, lanes], h_sent.at[k, part],
            h_landed.at[head, part], gather.device(z, *group[k]),
        )

    def gate_from(k, part):
        lanes = pl.ds(part * span, span)
        at = 2 * group[k][1] + group[k][0]
        return remote(
            gate_mine.at[:, lanes], gate_all.at[at, :, lanes], h_sent.at[k, part],
            h_landed.at[at, part], gather.device(z, *group[k]),
        )

    def keep_out(k):
        made = (rows_all, mix_all, conv_all, q_all, k_all, v_all, z_all)[k]
        return pltpu.make_async_copy(made, kept_outs[k], out_sem.at[k])

    def lift_up(yy, part):
        here = [
            pl.ds(pl.multiple_of((2 * zz + yy) * block + part * size, size), size)
            for zz in range(4)
        ]
        rows = jnp.concatenate([rows_all[at] for at in here], axis=0)
        mix = mm(rows, w_mix[...]).astype(bf16)
        gate_z = mm(rows, w_gate[...])
        for k, at in enumerate(here):
            mix_all[at] = mix[size * k : size * k + size]
            z_all[at] = gate_z[size * k : size * k + size]

    def arrived(yy, part):
        @pl.when(jnp.logical_not(normed.enters))
        def _():
            for zz in range(4):
                normed.to_core(zz, yy, 0, part).wait_recv()

    @pl.when(step == 0)
    def _():
        greet(normed.others() + [gather.device(z, 1 - y, 1 - c)])
        for p in range(3):
            gate_parts[p, 0:24] = jnp.concatenate(split_three(gate_own[8 * p : 8 * p + 8, :]), axis=0)
            gate_parts[p, 24:32] = jnp.zeros_like(gate_parts[p, 24:32])
        for part in range(parts):
            here = pl.ds(part * size, size)
            for m in range(2):
                staged[m, here] = (
                    normalize(tokens[m, here].astype(f32))[0] * ln_gain[...]
                ).astype(bf16)
            normed.start(part)
        for part in range(parts):
            for k in range(4):
                normed.pass_column(k, part)
            if part == parts - 1:
                for later in range(parts):
                    gather.start(later)
            arrived(y, part)
            lift_up(y, part)
            if part > 0:
                for k in range(4):
                    normed.pass_row(k, part - 1)
                arrived(1 - y, part - 1)
                lift_up(1 - y, part - 1)
        for k in range(4):
            normed.pass_row(k, parts - 1)
        arrived(1 - y, parts - 1)
        lift_up(1 - y, parts - 1)
        for k in (0, 1, 6):
            keep_out(k).start()

    @pl.when(step < blocks)
    def _():
        here = pl.ds(pl.multiple_of(step * block, block), block)
        edge = pl.ds(pl.multiple_of(jnp.maximum(step * block - 16, 0), 16), 16)
        before = jnp.where(step == 0, 0.0, mix_all[edge][8:16].astype(f32))
        conv, q, k, v, gate = lift_rest(
            mix_all[here], before, w_q, w_k, w_v, conv_w, conv_b, gate_parts
        )
        for ref, made in zip((conv_all, q_all, k_all, v_all), (conv, q, k, v)):
            ref[here] = made
        gate_mine[:, here] = gate
        gate_all[head, :, here] = gate

    @pl.when(step == blocks - 1)
    def _():
        for k in (2, 3, 4, 5):
            keep_out(k).start()

    for part in range(2):

        @pl.when(step == (blocks // 2) * (part + 1) - 1)
        def _():
            for k in range(3):
                gate_to(k, part).start()

        @pl.when(step == blocks + (blocks // 2) * part)
        def _():
            for k in range(3):
                gate_from(k, part).wait_recv()

    @pl.when(step >= blocks)
    def _():
        here = pl.ds(pl.multiple_of((step - blocks) * block, block), block)
        for row, at in enumerate((head, heads + head)):
            total = gate_all[0, pl.ds(at, 1), here]
            for h in range(1, heads):
                total = total + gate_all[h, pl.ds(at, 1), here]
            if row == 1:
                total = total + gate_b[head]
            gates[row : row + 1, :] = total
        cell_forward_kernel(
            False, None, gates, q_all.at[here], k_all.at[here], v_all.at[here], conv_all.at[here],
            z_all.at[here], out_gain, skip_gain, w_down, *cell_outs, *state, start=blocks,
        )

    def columns(part, ks=(1, 2, 3)):
        return [partial(gather.pass_column, k, part) for k in ks]

    def rows(part, ks=(0, 1, 2, 3)):
        return [partial(gather.pass_row, k, part) for k in ks]

    plan = {
        0: [do for part in range(parts) for do in columns(part, (0,))],
        2: columns(0),
        5: columns(1) + [do for part in range(parts) for do in rows(part, (0,))],
        7: columns(2) + rows(0, (1, 2, 3)),
        9: columns(3) + rows(1, (1, 2, 3)),
        11: rows(2, (1, 2, 3)),
        13: rows(3, (1, 2, 3)),
    }
    for when, work in plan.items():

        @pl.when(step == when)
        def _():
            for do in work:
                do()

    @pl.when(step == 2 * blocks - 1)
    def _():
        for k in range(7):
            keep_out(k).wait()
        normed.finish(False)
        gather.finish(True)
        for k in range(3):
            for part in range(2):
                gate_to(k, part).wait_send()


def rise(
    tokens, ln_gain, w_up, w_query, w_key, w_value, conv_w, conv_b, gate_own, gate_b, out_gain,
    skip_gain, w_down, cot,
):
    heads, size, _ = w_query.shape
    micro, block, width = cot.shape
    steps = 8
    count = steps * block
    late = lambda g: jnp.maximum(g - steps, 0)
    by_row = lambda n, at: pl.BlockSpec((block, n), lambda g: (at(g), 0))
    kept = lambda shape, index: pl.BlockSpec(shape, index, pipeline_mode=pl.Buffered(1))
    weight = kept((1, size, size), lambda g: (own_head(), 0, 0))
    lanes = lambda rows: kept((rows, size), lambda g: (0, own_head()))
    anywhere = pl.BlockSpec(memory_space=pl.ANY)
    own = kept(cot.shape, lambda g: (0, 0, 0))
    specs = [
        own, kept(ln_gain.shape, lambda g: (0, 0)), lanes(width),
        kept((width, size), lambda g: (0, heads + own_head())),
        weight, weight, weight, lanes(4), lanes(1), kept(gate_own.shape, lambda g: (0, 0)),
        pl.BlockSpec(memory_space=pltpu.SMEM), lanes(1), lanes(1),
        kept((size, width), lambda g: (own_head(), 0)), own,
    ]
    whole = [((count, width), bf16)] + [((count, size), bf16)] * 5 + [((count, size), f32)]
    outs = [struct(*value) for value in whole]
    out_specs = [anywhere] * 7
    outs += [
        struct((count, width), bf16), struct((count, size), f32),
        struct((steps, size, size), bf16), struct((steps, 8, size), f32),
        struct((count, block), bf16), struct((count, 128), f32), struct((8, count), f32),
        struct((count, width), bf16),
    ]
    out_specs += [
        by_row(width, late), by_row(size, late),
        pl.BlockSpec((1, size, size), lambda g: (late(g), 0, 0)),
        pl.BlockSpec((1, 8, size), lambda g: (late(g), 0, 0)),
        by_row(block, late), by_row(128, late),
        pl.BlockSpec((8, block), lambda g: (0, late(g))), anywhere,
    ]
    scratch = whole + [((micro, block, width), bf16)]
    scratch += [((8, count), f32), ((heads, 8, count), f32), ((8, block), f32)]
    scratch += [((3, 32, size), bf16)]
    scratch += [((size, size), f32), ((8, size), f32), ((8, 128), f32)]
    return pl.pallas_call(
        rise_kernel,
        grid=(2 * steps,),
        in_specs=specs,
        out_specs=out_specs,
        out_shape=outs,
        scratch_shapes=[pltpu.VMEM(shape, dtype) for shape, dtype in scratch]
        + [pltpu.SemaphoreType.DMA(shape) for shape in ((3, 2), (4, 2), (7,))]
        + gather_sems(4) * 2,
        compiler_params=pltpu.CompilerParams(
            dimension_semantics=("arbitrary",), collective_id=3, has_side_effects=True,
            vmem_limit_bytes=vmem_bytes,
        ),
        name="rise",
    )(
        tokens, ln_gain, w_up, w_up, w_query, w_key, w_value, conv_w, conv_b, gate_own, gate_b,
        out_gain, skip_gain, w_down, cot,
    )


def own_head():
    first, z, y, x, c = where_am_i()
    return 2 * c + y


def settle_kernel(*refs):
    ins, refs = refs[:16], refs[16:]
    part_ref, tokens_ref, *refs = refs
    (dq_out, dk_out, dv_out, dskip_out, dz_out, g_down_out, g_z_out, g_gain_out,
     block_out, gate_out, *refs) = refs
    state, (gate_rows, gate_all, own, from_core, kept, to_row, from_row, to_owner, owned, *sems) = (
        refs[:5], refs[5:],
    )
    own_sem, c_sent, c_landed, y_sent, y_landed, o_sent, o_landed, h_sent, h_landed = sems
    step = pl.program_id(0)
    first, z, y, x, c = where_am_i()
    head = 2 * c + y
    high, low = halves_of(z, 4)
    half = own.shape[1]
    block = ins[1].shape[0]

    def device(zz, yy, cc):
        return (first + 2 * zz + yy, 2 * x + cc)

    around = [turn(z + k, 4) for k in range(1, 4)]
    order = around + [z]
    group = [(1 - y, c), (y, 1 - c), (1 - y, 1 - c)]

    def rows_of(at, cc):
        return part_ref.at[pl.ds(pl.multiple_of((2 * at + cc) * half, half), half)]

    def load(at):
        return pltpu.make_async_copy(rows_of(at, c), own.at[at], own_sem.at[at])

    def to_c(at):
        return remote(
            rows_of(at, 1 - c), from_core.at[at], c_sent.at[at], c_landed.at[at],
            device(z, y, 1 - c),
        )

    def to_y(zz):
        return remote(
            to_row.at[zz], from_row.at[zz], y_sent.at[zz], y_landed.at[zz], device(z, 1 - y, c)
        )

    def to_o(zz):
        return remote(
            to_owner.at[zz], owned.at[low, c], o_sent.at[zz], o_landed.at[low, c],
            device(zz, y, high),
        )

    def core_sum(at):
        load(at).wait()
        to_c(at).wait_recv()
        return (own[at].astype(f32) + from_core[at].astype(f32)).astype(bf16)

    def core_step(zz):
        to_row[zz] = core_sum(2 * zz + 1 - y)
        to_y(zz).start()
        kept[zz] = core_sum(2 * zz + y)

    def row_sum(zz):
        to_y(zz).wait_recv()
        return (kept[zz].astype(f32) + from_row[zz].astype(f32)).astype(bf16)

    enters = high == c

    def row_step(zz):
        to_owner[zz] = row_sum(zz)
        to_o(zz).start()

    def gate_to(k):
        yy, cc = group[k]
        return remote(
            gate_rows, gate_all.at[head], h_sent.at[k], h_landed.at[head], device(z, yy, cc)
        )

    def gate_from(k):
        at = 2 * group[k][1] + group[k][0]
        return remote(
            gate_rows, gate_all.at[at], h_sent.at[k], h_landed.at[at], device(z, *group[k])
        )

    @pl.when(step == 0)
    def _():
        others = [device(z, yy, cc) for yy, cc in group]
        for zz in around:
            others += [device(zz, y, c), device(zz, y, 1 - c)]
        greet(others)
        for zz in order:
            for yy in (1 - y, y):
                to_c(2 * zz + yy).start()
                load(2 * zz + yy).start()

    now = pl.num_programs(0) - 1 - step
    lanes = pl.ds(pl.multiple_of(now * block, block), block)
    cell_backward_kernel(
        False, None, *ins, dq_out, dk_out, dv_out, dskip_out, dz_out, gate_rows.at[:, lanes],
        g_down_out, g_z_out, g_gain_out, *state,
    )

    for k in range(4):
        pl.when(step == k)(lambda: core_step(order[k]))
    for k, when in enumerate((2, 4, 5)):
        pl.when(step == when)(lambda: row_step(order[k]))

    @pl.when(step == pl.num_programs(0) - 1)
    def _():
        for k in range(3):
            gate_to(k).start()
        gate_all[head] = gate_rows[...]

        @pl.when(enters)
        def _():
            owned[low, c] = row_sum(z)

        @pl.when(jnp.logical_not(enters))
        def _():
            row_step(z)

        for m in range(2):
            for cc in range(2):
                own_part = jnp.logical_and(2 * c + m == z, c == cc)
                landed = remote(
                    to_owner.at[0], owned.at[m, cc], o_sent.at[0], o_landed.at[m, cc],
                    device(2 * c + m, y, cc),
                )
                pl.when(jnp.logical_not(own_part))(lambda: landed.wait_recv())
                here = pl.ds(cc * half, half)
                block_out[m, here] = (
                    tokens_ref[m, here].astype(f32) + owned[m, cc].astype(f32)
                ).astype(bf16)
        for k in range(3):
            gate_from(k).wait_recv()
        heads = gate_all.shape[0]
        for h in range(heads):
            gate_out[h : h + 1, :] = gate_all[h, 0:1, :]
            gate_out[heads + h : heads + h + 1, :] = gate_all[h, 1:2, :]
        for k in range(3):
            gate_to(k).wait_send()
            to_o(order[k]).wait_send()
        pl.when(jnp.logical_not(enters))(lambda: to_o(z).wait_send())
        for zz in range(4):
            to_y(zz).wait_send()
        for at in range(8):
            to_c(at).wait_send()


def settle(
    part, tokens, rows, q, k, v, conv, gate_z, normed, states, norms, weights, cols, cot, rows_in,
    out_gain, skip_gain, w_down,
):
    count, size = q.shape
    width = w_down.shape[1]
    micro, block, _ = tokens.shape
    half = block // 2
    length = chunk_len
    end = count // length - 1
    by_row = lambda n: pl.BlockSpec((length, n), lambda g: (end - g, 0))
    gain = pl.BlockSpec((1, size), lambda g: (0, own_head()), pipeline_mode=pl.Buffered(1))
    kept = lambda value: pl.BlockSpec(
        value.shape, lambda g: (0,) * len(value.shape), pipeline_mode=pl.Buffered(1)
    )
    specs = [pl.BlockSpec((8, length), lambda g: (0, end - g))] + [by_row(size)] * 6
    specs += [
        pl.BlockSpec((1, size, size), lambda g: (end - g, 0, 0)),
        pl.BlockSpec((1, 8, size), lambda g: (end - g, 0, 0)),
        by_row(length), by_row(128), by_row(width), by_row(width), gain, gain,
        pl.BlockSpec((size, width), lambda g: (own_head(), 0), pipeline_mode=pl.Buffered(1)),
        pl.BlockSpec(memory_space=pl.ANY), kept(tokens),
    ]
    whole = [
        struct((2, size, width // 2), bf16), struct((width, size), bf16), struct((8, size), f32),
        struct(tokens.shape, bf16), struct((8, count), f32),
    ]
    outs = [struct((count, size), f32)] * 4 + [struct((count, size), bf16)] + whole
    scratch = [
        ((size, size), f32), ((8, size), f32), ((size, width), f32), ((width, size), f32),
        ((8, size), f32), ((8, count), f32), ((4, 8, count), f32),
        ((8, half, width), bf16), ((8, half, width), bf16), ((4, half, width), bf16),
        ((4, half, width), bf16), ((4, half, width), bf16), ((4, half, width), bf16),
        ((2, 2, half, width), bf16),
    ]
    sems = [(8,), (8,), (8,), (4,), (4,), (4,), (2, 2), (3,), (4,)]
    return pl.pallas_call(
        settle_kernel,
        grid=(count // length,),
        in_specs=specs,
        out_specs=[by_row(size)] * 5 + [kept(value) for value in whole],
        out_shape=outs,
        scratch_shapes=[pltpu.VMEM(shape, dtype) for shape, dtype in scratch]
        + [pltpu.SemaphoreType.DMA(shape) for shape in sems],
        compiler_params=pltpu.CompilerParams(
            dimension_semantics=("arbitrary",), collective_id=2, has_side_effects=True,
            vmem_limit_bytes=60 * 2**20,
        ),
        cost_estimate=pl.CostEstimate(
            flops=2 * count * size * (4 * length + 4 * size + 3 * width),
            bytes_accessed=48 * 2**20, transcendentals=0,
        ),
        name="settle",
    )(
        rows, q, k, v, conv, gate_z, normed, states, norms, weights, cols, cot, rows_in,
        out_gain, skip_gain, w_down, part, tokens,
    )


def drain_kernel(
    d_gate, dq, dk, dv, mix_ref, conv, q_ref, k_ref, v_ref,
    dskip, dskip_next, dz, mix_before, mix_next, normed,
    gate_own, g_gain, w_query, w_key, w_value, w_up, conv_w, conv_b,
    down_ref, lifted_ref, rows_ref, cot_ref, gain_ref, *refs
):
    grad_out, up_out, query_out, key_out, value_out, down_out, small_out, *refs = refs
    w_q, w_k, w_v, w_mix, w_gate, taps_w, taps_b, gate_pairs, q_all, k_all, v_all, *refs = refs
    g_q, g_k, g_v, g_small, rows_all, lifted_all, part_all, *refs = refs
    from_core, kept, to_row, from_row, to_owner, owned, *refs = refs
    give_up, give_square, *refs = refs
    cross_go, cross_got, *refs = refs
    from_x, totals, refs = refs[:3], (*refs[3:6], None, refs[6]), refs[7:]
    from_near, pairs, from_far, ends = (refs[k : 20 : 4] for k in range(4))
    refs = refs[20:]
    up_go, up_got, sq_go, sq_got, dn_go, dn_got, small_x, small_sum, small_z, small_all, *refs = refs
    c_sent, c_landed, y_sent, y_landed, o_sent, o_landed, *refs = refs
    x_sent, x_landed, near_sent, near_landed, far_sent, far_landed, *refs = refs
    cross_sem, w_sem, up_sem, sq_sent, sq_landed, dn_sent, dn_landed, sx_sem, sz_sent, sz_landed, *refs = refs
    sh_sent, sh_landed = refs
    step = pl.program_id(0)
    blocks, block, width = part_all.shape
    half = block // 2
    size = g_q.shape[0]
    first, z, y, x, c = where_am_i()
    head = 2 * c + y
    high, low = halves_of(z, 4)

    def device(zz, yy, cc, xx=x):
        return (first + 2 * zz + yy, 2 * xx + cc)

    around = [turn(z + k, 4) for k in range(1, 4)]
    group = [(1 - y, c), (y, 1 - c), (1 - y, 1 - c)]

    def down_rows(q):
        tall = down_ref.shape[1] // 4
        return pl.ds(q * tall, tall)

    def up_rows(q):
        tall = lifted_ref.shape[0] // 4
        return pl.ds(q * tall, tall)

    def to_x(p, q):
        give = (give_up, give_square)[p].at[q] if p < 2 else down_ref.at[1 - x, down_rows(q)]
        return remote(
            give, from_x[p].at[q], x_sent.at[p, q], x_landed.at[p, q], device(z, y, c, 1 - x)
        )

    def before_near(p, q):
        if p == 3:
            return lifted_ref.at[up_rows(q), pl.ds(size // 2, size // 2)]
        return totals[p].at[q]

    def to_near(p, q):
        return remote(
            before_near(p, q), from_near[p].at[q // 2], near_sent.at[p, q], near_landed.at[p, q],
            device(z + 1 - 2 * low, y, c),
        )

    def start_near(p, q):
        pl.when(low != q % 2)(lambda: to_near(p, q).start())

    def to_far(p, q):
        return remote(
            pairs[p].at[q // 2], from_far[p], far_sent.at[p, q], far_landed.at[p, q],
            device(z + 2 - 4 * high, y, c),
        )

    def x_step(p, q):
        to_x(p, q).wait_recv()
        own = totals[p][q] if p < 2 else down_ref[x, down_rows(q)]
        totals[p][q] = (own.astype(f32) + from_x[p][q].astype(f32)).astype(bf16)
        start_near(p, q)

    def near_step(p, q):
        @pl.when(low == q % 2)
        def _():
            to_near(p, q).wait_recv()
            pairs[p][q // 2] = (
                before_near(p, q)[...].astype(f32) + from_near[p][q // 2].astype(f32)
            ).astype(bf16)
            pl.when(high != q // 2)(lambda: to_far(p, q).start())

    def far_step(p, q):
        @pl.when(z == q)
        def _():
            to_far(p, q).wait_recv()
            total = pairs[p][q // 2].astype(f32) + from_far[p][...].astype(f32)
            ends[p][:, : total.shape[1]] = total

    def to_cross():
        return remote(cross_go, cross_got, cross_sem.at[0], cross_sem.at[1], device(z, y, c, 1 - x))

    def cross(p):
        cross_go[...] = ends[p][...].astype(bf16)
        to_cross().start()

    def weight_copies():
        lanes = pl.ds(pl.multiple_of(head * size, size), size)
        gate_lanes = pl.ds(pl.multiple_of((w_query.shape[0] + head) * size, size), size)
        pairs_of = [
            (w_query.at[head], w_q), (w_key.at[head], w_k), (w_value.at[head], w_v),
            (w_up.at[:, lanes], w_mix), (w_up.at[:, gate_lanes], w_gate),
            (conv_w.at[:, lanes], taps_w), (conv_b.at[:, lanes], taps_b),
        ]
        return [
            pltpu.make_async_copy(src, dst, w_sem.at[k]) for k, (src, dst) in enumerate(pairs_of)
        ]

    def to_c(at):
        there = pl.ds(pl.multiple_of((1 - c) * half, half), half)
        return remote(
            part_all.at[at, there], from_core.at[at], c_sent.at[at], c_landed.at[at],
            device(z, y, 1 - c),
        )

    def to_y(zz):
        return remote(
            to_row.at[zz], from_row.at[zz], y_sent.at[zz], y_landed.at[zz], device(z, 1 - y, c)
        )

    def to_o(zz):
        return remote(
            to_owner.at[zz], owned.at[low, c], o_sent.at[zz], o_landed.at[low, c],
            device(zz, y, high),
        )

    def stays(zz):
        return jnp.logical_and(z == zz, high == c)

    def core_step(at):
        zz, yy = halves_of(at, 8)
        to_c(at).wait_recv()
        here = pl.ds(pl.multiple_of(c * half, half), half)
        value = (part_all[at, here].astype(f32) + from_core[at].astype(f32)).astype(bf16)

        @pl.when(yy == y)
        def _():
            kept[zz] = value

        @pl.when(yy != y)
        def _():
            to_row[zz] = value
            to_y(zz).start()

    def row_step(zz):
        to_y(zz).wait_recv()
        to_owner[zz] = (kept[zz].astype(f32) + from_row[zz].astype(f32)).astype(bf16)

        @pl.when(stays(zz))
        def _():
            owned[low, c] = to_owner[zz]

        pl.when(jnp.logical_not(stays(zz)))(lambda: to_o(zz).start())

    def to_group(k, src, dst, sent, landed):
        yy, cc = group[k]
        return remote(src, dst, sent.at[k], landed, device(z, yy, cc))

    def small_to_x():
        return remote(g_small, small_x, sx_sem.at[0], sx_sem.at[1], device(z, y, c, 1 - x))

    def small_to_z(k):
        return remote(
            small_sum, small_z.at[z], sz_sent.at[k], sz_landed.at[z], device(around[k], y, c)
        )

    def small_from_z(k):
        return remote(
            small_sum, small_z.at[around[k]], sz_sent.at[k], sz_landed.at[around[k]],
            device(around[k], y, c),
        )

    def small_to_head(k):
        return to_group(k, small_all.at[head], small_all.at[head], sh_sent, sh_landed.at[head])

    def small_from_head(k):
        at = 2 * group[k][1] + group[k][0]
        return to_group(k, small_all.at[at], small_all.at[at], sh_sent, sh_landed.at[at])

    def up_to_y():
        return remote(up_go, up_got, up_sem.at[0], up_sem.at[1], device(z, 1 - y, c))

    def square_to(k):
        yy, cc = group[k]
        return to_group(k, sq_go.at[yy, cc], sq_got.at[head], sq_sent, sq_landed.at[head])

    def square_from(k):
        at = 2 * group[k][1] + group[k][0]
        return to_group(k, sq_go.at[0, 0], sq_got.at[at], sq_sent, sq_landed.at[at])

    def down_to(cc):
        return remote(
            dn_go.at[cc], dn_got.at[low], dn_sent.at[cc], dn_landed.at[low],
            device(head, high, cc),
        )

    def down_from(k):
        return remote(
            dn_go.at[0], dn_got.at[k], dn_sent.at[0], dn_landed.at[k],
            device(2 * y + k, low, high),
        )

    home = jnp.logical_and(head == z, high == y)

    @pl.when(step == 0)
    def _():
        others = [device(z, yy, cc) for yy, cc in group] + [device(z, y, c, 1 - x)]
        for zz in around:
            others += [device(zz, yy, cc) for yy, cc in [(y, c)] + group]
        greet(others)
        for q in range(4):
            to_x(2, q).start()
        for q in range(4):
            start_near(3, q)
        for p in range(3):
            one, two, three = split_three(gate_own[8 * p : 8 * p + 8, :])
            gate_pairs[:, size * p : size * p + size] = jnp.concatenate(
                [one, one, one, two, two, three], axis=0
            )
        for copy in weight_copies():
            copy.start()
        for ref in (g_q, g_k, g_v, g_small):
            ref[...] = jnp.zeros_like(ref)
        for ref in (q_all, k_all, v_all):
            ref[blocks * block :] = jnp.zeros_like(ref[blocks * block :])

    order = around + [z]
    tall, wide = size // 4, size // 2

    @pl.when(step < blocks)
    def _():
        lows = lower_first(
            d_gate, dq, dk, dv, mix_ref, conv, q_ref, k_ref, v_ref, gate_pairs, g_q, g_k, g_v, g_small
        )
        here = pl.ds(pl.multiple_of(step * block, block), block)
        for ref, value in zip((q_all, k_all, v_all), lows):
            ref[here] = value

    @pl.when(step == blocks - 1)
    def _():
        for q in range(4):
            rows_q = slice(tall * q, tall * q + tall)
            for at, ref in enumerate((g_q, g_k, g_v)):
                lanes = slice(wide * at, wide * at + wide)
                left, right = ref[rows_q, :wide], ref[rows_q, wide:]
                totals[1][q, :, lanes] = jnp.where(x == 0, left, right).astype(bf16)
                give_square[q, :, lanes] = jnp.where(x == 0, right, left).astype(bf16)
            to_x(1, q).start()
        for copy in weight_copies():
            copy.wait()

    @pl.when(step >= blocks)
    def _():
        now = drain_order(step, blocks)
        here = pl.ds(pl.multiple_of(now * block, block), block)
        more = pl.ds(pl.multiple_of(now * block, block), block + mix_next.shape[0])
        rows, d_mix, d_normed = lower_block(
            now == 0, now == blocks - 1, (q_all[more], k_all[more], v_all[here]),
            dskip, dskip_next, dz, mix_ref, mix_before, mix_next, normed,
            w_q, w_k, w_v, w_mix, w_gate, taps_w, taps_b, g_small,
        )
        rows_all[here] = rows
        lifted_all[here] = d_mix
        part_all[now] = d_normed.astype(bf16)
        to_c(now).start()
        pl.when(step > blocks)(lambda: core_step(drain_order(step - 1, blocks)))

    def at_end(when, *work):
        @pl.when(step == blocks + when)
        def _():
            for do in work:
                do()

    def spread_down():
        span = dn_go.shape[2]
        for cc in range(2):
            dn_go[cc] = ends[2][:, span * cc : span * cc + span].astype(bf16)
            left_here = jnp.logical_and(home, c == cc)

            @pl.when(left_here)
            def _():
                dn_got[low] = dn_go[cc]

            pl.when(jnp.logical_not(left_here))(lambda: down_to(cc).start())

    def every(do, p):
        return [partial(do, p, q) for q in range(4)]

    def early_cross():
        pl.when(x == 0)(lambda: cross(3))

    at_end(-3, *every(near_step, 3))
    at_end(-1, *every(x_step, 2))
    at_end(1, *every(far_step, 3), early_cross)
    at_end(2, *every(near_step, 2), partial(x_step, 1, 0))
    at_end(4, partial(x_step, 1, 1), partial(near_step, 1, 0), *every(far_step, 2), spread_down)
    at_end(5, partial(row_step, order[0]))
    at_end(6, partial(x_step, 1, 2), partial(near_step, 1, 1))
    at_end(7, partial(row_step, order[1]), partial(x_step, 1, 3))

    def norm_back(m, cc):
        own_part = jnp.logical_and(2 * c + m == z, c == cc)
        landed = remote(
            to_owner.at[0], owned.at[m, cc], o_sent.at[0], o_landed.at[m, cc],
            device(2 * c + m, y, cc),
        )
        pl.when(jnp.logical_not(own_part))(lambda: landed.wait_recv())
        rows_here = pl.ds(cc * half, half)
        row_hat, rstd = normalize(rows_ref[m, rows_here].astype(f32))
        scaled = owned[m, cc].astype(f32) * gain_ref[...]
        d_row = rstd * (
            scaled
            - jnp.mean(scaled, axis=-1, keepdims=True)
            - row_hat * jnp.mean(scaled * row_hat, axis=-1, keepdims=True)
        )
        grad_out[m, rows_here] = (cot_ref[m, rows_here].astype(f32) + d_row).astype(bf16)

    def small_after_x():
        small_to_x().wait_recv()
        small_sum[...] = g_small[...] + small_x[...]
        small_z[z] = small_sum[...]
        for k in range(3):
            small_to_z(k).start()

    def small_after_z():
        for k in range(3):
            small_from_z(k).wait_recv()
        total = small_z[0]
        for zz in range(1, 4):
            total = total + small_z[zz]
        small_all[head] = total
        for k in range(3):
            small_to_head(k).start()

    def spread_square():
        for yy in range(2):
            for cc in range(2):
                for a in range(3):
                    sq_go[yy, cc, :, tall * a : tall * a + tall] = ends[1][
                        tall // 2 * yy : tall // 2 * yy + tall // 2,
                        (2 * a + cc) * tall : (2 * a + cc) * tall + tall,
                    ].astype(bf16)
        sq_got[head] = sq_go[y, c]
        for k in range(3):
            square_to(k).start()

    @pl.when(step == 2 * blocks - 1)
    def _():
        g_small[29:32, :] = g_gain[0:3, :]
        small_to_x().start()
        for q in range(4):
            got = mm_tn(rows_all[:, block * q : block * q + block], lifted_all[...]).astype(bf16)
            given = lifted_ref[up_rows(q), :wide]
            totals[0][q] = jnp.where(x == 0, got[:, :wide], given)
            give_up[q] = jnp.where(x == 0, given, got[:, :wide])
            totals[4][q] = got[:, wide:]
            to_x(0, q).start()
            start_near(4, q)
            if q == 0:
                core_step(2 * z + y)
        small_after_x()
        row_step(order[2])
        near_step(1, 2)
        near_step(1, 3)
        x_step(0, 0)
        near_step(4, 0)
        near_step(4, 1)
        far_step(1, 0)
        far_step(1, 1)
        row_step(z)
        x_step(0, 1)
        near_step(4, 2)
        near_step(4, 3)
        small_after_z()
        x_step(0, 2)
        near_step(0, 0)
        near_step(0, 1)
        far_step(1, 2)
        far_step(1, 3)
        spread_square()
        x_step(0, 3)
        for q in range(4):
            far_step(4, q)
        pl.when(x == 1)(lambda: cross(4))
        near_step(0, 2)
        for m in range(2):
            for cc in range(2):
                norm_back(m, cc)
        near_step(0, 3)
        for q in range(4):
            far_step(0, q)
        to_cross().wait_recv()
        kept_half = jnp.where(x == 0, ends[4][...], ends[3][...])
        ends[0][:, wide:] = kept_half + cross_got[...].astype(f32)
        value = ends[0][...]
        mine = jnp.where(y == 0, value[:half], value[half:])
        up_go[...] = jnp.where(y == 0, value[half:], value[:half]).astype(bf16)
        up_to_y().start()
        for yy in range(2):

            @pl.when(y == yy)
            def _():
                up_out[:, size * yy : size * yy + size] = mine

        for k in range(3):
            small_from_head(k).wait_recv()
        small_out[...] = small_all[...]
        for k in range(3):
            square_from(k).wait_recv()
        for a, ref in enumerate((query_out, key_out, value_out)):
            ref[...] = sq_got[:, :, tall * a : tall * a + tall].astype(f32)
        for k in range(2):
            mine = jnp.logical_and(home, jnp.logical_and(low == k, high == c))
            pl.when(jnp.logical_not(mine))(lambda: down_from(k).wait_recv())
            deep = dn_got.shape[1]
            down_out[deep * k : deep * k + deep] = dn_got[k].astype(f32)
        up_to_y().wait_recv()
        for yy in range(2):

            @pl.when(y == yy)
            def _():
                up_out[:, size * (1 - yy) : size * (1 - yy) + size] = up_got[...].astype(f32)

        small_to_x().wait_send()
        up_to_y().wait_send()
        to_cross().wait_send()
        for p in range(5):
            for q in range(4):
                if p < 3:
                    to_x(p, q).wait_send()
                pl.when(low != q % 2)(lambda: to_near(p, q).wait_send())
                passes = jnp.logical_and(low == q % 2, high != q // 2)
                pl.when(passes)(lambda: to_far(p, q).wait_send())
        for at in range(blocks):
            to_c(at).wait_send()
        for zz in range(4):
            to_y(zz).wait_send()
            pl.when(jnp.logical_not(stays(zz)))(lambda: to_o(zz).wait_send())
        for k in range(3):
            small_to_z(k).wait_send()
            small_to_head(k).wait_send()
            square_to(k).wait_send()
        for cc in range(2):
            left_here = jnp.logical_and(home, c == cc)
            pl.when(jnp.logical_not(left_here))(lambda: down_to(cc).wait_send())


def drain_order(step, blocks):
    first, z, y, x, c = where_am_i()
    k, odd = halves_of(jnp.maximum(step - blocks, 0), blocks)
    return 2 * turn(z + 1 + k, 4) + jnp.where(odd == 0, 1 - y, y)


def drain(inputs, down, lifted, rows, cot, gain):
    (d_gate, dq, dk, dv, dskip, dz, mix, conv, q, k, v, normed,
     w_query, w_key, w_value, w_up, conv_w, conv_b, gate_own, g_gain) = inputs
    tokens, size = q.shape
    micro, block, width = rows.shape
    half = block // 2
    lines = 40
    steps = tokens // block
    early = lambda g: jnp.minimum(g, steps - 1)
    late = lambda g: drain_order(g, steps)
    both = lambda g: jnp.where(g < steps, g, drain_order(g, steps))
    edge = lambda at: pl.BlockSpec(
        (16, size), lambda g: (jnp.clip(at(g), 0, tokens // 16 - 1), 0)
    )
    before = edge(lambda g: late(g) * (block // 16) - 1)
    behind = edge(lambda g: (late(g) + 1) * (block // 16))
    by_row = lambda n, at: pl.BlockSpec((block, n), lambda g: (at(g), 0))
    kept = lambda value: pl.BlockSpec(
        value.shape, lambda g: (0,) * value.ndim, pipeline_mode=pl.Buffered(1)
    )
    anywhere = pl.BlockSpec(memory_space=pl.ANY)
    arguments = (
        d_gate, dq, dk, dv, mix, conv, q, k, v, dskip, dskip, dz, mix, mix, normed, gate_own, g_gain,
        w_query, w_key, w_value, w_up, conv_w, conv_b, down, lifted, rows, cot, gain,
    )
    specs = [pl.BlockSpec((8, block), lambda g: (0, early(g)))] + [by_row(size, early)] * 3
    specs += [by_row(size, both)] + [by_row(size, early)] * 4
    specs += [by_row(size, late), behind, by_row(size, late), before, behind, by_row(width, late)]
    specs += [kept(gate_own), kept(g_gain)]
    specs += [anywhere] * 6 + [kept(value) for value in (down, lifted, rows, cot, gain)]
    scratch = [((size, size), bf16)] * 3 + [((width, size), bf16)] * 2
    scratch += [((4, size), f32), ((1, size), f32), ((48, 3 * size), bf16)]
    scratch += [((tokens + 16, size), bf16)] * 3
    scratch += [((size, size), f32)] * 3 + [((lines, size), f32)]
    scratch += [((tokens, width), bf16), ((tokens, size), bf16), ((8, block, width), bf16)]
    scratch += [
        ((8, half, width), bf16), ((4, half, width), bf16), ((4, half, width), bf16),
        ((4, half, width), bf16), ((4, half, width), bf16), ((2, 2, half, width), bf16),
    ]
    up = (width // 4, size // 2)
    pieces = [up, (size // 4, 3 * size // 2), (size // 4, width // 2), up, up]
    scratch += [((4, *piece), bf16) for piece in pieces[:2]] + [(up, bf16)] * 2
    scratch += [((4, *piece), bf16) for piece in pieces[:3] + pieces[:3] + pieces[4:]]
    for piece in pieces:
        scratch += [((2, *piece), bf16)] * 2 + [(piece, bf16), (piece, f32)]
    scratch[-17] = ((up[0], size), f32)
    scratch += [
        ((width // 8, size), bf16), ((width // 8, size), bf16),
        ((2, 2, size // 8, 3 * size // 4), bf16), ((4, size // 8, 3 * size // 4), bf16),
        ((2, size // 4, width // 4), bf16), ((2, size // 4, width // 4), bf16),
        ((lines, size), f32), ((lines, size), f32), ((4, lines, size), f32), ((4, lines, size), f32),
    ]
    sems = [(8,), (8,), (4,), (4,), (4,), (2, 2)] + [(5, 4)] * 6
    sems += [(2,), (7,), (2,), (3,), (4,), (2,), (2,), (2,), (3,), (4,), (3,), (4,)]
    square = struct((4, size // 8, size // 4), f32)
    outs = [
        struct(rows.shape, bf16), struct((width // 8, 2 * size), f32), square, square, square,
        struct((size // 2, width // 4), f32), struct((4, lines, size), f32),
    ]
    return pl.pallas_call(
        drain_kernel,
        grid=(2 * steps,),
        in_specs=specs,
        out_specs=[kept(value) for value in outs],
        scratch_shapes=[pltpu.VMEM(shape, dtype) for shape, dtype in scratch]
        + [pltpu.SemaphoreType.DMA(shape) for shape in sems],
        out_shape=outs,
        compiler_params=pltpu.CompilerParams(
            dimension_semantics=("arbitrary",), collective_id=1, has_side_effects=True,
            vmem_limit_bytes=60 * 2**20,
        ),
        cost_estimate=pl.CostEstimate(
            flops=2 * tokens * size * (6 * size + 4 * width), bytes_accessed=48 * 2**20,
            transcendentals=0,
        ),
        name="drain",
    )(*arguments)


def spread_kernel(small, gain, *refs):
    count = (len(refs) - 7) // 2
    for k in range(count):
        refs[count + 7 + k][...] = refs[k][...]
    ln_out, conv_out, bias_out, gate_out, forget_out, out_gain, skip_gain = refs[count : count + 7]
    heads, _, size = small.shape
    total = small[0, 32:34, :]
    for h in range(1, heads):
        total = total + small[h, 32:34, :]
    for k in range(2):
        lanes = slice(size * k, size * k + size)
        ln_out[:, lanes] = total[k : k + 1, :] / gain[:, lanes]
    for h in range(heads):
        lanes = slice(size * h, size * h + size)
        conv_out[:, lanes] = small[h, 24:28, :]
        bias_out[:, lanes] = small[h, 28:29, :]
        out_gain[:, lanes] = small[h, 29:30, :]
        skip_gain[:, lanes] = small[h, 30:31, :]
        forget_out[:, h : h + 1] = small[h, 31:32, 0:1]
        for p in range(3):
            start = (heads * p + h) * size
            gate_out[:, start : start + size] = small[h, 8 * p : 8 * p + 8, :]


def spread(small, gain, *made):
    heads, _, size = small.shape
    inner = heads * size
    shapes = [gain.shape, (4, inner), (1, inner), (8, 3 * inner), (1, heads), (1, inner), (1, inner)]
    return pl.pallas_call(
        spread_kernel,
        out_shape=[struct(shape, f32) for shape in shapes]
        + [struct(value.shape, value.dtype) for value in made],
        name="spread",
        compiler_params=pltpu.CompilerParams(vmem_limit_bytes=62 * 2**20),
    )(small, gain, *made)


def swap(value, axis, mask):
    count = lax.axis_size(axis)
    return lax.ppermute(value, axis, [(s, s ^ mask) for s in range(count)])


def part_of(value, at, count, axis):
    size = value.shape[axis] // count
    return lax.dynamic_slice_in_dim(value, at * size, size, axis)


def halved(value, bit, dim, axis, mask):
    kept = part_of(value, bit, 2, dim).astype(f32)
    return kept + swap(part_of(value, 1 - bit, 2, dim), axis, mask).astype(f32)


def paired(mine, other, bit, dim):
    return jnp.where(
        bit == 0, jnp.concatenate([mine, other], dim), jnp.concatenate([other, mine], dim)
    )


def place():
    at_seq, at_batch = lax.axis_index("seq"), lax.axis_index("batch")
    return (at_seq % 8) // 2, at_seq % 2, at_batch // 2, at_batch % 2


def sent_across(blocks, z):
    got = [lax.dynamic_index_in_dim(blocks, z, 0, keepdims=False)]
    for k in range(1, 4):
        got.append(swap(lax.dynamic_index_in_dim(blocks, z ^ k, 0, keepdims=False), "seq", 2 * k))
    return got


def in_order(got, z):
    got = jnp.stack(got)
    return jnp.stack([lax.dynamic_index_in_dim(got, z ^ k, 0, keepdims=False) for k in range(4)])


def gather_sequence(own):
    z, y, x, c = place()
    micro, rows, width = own.shape
    slots = paired(own, swap(own, "batch", 1), c, 0)
    blocks = in_order(sent_across(part_of(slots, c, 2, 2), z), z)[:, None]
    both = paired(blocks, swap(blocks, "seq", 1), y, 1)
    return paired(both, swap(both, "batch", 1), c, 3).reshape(8 * rows, width)


def scatter_first(parts):
    z, y, x, c = place()
    blocks = parts.reshape(4, 2, -1, parts.shape[1])
    return halved(blocks, c, 2, "batch", 1).astype(bf16)


def scatter_last(slots):
    z, y, x, c = place()
    other = swap(part_of(slots, 1 - c, 2, 0), "batch", 1)
    return paired(part_of(slots, c, 2, 0), other, c, 1).astype(f32)


def scatter_sequence(parts):
    z, y, x, c = place()
    blocks = scatter_first(parts)
    blocks = halved(blocks, y, 1, "seq", 1).astype(bf16)[:, 0]
    return scatter_last(in_order(sent_across(blocks, z), z))


def total_over_heads(value):
    value = value + swap(value, "batch", 1)
    return value + swap(value, "seq", 1)


def over_ranges(value, count):
    size = lax.axis_size("seq")
    groups = [[first + 8 * k for k in range(count)] for first in range(8)]
    return lax.all_gather(value, "seq", axis_index_groups=groups) if size > 8 else value[None]


def state_before(state, norm, level, total, ranges):
    index = lax.axis_index("seq") // 8
    summary = (state, norm[0], level[0, 0], total)
    everything = jax.tree.map(lambda part: over_ranges(part, ranges), summary)
    before = state_identity(summary)
    for k in range(ranges - 1):
        new = combine_states(before, jax.tree.map(lambda part: part[k], everything))
        before = jax.tree.map(lambda a, b: jnp.where(k < index, a, b), new, before)
    return (
        before[0],
        jnp.broadcast_to(before[1], norm.shape),
        jnp.broadcast_to(before[2], level.shape),
    )


def cotangent_after(d_state, d_norm, keep, ranges):
    index = lax.axis_index("seq") // 8
    own = (d_state, d_norm)
    everything = jax.tree.map(lambda part: over_ranges(part, ranges), own)
    keeps = over_ranges(keep, ranges)
    after = jax.tree.map(jnp.zeros_like, own)
    for k in range(ranges - 1, 0, -1):
        new = jax.tree.map(lambda a, b: a[k] + keeps[k] * b, everything, after)
        after = jax.tree.map(lambda a, b: jnp.where(k > index, a, b), new, after)
    return after


def reduce_blocks(at, up, square, down, heads):
    count, batch_count = lax.axis_size("seq"), lax.axis_size("batch")
    g_m, g_z = up
    width, size = g_m.shape
    half = size // 2
    squares = [
        jnp.concatenate([square[0, :, k : k + half], square[1, :, k : k + half]], 1)
        for k in range(0, 3 * half, half)
    ]
    g_down = jnp.concatenate([down[0], down[1]], 1)
    inner = heads * size
    up = jnp.zeros((width, 2 * inner), f32)
    up = lax.dynamic_update_slice_in_dim(up, g_m.astype(f32), at * size, 1)
    up = lax.dynamic_update_slice_in_dim(up, g_z.astype(f32), inner + at * size, 1)
    down = lax.dynamic_update_slice_in_dim(
        jnp.zeros((inner, width), f32), g_down.astype(f32), at * size, 0
    )
    full = [up, down]
    for g in squares:
        full.append(
            lax.dynamic_update_slice_in_dim(
                jnp.zeros((heads, size, size), f32), g.astype(f32)[None], at, 0
            )
        )
    blocks = tuple(to_device_blocks(g, count, batch_count) for g in full)
    pieces = lax.psum_scatter(blocks, ("seq", "batch"), scatter_dimension=0, tiled=True)
    s_up, s_down, s_query, s_key, s_value = tuple(p[0] for p in pieces)
    return s_up, jnp.stack([s_query, s_key, s_value], 1), s_down


def head_device(
    tokens, ln_gain, w_up, conv_w, conv_b, w_query, w_key, w_value, gate_w, gate_b,
    out_gain, skip_gain, w_down, d_out,
):
    z, y, x, c = place()
    at = 2 * c + y
    ranges = lax.axis_size("seq") // 8
    direct = ranges == 1 and lax.axis_size("batch") == 4
    head = jnp.reshape(at, (1,)).astype(jnp.int32)
    heads, size, _ = w_query.shape
    inner = heads * size
    conv_row = conv_b.reshape(1, inner)
    out_row = out_gain.reshape(1, inner)
    skip_row = skip_gain.reshape(1, inner)

    gate_own = lax.dynamic_index_in_dim(
        gate_w.reshape(3, heads, size, 8), at, 1, keepdims=False
    ).transpose(0, 2, 1)
    gate_rows = gate_own.reshape(24, size)
    high = lax.reduce_precision(gate_own, 8, 7)
    middle = lax.reduce_precision(gate_own - high, 8, 7)
    low = lax.reduce_precision(gate_own - high - middle, 8, 7)
    gate_parts = jnp.concatenate([high, middle, low, jnp.zeros_like(high)], 1).astype(bf16)
    gate_pairs = (
        jnp.concatenate([high, high, high, middle, middle, low], 1)
        .astype(bf16)
        .transpose(1, 0, 2)
        .reshape(48, 3 * size)
    )

    if direct:
        (normed, mix, conv, q, k, v, gate_z,
         part, head_normed, states, norms, weights, cols, rows, cot) = rise(
            tokens[:, 0], ln_gain[None], w_up, w_query, w_key, w_value, conv_w, conv_row, gate_rows, gate_b,
            out_row, skip_row, w_down, d_out[:, 0],
        )
    else:
        normed = gather_normed(tokens[:, 0], ln_gain[None])
        cot = gather_sequence(d_out[:, 0])
        first = () if ranges == 1 else (shifted(normed[-16:], "seq", 8),)
        mix, conv, q, k, v, gate_z, gates, *halo = lift(
            head, normed, w_up, w_query, w_key, w_value, conv_w, conv_row, gate_parts, *first
        )
        gates = total_over_heads(gates)
        gates = jnp.concatenate(
            [
                lax.dynamic_slice_in_dim(gates, at, 1, 0),
                lax.dynamic_slice_in_dim(gates, heads + at, 1, 0)
                + lax.dynamic_slice_in_dim(gate_b, at, 1, 0)[:, None],
            ]
        )
        first = ()
        if ranges > 1:
            first = (
                jnp.zeros((size, size), f32),
                jnp.zeros((8, size), f32),
                jnp.full((8, 128), floor_value, f32),
            )
            *_, state, norm, level = cell_forward(
                head, gates, q, k, v, conv, gate_z, out_row, skip_row, w_down, *first
            )
            total = jnp.sum(jax.nn.log_sigmoid(gates[1]))
            first = state_before(state, norm, level, total, ranges)
        part, head_normed, states, norms, weights, cols, rows, *last = cell_forward(
            head, gates, q, k, v, conv, gate_z, out_row, skip_row, w_down, *first
        )
    cell_args = (
        rows, q, k, v, conv, gate_z, head_normed, states, norms, weights, cols, cot, normed,
        out_row, skip_row, w_down,
    )
    if direct:
        dq, dk, dv, dskip, dz, g_down, g_z, g_gain, block_rows, d_gate = settle(
            part, tokens[:, 0], *cell_args
        )
    else:
        block_rows = (tokens[:, 0].astype(f32) + scatter_sequence(part)).astype(bf16)
        after = ()
        if ranges > 1:
            after = (jnp.zeros((size, size), f32), jnp.zeros((8, size), f32))
            *_, d_state, d_norm = cell_backward(head, *cell_args, *after)
            keep = jnp.exp(total + first[2][0, 0] - last[2][0, 0])
            after = cotangent_after(d_state, d_norm, keep, ranges)
        dq, dk, dv, dskip, dz, d_rows, g_down, g_z, g_gain, *_ = cell_backward(
            head, *cell_args, *after
        )
        index = jnp.arange(2 * heads)[:, None]
        d_gate = jnp.where(
            index == at, d_rows[0:1], jnp.where(index == heads + at, d_rows[1:2], 0.0)
        )
        d_gate = total_over_heads(d_gate)
    lower_args = (
        d_gate, dq, dk, dv, dskip, dz, mix, conv, q, k, v, normed,
        w_query, w_key, w_value, w_up, conv_w, conv_row, gate_pairs, g_gain,
    )
    if direct:
        grad_rows, s_up, s_query, s_key, s_value, s_down, small = drain(
            (*lower_args[:18], gate_rows, g_gain), g_down, g_z, tokens[:, 0], d_out[:, 0], ln_gain[None]
        )
    else:
        first = ()
        if ranges > 1:
            *_, later = lower(head, *lower_args, halo[0], jnp.zeros((8, size), f32))
            first = (halo[0], shifted(later, "seq", -8))
        d_part, square, up, small, *_ = lower(head, *lower_args, *first)
    if not direct:
        d_normed = scatter_sequence(d_part)
        row_f = tokens[:, 0].astype(f32)
        centre = row_f - jnp.mean(row_f, axis=-1, keepdims=True)
        rstd = lax.rsqrt(jnp.mean(centre * centre, axis=-1, keepdims=True) + norm_epsilon)
        row_hat = centre * rstd
        scaled = d_normed * ln_gain
        d_row = rstd * (
            scaled
            - jnp.mean(scaled, axis=-1, keepdims=True)
            - row_hat * jnp.mean(scaled * row_hat, axis=-1, keepdims=True)
        )
        grad_rows = (d_out[:, 0].astype(f32) + d_row).astype(bf16)
        s_up, squares, s_down = reduce_blocks(at, up, square, g_down, heads)
        s_query, s_key, s_value = squares[:, 0], squares[:, 1], squares[:, 2]
        small = jnp.where(jnp.arange(heads)[:, None, None] == at, small, 0.0)
        small = lax.psum(small, ("seq", "batch"))
    (s_ln, s_conv_w, s_conv_b, s_gate_w, s_gate_b, s_out_gain, s_skip,
     block_rows, grad_rows, s_up, s_query, s_key, s_value, s_down) = spread(
        small, ln_gain[None], block_rows, grad_rows, s_up, s_query, s_key, s_value, s_down
    )
    return (
        block_rows[:, None],
        grad_rows[:, None],
        s_ln[0],
        s_up,
        s_conv_w,
        s_conv_b[0],
        s_query,
        s_key,
        s_value,
        s_gate_w.T,
        s_gate_b[0],
        s_out_gain[0],
        s_skip[0],
        s_down,
    )


def solution(mesh):
    placed = (P(None, "batch", "seq", None),) + (P(),) * 12 + (P(None, "batch", "seq", None),)
    return jax.shard_map(
        head_device,
        mesh=mesh,
        in_specs=placed,
        out_specs=(
            P(None, "batch", "seq", None),
            P(None, "batch", "seq", None),
            P(),
            P("seq", "batch"),
            P(),
            P(),
            P(None, "seq", "batch"),
            P(None, "seq", "batch"),
            P(None, "seq", "batch"),
            P(),
            P(),
            P(),
            P(),
            P("seq", "batch"),
        ),
        check_vma=False,
    )
```

```python
from functools import partial

import jax
import jax.numpy as jnp
from jax import lax
from jax.experimental import pallas as pl
from jax.experimental.pallas import tpu as pltpu
from jax.sharding import PartitionSpec as P

norm_epsilon = 1e-05
floor_value = -1e30


def shifted(value, axis, steps):
    count = lax.axis_size(axis)
    initial, last = (max(0, -steps), min(count, count - steps))
    return lax.ppermute(value, axis, [(source, source + steps) for source in range(initial, last)])


def combine_states(earlier, later):
    top = jnp.maximum(later[3] + earlier[2], later[2])
    keep_first = jnp.exp(later[3] + earlier[2] - top)
    keep_second = jnp.exp(later[2] - top)
    merged_c = keep_first[..., None, None] * earlier[0] + keep_second[..., None, None] * later[0]
    merged_n = keep_first[..., None] * earlier[1] + keep_second[..., None] * later[1]
    return (merged_c, merged_n, top, earlier[3] + later[3])


def state_identity(template):
    return (
        jnp.zeros_like(template[0]),
        jnp.zeros_like(template[1]),
        jnp.full_like(template[2], floor_value),
        jnp.zeros_like(template[3]),
    )


def head_output(hidden, out_gain, skip_gain, conv_out, gate_z):
    centre = hidden - jnp.mean(hidden, axis=-1, keepdims=True)
    spread = jnp.mean(centre * centre, axis=-1, keepdims=True)
    normed = centre * lax.rsqrt(spread + norm_epsilon)
    flat_out = normed.transpose(1, 0, 2).reshape(hidden.shape[1], -1) * out_gain
    return (flat_out + skip_gain * conv_out) * jax.nn.silu(gate_z)


def output_tail(
    query_f,
    key_f,
    value_f,
    gate_pre,
    conv_f,
    gate_z,
    out_gain,
    skip_gain,
    state_c,
    state_n,
    state_m,
):
    head_count = gate_pre.shape[1] // 2
    in_gate = gate_pre[:, :head_count].T
    log_forget = jax.nn.log_sigmoid(gate_pre[:, head_count:]).T
    hidden = cell_hidden(
        to_heads(query_f, head_count),
        to_heads(key_f, head_count),
        to_heads(value_f, head_count),
        in_gate,
        log_forget,
        state_c,
        state_n,
        state_m,
    )
    return head_output(hidden, out_gain, skip_gain, conv_f, gate_z)


def state_tail(key_f, value_f, gate_pre, state_c, state_n, state_m):
    head_count = gate_pre.shape[1] // 2
    in_gate = gate_pre[:, :head_count].T
    log_forget = jax.nn.log_sigmoid(gate_pre[:, head_count:]).T
    return cell_state(
        to_heads(key_f, head_count),
        to_heads(value_f, head_count),
        in_gate,
        log_forget,
        state_c,
        state_n,
        state_m,
    )


def to_device_blocks(grad_full, seq_count, batch_count):
    if grad_full.ndim == 2:
        rows, cols = grad_full.shape
        split = grad_full.reshape(seq_count, rows // seq_count, batch_count, cols // batch_count)
        return split.transpose(0, 2, 1, 3).reshape(
            seq_count * batch_count, rows // seq_count, cols // batch_count
        )
    heads, rows, cols = grad_full.shape
    split = grad_full.reshape(heads, seq_count, rows // seq_count, batch_count, cols // batch_count)
    return split.transpose(1, 3, 0, 2, 4).reshape(
        seq_count * batch_count, heads, rows // seq_count, cols // batch_count
    )


f32 = jnp.float32
bf16 = jnp.bfloat16
chunk_len = 256
wide_len = 512
vmem_bytes = 56 * 1024 * 1024


def mm(a, b):
    return lax.dot_general(a, b, (((1,), (0,)), ((), ())), preferred_element_type=f32)


def mm_nt(a, b):
    return lax.dot_general(a, b, (((1,), (1,)), ((), ())), preferred_element_type=f32)


def mm_tn(a, b):
    return lax.dot_general(a, b, (((0,), (0,)), ((), ())), preferred_element_type=f32)


def split_three(value):
    high = value.astype(bf16)
    rest = value - high.astype(f32)
    middle = rest.astype(bf16)
    low = (rest - middle.astype(f32)).astype(bf16)
    return high, middle, low


def conv_taps(ext, length):
    return [pltpu.roll(ext, 3 - j, 0)[8 : 8 + length] if j < 3 else ext[8 : 8 + length] for j in range(4)]


def lift_kernel(chained, head_ref, normed, w_mix, w_gate, w_q, w_k, w_v, conv_w, conv_b, gate_w, *refs):
    if chained:
        rows_before, *refs, halo_out, carry = refs
    else:
        *refs, carry = refs
    mix_out, conv_out, q_out, k_out, v_out, z_out, gate_out = refs
    length = normed.shape[0]

    @pl.when(pl.program_id(0) == 0)
    def _():
        if chained:
            mix_before = mm(rows_before[...], w_mix[...]).astype(bf16)
            halo_out[...] = mix_before
            carry[...] = mix_before[8:16].astype(f32)
        else:
            carry[...] = jnp.zeros_like(carry)

    rows = normed[...]
    mix = mm(rows, w_mix[...]).astype(bf16)
    mix_out[...] = mix
    z_out[...] = mm(rows, w_gate[...])
    mix_f = mix.astype(f32)
    taps = conv_taps(jnp.concatenate([carry[...], mix_f], axis=0), length)
    carry[...] = mix_f[length - 8 :]
    summed = conv_b[...]
    for j in range(4):
        summed = summed + conv_w[j : j + 1, :] * taps[j]
    conv = (summed * jax.nn.sigmoid(summed)).astype(bf16)
    conv_out[...] = conv
    q = mm(conv, w_q[0]).astype(bf16)
    k = mm(conv, w_k[0]).astype(bf16)
    v = mm(mix, w_v[0]).astype(bf16)
    q_out[...] = q
    k_out[...] = k
    v_out[...] = v
    parts = mm_nt(gate_w[0], q) + mm_nt(gate_w[1], k) + mm_nt(gate_w[2], v)
    gate_out[...] = parts[0:8] + parts[8:16] + parts[16:24]


def gate_rows(gates, causal, diagonal):
    in_row = gates[0:1, :]
    pre = gates[1:2, :]
    log_forget = jnp.minimum(pre, 0.0) - jnp.log1p(jnp.exp(-jnp.abs(pre)))
    run_col = jnp.sum(jnp.where(causal, log_forget, 0.0), axis=1, keepdims=True)
    run_row = jnp.sum(jnp.where(diagonal, run_col, 0.0), axis=0, keepdims=True)
    return in_row - run_row, run_col, log_forget


def masks(length):
    row = lax.broadcasted_iota(jnp.int32, (length, length), 0)
    col = lax.broadcasted_iota(jnp.int32, (length, length), 1)
    return row >= col, row == col


def cell_recur(gates, q_ref, k_ref, v_ref, state_out, norm_out, weight_out, row_out, state, norm, level):
    length = q_ref.shape[0]
    head_size = q_ref.shape[1]
    scale = head_size ** (-0.5)
    causal, diagonal = masks(length)
    a_row, run_col, log_forget = gate_rows(gates[...], causal, diagonal)
    before = level[0:1, 0:1]
    top = jnp.maximum(
        before, jnp.max(jnp.where(causal, a_row, floor_value), axis=1, keepdims=True)
    )
    decay = jnp.exp(jnp.where(causal, a_row - top, floor_value))
    q = q_ref[...]
    k = k_ref[...]
    v = v_ref[...]
    q_f = q.astype(f32)
    weights = decay * (mm_nt(q, k) * scale)
    weights_low = weights.astype(bf16)
    weight_out[...] = weights_low
    from_state = jnp.exp(before - top)
    state_low = state[...].astype(bf16)
    state_out[0] = state_low
    norm_row = norm[0:1, :]
    norm_out[0] = norm[...]
    numerator = mm(weights_low, v) + (from_state * scale) * mm(q, state_low)
    denominator = jnp.sum(weights, axis=1, keepdims=True) + (from_state * scale) * jnp.sum(
        q_f * norm_row, axis=1, keepdims=True
    )
    floor = jnp.exp(-(run_col + top))
    size = jnp.abs(denominator)
    inverse = 1.0 / jnp.maximum(size, floor)
    hidden = numerator * inverse
    slope = jnp.where(
        size > floor, jnp.where(denominator > 0, 1.0, -1.0) * inverse * norm_epsilon, 0.0
    )
    sub = lax.broadcasted_iota(jnp.int32, (8, length), 0)
    row_out[...] = jnp.where(sub == 0, a_row, 1.0 - jnp.exp(log_forget))
    last = top[length - 1 : length, :]
    a_col = jnp.sum(jnp.where(diagonal, a_row, 0.0), axis=1, keepdims=True)
    weighted = k.astype(f32) * jnp.exp(a_col - last)
    keep = jnp.exp(before - last)
    state[...] = keep * state[...] + mm_tn(weighted.astype(bf16), v)
    norm[...] = keep * norm[...] + jnp.sum(weighted, axis=0, keepdims=True)
    level[...] = jnp.broadcast_to(run_col[length - 1 : length, :] + last, level.shape)
    lane = lax.broadcasted_iota(jnp.int32, (length, 128), 1)
    packed = jnp.where(lane == 1, inverse, slope)
    packed = jnp.where(lane == 2, from_state, packed)
    return hidden, jnp.where(lane == 3, top, packed)


def cell_head(hidden, cols, conv_ref, z_ref, out_gain, skip_gain, w_down, part_out, normed_out, col_out):
    centre = hidden - jnp.mean(hidden, axis=1, keepdims=True)
    spread = jnp.mean(centre * centre, axis=1, keepdims=True)
    rstd = lax.rsqrt(spread + norm_epsilon)
    normed = centre * rstd
    normed_out[...] = normed
    gate_z = z_ref[...]
    gated = (normed * out_gain[...] + skip_gain[...] * conv_ref[...].astype(f32)) * (
        gate_z * jax.nn.sigmoid(gate_z)
    )
    part_out[...] = mm(gated.astype(bf16), w_down[...]).astype(bf16)
    lane = lax.broadcasted_iota(jnp.int32, cols.shape, 1)
    cols = jnp.where(lane == 0, rstd, cols)
    col_out[...] = jnp.where(lane == 4, cols * (rstd * rstd), cols)


def cell_forward_kernel(
    chained, head_ref, gates, q_ref, k_ref, v_ref, conv_ref, z_ref, out_gain, skip_gain, w_down, *refs
):
    if chained:
        *first, part_out, normed_out, state_out, norm_out, weight_out, col_out, row_out = refs[:10]
        *final, state, norm, level = refs[10:]
    else:
        part_out, normed_out, state_out, norm_out, weight_out, col_out, row_out = refs[:7]
        state, norm, level = refs[7:]

    @pl.when(pl.program_id(0) == 0)
    def _():
        if chained:
            for ref, value in zip((state, norm, level), first):
                ref[...] = value[...]
        else:
            state[...] = jnp.zeros_like(state)
            norm[...] = jnp.zeros_like(norm)
            level[...] = jnp.full_like(level, floor_value)

    hidden, cols = cell_recur(
        gates, q_ref, k_ref, v_ref, state_out, norm_out, weight_out, row_out, state, norm, level
    )
    cell_head(
        hidden, cols, conv_ref, z_ref, out_gain, skip_gain, w_down, part_out, normed_out, col_out
    )
    if chained:
        for ref, value in zip(final, (state, norm, level)):
            ref[...] = value[...]


def cell_backward_kernel(
    chained, head_ref, rows_ref, q_ref, k_ref, v_ref, conv_ref, z_ref, normed_ref, state_ref, norm_ref,
    weight_ref, col_ref, cot_ref, rows_in, out_gain, skip_gain, w_down, *refs
):
    if chained:
        first, refs = refs[:2], refs[2:]
    dq_out, dk_out, dv_out, dskip_out, dz_out, gate_out, g_down_out, g_z_out, g_gain_out, *refs = refs
    *final, d_state, d_norm, g_down, g_z, g_gain = refs
    length = q_ref.shape[0]
    head_size = q_ref.shape[1]
    scale = head_size ** (-0.5)

    @pl.when(pl.program_id(0) == 0)
    def _():
        if chained:
            d_state[...] = first[0][...]
            d_norm[...] = first[1][...]
        else:
            d_state[...] = jnp.zeros_like(d_state)
            d_norm[...] = jnp.zeros_like(d_norm)
        g_down[...] = jnp.zeros_like(g_down)
        g_z[...] = jnp.zeros_like(g_z)
        g_gain[...] = jnp.zeros_like(g_gain)

    causal, diagonal = masks(length)
    rstd = col_ref[:, 0:1]
    inverse = col_ref[:, 1:2]
    from_state = col_ref[:, 2:3]
    top = col_ref[:, 3:4]
    factor = col_ref[:, 4:5]
    a_row = rows_ref[0:1, :]
    q = q_ref[...]
    k = k_ref[...]
    v = v_ref[...]
    q_f = q.astype(f32)
    k_f = k.astype(f32)
    conv = conv_ref[...].astype(f32)
    normed = normed_ref[...]
    gate_z = z_ref[...]
    cot = cot_ref[...]
    opened = jax.nn.sigmoid(gate_z)
    silu = gate_z * opened
    head_in = normed * out_gain[...] + skip_gain[...] * conv
    g_down[...] += mm_tn((head_in * silu).astype(bf16), cot)
    d_gated = mm_nt(cot, w_down[...])
    d_z = (d_gated * head_in * (opened * (1.0 + gate_z * (1.0 - opened)))).astype(bf16)
    dz_out[...] = d_z
    g_z[...] += mm_tn(rows_in[...], d_z)
    d_head = d_gated * silu
    g_gain[0:1, :] += jnp.sum(d_head * normed, axis=0, keepdims=True)
    g_gain[1:2, :] += jnp.sum(d_head * conv, axis=0, keepdims=True)
    dskip_out[...] = skip_gain[...] * d_head
    d_hat = d_head * out_gain[...]
    along = jnp.sum(d_hat * normed, axis=1, keepdims=True)
    d_hidden = rstd * (
        d_hat - jnp.mean(d_hat, axis=1, keepdims=True) - normed * (along / head_size)
    )
    d_num = d_hidden * inverse
    d_den = -along * factor
    d_num_low = d_num.astype(bf16)
    decay = jnp.exp(jnp.where(causal, a_row - top, floor_value))
    d_scores = ((mm_nt(d_num_low, v) + d_den) * (decay * scale)).astype(bf16)
    through = from_state * scale
    dq_near = mm(d_scores, k)
    dq_far = (
        mm_nt((d_num * through).astype(bf16), state_ref[0])
        + (through * d_den) * norm_ref[0, 0:1, :]
    )
    last = top[length - 1 : length, :]
    keep = from_state[length - 1 : length, :]
    a_col = jnp.sum(jnp.where(diagonal, a_row, 0.0), axis=1, keepdims=True)
    key_weight = jnp.exp(a_col - last)
    d_state_low = d_state[...].astype(bf16)
    dk_near = mm_tn(d_scores, q)
    dk_far = key_weight * (mm_nt(v, d_state_low) + d_norm[0:1, :])
    dv = mm_tn(weight_ref[...], d_num_low) + mm((k_f * key_weight).astype(bf16), d_state_low)
    dq_out[...] = dq_near + dq_far
    dk_out[...] = dk_near + dk_far
    dv_out[...] = dv
    held = state_ref[0].astype(f32) * d_state[...]
    held = jnp.sum(jnp.sum(held, axis=0, keepdims=True) + norm_ref[0, 0:1, :] * d_norm[0:1, :])
    q_state = q_f * through
    d_state[...] = keep * d_state[...] + mm_tn(q_state.astype(bf16), d_num_low)
    d_norm[...] = keep * d_norm[...] + jnp.sum(q_state * d_den, axis=0, keepdims=True)
    q_dot = jnp.sum(q_f * (dq_near + dq_far), axis=1, keepdims=True)
    k_near = jnp.sum(k_f * dk_near, axis=1, keepdims=True)
    k_far = jnp.sum(k_f * dk_far, axis=1, keepdims=True)
    d_in = jnp.sum(jnp.where(diagonal, k_near + k_far, 0.0), axis=0, keepdims=True)
    d_log = jnp.sum(
        jnp.where(causal, q_dot - k_near, jnp.where(diagonal, 0.0, k_far)), axis=0, keepdims=True
    )
    d_log = d_log + keep * held
    sub = lax.broadcasted_iota(jnp.int32, (8, length), 0)
    d_pre = d_log * rows_ref[1:2, :]
    gate_out[...] = jnp.where(sub == 0, d_in, d_pre)
    g_gain[2:3, :] += jnp.broadcast_to(jnp.sum(d_pre, axis=1, keepdims=True), (1, head_size))

    @pl.when(pl.program_id(0) == pl.num_programs(0) - 1)
    def _():
        if chained:
            final[0][...] = d_state[...]
            final[1][...] = d_norm[...]
        half = g_down.shape[1] // 2
        g_down_out[0] = g_down[:, :half].astype(bf16)
        g_down_out[1] = g_down[:, half:].astype(bf16)
        g_z_out[...] = g_z[...].astype(bf16)
        g_gain_out[...] = g_gain[...]


def lower_first(d_gate, dq_ref, dk_ref, dv_ref, mix_ref, conv_ref, q_ref, k_ref, v_ref, gate_w,
                g_q, g_k, g_v, g_small):
    high, middle, low = split_three(d_gate[...])
    left = jnp.concatenate([high, middle, low, high, middle, high], axis=0)
    d_joined = mm_tn(left, gate_w[...])
    size = q_ref.shape[1]
    query_low = (dq_ref[...] + d_joined[:, :size]).astype(bf16)
    key_low = (dk_ref[...] + d_joined[:, size : 2 * size]).astype(bf16)
    value_low = (dv_ref[...] + d_joined[:, 2 * size :]).astype(bf16)
    conv = conv_ref[...]
    g_q[...] += mm_tn(conv, query_low)
    g_k[...] += mm_tn(conv, key_low)
    g_v[...] += mm_tn(mix_ref[...], value_low)
    three = jnp.concatenate([high, middle, low], axis=0)
    for at, ref in enumerate((q_ref, k_ref, v_ref)):
        got = mm(three, ref[...])
        g_small[8 * at : 8 * at + 8, :] += got[0:8] + got[8:16] + got[16:24]
    return query_low, key_low, value_low


def lower_second(
    edge, last, lows, dskip_ref, dz_ref, mix_ref, mix_before, normed, w_q, w_k, w_v, w_mix, w_gate,
    conv_w, conv_b, g_gain, g_small, later,
):
    query_low, key_low, value_low = lows
    length, size = mix_ref.shape
    mix = mix_ref[...]
    d_conv = dskip_ref[...] + mm_nt(query_low, w_q[...]) + mm_nt(key_low, w_k[...])
    halo = jnp.where(last, edge, mix_before[8:16, :].astype(f32))
    taps = conv_taps(jnp.concatenate([halo, mix.astype(f32)], axis=0), length)
    summed = conv_b[...]
    for j in range(4):
        summed = summed + conv_w[j : j + 1, :] * taps[j]
    opened = jax.nn.sigmoid(summed)
    d_summed = d_conv * (opened * (1.0 + summed * (1.0 - opened)))
    for j in range(4):
        g_small[24 + j : 25 + j, :] += jnp.sum(d_summed * taps[j], axis=0, keepdims=True)
    g_small[28:29, :] += jnp.sum(d_summed, axis=0, keepdims=True)
    ext = jnp.concatenate([d_summed, later[...]], axis=0)
    later[...] = d_summed[0:8]
    d_mix = conv_w[3:4, :] * d_summed
    for j in range(3):
        d_mix = d_mix + conv_w[j : j + 1, :] * pltpu.roll(ext, length + 8 - (3 - j), 0)[0:length]
    d_mix = (d_mix + mm_nt(value_low, w_v[...])).astype(bf16)
    d_z = dz_ref[...]
    rows = normed[...]
    d_normed = mm_nt(d_mix, w_mix[...]) + mm_nt(d_z, w_gate[...])
    g_ln = jnp.sum(d_normed * rows.astype(f32), axis=0, keepdims=True)
    g_small[32:33, :] += g_ln[:, :size]
    g_small[33:34, :] += g_ln[:, size:]

    @pl.when(last)
    def _():
        g_small[29:32, :] = g_gain[0:3, :]

    return rows, d_mix, d_z, d_normed


def lower_block(
    at_start, at_end, lows, dskip_ref, dskip_next, dz_ref, mix_ref, mix_before, mix_next, normed,
    w_q, w_k, w_v, w_mix, w_gate, conv_w, conv_b, g_small,
):
    query_low, key_low, value_low = lows
    length, size = mix_ref.shape
    extra = mix_next.shape[0]
    halo = jnp.where(at_start, 0.0, mix_before[8:16, :].astype(f32))
    ext = jnp.concatenate(
        [halo, mix_ref[...].astype(f32), mix_next[...].astype(f32)], axis=0
    )
    taps = conv_taps(ext, length + extra)
    summed = conv_b[...]
    for j in range(4):
        summed = summed + conv_w[j : j + 1, :] * taps[j]
    opened = jax.nn.sigmoid(summed)
    d_conv = jnp.concatenate([dskip_ref[...], dskip_next[...]], axis=0)
    d_conv = d_conv + mm_nt(query_low, w_q[...]) + mm_nt(key_low, w_k[...])
    d_summed = d_conv * (opened * (1.0 + summed * (1.0 - opened)))
    for j in range(4):
        g_small[24 + j : 25 + j, :] += jnp.sum(
            d_summed[:length] * taps[j][:length], axis=0, keepdims=True
        )
    g_small[28:29, :] += jnp.sum(d_summed[:length], axis=0, keepdims=True)
    row = lax.broadcasted_iota(jnp.int32, d_summed.shape, 0)
    d_summed = jnp.where(jnp.logical_and(at_end, row >= length), 0.0, d_summed)
    d_mix = conv_w[3:4, :] * d_summed[:length]
    for j in range(3):
        ahead = pltpu.roll(d_summed, length + extra - (3 - j), 0)[0:length]
        d_mix = d_mix + conv_w[j : j + 1, :] * ahead
    d_mix = (d_mix + mm_nt(value_low, w_v[...])).astype(bf16)
    rows = normed[...]
    d_normed = mm_nt(d_mix, w_mix[...]) + mm_nt(dz_ref[...], w_gate[...])
    g_ln = jnp.sum(d_normed * rows.astype(f32), axis=0, keepdims=True)
    g_small[32:33, :] += g_ln[:, :size]
    g_small[33:34, :] += g_ln[:, size:]
    return rows, d_mix, d_normed


def lower_kernel(chained, head_ref, *refs):
    ins, refs = refs[:22], list(refs[22:])
    edge = 0.0
    if chained:
        first_halo, first_later, *refs = refs
        edge = first_halo[8:16, :].astype(f32)
        later_out = refs.pop(4)
    part_out, square_out, up_out, small_out = refs[:4]
    g_q, g_k, g_v, g_m, g_z, g_small, later = refs[4:]
    step = pl.program_id(0)
    size = g_q.shape[0]

    @pl.when(step == 0)
    def _():
        for ref in (g_q, g_k, g_v, g_m, g_z, g_small, later):
            ref[...] = jnp.zeros_like(ref)
        if chained:
            later[...] = first_later[...]

    (d_gate, dq, dk, dv, dskip, dz, mix, mix_before, conv, q, k, v, normed,
     w_q, w_k, w_v, w_mix, w_gate, conv_w, conv_b, gate_w, g_gain) = ins
    lows = lower_first(d_gate, dq, dk, dv, mix, conv, q, k, v, gate_w, g_q, g_k, g_v, g_small)
    rows, d_mix, d_z, d_normed = lower_second(
        edge, step == pl.num_programs(0) - 1, lows, dskip, dz, mix, mix_before, normed,
        w_q.at[0], w_k.at[0], w_v.at[0], w_mix, w_gate, conv_w, conv_b, g_gain, g_small, later,
    )
    g_m[...] += mm_tn(rows, d_mix)
    g_z[...] += mm_tn(rows, d_z)
    part_out[...] = d_normed.astype(bf16)

    @pl.when(step == pl.num_programs(0) - 1)
    def _():
        half = size // 2
        for at, ref in enumerate((g_q, g_k, g_v)):
            square_out[0, :, half * at : half * at + half] = ref[:, :half].astype(bf16)
            square_out[1, :, half * at : half * at + half] = ref[:, half:].astype(bf16)
        up_out[0] = g_m[...].astype(bf16)
        up_out[1] = g_z[...].astype(bf16)
        small_out[...] = g_small[...]
        if chained:
            later_out[...] = later[...]


def struct(shape, dtype):
    return jax.ShapeDtypeStruct(shape, dtype)


def run_kernel(body, head, grid, inputs, in_specs, outs, out_specs, scratch, name, flops, nbytes):
    return pl.pallas_call(
        body,
        grid_spec=pltpu.PrefetchScalarGridSpec(
            num_scalar_prefetch=1,
            grid=(grid,),
            in_specs=in_specs,
            out_specs=out_specs,
            scratch_shapes=scratch,
        ),
        out_shape=outs,
        compiler_params=pltpu.CompilerParams(
            dimension_semantics=("arbitrary",), vmem_limit_bytes=vmem_bytes
        ),
        cost_estimate=pl.CostEstimate(flops=flops, bytes_accessed=nbytes, transcendentals=0),
        name=name,
    )(head, *inputs)


def fixed(shape, *index):
    return pl.BlockSpec(shape, lambda g, h: tuple(h[0] if i == "h" else i for i in index))


def lift(head, normed, w_up, w_query, w_key, w_value, conv_w, conv_b, gate_parts, *first):
    tokens, width = normed.shape
    heads, size, _ = w_query.shape
    length = wide_len
    by_row = lambda cols: pl.BlockSpec((length, cols), lambda g, h: (g, 0))
    weight = pl.BlockSpec((1, size, size), lambda g, h: (h[0], 0, 0))
    chained = len(first) > 0
    halo = [pl.BlockSpec((16, size), lambda g, h: (0, 0))] * chained
    return run_kernel(
        partial(lift_kernel, chained), head, tokens // length,
        (normed, w_up, w_up, w_query, w_key, w_value, conv_w, conv_b, gate_parts, *first),
        [
            by_row(width),
            pl.BlockSpec((width, size), lambda g, h: (0, h[0])),
            pl.BlockSpec((width, size), lambda g, h: (0, heads + h[0])),
            weight, weight, weight,
            pl.BlockSpec((4, size), lambda g, h: (0, h[0])),
            pl.BlockSpec((1, size), lambda g, h: (0, h[0])),
            pl.BlockSpec(gate_parts.shape, lambda g, h: (0, 0, 0)),
        ]
        + [pl.BlockSpec((16, width), lambda g, h: (0, 0))] * chained,
        [struct((tokens, size), bf16)] * 5
        + [struct((tokens, size), f32), struct((8, tokens), f32)]
        + [struct((16, size), bf16)] * chained,
        [by_row(size)] * 6 + [pl.BlockSpec((8, length), lambda g, h: (0, g))] + halo,
        [pltpu.VMEM((8, size), f32)],
        "lift", 2 * tokens * size * (2 * width + 3 * size), 24 * 2**20,
    )


def cell_forward(head, gates, q, k, v, conv, gate_z, out_gain, skip_gain, w_down, *first):
    tokens, size = q.shape
    width = w_down.shape[1]
    length = chunk_len
    steps = tokens // length
    by_row = lambda cols: pl.BlockSpec((length, cols), lambda g, h: (g, 0))
    gain = pl.BlockSpec((1, size), lambda g, h: (0, h[0]))
    carried = [struct(value.shape, f32) for value in first]
    carried_specs = [pl.BlockSpec(value.shape, lambda g, h: (0, 0)) for value in first]
    return run_kernel(
        partial(cell_forward_kernel, len(first) > 0), head, steps,
        (gates, q, k, v, conv, gate_z, out_gain, skip_gain, w_down, *first),
        [pl.BlockSpec((2, length), lambda g, h: (0, g))]
        + [by_row(size)] * 5
        + [gain, gain, pl.BlockSpec((size, width), lambda g, h: (h[0], 0))]
        + carried_specs,
        [
            struct((tokens, width), bf16),
            struct((tokens, size), f32),
            struct((steps, size, size), bf16),
            struct((steps, 8, size), f32),
            struct((tokens, length), bf16),
            struct((tokens, 128), f32),
            struct((8, tokens), f32),
        ]
        + carried,
        [
            by_row(width),
            by_row(size),
            pl.BlockSpec((1, size, size), lambda g, h: (g, 0, 0)),
            pl.BlockSpec((1, 8, size), lambda g, h: (g, 0, 0)),
            by_row(length),
            by_row(128),
            pl.BlockSpec((8, length), lambda g, h: (0, g)),
        ]
        + carried_specs,
        [pltpu.VMEM((size, size), f32), pltpu.VMEM((8, size), f32), pltpu.VMEM((8, 128), f32)],
        "cell_forward", 2 * tokens * size * (2 * length + 2 * size + width), 28 * 2**20,
    )


def cell_backward(
    head, rows, q, k, v, conv, gate_z, normed, states, norms, weights, cols, cot, rows_in,
    out_gain, skip_gain, w_down, *first,
):
    tokens, size = q.shape
    width = w_down.shape[1]
    length = chunk_len
    steps = tokens // length
    end = steps - 1
    by_row = lambda n: pl.BlockSpec((length, n), lambda g, h: (end - g, 0))
    gain = pl.BlockSpec((1, size), lambda g, h: (0, h[0]))
    whole = lambda shape: pl.BlockSpec(shape, lambda g, h: (0, 0))
    carried = [struct(value.shape, f32) for value in first]
    carried_specs = [whole(value.shape) for value in first]
    return run_kernel(
        partial(cell_backward_kernel, len(first) > 0), head, steps,
        (rows, q, k, v, conv, gate_z, normed, states, norms, weights, cols, cot, rows_in,
         out_gain, skip_gain, w_down, *first),
        [pl.BlockSpec((8, length), lambda g, h: (0, end - g))]
        + [by_row(size)] * 6
        + [
            pl.BlockSpec((1, size, size), lambda g, h: (end - g, 0, 0)),
            pl.BlockSpec((1, 8, size), lambda g, h: (end - g, 0, 0)),
            by_row(length),
            by_row(128),
            by_row(width),
            by_row(width),
            gain, gain,
            pl.BlockSpec((size, width), lambda g, h: (h[0], 0)),
        ]
        + carried_specs,
        [struct((tokens, size), f32)] * 4
        + [
            struct((tokens, size), bf16),
            struct((8, tokens), f32),
            struct((2, size, width // 2), bf16),
            struct((width, size), bf16),
            struct((8, size), f32),
        ]
        + carried,
        [by_row(size)] * 5
        + [
            pl.BlockSpec((8, length), lambda g, h: (0, end - g)),
            pl.BlockSpec((2, size, width // 2), lambda g, h: (0, 0, 0)),
            whole((width, size)),
            whole((8, size)),
        ]
        + carried_specs,
        [
            pltpu.VMEM((size, size), f32),
            pltpu.VMEM((8, size), f32),
            pltpu.VMEM((size, width), f32),
            pltpu.VMEM((width, size), f32),
            pltpu.VMEM((8, size), f32),
        ],
        "cell_backward", 2 * tokens * size * (4 * length + 4 * size + 2 * width), 44 * 2**20,
    )


def lower_inputs(
    length, d_gate, dq, dk, dv, dskip, dz, mix, conv, q, k, v, normed,
    w_query, w_key, w_value, w_up, conv_w, conv_b, gate_pairs, g_gain,
):
    tokens, size = q.shape
    width = normed.shape[1]
    heads = w_query.shape[0]
    end = tokens // length - 1
    by_row = lambda n: pl.BlockSpec((length, n), lambda g, h: (end - g, 0))
    kept = lambda shape, index: pl.BlockSpec(shape, index, pipeline_mode=pl.Buffered(1))
    weight = kept((1, size, size), lambda g, h: (h[0], 0, 0))
    inputs = (
        d_gate, dq, dk, dv, dskip, dz, mix, mix, conv, q, k, v, normed,
        w_query, w_key, w_value, w_up, w_up, conv_w, conv_b, gate_pairs, g_gain,
    )
    specs = [pl.BlockSpec((8, length), lambda g, h: (0, end - g))]
    specs += [by_row(size)] * 6
    specs += [
        pl.BlockSpec(
            (16, size), lambda g, h: (jnp.maximum((end - g) * (length // 16) - 1, 0), 0)
        )
    ]
    specs += [by_row(size)] * 4
    specs += [by_row(width), weight, weight, weight]
    specs += [
        kept((width, size), lambda g, h: (0, h[0])),
        kept((width, size), lambda g, h: (0, heads + h[0])),
        kept((4, size), lambda g, h: (0, h[0])),
        kept((1, size), lambda g, h: (0, h[0])),
        kept(gate_pairs.shape, lambda g, h: (0, 0)),
        kept(g_gain.shape, lambda g, h: (0, 0)),
    ]
    return inputs, specs


def lower(head, *inputs):
    inputs, first = inputs[:20], inputs[20:]
    tokens, size = inputs[1].shape
    width = inputs[11].shape[1]
    length = wide_len
    end = tokens // length - 1
    by_row = lambda n: pl.BlockSpec((length, n), lambda g, h: (end - g, 0))
    whole = lambda shape: pl.BlockSpec(shape, lambda g, h: (0, 0))
    chained = len(first) > 0
    inputs, specs = lower_inputs(length, *inputs)
    return run_kernel(
        partial(lower_kernel, chained), head, tokens // length,
        (*inputs, *first),
        specs + [whole(value.shape) for value in first],
        [struct((tokens, width), bf16)]
        + [struct((2, size, 3 * size // 2), bf16), struct((2, width, size), bf16)]
        + [struct((40, size), f32)]
        + [struct((8, size), f32)] * chained,
        [by_row(width)]
        + [
            pl.BlockSpec((2, size, 3 * size // 2), lambda g, h: (0, 0, 0)),
            pl.BlockSpec((2, width, size), lambda g, h: (0, 0, 0)),
        ]
        + [whole((40, size))]
        + [whole((8, size))] * chained,
        [pltpu.VMEM((size, size), f32)] * 3
        + [pltpu.VMEM((width, size), f32)] * 2
        + [pltpu.VMEM((40, size), f32), pltpu.VMEM((8, size), f32)],
        "lower", 2 * tokens * size * (6 * size + 4 * width), 48 * 2**20,
    )
MESH_ID = pl.DeviceIdType.MESH


def halves_of(value, count):
    whole = jnp.int32(0)
    for bound in range(2, count, 2):
        whole = whole + jnp.where(value >= bound, 1, 0)
    return whole, value - 2 * whole


def where_am_i():
    at_seq, at_batch = lax.axis_index("seq"), lax.axis_index("batch")
    first = jnp.int32(0)
    for bound in range(8, lax.axis_size("seq"), 8):
        first = first + jnp.where(at_seq >= bound, 8, 0)
    z, y = halves_of(at_seq - first, 8)
    x, c = halves_of(at_batch, lax.axis_size("batch"))
    return first, z, y, x, c


def turn(value, count):
    return jnp.where(value >= count, value - count, value)


def greet(others):
    barrier = pltpu.get_barrier_semaphore()
    for other in others:
        pl.semaphore_signal(barrier, 1, device_id=other, device_id_type=MESH_ID)
    pl.semaphore_wait(barrier, len(others))


def remote(src, dst, sent, landed, device):
    return pltpu.make_async_remote_copy(src, dst, sent, landed, device_id=device, device_id_type=MESH_ID)


def normalize(rows):
    centre = rows - jnp.mean(rows, axis=-1, keepdims=True)
    rstd = lax.rsqrt(jnp.mean(centre * centre, axis=-1, keepdims=True) + norm_epsilon)
    return centre * rstd, rstd


class Gather:
    def __init__(self, source, out_ref, block, cuts, sems):
        self.source, self.out_ref, self.block, self.cuts = source, out_ref, block, cuts
        self.parts = len(cuts)
        self.kept, self.z_sent, self.z_landed, self.y_sent, self.y_landed, *sems = sems
        self.c_sent, self.c_landed = sems
        self.first, self.z, self.y, self.x, self.c = where_am_i()
        self.enters = halves_of(self.z, 4)[0] == self.c

    def device(self, zz, yy, cc):
        return (self.first + 2 * zz + yy, 2 * self.x + cc)

    def others(self):
        others = [self.device(turn(self.z + k, 4), self.y, self.c) for k in range(1, 4)]
        return others + [self.device(self.z, 1 - self.y, self.c), self.device(self.z, self.y, 1 - self.c)]

    def rows(self, zz, yy, part):
        start, size = self.cuts[part]
        return self.out_ref.at[
            pl.ds(pl.multiple_of((2 * zz + yy) * self.block + start, 16), size)
        ]

    def away(self, m):
        return 2 * self.c + m != self.z

    def to_column(self, m, part):
        return remote(
            self.source(m, pl.ds(*self.cuts[part])), self.rows(self.z, self.y, part), self.z_sent.at[m, part],
            self.z_landed.at[self.z, part], self.device(2 * self.c + m, self.y, self.c),
        )

    def keep(self, m, part):
        return pltpu.make_async_copy(
            self.source(m, pl.ds(*self.cuts[part])), self.rows(self.z, self.y, part), self.kept.at[part]
        )

    def from_column(self, zz, part):
        here = self.rows(zz, self.y, part)
        return remote(
            here, here, self.z_sent.at[0, part], self.z_landed.at[zz, part],
            self.device(zz, self.y, self.c),
        )

    def to_row(self, zz, k, part):
        here = self.rows(zz, self.y, part)
        return remote(
            here, here, self.y_sent.at[k, part], self.y_landed.at[zz, part],
            self.device(self.z, 1 - self.y, self.c),
        )

    def from_row(self, zz, k, part):
        here = self.rows(zz, 1 - self.y, part)
        return remote(
            here, here, self.y_sent.at[k, part], self.y_landed.at[zz, part],
            self.device(self.z, 1 - self.y, self.c),
        )

    def to_core(self, zz, yy, k, part):
        here = self.rows(zz, yy, part)
        return remote(
            here, here, self.c_sent.at[k, part], self.c_landed.at[2 * zz + yy, part],
            self.device(self.z, self.y, 1 - self.c),
        )

    def start(self, part):
        for m in range(2):
            pl.when(self.away(m))(lambda: self.to_column(m, part).start())
            pl.when(jnp.logical_not(self.away(m)))(lambda: self.keep(m, part).start())

    def at(self, k):
        high, low = halves_of(self.z, 4)
        far = 2 * high if k < 2 else 2 - 2 * high
        return far + (low if k % 2 == 0 else 1 - low)

    def pass_column(self, k, part):
        @pl.when(self.enters)
        def _():
            if k == 0:
                self.keep(0, part).wait()
            else:
                self.from_column(self.at(k), part).wait_recv()
            self.to_row(self.at(k), k, part).start()
            self.to_core(self.at(k), self.y, k, part).start()

    def pass_row(self, k, part):
        @pl.when(self.enters)
        def _():
            self.from_row(self.at(k), k, part).wait_recv()
            self.to_core(self.at(k), 1 - self.y, 4 + k, part).start()

    def finish(self, wait_core):
        @pl.when(self.enters)
        def _():
            for k in range(4):
                for part in range(self.parts):
                    self.to_row(self.at(k), k, part).wait_send()
                    self.to_core(self.at(k), self.y, k, part).wait_send()
                    self.to_core(self.at(k), 1 - self.y, 4 + k, part).wait_send()

        if wait_core:

            @pl.when(jnp.logical_not(self.enters))
            def _():
                for zz in range(4):
                    for yy in range(2):
                        for part in range(self.parts):
                            self.to_core(zz, yy, 0, part).wait_recv()

        for m in range(2):
            for part in range(self.parts):
                pl.when(self.away(m))(lambda: self.to_column(m, part).wait_send())


def even_cuts(block, parts):
    size = block // parts
    return [(part * size, size) for part in range(parts)]


def falling_cuts(block):
    unit = block // 16
    return [(0, 5 * unit), (5 * unit, 5 * unit), (10 * unit, 4 * unit), (14 * unit, 2 * unit)]


def gather_sems(parts):
    shapes = [(parts,), (2, parts), (4, parts), (4, parts), (4, parts), (8, parts), (8, parts)]
    return [pltpu.SemaphoreType.DMA(shape) for shape in shapes]


def gather_kernel(rows_ref, gain_ref, out_ref, staged, *sems):
    parts = sems[0].shape[0]
    block = rows_ref.shape[1]
    cuts = even_cuts(block, parts)
    gather = Gather(lambda m, here: staged.at[m, here], out_ref, block, cuts, sems)
    greet(gather.others())
    for part in range(parts):
        here = pl.ds(*cuts[part])
        for m in range(2):
            staged[m, here] = (
                normalize(rows_ref[m, here].astype(f32))[0] * gain_ref[...]
            ).astype(bf16)
        gather.start(part)
    for part in range(parts):
        for k in range(4):
            gather.pass_column(k, part)
        if part > 0:
            for k in range(4):
                gather.pass_row(k, part - 1)
    for k in range(4):
        gather.pass_row(k, parts - 1)
    gather.finish(True)


def gather_normed(rows, gain):
    micro, block, width = rows.shape
    return pl.pallas_call(
        gather_kernel,
        out_shape=struct((8 * block, width), bf16),
        in_specs=[pl.BlockSpec(memory_space=pltpu.VMEM)] * 2,
        out_specs=pl.BlockSpec(memory_space=pl.ANY),
        scratch_shapes=[pltpu.VMEM((micro, block, width), bf16)] + gather_sems(4),
        compiler_params=pltpu.CompilerParams(
            collective_id=0, has_side_effects=True, vmem_limit_bytes=32 * 2**20
        ),
        name="gather_normed",
    )(rows, gain)


def lift_rest(rows, before, w_q, w_k, w_v, conv_w, conv_b, gate_parts):
    length = rows.shape[0]
    taps = conv_taps(jnp.concatenate([before, rows.astype(f32)], axis=0), length)
    summed = conv_b[...]
    for j in range(4):
        summed = summed + conv_w[j : j + 1, :] * taps[j]
    conv = (summed * jax.nn.sigmoid(summed)).astype(bf16)
    q = mm(conv, w_q[0]).astype(bf16)
    k = mm(conv, w_k[0]).astype(bf16)
    v = mm(rows, w_v[0]).astype(bf16)
    parts = mm_nt(gate_parts[0], q) + mm_nt(gate_parts[1], k) + mm_nt(gate_parts[2], v)
    return conv, q, k, v, parts[0:8] + parts[8:16] + parts[16:24]


def rise_kernel(
    tokens, ln_gain, w_mix, w_gate, w_q, w_k, w_v, conv_w, conv_b, gate_own, gate_b, out_gain,
    skip_gain, w_down, cot_ref, *refs
):
    kept_outs, cell_outs, (cot_out, *refs) = refs[:7], refs[7:14], refs[14:]
    rows_all, mix_all, conv_all, q_all, k_all, v_all, z_all, *refs = refs
    staged, gate_mine, gate_all, gates, gate_parts, hidden_kept, cols_kept, *refs = refs
    state, h_sent, h_landed, out_sem, *sems = refs[:3], *refs[3:]
    parts = sems[0].shape[0]
    step = pl.program_id(0)
    blocks = (pl.num_programs(0) - 1) // 2
    micro, block, width = cot_ref.shape
    cuts = falling_cuts(block)
    normed = Gather(lambda m, here: staged.at[m, here], rows_all, block, cuts, sems[:7])
    gather = Gather(
        lambda m, here: cot_ref.at[m, here], cot_out, block, even_cuts(block, parts), sems[7:]
    )
    z, y, c = gather.z, gather.y, gather.c
    head = 2 * c + y
    heads = gate_all.shape[0]
    group = [(1 - y, c), (y, 1 - c), (1 - y, 1 - c)]
    span = gate_mine.shape[1] // 2

    def gate_to(k, part):
        lanes = pl.ds(part * span, span)
        return remote(
            gate_mine.at[:, lanes], gate_all.at[head, :, lanes], h_sent.at[k, part],
            h_landed.at[head, part], gather.device(z, *group[k]),
        )

    def gate_from(k, part):
        lanes = pl.ds(part * span, span)
        at = 2 * group[k][1] + group[k][0]
        return remote(
            gate_mine.at[:, lanes], gate_all.at[at, :, lanes], h_sent.at[k, part],
            h_landed.at[at, part], gather.device(z, *group[k]),
        )

    def keep_out(k):
        made = (rows_all, mix_all, conv_all, q_all, k_all, v_all, z_all)[k]
        return pltpu.make_async_copy(made, kept_outs[k], out_sem.at[k])

    def lift_up(yy, part):
        start, size = cuts[part]
        here = [
            pl.ds(pl.multiple_of((2 * zz + yy) * block + start, 16), size) for zz in range(4)
        ]
        rows = jnp.concatenate([rows_all[at] for at in here], axis=0)
        mix = mm(rows, w_mix[...]).astype(bf16)
        gate_z = mm(rows, w_gate[...])
        for k, at in enumerate(here):
            mix_all[at] = mix[size * k : size * k + size]
            z_all[at] = gate_z[size * k : size * k + size]

    def arrived(yy, part):
        @pl.when(jnp.logical_not(normed.enters))
        def _():
            for zz in range(4):
                normed.to_core(zz, yy, 0, part).wait_recv()

    @pl.when(step == 0)
    def _():
        greet(normed.others() + [gather.device(z, 1 - y, 1 - c)])
        for p in range(3):
            gate_parts[p, 0:24] = jnp.concatenate(split_three(gate_own[8 * p : 8 * p + 8, :]), axis=0)
            gate_parts[p, 24:32] = jnp.zeros_like(gate_parts[p, 24:32])
        for part in range(parts):
            here = pl.ds(*cuts[part])
            for m in range(2):
                staged[m, here] = (
                    normalize(tokens[m, here].astype(f32))[0] * ln_gain[...]
                ).astype(bf16)
            normed.start(part)
        for part in range(parts):
            for k in range(4):
                normed.pass_column(k, part)
            if part == parts - 1:
                for later in range(parts):
                    gather.start(later)
            arrived(y, part)
            lift_up(y, part)
            if part > 0:
                for k in range(4):
                    normed.pass_row(k, part - 1)
                arrived(1 - y, part - 1)
                lift_up(1 - y, part - 1)
        for k in range(4):
            normed.pass_row(k, parts - 1)
        arrived(1 - y, parts - 1)
        lift_up(1 - y, parts - 1)
        for k in (0, 1, 6):
            keep_out(k).start()

    @pl.when(step < blocks)
    def _():
        here = pl.ds(pl.multiple_of(step * block, block), block)
        edge = pl.ds(pl.multiple_of(jnp.maximum(step * block - 16, 0), 16), 16)
        before = jnp.where(step == 0, 0.0, mix_all[edge][8:16].astype(f32))
        conv, q, k, v, gate = lift_rest(
            mix_all[here], before, w_q, w_k, w_v, conv_w, conv_b, gate_parts
        )
        for ref, made in zip((conv_all, q_all, k_all, v_all), (conv, q, k, v)):
            ref[here] = made
        gate_mine[:, here] = gate
        gate_all[head, :, here] = gate

    @pl.when(step == blocks - 1)
    def _():
        for k in (2, 3, 4, 5):
            keep_out(k).start()

    for part in range(2):

        @pl.when(step == (blocks // 2) * (part + 1) - 1)
        def _():
            for k in range(3):
                gate_to(k, part).start()

        @pl.when(step == blocks + (blocks // 2) * part)
        def _():
            for k in range(3):
                gate_from(k, part).wait_recv()

    part_out, normed_out, state_out, norm_out, weight_out, col_out, row_out = cell_outs

    def recur():
        here = pl.ds(pl.multiple_of((step - blocks) * block, block), block)
        for row, at in enumerate((head, heads + head)):
            total = gate_all[0, pl.ds(at, 1), here]
            for h in range(1, heads):
                total = total + gate_all[h, pl.ds(at, 1), here]
            if row == 1:
                total = total + gate_b[head]
            gates[row : row + 1, :] = total
        return cell_recur(
            gates, q_all.at[here], k_all.at[here], v_all.at[here],
            state_out, norm_out, weight_out, row_out, *state,
        )

    def head_of_last():
        here = pl.ds(pl.multiple_of((step - blocks - 1) * block, block), block)
        cell_head(
            hidden_kept[...], cols_kept[...], conv_all.at[here], z_all.at[here],
            out_gain, skip_gain, w_down, part_out, normed_out, col_out,
        )

    @pl.when(step == blocks)
    def _():
        state[0][...] = jnp.zeros_like(state[0])
        state[1][...] = jnp.zeros_like(state[1])
        state[2][...] = jnp.full_like(state[2], floor_value)
        hidden_kept[...], cols_kept[...] = recur()

    @pl.when(jnp.logical_and(step > blocks, step < 2 * blocks))
    def _():
        head_of_last()
        hidden_kept[...], cols_kept[...] = recur()

    pl.when(step == 2 * blocks)(head_of_last)

    def columns(part, ks=(1, 2, 3)):
        return [partial(gather.pass_column, k, part) for k in ks]

    def rows(part, ks=(0, 1, 2, 3)):
        return [partial(gather.pass_row, k, part) for k in ks]

    plan = {
        0: [do for part in range(parts) for do in columns(part, (0,))],
        2: columns(0),
        5: columns(1) + [do for part in range(parts) for do in rows(part, (0,))],
        7: columns(2) + rows(0, (1, 2, 3)),
        9: columns(3) + rows(1, (1, 2, 3)),
        11: rows(2, (1, 2, 3)),
        13: rows(3, (1, 2, 3)),
    }
    for when, work in plan.items():

        @pl.when(step == when)
        def _():
            for do in work:
                do()

    @pl.when(step == 2 * blocks)
    def _():
        for k in range(7):
            keep_out(k).wait()
        normed.finish(False)
        gather.finish(True)
        for k in range(3):
            for part in range(2):
                gate_to(k, part).wait_send()


def rise(
    tokens, ln_gain, w_up, w_query, w_key, w_value, conv_w, conv_b, gate_own, gate_b, out_gain,
    skip_gain, w_down, cot,
):
    heads, size, _ = w_query.shape
    micro, block, width = cot.shape
    steps = 8
    count = steps * block
    late = lambda g: jnp.clip(g - steps, 0, steps - 1)
    after = lambda g: jnp.clip(g - steps - 1, 0, steps - 1)
    by_row = lambda n, at: pl.BlockSpec((block, n), lambda g: (at(g), 0))
    kept = lambda shape, index: pl.BlockSpec(shape, index, pipeline_mode=pl.Buffered(1))
    weight = kept((1, size, size), lambda g: (own_head(), 0, 0))
    lanes = lambda rows: kept((rows, size), lambda g: (0, own_head()))
    anywhere = pl.BlockSpec(memory_space=pl.ANY)
    own = kept(cot.shape, lambda g: (0, 0, 0))
    specs = [
        own, kept(ln_gain.shape, lambda g: (0, 0)), lanes(width),
        kept((width, size), lambda g: (0, heads + own_head())),
        weight, weight, weight, lanes(4), lanes(1), kept(gate_own.shape, lambda g: (0, 0)),
        pl.BlockSpec(memory_space=pltpu.SMEM), lanes(1), lanes(1),
        kept((size, width), lambda g: (own_head(), 0)), own,
    ]
    whole = [((count, width), bf16)] + [((count, size), bf16)] * 5 + [((count, size), f32)]
    outs = [struct(*value) for value in whole]
    out_specs = [anywhere] * 7
    outs += [
        struct((count, width), bf16), struct((count, size), f32),
        struct((steps, size, size), bf16), struct((steps, 8, size), f32),
        struct((count, block), bf16), struct((count, 128), f32), struct((8, count), f32),
        struct((count, width), bf16),
    ]
    out_specs += [
        by_row(width, after), by_row(size, after),
        pl.BlockSpec((1, size, size), lambda g: (late(g), 0, 0)),
        pl.BlockSpec((1, 8, size), lambda g: (late(g), 0, 0)),
        by_row(block, late), by_row(128, after),
        pl.BlockSpec((8, block), lambda g: (0, late(g))), anywhere,
    ]
    scratch = whole + [((micro, block, width), bf16)]
    scratch += [((8, count), f32), ((heads, 8, count), f32), ((8, block), f32)]
    scratch += [((3, 32, size), bf16), ((block, size), f32), ((block, 128), f32)]
    scratch += [((size, size), f32), ((8, size), f32), ((8, 128), f32)]
    return pl.pallas_call(
        rise_kernel,
        grid=(2 * steps + 1,),
        in_specs=specs,
        out_specs=out_specs,
        out_shape=outs,
        scratch_shapes=[pltpu.VMEM(shape, dtype) for shape, dtype in scratch]
        + [pltpu.SemaphoreType.DMA(shape) for shape in ((3, 2), (4, 2), (7,))]
        + gather_sems(4) * 2,
        compiler_params=pltpu.CompilerParams(
            dimension_semantics=("arbitrary",), collective_id=3, has_side_effects=True,
            vmem_limit_bytes=vmem_bytes,
        ),
        name="rise",
    )(
        tokens, ln_gain, w_up, w_up, w_query, w_key, w_value, conv_w, conv_b, gate_own, gate_b,
        out_gain, skip_gain, w_down, cot,
    )


def own_head():
    first, z, y, x, c = where_am_i()
    return 2 * c + y


def settle_kernel(*refs):
    ins, refs = refs[:16], refs[16:]
    part_ref, tokens_ref, *refs = refs
    (dq_out, dk_out, dv_out, dskip_out, dz_out, g_down_out, g_z_out, g_gain_out,
     block_out, gate_out, *refs) = refs
    state, (gate_rows, gate_all, own, from_core, kept, to_row, from_row, to_owner, owned, *sems) = (
        refs[:5], refs[5:],
    )
    own_sem, c_sent, c_landed, y_sent, y_landed, o_sent, o_landed, h_sent, h_landed = sems
    step = pl.program_id(0)
    first, z, y, x, c = where_am_i()
    head = 2 * c + y
    high, low = halves_of(z, 4)
    half = own.shape[1]
    block = ins[1].shape[0]

    def device(zz, yy, cc):
        return (first + 2 * zz + yy, 2 * x + cc)

    around = [turn(z + k, 4) for k in range(1, 4)]
    order = around + [z]
    group = [(1 - y, c), (y, 1 - c), (1 - y, 1 - c)]

    def rows_of(at, cc):
        return part_ref.at[pl.ds(pl.multiple_of((2 * at + cc) * half, half), half)]

    def load(at):
        return pltpu.make_async_copy(rows_of(at, c), own.at[at], own_sem.at[at])

    def to_c(at):
        return remote(
            rows_of(at, 1 - c), from_core.at[at], c_sent.at[at], c_landed.at[at],
            device(z, y, 1 - c),
        )

    def to_y(zz):
        return remote(
            to_row.at[zz], from_row.at[zz], y_sent.at[zz], y_landed.at[zz], device(z, 1 - y, c)
        )

    def to_o(zz):
        return remote(
            to_owner.at[zz], owned.at[low, c], o_sent.at[zz], o_landed.at[low, c],
            device(zz, y, high),
        )

    def core_sum(at):
        load(at).wait()
        to_c(at).wait_recv()
        return (own[at].astype(f32) + from_core[at].astype(f32)).astype(bf16)

    def core_step(zz):
        to_row[zz] = core_sum(2 * zz + 1 - y)
        to_y(zz).start()
        kept[zz] = core_sum(2 * zz + y)

    def row_sum(zz):
        to_y(zz).wait_recv()
        return (kept[zz].astype(f32) + from_row[zz].astype(f32)).astype(bf16)

    enters = high == c

    def row_step(zz):
        to_owner[zz] = row_sum(zz)
        to_o(zz).start()

    def gate_to(k):
        yy, cc = group[k]
        return remote(
            gate_rows, gate_all.at[head], h_sent.at[k], h_landed.at[head], device(z, yy, cc)
        )

    def gate_from(k):
        at = 2 * group[k][1] + group[k][0]
        return remote(
            gate_rows, gate_all.at[at], h_sent.at[k], h_landed.at[at], device(z, *group[k])
        )

    @pl.when(step == 0)
    def _():
        others = [device(z, yy, cc) for yy, cc in group]
        for zz in around:
            others += [device(zz, y, c), device(zz, y, 1 - c)]
        greet(others)
        for zz in order:
            for yy in (1 - y, y):
                to_c(2 * zz + yy).start()
                load(2 * zz + yy).start()

    now = pl.num_programs(0) - 1 - step
    lanes = pl.ds(pl.multiple_of(now * block, block), block)
    cell_backward_kernel(
        False, None, *ins, dq_out, dk_out, dv_out, dskip_out, dz_out, gate_rows.at[:, lanes],
        g_down_out, g_z_out, g_gain_out, *state,
    )

    for k in range(4):
        pl.when(step == k)(lambda: core_step(order[k]))
    for k, when in enumerate((1, 3, 5)):
        pl.when(step == when)(lambda: row_step(order[k]))

    @pl.when(step == pl.num_programs(0) - 1)
    def _():
        for k in range(3):
            gate_to(k).start()
        gate_all[head] = gate_rows[...]

        @pl.when(enters)
        def _():
            owned[low, c] = row_sum(z)

        @pl.when(jnp.logical_not(enters))
        def _():
            row_step(z)

        for m in range(2):
            for cc in range(2):
                own_part = jnp.logical_and(2 * c + m == z, c == cc)
                landed = remote(
                    to_owner.at[0], owned.at[m, cc], o_sent.at[0], o_landed.at[m, cc],
                    device(2 * c + m, y, cc),
                )
                pl.when(jnp.logical_not(own_part))(lambda: landed.wait_recv())
                here = pl.ds(cc * half, half)
                block_out[m, here] = (
                    tokens_ref[m, here].astype(f32) + owned[m, cc].astype(f32)
                ).astype(bf16)
        for k in range(3):
            gate_from(k).wait_recv()
        heads = gate_all.shape[0]
        for h in range(heads):
            gate_out[h : h + 1, :] = gate_all[h, 0:1, :]
            gate_out[heads + h : heads + h + 1, :] = gate_all[h, 1:2, :]
        for k in range(3):
            gate_to(k).wait_send()
            to_o(order[k]).wait_send()
        pl.when(jnp.logical_not(enters))(lambda: to_o(z).wait_send())
        for zz in range(4):
            to_y(zz).wait_send()
        for at in range(8):
            to_c(at).wait_send()


def settle(
    part, tokens, rows, q, k, v, conv, gate_z, normed, states, norms, weights, cols, cot, rows_in,
    out_gain, skip_gain, w_down,
):
    count, size = q.shape
    width = w_down.shape[1]
    micro, block, _ = tokens.shape
    half = block // 2
    length = chunk_len
    end = count // length - 1
    by_row = lambda n: pl.BlockSpec((length, n), lambda g: (end - g, 0))
    gain = pl.BlockSpec((1, size), lambda g: (0, own_head()), pipeline_mode=pl.Buffered(1))
    kept = lambda value: pl.BlockSpec(
        value.shape, lambda g: (0,) * len(value.shape), pipeline_mode=pl.Buffered(1)
    )
    specs = [pl.BlockSpec((8, length), lambda g: (0, end - g))] + [by_row(size)] * 6
    specs += [
        pl.BlockSpec((1, size, size), lambda g: (end - g, 0, 0)),
        pl.BlockSpec((1, 8, size), lambda g: (end - g, 0, 0)),
        by_row(length), by_row(128), by_row(width), by_row(width), gain, gain,
        pl.BlockSpec((size, width), lambda g: (own_head(), 0), pipeline_mode=pl.Buffered(1)),
        pl.BlockSpec(memory_space=pl.ANY), kept(tokens),
    ]
    whole = [
        struct((2, size, width // 2), bf16), struct((width, size), bf16), struct((8, size), f32),
        struct(tokens.shape, bf16), struct((8, count), f32),
    ]
    outs = [struct((count, size), f32)] * 4 + [struct((count, size), bf16)] + whole
    scratch = [
        ((size, size), f32), ((8, size), f32), ((size, width), f32), ((width, size), f32),
        ((8, size), f32), ((8, count), f32), ((4, 8, count), f32),
        ((8, half, width), bf16), ((8, half, width), bf16), ((4, half, width), bf16),
        ((4, half, width), bf16), ((4, half, width), bf16), ((4, half, width), bf16),
        ((2, 2, half, width), bf16),
    ]
    sems = [(8,), (8,), (8,), (4,), (4,), (4,), (2, 2), (3,), (4,)]
    return pl.pallas_call(
        settle_kernel,
        grid=(count // length,),
        in_specs=specs,
        out_specs=[by_row(size)] * 5 + [kept(value) for value in whole],
        out_shape=outs,
        scratch_shapes=[pltpu.VMEM(shape, dtype) for shape, dtype in scratch]
        + [pltpu.SemaphoreType.DMA(shape) for shape in sems],
        compiler_params=pltpu.CompilerParams(
            dimension_semantics=("arbitrary",), collective_id=2, has_side_effects=True,
            vmem_limit_bytes=60 * 2**20,
        ),
        cost_estimate=pl.CostEstimate(
            flops=2 * count * size * (4 * length + 4 * size + 3 * width),
            bytes_accessed=48 * 2**20, transcendentals=0,
        ),
        name="settle",
    )(
        rows, q, k, v, conv, gate_z, normed, states, norms, weights, cols, cot, rows_in,
        out_gain, skip_gain, w_down, part, tokens,
    )


def drain_kernel(
    d_gate, dq, dk, dv, mix_ref, conv, q_ref, k_ref, v_ref,
    dskip, dskip_next, dz, mix_before, mix_next, normed,
    gate_own, g_gain, w_query, w_key, w_value, w_up, conv_w, conv_b,
    down_ref, lifted_ref, rows_ref, cot_ref, gain_ref, *refs
):
    grad_out, up_out, query_out, key_out, value_out, down_out, small_out, *refs = refs
    w_q, w_k, w_v, w_mix, w_gate, taps_w, taps_b, gate_pairs, q_all, k_all, v_all, *refs = refs
    g_q, g_k, g_v, g_small, rows_all, lifted_all, part_all, *refs = refs
    from_core, kept, to_row, from_row, to_owner, owned, *refs = refs
    give_up, give_square, *refs = refs
    cross_go, cross_got, *refs = refs
    from_x, totals, refs = refs[:3], (*refs[3:6], None, refs[6]), refs[7:]
    from_near, pairs, from_far, ends = (refs[k : 20 : 4] for k in range(4))
    refs = refs[20:]
    up_go, up_got, sq_go, sq_got, dn_go, dn_got, small_x, small_sum, small_z, small_all, *refs = refs
    c_sent, c_landed, y_sent, y_landed, o_sent, o_landed, *refs = refs
    x_sent, x_landed, near_sent, near_landed, far_sent, far_landed, *refs = refs
    cross_sem, w_sem, up_sem, sq_sent, sq_landed, dn_sent, dn_landed, sx_sem, sz_sent, sz_landed, *refs = refs
    sh_sent, sh_landed = refs
    step = pl.program_id(0)
    blocks, block, width = part_all.shape
    half = block // 2
    size = g_q.shape[0]
    first, z, y, x, c = where_am_i()
    head = 2 * c + y
    high, low = halves_of(z, 4)

    def device(zz, yy, cc, xx=x):
        return (first + 2 * zz + yy, 2 * xx + cc)

    around = [turn(z + k, 4) for k in range(1, 4)]
    group = [(1 - y, c), (y, 1 - c), (1 - y, 1 - c)]

    def down_rows(q):
        tall = down_ref.shape[1] // 4
        return pl.ds(q * tall, tall)

    def up_rows(q):
        tall = lifted_ref.shape[0] // 4
        return pl.ds(q * tall, tall)

    def to_x(p, q):
        give = (give_up, give_square)[p].at[q] if p < 2 else down_ref.at[1 - x, down_rows(q)]
        return remote(
            give, from_x[p].at[q], x_sent.at[p, q], x_landed.at[p, q], device(z, y, c, 1 - x)
        )

    def before_near(p, q):
        if p == 3:
            return lifted_ref.at[up_rows(q), pl.ds(size // 2, size // 2)]
        return totals[p].at[q]

    def to_near(p, q):
        return remote(
            before_near(p, q), from_near[p].at[q // 2], near_sent.at[p, q], near_landed.at[p, q],
            device(z + 1 - 2 * low, y, c),
        )

    def start_near(p, q):
        pl.when(low != q % 2)(lambda: to_near(p, q).start())

    def to_far(p, q):
        return remote(
            pairs[p].at[q // 2], from_far[p], far_sent.at[p, q], far_landed.at[p, q],
            device(z + 2 - 4 * high, y, c),
        )

    def x_step(p, q):
        to_x(p, q).wait_recv()
        own = totals[p][q] if p < 2 else down_ref[x, down_rows(q)]
        totals[p][q] = (own.astype(f32) + from_x[p][q].astype(f32)).astype(bf16)
        start_near(p, q)

    def near_step(p, q):
        @pl.when(low == q % 2)
        def _():
            to_near(p, q).wait_recv()
            pairs[p][q // 2] = (
                before_near(p, q)[...].astype(f32) + from_near[p][q // 2].astype(f32)
            ).astype(bf16)
            pl.when(high != q // 2)(lambda: to_far(p, q).start())

    def far_step(p, q):
        @pl.when(z == q)
        def _():
            to_far(p, q).wait_recv()
            total = pairs[p][q // 2].astype(f32) + from_far[p][...].astype(f32)
            ends[p][:, : total.shape[1]] = total

    def to_cross():
        return remote(cross_go, cross_got, cross_sem.at[0], cross_sem.at[1], device(z, y, c, 1 - x))

    def cross(p):
        cross_go[...] = ends[p][...].astype(bf16)
        to_cross().start()

    def weight_copies():
        lanes = pl.ds(pl.multiple_of(head * size, size), size)
        gate_lanes = pl.ds(pl.multiple_of((w_query.shape[0] + head) * size, size), size)
        pairs_of = [
            (w_query.at[head], w_q), (w_key.at[head], w_k), (w_value.at[head], w_v),
            (w_up.at[:, lanes], w_mix), (w_up.at[:, gate_lanes], w_gate),
            (conv_w.at[:, lanes], taps_w), (conv_b.at[:, lanes], taps_b),
        ]
        return [
            pltpu.make_async_copy(src, dst, w_sem.at[k]) for k, (src, dst) in enumerate(pairs_of)
        ]

    def to_c(at):
        there = pl.ds(pl.multiple_of((1 - c) * half, half), half)
        return remote(
            part_all.at[at, there], from_core.at[at], c_sent.at[at], c_landed.at[at],
            device(z, y, 1 - c),
        )

    def to_y(zz):
        return remote(
            to_row.at[zz], from_row.at[zz], y_sent.at[zz], y_landed.at[zz], device(z, 1 - y, c)
        )

    def to_o(zz):
        return remote(
            to_owner.at[zz], owned.at[low, c], o_sent.at[zz], o_landed.at[low, c],
            device(zz, y, high),
        )

    def stays(zz):
        return jnp.logical_and(z == zz, high == c)

    def core_step(at):
        zz, yy = halves_of(at, 8)
        to_c(at).wait_recv()
        here = pl.ds(pl.multiple_of(c * half, half), half)
        value = (part_all[at, here].astype(f32) + from_core[at].astype(f32)).astype(bf16)

        @pl.when(yy == y)
        def _():
            kept[zz] = value

        @pl.when(yy != y)
        def _():
            to_row[zz] = value
            to_y(zz).start()

    def row_step(zz):
        to_y(zz).wait_recv()
        to_owner[zz] = (kept[zz].astype(f32) + from_row[zz].astype(f32)).astype(bf16)

        @pl.when(stays(zz))
        def _():
            owned[low, c] = to_owner[zz]

        pl.when(jnp.logical_not(stays(zz)))(lambda: to_o(zz).start())

    def to_group(k, src, dst, sent, landed):
        yy, cc = group[k]
        return remote(src, dst, sent.at[k], landed, device(z, yy, cc))

    def small_to_x():
        return remote(g_small, small_x, sx_sem.at[0], sx_sem.at[1], device(z, y, c, 1 - x))

    def small_to_z(k):
        return remote(
            small_sum, small_z.at[z], sz_sent.at[k], sz_landed.at[z], device(around[k], y, c)
        )

    def small_from_z(k):
        return remote(
            small_sum, small_z.at[around[k]], sz_sent.at[k], sz_landed.at[around[k]],
            device(around[k], y, c),
        )

    def small_to_head(k):
        return to_group(k, small_all.at[head], small_all.at[head], sh_sent, sh_landed.at[head])

    def small_from_head(k):
        at = 2 * group[k][1] + group[k][0]
        return to_group(k, small_all.at[at], small_all.at[at], sh_sent, sh_landed.at[at])

    def up_to_y():
        return remote(up_go, up_got, up_sem.at[0], up_sem.at[1], device(z, 1 - y, c))

    def square_to(k):
        yy, cc = group[k]
        return to_group(k, sq_go.at[yy, cc], sq_got.at[head], sq_sent, sq_landed.at[head])

    def square_from(k):
        at = 2 * group[k][1] + group[k][0]
        return to_group(k, sq_go.at[0, 0], sq_got.at[at], sq_sent, sq_landed.at[at])

    def down_to(cc):
        return remote(
            dn_go.at[cc], dn_got.at[low], dn_sent.at[cc], dn_landed.at[low],
            device(head, high, cc),
        )

    def down_from(k):
        return remote(
            dn_go.at[0], dn_got.at[k], dn_sent.at[0], dn_landed.at[k],
            device(2 * y + k, low, high),
        )

    home = jnp.logical_and(head == z, high == y)

    @pl.when(step == 0)
    def _():
        others = [device(z, yy, cc) for yy, cc in group] + [device(z, y, c, 1 - x)]
        for zz in around:
            others += [device(zz, yy, cc) for yy, cc in [(y, c)] + group]
        greet(others)
        for q in range(4):
            to_x(2, q).start()
        for q in range(4):
            start_near(3, q)
        for p in range(3):
            one, two, three = split_three(gate_own[8 * p : 8 * p + 8, :])
            gate_pairs[:, size * p : size * p + size] = jnp.concatenate(
                [one, one, one, two, two, three], axis=0
            )
        for copy in weight_copies():
            copy.start()
        for ref in (g_q, g_k, g_v, g_small):
            ref[...] = jnp.zeros_like(ref)
        for ref in (q_all, k_all, v_all):
            ref[blocks * block :] = jnp.zeros_like(ref[blocks * block :])

    order = around + [z]
    tall, wide = size // 4, size // 2

    @pl.when(step < blocks)
    def _():
        lows = lower_first(
            d_gate, dq, dk, dv, mix_ref, conv, q_ref, k_ref, v_ref, gate_pairs, g_q, g_k, g_v, g_small
        )
        here = pl.ds(pl.multiple_of(step * block, block), block)
        for ref, value in zip((q_all, k_all, v_all), lows):
            ref[here] = value

    @pl.when(step == blocks - 1)
    def _():
        for q in range(4):
            rows_q = slice(tall * q, tall * q + tall)
            for at, ref in enumerate((g_q, g_k, g_v)):
                lanes = slice(wide * at, wide * at + wide)
                left, right = ref[rows_q, :wide], ref[rows_q, wide:]
                totals[1][q, :, lanes] = jnp.where(x == 0, left, right).astype(bf16)
                give_square[q, :, lanes] = jnp.where(x == 0, right, left).astype(bf16)
            to_x(1, q).start()
        for copy in weight_copies():
            copy.wait()

    @pl.when(step >= blocks)
    def _():
        now = drain_order(step, blocks)
        here = pl.ds(pl.multiple_of(now * block, block), block)
        more = pl.ds(pl.multiple_of(now * block, block), block + mix_next.shape[0])
        rows, d_mix, d_normed = lower_block(
            now == 0, now == blocks - 1, (q_all[more], k_all[more], v_all[here]),
            dskip, dskip_next, dz, mix_ref, mix_before, mix_next, normed,
            w_q, w_k, w_v, w_mix, w_gate, taps_w, taps_b, g_small,
        )
        rows_all[here] = rows
        lifted_all[here] = d_mix
        part_all[now] = d_normed.astype(bf16)
        to_c(now).start()
        pl.when(step > blocks)(lambda: core_step(drain_order(step - 1, blocks)))

    def at_end(when, *work):
        @pl.when(step == blocks + when)
        def _():
            for do in work:
                do()

    def spread_down():
        span = dn_go.shape[2]
        for cc in range(2):
            dn_go[cc] = ends[2][:, span * cc : span * cc + span].astype(bf16)
            left_here = jnp.logical_and(home, c == cc)

            @pl.when(left_here)
            def _():
                dn_got[low] = dn_go[cc]

            pl.when(jnp.logical_not(left_here))(lambda: down_to(cc).start())

    def every(do, p):
        return [partial(do, p, q) for q in range(4)]

    def early_cross():
        pl.when(x == 0)(lambda: cross(3))

    at_end(-3, *every(near_step, 3))
    at_end(-1, *every(x_step, 2))
    at_end(1, *every(far_step, 3), early_cross)
    at_end(2, *every(near_step, 2), partial(x_step, 1, 0))
    at_end(4, partial(x_step, 1, 1), partial(near_step, 1, 0), *every(far_step, 2), spread_down)
    at_end(5, partial(row_step, order[0]))
    at_end(6, partial(x_step, 1, 2), partial(near_step, 1, 1))
    at_end(7, partial(row_step, order[1]), partial(x_step, 1, 3))

    def norm_back(m, cc):
        own_part = jnp.logical_and(2 * c + m == z, c == cc)
        landed = remote(
            to_owner.at[0], owned.at[m, cc], o_sent.at[0], o_landed.at[m, cc],
            device(2 * c + m, y, cc),
        )
        pl.when(jnp.logical_not(own_part))(lambda: landed.wait_recv())
        rows_here = pl.ds(cc * half, half)
        row_hat, rstd = normalize(rows_ref[m, rows_here].astype(f32))
        scaled = owned[m, cc].astype(f32) * gain_ref[...]
        d_row = rstd * (
            scaled
            - jnp.mean(scaled, axis=-1, keepdims=True)
            - row_hat * jnp.mean(scaled * row_hat, axis=-1, keepdims=True)
        )
        grad_out[m, rows_here] = (cot_ref[m, rows_here].astype(f32) + d_row).astype(bf16)

    def small_after_x():
        small_to_x().wait_recv()
        small_sum[...] = g_small[...] + small_x[...]
        small_z[z] = small_sum[...]
        for k in range(3):
            small_to_z(k).start()

    def small_after_z():
        for k in range(3):
            small_from_z(k).wait_recv()
        total = small_z[0]
        for zz in range(1, 4):
            total = total + small_z[zz]
        small_all[head] = total
        for k in range(3):
            small_to_head(k).start()

    def spread_square():
        for yy in range(2):
            for cc in range(2):
                for a in range(3):
                    sq_go[yy, cc, :, tall * a : tall * a + tall] = ends[1][
                        tall // 2 * yy : tall // 2 * yy + tall // 2,
                        (2 * a + cc) * tall : (2 * a + cc) * tall + tall,
                    ].astype(bf16)
        sq_got[head] = sq_go[y, c]
        for k in range(3):
            square_to(k).start()

    @pl.when(step == 2 * blocks - 1)
    def _():
        g_small[29:32, :] = g_gain[0:3, :]
        small_to_x().start()
        for q in range(4):
            got = mm_tn(rows_all[:, block * q : block * q + block], lifted_all[...]).astype(bf16)
            given = lifted_ref[up_rows(q), :wide]
            totals[0][q] = jnp.where(x == 0, got[:, :wide], given)
            give_up[q] = jnp.where(x == 0, given, got[:, :wide])
            totals[4][q] = got[:, wide:]
            to_x(0, q).start()
            start_near(4, q)
            if q == 0:
                core_step(2 * z + y)
        small_after_x()
        row_step(order[2])
        near_step(1, 2)
        near_step(1, 3)
        x_step(0, 0)
        near_step(4, 0)
        near_step(4, 1)
        far_step(1, 0)
        far_step(1, 1)
        row_step(z)
        x_step(0, 1)
        near_step(4, 2)
        near_step(4, 3)
        small_after_z()
        x_step(0, 2)
        near_step(0, 0)
        near_step(0, 1)
        far_step(1, 2)
        far_step(1, 3)
        spread_square()
        x_step(0, 3)
        for q in range(4):
            far_step(4, q)
        pl.when(x == 1)(lambda: cross(4))
        near_step(0, 2)
        for m in range(2):
            for cc in range(2):
                norm_back(m, cc)
        near_step(0, 3)
        for q in range(4):
            far_step(0, q)
        to_cross().wait_recv()
        kept_half = jnp.where(x == 0, ends[4][...], ends[3][...])
        ends[0][:, wide:] = kept_half + cross_got[...].astype(f32)
        value = ends[0][...]
        mine = jnp.where(y == 0, value[:half], value[half:])
        up_go[...] = jnp.where(y == 0, value[half:], value[:half]).astype(bf16)
        up_to_y().start()
        for yy in range(2):

            @pl.when(y == yy)
            def _():
                up_out[:, size * yy : size * yy + size] = mine

        for k in range(3):
            small_from_head(k).wait_recv()
        small_out[...] = small_all[...]
        for k in range(3):
            square_from(k).wait_recv()
        for a, ref in enumerate((query_out, key_out, value_out)):
            ref[...] = sq_got[:, :, tall * a : tall * a + tall].astype(f32)
        for k in range(2):
            mine = jnp.logical_and(home, jnp.logical_and(low == k, high == c))
            pl.when(jnp.logical_not(mine))(lambda: down_from(k).wait_recv())
            deep = dn_got.shape[1]
            down_out[deep * k : deep * k + deep] = dn_got[k].astype(f32)
        up_to_y().wait_recv()
        for yy in range(2):

            @pl.when(y == yy)
            def _():
                up_out[:, size * (1 - yy) : size * (1 - yy) + size] = up_got[...].astype(f32)

        small_to_x().wait_send()
        up_to_y().wait_send()
        to_cross().wait_send()
        for p in range(5):
            for q in range(4):
                if p < 3:
                    to_x(p, q).wait_send()
                pl.when(low != q % 2)(lambda: to_near(p, q).wait_send())
                passes = jnp.logical_and(low == q % 2, high != q // 2)
                pl.when(passes)(lambda: to_far(p, q).wait_send())
        for at in range(blocks):
            to_c(at).wait_send()
        for zz in range(4):
            to_y(zz).wait_send()
            pl.when(jnp.logical_not(stays(zz)))(lambda: to_o(zz).wait_send())
        for k in range(3):
            small_to_z(k).wait_send()
            small_to_head(k).wait_send()
            square_to(k).wait_send()
        for cc in range(2):
            left_here = jnp.logical_and(home, c == cc)
            pl.when(jnp.logical_not(left_here))(lambda: down_to(cc).wait_send())


def drain_order(step, blocks):
    first, z, y, x, c = where_am_i()
    k, odd = halves_of(jnp.maximum(step - blocks, 0), blocks)
    return 2 * turn(z + 1 + k, 4) + jnp.where(odd == 0, 1 - y, y)


def drain(inputs, down, lifted, rows, cot, gain):
    (d_gate, dq, dk, dv, dskip, dz, mix, conv, q, k, v, normed,
     w_query, w_key, w_value, w_up, conv_w, conv_b, gate_own, g_gain) = inputs
    tokens, size = q.shape
    micro, block, width = rows.shape
    half = block // 2
    lines = 40
    steps = tokens // block
    early = lambda g: jnp.minimum(g, steps - 1)
    late = lambda g: drain_order(g, steps)
    both = lambda g: jnp.where(g < steps, g, drain_order(g, steps))
    edge = lambda at: pl.BlockSpec(
        (16, size), lambda g: (jnp.clip(at(g), 0, tokens // 16 - 1), 0)
    )
    before = edge(lambda g: late(g) * (block // 16) - 1)
    behind = edge(lambda g: (late(g) + 1) * (block // 16))
    by_row = lambda n, at: pl.BlockSpec((block, n), lambda g: (at(g), 0))
    kept = lambda value: pl.BlockSpec(
        value.shape, lambda g: (0,) * value.ndim, pipeline_mode=pl.Buffered(1)
    )
    anywhere = pl.BlockSpec(memory_space=pl.ANY)
    arguments = (
        d_gate, dq, dk, dv, mix, conv, q, k, v, dskip, dskip, dz, mix, mix, normed, gate_own, g_gain,
        w_query, w_key, w_value, w_up, conv_w, conv_b, down, lifted, rows, cot, gain,
    )
    specs = [pl.BlockSpec((8, block), lambda g: (0, early(g)))] + [by_row(size, early)] * 3
    specs += [by_row(size, both)] + [by_row(size, early)] * 4
    specs += [by_row(size, late), behind, by_row(size, late), before, behind, by_row(width, late)]
    specs += [kept(gate_own), kept(g_gain)]
    specs += [anywhere] * 6 + [kept(value) for value in (down, lifted, rows, cot, gain)]
    scratch = [((size, size), bf16)] * 3 + [((width, size), bf16)] * 2
    scratch += [((4, size), f32), ((1, size), f32), ((48, 3 * size), bf16)]
    scratch += [((tokens + 16, size), bf16)] * 3
    scratch += [((size, size), f32)] * 3 + [((lines, size), f32)]
    scratch += [((tokens, width), bf16), ((tokens, size), bf16), ((8, block, width), bf16)]
    scratch += [
        ((8, half, width), bf16), ((4, half, width), bf16), ((4, half, width), bf16),
        ((4, half, width), bf16), ((4, half, width), bf16), ((2, 2, half, width), bf16),
    ]
    up = (width // 4, size // 2)
    pieces = [up, (size // 4, 3 * size // 2), (size // 4, width // 2), up, up]
    scratch += [((4, *piece), bf16) for piece in pieces[:2]] + [(up, bf16)] * 2
    scratch += [((4, *piece), bf16) for piece in pieces[:3] + pieces[:3] + pieces[4:]]
    for piece in pieces:
        scratch += [((2, *piece), bf16)] * 2 + [(piece, bf16), (piece, f32)]
    scratch[-17] = ((up[0], size), f32)
    scratch += [
        ((width // 8, size), bf16), ((width // 8, size), bf16),
        ((2, 2, size // 8, 3 * size // 4), bf16), ((4, size // 8, 3 * size // 4), bf16),
        ((2, size // 4, width // 4), bf16), ((2, size // 4, width // 4), bf16),
        ((lines, size), f32), ((lines, size), f32), ((4, lines, size), f32), ((4, lines, size), f32),
    ]
    sems = [(8,), (8,), (4,), (4,), (4,), (2, 2)] + [(5, 4)] * 6
    sems += [(2,), (7,), (2,), (3,), (4,), (2,), (2,), (2,), (3,), (4,), (3,), (4,)]
    square = struct((4, size // 8, size // 4), f32)
    outs = [
        struct(rows.shape, bf16), struct((width // 8, 2 * size), f32), square, square, square,
        struct((size // 2, width // 4), f32), struct((4, lines, size), f32),
    ]
    return pl.pallas_call(
        drain_kernel,
        grid=(2 * steps,),
        in_specs=specs,
        out_specs=[kept(value) for value in outs],
        scratch_shapes=[pltpu.VMEM(shape, dtype) for shape, dtype in scratch]
        + [pltpu.SemaphoreType.DMA(shape) for shape in sems],
        out_shape=outs,
        compiler_params=pltpu.CompilerParams(
            dimension_semantics=("arbitrary",), collective_id=1, has_side_effects=True,
            vmem_limit_bytes=60 * 2**20,
        ),
        cost_estimate=pl.CostEstimate(
            flops=2 * tokens * size * (6 * size + 4 * width), bytes_accessed=48 * 2**20,
            transcendentals=0,
        ),
        name="drain",
    )(*arguments)


def spread_kernel(small, gain, *refs):
    count = (len(refs) - 7) // 2
    for k in range(count):
        refs[count + 7 + k][...] = refs[k][...]
    ln_out, conv_out, bias_out, gate_out, forget_out, out_gain, skip_gain = refs[count : count + 7]
    heads, _, size = small.shape
    total = small[0, 32:34, :]
    for h in range(1, heads):
        total = total + small[h, 32:34, :]
    for k in range(2):
        lanes = slice(size * k, size * k + size)
        ln_out[:, lanes] = total[k : k + 1, :] / gain[:, lanes]
    for h in range(heads):
        lanes = slice(size * h, size * h + size)
        conv_out[:, lanes] = small[h, 24:28, :]
        bias_out[:, lanes] = small[h, 28:29, :]
        out_gain[:, lanes] = small[h, 29:30, :]
        skip_gain[:, lanes] = small[h, 30:31, :]
        forget_out[:, h : h + 1] = small[h, 31:32, 0:1]
        for p in range(3):
            start = (heads * p + h) * size
            gate_out[:, start : start + size] = small[h, 8 * p : 8 * p + 8, :]


def spread(small, gain, *made):
    heads, _, size = small.shape
    inner = heads * size
    shapes = [gain.shape, (4, inner), (1, inner), (8, 3 * inner), (1, heads), (1, inner), (1, inner)]
    return pl.pallas_call(
        spread_kernel,
        out_shape=[struct(shape, f32) for shape in shapes]
        + [struct(value.shape, value.dtype) for value in made],
        name="spread",
        compiler_params=pltpu.CompilerParams(vmem_limit_bytes=62 * 2**20),
    )(small, gain, *made)


def swap(value, axis, mask):
    count = lax.axis_size(axis)
    return lax.ppermute(value, axis, [(s, s ^ mask) for s in range(count)])


def part_of(value, at, count, axis):
    size = value.shape[axis] // count
    return lax.dynamic_slice_in_dim(value, at * size, size, axis)


def halved(value, bit, dim, axis, mask):
    kept = part_of(value, bit, 2, dim).astype(f32)
    return kept + swap(part_of(value, 1 - bit, 2, dim), axis, mask).astype(f32)


def paired(mine, other, bit, dim):
    return jnp.where(
        bit == 0, jnp.concatenate([mine, other], dim), jnp.concatenate([other, mine], dim)
    )


def place():
    at_seq, at_batch = lax.axis_index("seq"), lax.axis_index("batch")
    return (at_seq % 8) // 2, at_seq % 2, at_batch // 2, at_batch % 2


def sent_across(blocks, z):
    got = [lax.dynamic_index_in_dim(blocks, z, 0, keepdims=False)]
    for k in range(1, 4):
        got.append(swap(lax.dynamic_index_in_dim(blocks, z ^ k, 0, keepdims=False), "seq", 2 * k))
    return got


def in_order(got, z):
    got = jnp.stack(got)
    return jnp.stack([lax.dynamic_index_in_dim(got, z ^ k, 0, keepdims=False) for k in range(4)])


def gather_sequence(own):
    z, y, x, c = place()
    micro, rows, width = own.shape
    slots = paired(own, swap(own, "batch", 1), c, 0)
    blocks = in_order(sent_across(part_of(slots, c, 2, 2), z), z)[:, None]
    both = paired(blocks, swap(blocks, "seq", 1), y, 1)
    return paired(both, swap(both, "batch", 1), c, 3).reshape(8 * rows, width)


def scatter_first(parts):
    z, y, x, c = place()
    blocks = parts.reshape(4, 2, -1, parts.shape[1])
    return halved(blocks, c, 2, "batch", 1).astype(bf16)


def scatter_last(slots):
    z, y, x, c = place()
    other = swap(part_of(slots, 1 - c, 2, 0), "batch", 1)
    return paired(part_of(slots, c, 2, 0), other, c, 1).astype(f32)


def scatter_sequence(parts):
    z, y, x, c = place()
    blocks = scatter_first(parts)
    blocks = halved(blocks, y, 1, "seq", 1).astype(bf16)[:, 0]
    return scatter_last(in_order(sent_across(blocks, z), z))


def total_over_heads(value):
    value = value + swap(value, "batch", 1)
    return value + swap(value, "seq", 1)


def over_ranges(value, count):
    size = lax.axis_size("seq")
    groups = [[first + 8 * k for k in range(count)] for first in range(8)]
    return lax.all_gather(value, "seq", axis_index_groups=groups) if size > 8 else value[None]


def state_before(state, norm, level, total, ranges):
    index = lax.axis_index("seq") // 8
    summary = (state, norm[0], level[0, 0], total)
    everything = jax.tree.map(lambda part: over_ranges(part, ranges), summary)
    before = state_identity(summary)
    for k in range(ranges - 1):
        new = combine_states(before, jax.tree.map(lambda part: part[k], everything))
        before = jax.tree.map(lambda a, b: jnp.where(k < index, a, b), new, before)
    return (
        before[0],
        jnp.broadcast_to(before[1], norm.shape),
        jnp.broadcast_to(before[2], level.shape),
    )


def cotangent_after(d_state, d_norm, keep, ranges):
    index = lax.axis_index("seq") // 8
    own = (d_state, d_norm)
    everything = jax.tree.map(lambda part: over_ranges(part, ranges), own)
    keeps = over_ranges(keep, ranges)
    after = jax.tree.map(jnp.zeros_like, own)
    for k in range(ranges - 1, 0, -1):
        new = jax.tree.map(lambda a, b: a[k] + keeps[k] * b, everything, after)
        after = jax.tree.map(lambda a, b: jnp.where(k > index, a, b), new, after)
    return after


def reduce_blocks(at, up, square, down, heads):
    count, batch_count = lax.axis_size("seq"), lax.axis_size("batch")
    g_m, g_z = up
    width, size = g_m.shape
    half = size // 2
    squares = [
        jnp.concatenate([square[0, :, k : k + half], square[1, :, k : k + half]], 1)
        for k in range(0, 3 * half, half)
    ]
    g_down = jnp.concatenate([down[0], down[1]], 1)
    inner = heads * size
    up = jnp.zeros((width, 2 * inner), f32)
    up = lax.dynamic_update_slice_in_dim(up, g_m.astype(f32), at * size, 1)
    up = lax.dynamic_update_slice_in_dim(up, g_z.astype(f32), inner + at * size, 1)
    down = lax.dynamic_update_slice_in_dim(
        jnp.zeros((inner, width), f32), g_down.astype(f32), at * size, 0
    )
    full = [up, down]
    for g in squares:
        full.append(
            lax.dynamic_update_slice_in_dim(
                jnp.zeros((heads, size, size), f32), g.astype(f32)[None], at, 0
            )
        )
    blocks = tuple(to_device_blocks(g, count, batch_count) for g in full)
    pieces = lax.psum_scatter(blocks, ("seq", "batch"), scatter_dimension=0, tiled=True)
    s_up, s_down, s_query, s_key, s_value = tuple(p[0] for p in pieces)
    return s_up, jnp.stack([s_query, s_key, s_value], 1), s_down


def head_device(
    tokens, ln_gain, w_up, conv_w, conv_b, w_query, w_key, w_value, gate_w, gate_b,
    out_gain, skip_gain, w_down, d_out,
):
    z, y, x, c = place()
    at = 2 * c + y
    ranges = lax.axis_size("seq") // 8
    direct = ranges == 1 and lax.axis_size("batch") == 4
    head = jnp.reshape(at, (1,)).astype(jnp.int32)
    heads, size, _ = w_query.shape
    inner = heads * size
    conv_row = conv_b.reshape(1, inner)
    out_row = out_gain.reshape(1, inner)
    skip_row = skip_gain.reshape(1, inner)

    gate_own = lax.dynamic_index_in_dim(
        gate_w.reshape(3, heads, size, 8), at, 1, keepdims=False
    ).transpose(0, 2, 1)
    gate_rows = gate_own.reshape(24, size)
    high = lax.reduce_precision(gate_own, 8, 7)
    middle = lax.reduce_precision(gate_own - high, 8, 7)
    low = lax.reduce_precision(gate_own - high - middle, 8, 7)
    gate_parts = jnp.concatenate([high, middle, low, jnp.zeros_like(high)], 1).astype(bf16)
    gate_pairs = (
        jnp.concatenate([high, high, high, middle, middle, low], 1)
        .astype(bf16)
        .transpose(1, 0, 2)
        .reshape(48, 3 * size)
    )

    if direct:
        (normed, mix, conv, q, k, v, gate_z,
         part, head_normed, states, norms, weights, cols, rows, cot) = rise(
            tokens[:, 0], ln_gain[None], w_up, w_query, w_key, w_value, conv_w, conv_row, gate_rows, gate_b,
            out_row, skip_row, w_down, d_out[:, 0],
        )
    else:
        normed = gather_normed(tokens[:, 0], ln_gain[None])
        cot = gather_sequence(d_out[:, 0])
        first = () if ranges == 1 else (shifted(normed[-16:], "seq", 8),)
        mix, conv, q, k, v, gate_z, gates, *halo = lift(
            head, normed, w_up, w_query, w_key, w_value, conv_w, conv_row, gate_parts, *first
        )
        gates = total_over_heads(gates)
        gates = jnp.concatenate(
            [
                lax.dynamic_slice_in_dim(gates, at, 1, 0),
                lax.dynamic_slice_in_dim(gates, heads + at, 1, 0)
                + lax.dynamic_slice_in_dim(gate_b, at, 1, 0)[:, None],
            ]
        )
        first = ()
        if ranges > 1:
            first = (
                jnp.zeros((size, size), f32),
                jnp.zeros((8, size), f32),
                jnp.full((8, 128), floor_value, f32),
            )
            *_, state, norm, level = cell_forward(
                head, gates, q, k, v, conv, gate_z, out_row, skip_row, w_down, *first
            )
            total = jnp.sum(jax.nn.log_sigmoid(gates[1]))
            first = state_before(state, norm, level, total, ranges)
        part, head_normed, states, norms, weights, cols, rows, *last = cell_forward(
            head, gates, q, k, v, conv, gate_z, out_row, skip_row, w_down, *first
        )
    cell_args = (
        rows, q, k, v, conv, gate_z, head_normed, states, norms, weights, cols, cot, normed,
        out_row, skip_row, w_down,
    )
    if direct:
        dq, dk, dv, dskip, dz, g_down, g_z, g_gain, block_rows, d_gate = settle(
            part, tokens[:, 0], *cell_args
        )
    else:
        block_rows = (tokens[:, 0].astype(f32) + scatter_sequence(part)).astype(bf16)
        after = ()
        if ranges > 1:
            after = (jnp.zeros((size, size), f32), jnp.zeros((8, size), f32))
            *_, d_state, d_norm = cell_backward(head, *cell_args, *after)
            keep = jnp.exp(total + first[2][0, 0] - last[2][0, 0])
            after = cotangent_after(d_state, d_norm, keep, ranges)
        dq, dk, dv, dskip, dz, d_rows, g_down, g_z, g_gain, *_ = cell_backward(
            head, *cell_args, *after
        )
        index = jnp.arange(2 * heads)[:, None]
        d_gate = jnp.where(
            index == at, d_rows[0:1], jnp.where(index == heads + at, d_rows[1:2], 0.0)
        )
        d_gate = total_over_heads(d_gate)
    lower_args = (
        d_gate, dq, dk, dv, dskip, dz, mix, conv, q, k, v, normed,
        w_query, w_key, w_value, w_up, conv_w, conv_row, gate_pairs, g_gain,
    )
    if direct:
        grad_rows, s_up, s_query, s_key, s_value, s_down, small = drain(
            (*lower_args[:18], gate_rows, g_gain), g_down, g_z, tokens[:, 0], d_out[:, 0], ln_gain[None]
        )
    else:
        first = ()
        if ranges > 1:
            *_, later = lower(head, *lower_args, halo[0], jnp.zeros((8, size), f32))
            first = (halo[0], shifted(later, "seq", -8))
        d_part, square, up, small, *_ = lower(head, *lower_args, *first)
    if not direct:
        d_normed = scatter_sequence(d_part)
        row_f = tokens[:, 0].astype(f32)
        centre = row_f - jnp.mean(row_f, axis=-1, keepdims=True)
        rstd = lax.rsqrt(jnp.mean(centre * centre, axis=-1, keepdims=True) + norm_epsilon)
        row_hat = centre * rstd
        scaled = d_normed * ln_gain
        d_row = rstd * (
            scaled
            - jnp.mean(scaled, axis=-1, keepdims=True)
            - row_hat * jnp.mean(scaled * row_hat, axis=-1, keepdims=True)
        )
        grad_rows = (d_out[:, 0].astype(f32) + d_row).astype(bf16)
        s_up, squares, s_down = reduce_blocks(at, up, square, g_down, heads)
        s_query, s_key, s_value = squares[:, 0], squares[:, 1], squares[:, 2]
        small = jnp.where(jnp.arange(heads)[:, None, None] == at, small, 0.0)
        small = lax.psum(small, ("seq", "batch"))
    (s_ln, s_conv_w, s_conv_b, s_gate_w, s_gate_b, s_out_gain, s_skip,
     block_rows, grad_rows, s_up, s_query, s_key, s_value, s_down) = spread(
        small, ln_gain[None], block_rows, grad_rows, s_up, s_query, s_key, s_value, s_down
    )
    return (
        block_rows[:, None],
        grad_rows[:, None],
        s_ln[0],
        s_up,
        s_conv_w,
        s_conv_b[0],
        s_query,
        s_key,
        s_value,
        s_gate_w.T,
        s_gate_b[0],
        s_out_gain[0],
        s_skip[0],
        s_down,
    )


def solution(mesh):
    placed = (P(None, "batch", "seq", None),) + (P(),) * 12 + (P(None, "batch", "seq", None),)
    return jax.shard_map(
        head_device,
        mesh=mesh,
        in_specs=placed,
        out_specs=(
            P(None, "batch", "seq", None),
            P(None, "batch", "seq", None),
            P(),
            P("seq", "batch"),
            P(),
            P(),
            P(None, "seq", "batch"),
            P(None, "seq", "batch"),
            P(None, "seq", "batch"),
            P(),
            P(),
            P(),
            P(),
            P("seq", "batch"),
        ),
        check_vma=False,
    )
```

```python
from functools import partial

import jax
import jax.numpy as jnp
from jax import lax
from jax.experimental import pallas as pl
from jax.experimental.pallas import tpu as pltpu
from jax.sharding import PartitionSpec as P

norm_epsilon = 1e-05
floor_value = -1e30


def shifted(value, axis, steps):
    count = lax.axis_size(axis)
    initial, last = (max(0, -steps), min(count, count - steps))
    return lax.ppermute(value, axis, [(source, source + steps) for source in range(initial, last)])


def combine_states(earlier, later):
    top = jnp.maximum(later[3] + earlier[2], later[2])
    keep_first = jnp.exp(later[3] + earlier[2] - top)
    keep_second = jnp.exp(later[2] - top)
    merged_c = keep_first[..., None, None] * earlier[0] + keep_second[..., None, None] * later[0]
    merged_n = keep_first[..., None] * earlier[1] + keep_second[..., None] * later[1]
    return (merged_c, merged_n, top, earlier[3] + later[3])


def state_identity(template):
    return (
        jnp.zeros_like(template[0]),
        jnp.zeros_like(template[1]),
        jnp.full_like(template[2], floor_value),
        jnp.zeros_like(template[3]),
    )


def head_output(hidden, out_gain, skip_gain, conv_out, gate_z):
    centre = hidden - jnp.mean(hidden, axis=-1, keepdims=True)
    spread = jnp.mean(centre * centre, axis=-1, keepdims=True)
    normed = centre * lax.rsqrt(spread + norm_epsilon)
    flat_out = normed.transpose(1, 0, 2).reshape(hidden.shape[1], -1) * out_gain
    return (flat_out + skip_gain * conv_out) * jax.nn.silu(gate_z)


def output_tail(
    query_f,
    key_f,
    value_f,
    gate_pre,
    conv_f,
    gate_z,
    out_gain,
    skip_gain,
    state_c,
    state_n,
    state_m,
):
    head_count = gate_pre.shape[1] // 2
    in_gate = gate_pre[:, :head_count].T
    log_forget = jax.nn.log_sigmoid(gate_pre[:, head_count:]).T
    hidden = cell_hidden(
        to_heads(query_f, head_count),
        to_heads(key_f, head_count),
        to_heads(value_f, head_count),
        in_gate,
        log_forget,
        state_c,
        state_n,
        state_m,
    )
    return head_output(hidden, out_gain, skip_gain, conv_f, gate_z)


def state_tail(key_f, value_f, gate_pre, state_c, state_n, state_m):
    head_count = gate_pre.shape[1] // 2
    in_gate = gate_pre[:, :head_count].T
    log_forget = jax.nn.log_sigmoid(gate_pre[:, head_count:]).T
    return cell_state(
        to_heads(key_f, head_count),
        to_heads(value_f, head_count),
        in_gate,
        log_forget,
        state_c,
        state_n,
        state_m,
    )


def to_device_blocks(grad_full, seq_count, batch_count):
    if grad_full.ndim == 2:
        rows, cols = grad_full.shape
        split = grad_full.reshape(seq_count, rows // seq_count, batch_count, cols // batch_count)
        return split.transpose(0, 2, 1, 3).reshape(
            seq_count * batch_count, rows // seq_count, cols // batch_count
        )
    heads, rows, cols = grad_full.shape
    split = grad_full.reshape(heads, seq_count, rows // seq_count, batch_count, cols // batch_count)
    return split.transpose(1, 3, 0, 2, 4).reshape(
        seq_count * batch_count, heads, rows // seq_count, cols // batch_count
    )


f32 = jnp.float32
bf16 = jnp.bfloat16
chunk_len = 256
wide_len = 512
vmem_bytes = 56 * 1024 * 1024


def mm(a, b):
    return lax.dot_general(a, b, (((1,), (0,)), ((), ())), preferred_element_type=f32)


def mm_nt(a, b):
    return lax.dot_general(a, b, (((1,), (1,)), ((), ())), preferred_element_type=f32)


def mm_tn(a, b):
    return lax.dot_general(a, b, (((0,), (0,)), ((), ())), preferred_element_type=f32)


def split_three(value):
    high = value.astype(bf16)
    rest = value - high.astype(f32)
    middle = rest.astype(bf16)
    low = (rest - middle.astype(f32)).astype(bf16)
    return high, middle, low


def conv_taps(ext, length):
    return [pltpu.roll(ext, 3 - j, 0)[8 : 8 + length] if j < 3 else ext[8 : 8 + length] for j in range(4)]


def lift_kernel(chained, head_ref, normed, w_mix, w_gate, w_q, w_k, w_v, conv_w, conv_b, gate_w, *refs):
    if chained:
        rows_before, *refs, halo_out, carry = refs
    else:
        *refs, carry = refs
    mix_out, conv_out, q_out, k_out, v_out, z_out, gate_out = refs
    length = normed.shape[0]

    @pl.when(pl.program_id(0) == 0)
    def _():
        if chained:
            mix_before = mm(rows_before[...], w_mix[...]).astype(bf16)
            halo_out[...] = mix_before
            carry[...] = mix_before[8:16].astype(f32)
        else:
            carry[...] = jnp.zeros_like(carry)

    rows = normed[...]
    mix = mm(rows, w_mix[...]).astype(bf16)
    mix_out[...] = mix
    z_out[...] = mm(rows, w_gate[...])
    mix_f = mix.astype(f32)
    taps = conv_taps(jnp.concatenate([carry[...], mix_f], axis=0), length)
    carry[...] = mix_f[length - 8 :]
    summed = conv_b[...]
    for j in range(4):
        summed = summed + conv_w[j : j + 1, :] * taps[j]
    conv = (summed * jax.nn.sigmoid(summed)).astype(bf16)
    conv_out[...] = conv
    q = mm(conv, w_q[0]).astype(bf16)
    k = mm(conv, w_k[0]).astype(bf16)
    v = mm(mix, w_v[0]).astype(bf16)
    q_out[...] = q
    k_out[...] = k
    v_out[...] = v
    parts = mm_nt(gate_w[0], q) + mm_nt(gate_w[1], k) + mm_nt(gate_w[2], v)
    gate_out[...] = parts[0:8] + parts[8:16] + parts[16:24]


def gate_rows(gates, causal, diagonal):
    in_row = gates[0:1, :]
    pre = gates[1:2, :]
    log_forget = jnp.minimum(pre, 0.0) - jnp.log1p(jnp.exp(-jnp.abs(pre)))
    run_col = jnp.sum(jnp.where(causal, log_forget, 0.0), axis=1, keepdims=True)
    run_row = jnp.sum(jnp.where(diagonal, run_col, 0.0), axis=0, keepdims=True)
    return in_row - run_row, run_col, log_forget


def masks(length):
    row = lax.broadcasted_iota(jnp.int32, (length, length), 0)
    col = lax.broadcasted_iota(jnp.int32, (length, length), 1)
    return row >= col, row == col


def cell_recur(gates, q_ref, k_ref, v_ref, state_out, norm_out, weight_out, row_out, state, norm, level):
    length = q_ref.shape[0]
    head_size = q_ref.shape[1]
    scale = head_size ** (-0.5)
    causal, diagonal = masks(length)
    a_row, run_col, log_forget = gate_rows(gates[...], causal, diagonal)
    before = level[0:1, 0:1]
    top = jnp.maximum(
        before, jnp.max(jnp.where(causal, a_row, floor_value), axis=1, keepdims=True)
    )
    decay = jnp.exp(jnp.where(causal, a_row - top, floor_value))
    q = q_ref[...]
    k = k_ref[...]
    v = v_ref[...]
    q_f = q.astype(f32)
    weights = decay * (mm_nt(q, k) * scale)
    weights_low = weights.astype(bf16)
    weight_out[...] = weights_low
    from_state = jnp.exp(before - top)
    state_low = state[...].astype(bf16)
    state_out[0] = state_low
    norm_row = norm[0:1, :]
    norm_out[0] = norm[...]
    numerator = mm(weights_low, v) + (from_state * scale) * mm(q, state_low)
    denominator = jnp.sum(weights, axis=1, keepdims=True) + (from_state * scale) * jnp.sum(
        q_f * norm_row, axis=1, keepdims=True
    )
    floor = jnp.exp(-(run_col + top))
    size = jnp.abs(denominator)
    inverse = 1.0 / jnp.maximum(size, floor)
    hidden = numerator * inverse
    slope = jnp.where(
        size > floor, jnp.where(denominator > 0, 1.0, -1.0) * inverse * norm_epsilon, 0.0
    )
    sub = lax.broadcasted_iota(jnp.int32, (8, length), 0)
    row_out[...] = jnp.where(sub == 0, a_row, 1.0 - jnp.exp(log_forget))
    last = top[length - 1 : length, :]
    a_col = jnp.sum(jnp.where(diagonal, a_row, 0.0), axis=1, keepdims=True)
    weighted = k.astype(f32) * jnp.exp(a_col - last)
    keep = jnp.exp(before - last)
    state[...] = keep * state[...] + mm_tn(weighted.astype(bf16), v)
    norm[...] = keep * norm[...] + jnp.sum(weighted, axis=0, keepdims=True)
    level[...] = jnp.broadcast_to(run_col[length - 1 : length, :] + last, level.shape)
    lane = lax.broadcasted_iota(jnp.int32, (length, 128), 1)
    packed = jnp.where(lane == 1, inverse, slope)
    packed = jnp.where(lane == 2, from_state, packed)
    return hidden, jnp.where(lane == 3, top, packed)


def cell_head(hidden, cols, conv_ref, z_ref, out_gain, skip_gain, w_down, part_out, normed_out, col_out):
    centre = hidden - jnp.mean(hidden, axis=1, keepdims=True)
    spread = jnp.mean(centre * centre, axis=1, keepdims=True)
    rstd = lax.rsqrt(spread + norm_epsilon)
    normed = centre * rstd
    normed_out[...] = normed
    gate_z = z_ref[...]
    gated = (normed * out_gain[...] + skip_gain[...] * conv_ref[...].astype(f32)) * (
        gate_z * jax.nn.sigmoid(gate_z)
    )
    part_out[...] = mm(gated.astype(bf16), w_down[...]).astype(bf16)
    lane = lax.broadcasted_iota(jnp.int32, cols.shape, 1)
    cols = jnp.where(lane == 0, rstd, cols)
    col_out[...] = jnp.where(lane == 4, cols * (rstd * rstd), cols)


def cell_forward_kernel(
    chained, head_ref, gates, q_ref, k_ref, v_ref, conv_ref, z_ref, out_gain, skip_gain, w_down, *refs
):
    if chained:
        *first, part_out, normed_out, state_out, norm_out, weight_out, col_out, row_out = refs[:10]
        *final, state, norm, level = refs[10:]
    else:
        part_out, normed_out, state_out, norm_out, weight_out, col_out, row_out = refs[:7]
        state, norm, level = refs[7:]

    @pl.when(pl.program_id(0) == 0)
    def _():
        if chained:
            for ref, value in zip((state, norm, level), first):
                ref[...] = value[...]
        else:
            state[...] = jnp.zeros_like(state)
            norm[...] = jnp.zeros_like(norm)
            level[...] = jnp.full_like(level, floor_value)

    hidden, cols = cell_recur(
        gates, q_ref, k_ref, v_ref, state_out, norm_out, weight_out, row_out, state, norm, level
    )
    cell_head(
        hidden, cols, conv_ref, z_ref, out_gain, skip_gain, w_down, part_out, normed_out, col_out
    )
    if chained:
        for ref, value in zip(final, (state, norm, level)):
            ref[...] = value[...]


def cell_backward_kernel(
    chained, head_ref, rows_ref, q_ref, k_ref, v_ref, conv_ref, z_ref, normed_ref, state_ref, norm_ref,
    weight_ref, col_ref, cot_ref, rows_in, out_gain, skip_gain, w_down, *refs
):
    if chained:
        first, refs = refs[:2], refs[2:]
    dq_out, dk_out, dv_out, dskip_out, dz_out, gate_out, g_down_out, g_z_out, g_gain_out, *refs = refs
    *final, d_state, d_norm, g_down, g_z, g_gain = refs
    length = q_ref.shape[0]
    head_size = q_ref.shape[1]
    scale = head_size ** (-0.5)

    @pl.when(pl.program_id(0) == 0)
    def _():
        if chained:
            d_state[...] = first[0][...]
            d_norm[...] = first[1][...]
        else:
            d_state[...] = jnp.zeros_like(d_state)
            d_norm[...] = jnp.zeros_like(d_norm)
        g_down[...] = jnp.zeros_like(g_down)
        g_z[...] = jnp.zeros_like(g_z)
        g_gain[...] = jnp.zeros_like(g_gain)

    causal, diagonal = masks(length)
    rstd = col_ref[:, 0:1]
    inverse = col_ref[:, 1:2]
    from_state = col_ref[:, 2:3]
    top = col_ref[:, 3:4]
    factor = col_ref[:, 4:5]
    a_row = rows_ref[0:1, :]
    q = q_ref[...]
    k = k_ref[...]
    v = v_ref[...]
    q_f = q.astype(f32)
    k_f = k.astype(f32)
    conv = conv_ref[...].astype(f32)
    normed = normed_ref[...]
    gate_z = z_ref[...]
    cot = cot_ref[...]
    opened = jax.nn.sigmoid(gate_z)
    silu = gate_z * opened
    head_in = normed * out_gain[...] + skip_gain[...] * conv
    g_down[...] += mm_tn((head_in * silu).astype(bf16), cot)
    d_gated = mm_nt(cot, w_down[...])
    d_z = (d_gated * head_in * (opened * (1.0 + gate_z * (1.0 - opened)))).astype(bf16)
    dz_out[...] = d_z
    g_z[...] += mm_tn(rows_in[...], d_z)
    d_head = d_gated * silu
    g_gain[0:1, :] += jnp.sum(d_head * normed, axis=0, keepdims=True)
    g_gain[1:2, :] += jnp.sum(d_head * conv, axis=0, keepdims=True)
    dskip_out[...] = skip_gain[...] * d_head
    d_hat = d_head * out_gain[...]
    along = jnp.sum(d_hat * normed, axis=1, keepdims=True)
    d_hidden = rstd * (
        d_hat - jnp.mean(d_hat, axis=1, keepdims=True) - normed * (along / head_size)
    )
    d_num = d_hidden * inverse
    d_den = -along * factor
    d_num_low = d_num.astype(bf16)
    decay = jnp.exp(jnp.where(causal, a_row - top, floor_value))
    d_scores = ((mm_nt(d_num_low, v) + d_den) * (decay * scale)).astype(bf16)
    through = from_state * scale
    dq_near = mm(d_scores, k)
    dq_far = (
        mm_nt((d_num * through).astype(bf16), state_ref[0])
        + (through * d_den) * norm_ref[0, 0:1, :]
    )
    last = top[length - 1 : length, :]
    keep = from_state[length - 1 : length, :]
    a_col = jnp.sum(jnp.where(diagonal, a_row, 0.0), axis=1, keepdims=True)
    key_weight = jnp.exp(a_col - last)
    d_state_low = d_state[...].astype(bf16)
    dk_near = mm_tn(d_scores, q)
    dk_far = key_weight * (mm_nt(v, d_state_low) + d_norm[0:1, :])
    dv = mm_tn(weight_ref[...], d_num_low) + mm((k_f * key_weight).astype(bf16), d_state_low)
    dq_out[...] = dq_near + dq_far
    dk_out[...] = dk_near + dk_far
    dv_out[...] = dv
    held = state_ref[0].astype(f32) * d_state[...]
    held = jnp.sum(jnp.sum(held, axis=0, keepdims=True) + norm_ref[0, 0:1, :] * d_norm[0:1, :])
    q_state = q_f * through
    d_state[...] = keep * d_state[...] + mm_tn(q_state.astype(bf16), d_num_low)
    d_norm[...] = keep * d_norm[...] + jnp.sum(q_state * d_den, axis=0, keepdims=True)
    q_dot = jnp.sum(q_f * (dq_near + dq_far), axis=1, keepdims=True)
    k_near = jnp.sum(k_f * dk_near, axis=1, keepdims=True)
    k_far = jnp.sum(k_f * dk_far, axis=1, keepdims=True)
    d_in = jnp.sum(jnp.where(diagonal, k_near + k_far, 0.0), axis=0, keepdims=True)
    d_log = jnp.sum(
        jnp.where(causal, q_dot - k_near, jnp.where(diagonal, 0.0, k_far)), axis=0, keepdims=True
    )
    d_log = d_log + keep * held
    sub = lax.broadcasted_iota(jnp.int32, (8, length), 0)
    d_pre = d_log * rows_ref[1:2, :]
    gate_out[...] = jnp.where(sub == 0, d_in, d_pre)
    g_gain[2:3, :] += jnp.broadcast_to(jnp.sum(d_pre, axis=1, keepdims=True), (1, head_size))

    @pl.when(pl.program_id(0) == pl.num_programs(0) - 1)
    def _():
        if chained:
            final[0][...] = d_state[...]
            final[1][...] = d_norm[...]
        half = g_down.shape[1] // 2
        g_down_out[0] = g_down[:, :half].astype(bf16)
        g_down_out[1] = g_down[:, half:].astype(bf16)
        g_z_out[...] = g_z[...].astype(bf16)
        g_gain_out[...] = g_gain[...]


def lower_first(d_gate, dq_ref, dk_ref, dv_ref, mix_ref, conv_ref, q_ref, k_ref, v_ref, gate_w,
                g_q, g_k, g_v, g_small):
    high, middle, low = split_three(d_gate[...])
    left = jnp.concatenate([high, middle, low, high, middle, high], axis=0)
    d_joined = mm_tn(left, gate_w[...])
    size = q_ref.shape[1]
    query_low = (dq_ref[...] + d_joined[:, :size]).astype(bf16)
    key_low = (dk_ref[...] + d_joined[:, size : 2 * size]).astype(bf16)
    value_low = (dv_ref[...] + d_joined[:, 2 * size :]).astype(bf16)
    conv = conv_ref[...]
    g_q[...] += mm_tn(conv, query_low)
    g_k[...] += mm_tn(conv, key_low)
    g_v[...] += mm_tn(mix_ref[...], value_low)
    three = jnp.concatenate([high, middle, low], axis=0)
    for at, ref in enumerate((q_ref, k_ref, v_ref)):
        got = mm(three, ref[...])
        g_small[8 * at : 8 * at + 8, :] += got[0:8] + got[8:16] + got[16:24]
    return query_low, key_low, value_low


def lower_second(
    edge, last, lows, dskip_ref, dz_ref, mix_ref, mix_before, normed, w_q, w_k, w_v, w_mix, w_gate,
    conv_w, conv_b, g_gain, g_small, later,
):
    query_low, key_low, value_low = lows
    length, size = mix_ref.shape
    mix = mix_ref[...]
    d_conv = dskip_ref[...] + mm_nt(query_low, w_q[...]) + mm_nt(key_low, w_k[...])
    halo = jnp.where(last, edge, mix_before[8:16, :].astype(f32))
    taps = conv_taps(jnp.concatenate([halo, mix.astype(f32)], axis=0), length)
    summed = conv_b[...]
    for j in range(4):
        summed = summed + conv_w[j : j + 1, :] * taps[j]
    opened = jax.nn.sigmoid(summed)
    d_summed = d_conv * (opened * (1.0 + summed * (1.0 - opened)))
    for j in range(4):
        g_small[24 + j : 25 + j, :] += jnp.sum(d_summed * taps[j], axis=0, keepdims=True)
    g_small[28:29, :] += jnp.sum(d_summed, axis=0, keepdims=True)
    ext = jnp.concatenate([d_summed, later[...]], axis=0)
    later[...] = d_summed[0:8]
    d_mix = conv_w[3:4, :] * d_summed
    for j in range(3):
        d_mix = d_mix + conv_w[j : j + 1, :] * pltpu.roll(ext, length + 8 - (3 - j), 0)[0:length]
    d_mix = (d_mix + mm_nt(value_low, w_v[...])).astype(bf16)
    d_z = dz_ref[...]
    rows = normed[...]
    d_normed = mm_nt(d_mix, w_mix[...]) + mm_nt(d_z, w_gate[...])
    g_ln = jnp.sum(d_normed * rows.astype(f32), axis=0, keepdims=True)
    g_small[32:33, :] += g_ln[:, :size]
    g_small[33:34, :] += g_ln[:, size:]

    @pl.when(last)
    def _():
        g_small[29:32, :] = g_gain[0:3, :]

    return rows, d_mix, d_z, d_normed


def lower_block(
    at_start, at_end, lows, dskip_ref, dskip_next, dz_ref, mix_ref, mix_before, mix_next, normed,
    w_q, w_k, w_v, w_mix, w_gate, conv_w, conv_b, g_small,
):
    query_low, key_low, value_low = lows
    length, size = mix_ref.shape
    extra = mix_next.shape[0]
    halo = jnp.where(at_start, 0.0, mix_before[8:16, :].astype(f32))
    ext = jnp.concatenate(
        [halo, mix_ref[...].astype(f32), mix_next[...].astype(f32)], axis=0
    )
    taps = conv_taps(ext, length + extra)
    summed = conv_b[...]
    for j in range(4):
        summed = summed + conv_w[j : j + 1, :] * taps[j]
    opened = jax.nn.sigmoid(summed)
    d_conv = jnp.concatenate([dskip_ref[...], dskip_next[...]], axis=0)
    d_conv = d_conv + mm_nt(query_low, w_q[...]) + mm_nt(key_low, w_k[...])
    d_summed = d_conv * (opened * (1.0 + summed * (1.0 - opened)))
    for j in range(4):
        g_small[24 + j : 25 + j, :] += jnp.sum(
            d_summed[:length] * taps[j][:length], axis=0, keepdims=True
        )
    g_small[28:29, :] += jnp.sum(d_summed[:length], axis=0, keepdims=True)
    row = lax.broadcasted_iota(jnp.int32, d_summed.shape, 0)
    d_summed = jnp.where(jnp.logical_and(at_end, row >= length), 0.0, d_summed)
    d_mix = conv_w[3:4, :] * d_summed[:length]
    for j in range(3):
        ahead = pltpu.roll(d_summed, length + extra - (3 - j), 0)[0:length]
        d_mix = d_mix + conv_w[j : j + 1, :] * ahead
    d_mix = (d_mix + mm_nt(value_low, w_v[...])).astype(bf16)
    rows = normed[...]
    d_normed = mm_nt(d_mix, w_mix[...]) + mm_nt(dz_ref[...], w_gate[...])
    g_ln = jnp.sum(d_normed * rows.astype(f32), axis=0, keepdims=True)
    g_small[32:33, :] += g_ln[:, :size]
    g_small[33:34, :] += g_ln[:, size:]
    return rows, d_mix, d_normed


def lower_kernel(chained, head_ref, *refs):
    ins, refs = refs[:22], list(refs[22:])
    edge = 0.0
    if chained:
        first_halo, first_later, *refs = refs
        edge = first_halo[8:16, :].astype(f32)
        later_out = refs.pop(4)
    part_out, square_out, up_out, small_out = refs[:4]
    g_q, g_k, g_v, g_m, g_z, g_small, later = refs[4:]
    step = pl.program_id(0)
    size = g_q.shape[0]

    @pl.when(step == 0)
    def _():
        for ref in (g_q, g_k, g_v, g_m, g_z, g_small, later):
            ref[...] = jnp.zeros_like(ref)
        if chained:
            later[...] = first_later[...]

    (d_gate, dq, dk, dv, dskip, dz, mix, mix_before, conv, q, k, v, normed,
     w_q, w_k, w_v, w_mix, w_gate, conv_w, conv_b, gate_w, g_gain) = ins
    lows = lower_first(d_gate, dq, dk, dv, mix, conv, q, k, v, gate_w, g_q, g_k, g_v, g_small)
    rows, d_mix, d_z, d_normed = lower_second(
        edge, step == pl.num_programs(0) - 1, lows, dskip, dz, mix, mix_before, normed,
        w_q.at[0], w_k.at[0], w_v.at[0], w_mix, w_gate, conv_w, conv_b, g_gain, g_small, later,
    )
    g_m[...] += mm_tn(rows, d_mix)
    g_z[...] += mm_tn(rows, d_z)
    part_out[...] = d_normed.astype(bf16)

    @pl.when(step == pl.num_programs(0) - 1)
    def _():
        half = size // 2
        for at, ref in enumerate((g_q, g_k, g_v)):
            square_out[0, :, half * at : half * at + half] = ref[:, :half].astype(bf16)
            square_out[1, :, half * at : half * at + half] = ref[:, half:].astype(bf16)
        up_out[0] = g_m[...].astype(bf16)
        up_out[1] = g_z[...].astype(bf16)
        small_out[...] = g_small[...]
        if chained:
            later_out[...] = later[...]


def struct(shape, dtype):
    return jax.ShapeDtypeStruct(shape, dtype)


def run_kernel(body, head, grid, inputs, in_specs, outs, out_specs, scratch, name, flops, nbytes):
    return pl.pallas_call(
        body,
        grid_spec=pltpu.PrefetchScalarGridSpec(
            num_scalar_prefetch=1,
            grid=(grid,),
            in_specs=in_specs,
            out_specs=out_specs,
            scratch_shapes=scratch,
        ),
        out_shape=outs,
        compiler_params=pltpu.CompilerParams(
            dimension_semantics=("arbitrary",), vmem_limit_bytes=vmem_bytes
        ),
        cost_estimate=pl.CostEstimate(flops=flops, bytes_accessed=nbytes, transcendentals=0),
        name=name,
    )(head, *inputs)


def fixed(shape, *index):
    return pl.BlockSpec(shape, lambda g, h: tuple(h[0] if i == "h" else i for i in index))


def lift(head, normed, w_up, w_query, w_key, w_value, conv_w, conv_b, gate_parts, *first):
    tokens, width = normed.shape
    heads, size, _ = w_query.shape
    length = wide_len
    by_row = lambda cols: pl.BlockSpec((length, cols), lambda g, h: (g, 0))
    weight = pl.BlockSpec((1, size, size), lambda g, h: (h[0], 0, 0))
    chained = len(first) > 0
    halo = [pl.BlockSpec((16, size), lambda g, h: (0, 0))] * chained
    return run_kernel(
        partial(lift_kernel, chained), head, tokens // length,
        (normed, w_up, w_up, w_query, w_key, w_value, conv_w, conv_b, gate_parts, *first),
        [
            by_row(width),
            pl.BlockSpec((width, size), lambda g, h: (0, h[0])),
            pl.BlockSpec((width, size), lambda g, h: (0, heads + h[0])),
            weight, weight, weight,
            pl.BlockSpec((4, size), lambda g, h: (0, h[0])),
            pl.BlockSpec((1, size), lambda g, h: (0, h[0])),
            pl.BlockSpec(gate_parts.shape, lambda g, h: (0, 0, 0)),
        ]
        + [pl.BlockSpec((16, width), lambda g, h: (0, 0))] * chained,
        [struct((tokens, size), bf16)] * 5
        + [struct((tokens, size), f32), struct((8, tokens), f32)]
        + [struct((16, size), bf16)] * chained,
        [by_row(size)] * 6 + [pl.BlockSpec((8, length), lambda g, h: (0, g))] + halo,
        [pltpu.VMEM((8, size), f32)],
        "lift", 2 * tokens * size * (2 * width + 3 * size), 24 * 2**20,
    )


def cell_forward(head, gates, q, k, v, conv, gate_z, out_gain, skip_gain, w_down, *first):
    tokens, size = q.shape
    width = w_down.shape[1]
    length = chunk_len
    steps = tokens // length
    by_row = lambda cols: pl.BlockSpec((length, cols), lambda g, h: (g, 0))
    gain = pl.BlockSpec((1, size), lambda g, h: (0, h[0]))
    carried = [struct(value.shape, f32) for value in first]
    carried_specs = [pl.BlockSpec(value.shape, lambda g, h: (0, 0)) for value in first]
    return run_kernel(
        partial(cell_forward_kernel, len(first) > 0), head, steps,
        (gates, q, k, v, conv, gate_z, out_gain, skip_gain, w_down, *first),
        [pl.BlockSpec((2, length), lambda g, h: (0, g))]
        + [by_row(size)] * 5
        + [gain, gain, pl.BlockSpec((size, width), lambda g, h: (h[0], 0))]
        + carried_specs,
        [
            struct((tokens, width), bf16),
            struct((tokens, size), f32),
            struct((steps, size, size), bf16),
            struct((steps, 8, size), f32),
            struct((tokens, length), bf16),
            struct((tokens, 128), f32),
            struct((8, tokens), f32),
        ]
        + carried,
        [
            by_row(width),
            by_row(size),
            pl.BlockSpec((1, size, size), lambda g, h: (g, 0, 0)),
            pl.BlockSpec((1, 8, size), lambda g, h: (g, 0, 0)),
            by_row(length),
            by_row(128),
            pl.BlockSpec((8, length), lambda g, h: (0, g)),
        ]
        + carried_specs,
        [pltpu.VMEM((size, size), f32), pltpu.VMEM((8, size), f32), pltpu.VMEM((8, 128), f32)],
        "cell_forward", 2 * tokens * size * (2 * length + 2 * size + width), 28 * 2**20,
    )


def cell_backward(
    head, rows, q, k, v, conv, gate_z, normed, states, norms, weights, cols, cot, rows_in,
    out_gain, skip_gain, w_down, *first,
):
    tokens, size = q.shape
    width = w_down.shape[1]
    length = chunk_len
    steps = tokens // length
    end = steps - 1
    by_row = lambda n: pl.BlockSpec((length, n), lambda g, h: (end - g, 0))
    gain = pl.BlockSpec((1, size), lambda g, h: (0, h[0]))
    whole = lambda shape: pl.BlockSpec(shape, lambda g, h: (0, 0))
    carried = [struct(value.shape, f32) for value in first]
    carried_specs = [whole(value.shape) for value in first]
    return run_kernel(
        partial(cell_backward_kernel, len(first) > 0), head, steps,
        (rows, q, k, v, conv, gate_z, normed, states, norms, weights, cols, cot, rows_in,
         out_gain, skip_gain, w_down, *first),
        [pl.BlockSpec((8, length), lambda g, h: (0, end - g))]
        + [by_row(size)] * 6
        + [
            pl.BlockSpec((1, size, size), lambda g, h: (end - g, 0, 0)),
            pl.BlockSpec((1, 8, size), lambda g, h: (end - g, 0, 0)),
            by_row(length),
            by_row(128),
            by_row(width),
            by_row(width),
            gain, gain,
            pl.BlockSpec((size, width), lambda g, h: (h[0], 0)),
        ]
        + carried_specs,
        [struct((tokens, size), f32)] * 4
        + [
            struct((tokens, size), bf16),
            struct((8, tokens), f32),
            struct((2, size, width // 2), bf16),
            struct((width, size), bf16),
            struct((8, size), f32),
        ]
        + carried,
        [by_row(size)] * 5
        + [
            pl.BlockSpec((8, length), lambda g, h: (0, end - g)),
            pl.BlockSpec((2, size, width // 2), lambda g, h: (0, 0, 0)),
            whole((width, size)),
            whole((8, size)),
        ]
        + carried_specs,
        [
            pltpu.VMEM((size, size), f32),
            pltpu.VMEM((8, size), f32),
            pltpu.VMEM((size, width), f32),
            pltpu.VMEM((width, size), f32),
            pltpu.VMEM((8, size), f32),
        ],
        "cell_backward", 2 * tokens * size * (4 * length + 4 * size + 2 * width), 44 * 2**20,
    )


def lower_inputs(
    length, d_gate, dq, dk, dv, dskip, dz, mix, conv, q, k, v, normed,
    w_query, w_key, w_value, w_up, conv_w, conv_b, gate_pairs, g_gain,
):
    tokens, size = q.shape
    width = normed.shape[1]
    heads = w_query.shape[0]
    end = tokens // length - 1
    by_row = lambda n: pl.BlockSpec((length, n), lambda g, h: (end - g, 0))
    kept = lambda shape, index: pl.BlockSpec(shape, index, pipeline_mode=pl.Buffered(1))
    weight = kept((1, size, size), lambda g, h: (h[0], 0, 0))
    inputs = (
        d_gate, dq, dk, dv, dskip, dz, mix, mix, conv, q, k, v, normed,
        w_query, w_key, w_value, w_up, w_up, conv_w, conv_b, gate_pairs, g_gain,
    )
    specs = [pl.BlockSpec((8, length), lambda g, h: (0, end - g))]
    specs += [by_row(size)] * 6
    specs += [
        pl.BlockSpec(
            (16, size), lambda g, h: (jnp.maximum((end - g) * (length // 16) - 1, 0), 0)
        )
    ]
    specs += [by_row(size)] * 4
    specs += [by_row(width), weight, weight, weight]
    specs += [
        kept((width, size), lambda g, h: (0, h[0])),
        kept((width, size), lambda g, h: (0, heads + h[0])),
        kept((4, size), lambda g, h: (0, h[0])),
        kept((1, size), lambda g, h: (0, h[0])),
        kept(gate_pairs.shape, lambda g, h: (0, 0)),
        kept(g_gain.shape, lambda g, h: (0, 0)),
    ]
    return inputs, specs


def lower(head, *inputs):
    inputs, first = inputs[:20], inputs[20:]
    tokens, size = inputs[1].shape
    width = inputs[11].shape[1]
    length = wide_len
    end = tokens // length - 1
    by_row = lambda n: pl.BlockSpec((length, n), lambda g, h: (end - g, 0))
    whole = lambda shape: pl.BlockSpec(shape, lambda g, h: (0, 0))
    chained = len(first) > 0
    inputs, specs = lower_inputs(length, *inputs)
    return run_kernel(
        partial(lower_kernel, chained), head, tokens // length,
        (*inputs, *first),
        specs + [whole(value.shape) for value in first],
        [struct((tokens, width), bf16)]
        + [struct((2, size, 3 * size // 2), bf16), struct((2, width, size), bf16)]
        + [struct((40, size), f32)]
        + [struct((8, size), f32)] * chained,
        [by_row(width)]
        + [
            pl.BlockSpec((2, size, 3 * size // 2), lambda g, h: (0, 0, 0)),
            pl.BlockSpec((2, width, size), lambda g, h: (0, 0, 0)),
        ]
        + [whole((40, size))]
        + [whole((8, size))] * chained,
        [pltpu.VMEM((size, size), f32)] * 3
        + [pltpu.VMEM((width, size), f32)] * 2
        + [pltpu.VMEM((40, size), f32), pltpu.VMEM((8, size), f32)],
        "lower", 2 * tokens * size * (6 * size + 4 * width), 48 * 2**20,
    )
MESH_ID = pl.DeviceIdType.MESH


def halves_of(value, count):
    whole = jnp.int32(0)
    for bound in range(2, count, 2):
        whole = whole + jnp.where(value >= bound, 1, 0)
    return whole, value - 2 * whole


def where_am_i():
    at_seq, at_batch = lax.axis_index("seq"), lax.axis_index("batch")
    first = jnp.int32(0)
    for bound in range(8, lax.axis_size("seq"), 8):
        first = first + jnp.where(at_seq >= bound, 8, 0)
    z, y = halves_of(at_seq - first, 8)
    x, c = halves_of(at_batch, lax.axis_size("batch"))
    return first, z, y, x, c


def turn(value, count):
    return jnp.where(value >= count, value - count, value)


def greet(others):
    barrier = pltpu.get_barrier_semaphore()
    for other in others:
        pl.semaphore_signal(barrier, 1, device_id=other, device_id_type=MESH_ID)
    pl.semaphore_wait(barrier, len(others))


def remote(src, dst, sent, landed, device):
    return pltpu.make_async_remote_copy(src, dst, sent, landed, device_id=device, device_id_type=MESH_ID)


def normalize(rows):
    centre = rows - jnp.mean(rows, axis=-1, keepdims=True)
    rstd = lax.rsqrt(jnp.mean(centre * centre, axis=-1, keepdims=True) + norm_epsilon)
    return centre * rstd, rstd


class Gather:
    def __init__(self, source, out_ref, block, cuts, sems):
        self.source, self.out_ref, self.block, self.cuts = source, out_ref, block, cuts
        self.parts = len(cuts)
        self.kept, self.z_sent, self.z_landed, self.y_sent, self.y_landed, *sems = sems
        self.c_sent, self.c_landed = sems
        self.first, self.z, self.y, self.x, self.c = where_am_i()
        self.enters = halves_of(self.z, 4)[0] == self.c

    def device(self, zz, yy, cc):
        return (self.first + 2 * zz + yy, 2 * self.x + cc)

    def others(self):
        others = [self.device(turn(self.z + k, 4), self.y, self.c) for k in range(1, 4)]
        return others + [self.device(self.z, 1 - self.y, self.c), self.device(self.z, self.y, 1 - self.c)]

    def rows(self, zz, yy, part):
        start, size = self.cuts[part]
        return self.out_ref.at[
            pl.ds(pl.multiple_of((2 * zz + yy) * self.block + start, 16), size)
        ]

    def away(self, m):
        return 2 * self.c + m != self.z

    def to_column(self, m, part):
        return remote(
            self.source(m, pl.ds(*self.cuts[part])), self.rows(self.z, self.y, part), self.z_sent.at[m, part],
            self.z_landed.at[self.z, part], self.device(2 * self.c + m, self.y, self.c),
        )

    def keep(self, m, part):
        return pltpu.make_async_copy(
            self.source(m, pl.ds(*self.cuts[part])), self.rows(self.z, self.y, part), self.kept.at[part]
        )

    def from_column(self, zz, part):
        here = self.rows(zz, self.y, part)
        return remote(
            here, here, self.z_sent.at[0, part], self.z_landed.at[zz, part],
            self.device(zz, self.y, self.c),
        )

    def to_row(self, zz, k, part):
        here = self.rows(zz, self.y, part)
        return remote(
            here, here, self.y_sent.at[k, part], self.y_landed.at[zz, part],
            self.device(self.z, 1 - self.y, self.c),
        )

    def from_row(self, zz, k, part):
        here = self.rows(zz, 1 - self.y, part)
        return remote(
            here, here, self.y_sent.at[k, part], self.y_landed.at[zz, part],
            self.device(self.z, 1 - self.y, self.c),
        )

    def to_core(self, zz, yy, k, part):
        here = self.rows(zz, yy, part)
        return remote(
            here, here, self.c_sent.at[k, part], self.c_landed.at[2 * zz + yy, part],
            self.device(self.z, self.y, 1 - self.c),
        )

    def start(self, part):
        for m in range(2):
            pl.when(self.away(m))(lambda: self.to_column(m, part).start())
            pl.when(jnp.logical_not(self.away(m)))(lambda: self.keep(m, part).start())

    def at(self, k):
        high, low = halves_of(self.z, 4)
        far = 2 * high if k < 2 else 2 - 2 * high
        return far + (low if k % 2 == 0 else 1 - low)

    def pass_column(self, k, part):
        @pl.when(self.enters)
        def _():
            if k == 0:
                self.keep(0, part).wait()
            else:
                self.from_column(self.at(k), part).wait_recv()
            self.to_row(self.at(k), k, part).start()
            self.to_core(self.at(k), self.y, k, part).start()

    def pass_row(self, k, part):
        @pl.when(self.enters)
        def _():
            self.from_row(self.at(k), k, part).wait_recv()
            self.to_core(self.at(k), 1 - self.y, 4 + k, part).start()

    def finish(self, wait_core):
        @pl.when(self.enters)
        def _():
            for k in range(4):
                for part in range(self.parts):
                    self.to_row(self.at(k), k, part).wait_send()
                    self.to_core(self.at(k), self.y, k, part).wait_send()
                    self.to_core(self.at(k), 1 - self.y, 4 + k, part).wait_send()

        if wait_core:

            @pl.when(jnp.logical_not(self.enters))
            def _():
                for zz in range(4):
                    for yy in range(2):
                        for part in range(self.parts):
                            self.to_core(zz, yy, 0, part).wait_recv()

        for m in range(2):
            for part in range(self.parts):
                pl.when(self.away(m))(lambda: self.to_column(m, part).wait_send())


def even_cuts(block, parts):
    size = block // parts
    return [(part * size, size) for part in range(parts)]


def falling_cuts(block):
    unit = block // 16
    return [(0, 5 * unit), (5 * unit, 5 * unit), (10 * unit, 4 * unit), (14 * unit, 2 * unit)]


def gather_sems(parts):
    shapes = [(parts,), (2, parts), (4, parts), (4, parts), (4, parts), (8, parts), (8, parts)]
    return [pltpu.SemaphoreType.DMA(shape) for shape in shapes]


def gather_kernel(rows_ref, gain_ref, out_ref, staged, *sems):
    parts = sems[0].shape[0]
    block = rows_ref.shape[1]
    cuts = even_cuts(block, parts)
    gather = Gather(lambda m, here: staged.at[m, here], out_ref, block, cuts, sems)
    greet(gather.others())
    for part in range(parts):
        here = pl.ds(*cuts[part])
        for m in range(2):
            staged[m, here] = (
                normalize(rows_ref[m, here].astype(f32))[0] * gain_ref[...]
            ).astype(bf16)
        gather.start(part)
    for part in range(parts):
        for k in range(4):
            gather.pass_column(k, part)
        if part > 0:
            for k in range(4):
                gather.pass_row(k, part - 1)
    for k in range(4):
        gather.pass_row(k, parts - 1)
    gather.finish(True)


def gather_normed(rows, gain):
    micro, block, width = rows.shape
    return pl.pallas_call(
        gather_kernel,
        out_shape=struct((8 * block, width), bf16),
        in_specs=[pl.BlockSpec(memory_space=pltpu.VMEM)] * 2,
        out_specs=pl.BlockSpec(memory_space=pl.ANY),
        scratch_shapes=[pltpu.VMEM((micro, block, width), bf16)] + gather_sems(4),
        compiler_params=pltpu.CompilerParams(
            collective_id=0, has_side_effects=True, vmem_limit_bytes=32 * 2**20
        ),
        name="gather_normed",
    )(rows, gain)


def lift_rest(rows, before, w_q, w_k, w_v, conv_w, conv_b, gate_parts):
    length = rows.shape[0]
    taps = conv_taps(jnp.concatenate([before, rows.astype(f32)], axis=0), length)
    summed = conv_b[...]
    for j in range(4):
        summed = summed + conv_w[j : j + 1, :] * taps[j]
    conv = (summed * jax.nn.sigmoid(summed)).astype(bf16)
    q = mm(conv, w_q[0]).astype(bf16)
    k = mm(conv, w_k[0]).astype(bf16)
    v = mm(rows, w_v[0]).astype(bf16)
    parts = mm_nt(gate_parts[0], q) + mm_nt(gate_parts[1], k) + mm_nt(gate_parts[2], v)
    return conv, q, k, v, parts[0:8] + parts[8:16] + parts[16:24]


def rise_kernel(
    tokens, ln_gain, up_src, q_src, k_src, v_src, conv_w, conv_b, gate_own, gate_b, out_gain,
    skip_gain, down_src, cot_src, *refs
):
    kept_outs, cell_outs, (cot_out, *refs) = refs[:7], refs[7:14], refs[14:]
    rows_all, mix_all, conv_all, q_all, k_all, v_all, z_all, *refs = refs
    staged, gate_mine, gate_all, gates, gate_parts, hidden_kept, cols_kept, *refs = refs
    w_mix, w_gate, w_q, w_k, w_v, w_down, cot_ref, load_sem, *refs = refs
    state, h_sent, h_landed, out_sem, *sems = refs[:3], *refs[3:]
    parts = sems[0].shape[0]
    step = pl.program_id(0)
    blocks = (pl.num_programs(0) - 1) // 2
    micro, block, width = cot_ref.shape
    cuts = falling_cuts(block)
    normed = Gather(lambda m, here: staged.at[m, here], rows_all, block, cuts, sems[:7])
    gather = Gather(
        lambda m, here: cot_ref.at[m, here], cot_out, block, even_cuts(block, parts), sems[7:]
    )
    z, y, c = gather.z, gather.y, gather.c
    head = 2 * c + y
    heads = gate_all.shape[0]
    group = [(1 - y, c), (y, 1 - c), (1 - y, 1 - c)]
    span = gate_mine.shape[1] // 2

    def gate_to(k, part):
        lanes = pl.ds(part * span, span)
        return remote(
            gate_mine.at[:, lanes], gate_all.at[head, :, lanes], h_sent.at[k, part],
            h_landed.at[head, part], gather.device(z, *group[k]),
        )

    def gate_from(k, part):
        lanes = pl.ds(part * span, span)
        at = 2 * group[k][1] + group[k][0]
        return remote(
            gate_mine.at[:, lanes], gate_all.at[at, :, lanes], h_sent.at[k, part],
            h_landed.at[at, part], gather.device(z, *group[k]),
        )

    wide = w_mix.shape[1]
    own_lanes = pl.ds(pl.multiple_of(head * wide, wide), wide)
    gate_lanes = pl.ds(pl.multiple_of((heads + head) * wide, wide), wide)
    loads = [
        (up_src.at[:, own_lanes], w_mix), (up_src.at[:, gate_lanes], w_gate),
        (q_src.at[pl.ds(head, 1)], w_q), (k_src.at[pl.ds(head, 1)], w_k),
        (v_src.at[pl.ds(head, 1)], w_v), (down_src.at[own_lanes], w_down), (cot_src, cot_ref),
    ]

    def load(k):
        return pltpu.make_async_copy(*loads[k], load_sem.at[k])

    def keep_out(k):
        made = (rows_all, mix_all, conv_all, q_all, k_all, v_all, z_all)[k]
        return pltpu.make_async_copy(made, kept_outs[k], out_sem.at[k])

    def lift_up(yy, part):
        start, size = cuts[part]
        here = [
            pl.ds(pl.multiple_of((2 * zz + yy) * block + start, 16), size) for zz in range(4)
        ]
        rows = jnp.concatenate([rows_all[at] for at in here], axis=0)
        mix = mm(rows, w_mix[...]).astype(bf16)
        gate_z = mm(rows, w_gate[...])
        for k, at in enumerate(here):
            mix_all[at] = mix[size * k : size * k + size]
            z_all[at] = gate_z[size * k : size * k + size]

    def arrived(yy, part):
        @pl.when(jnp.logical_not(normed.enters))
        def _():
            for zz in range(4):
                normed.to_core(zz, yy, 0, part).wait_recv()

    @pl.when(step == 0)
    def _():
        greet(normed.others() + [gather.device(z, 1 - y, 1 - c)])
        for p in range(3):
            gate_parts[p, 0:24] = jnp.concatenate(split_three(gate_own[8 * p : 8 * p + 8, :]), axis=0)
            gate_parts[p, 24:32] = jnp.zeros_like(gate_parts[p, 24:32])
        for part in range(parts):
            here = pl.ds(*cuts[part])
            for m in range(2):
                staged[m, here] = (
                    normalize(tokens[m, here].astype(f32))[0] * ln_gain[...]
                ).astype(bf16)
            normed.start(part)
        for k in range(7):
            load(k).start()
        for part in range(parts):
            for k in range(4):
                normed.pass_column(k, part)
            if part == 0:
                for k in range(7):
                    load(k).wait()
            if part == parts - 1:
                for later in range(parts):
                    gather.start(later)
            arrived(y, part)
            lift_up(y, part)
            if part > 0:
                for k in range(4):
                    normed.pass_row(k, part - 1)
                arrived(1 - y, part - 1)
                lift_up(1 - y, part - 1)
        for k in range(4):
            normed.pass_row(k, parts - 1)
        arrived(1 - y, parts - 1)
        lift_up(1 - y, parts - 1)
        for k in (0, 1, 6):
            keep_out(k).start()

    @pl.when(step < blocks)
    def _():
        here = pl.ds(pl.multiple_of(step * block, block), block)
        edge = pl.ds(pl.multiple_of(jnp.maximum(step * block - 16, 0), 16), 16)
        before = jnp.where(step == 0, 0.0, mix_all[edge][8:16].astype(f32))
        conv, q, k, v, gate = lift_rest(
            mix_all[here], before, w_q, w_k, w_v, conv_w, conv_b, gate_parts
        )
        for ref, made in zip((conv_all, q_all, k_all, v_all), (conv, q, k, v)):
            ref[here] = made
        gate_mine[:, here] = gate
        gate_all[head, :, here] = gate

    @pl.when(step == blocks - 1)
    def _():
        for k in (2, 3, 4, 5):
            keep_out(k).start()

    for part in range(2):

        @pl.when(step == (blocks // 2) * (part + 1) - 1)
        def _():
            for k in range(3):
                gate_to(k, part).start()

        @pl.when(step == blocks + (blocks // 2) * part)
        def _():
            for k in range(3):
                gate_from(k, part).wait_recv()

    part_out, normed_out, state_out, norm_out, weight_out, col_out, row_out = cell_outs

    def recur():
        here = pl.ds(pl.multiple_of((step - blocks) * block, block), block)
        for row, at in enumerate((head, heads + head)):
            total = gate_all[0, pl.ds(at, 1), here]
            for h in range(1, heads):
                total = total + gate_all[h, pl.ds(at, 1), here]
            if row == 1:
                total = total + gate_b[head]
            gates[row : row + 1, :] = total
        return cell_recur(
            gates, q_all.at[here], k_all.at[here], v_all.at[here],
            state_out, norm_out, weight_out, row_out, *state,
        )

    def head_of_last():
        here = pl.ds(pl.multiple_of((step - blocks - 1) * block, block), block)
        cell_head(
            hidden_kept[...], cols_kept[...], conv_all.at[here], z_all.at[here],
            out_gain, skip_gain, w_down, part_out, normed_out, col_out,
        )

    @pl.when(step == blocks)
    def _():
        state[0][...] = jnp.zeros_like(state[0])
        state[1][...] = jnp.zeros_like(state[1])
        state[2][...] = jnp.full_like(state[2], floor_value)
        hidden_kept[...], cols_kept[...] = recur()

    @pl.when(jnp.logical_and(step > blocks, step < 2 * blocks))
    def _():
        head_of_last()
        hidden_kept[...], cols_kept[...] = recur()

    pl.when(step == 2 * blocks)(head_of_last)

    def columns(part, ks=(1, 2, 3)):
        return [partial(gather.pass_column, k, part) for k in ks]

    def rows(part, ks=(0, 1, 2, 3)):
        return [partial(gather.pass_row, k, part) for k in ks]

    plan = {
        0: [do for part in range(parts) for do in columns(part, (0,))],
        2: columns(0),
        5: columns(1) + [do for part in range(parts) for do in rows(part, (0,))],
        7: columns(2) + rows(0, (1, 2, 3)),
        9: columns(3) + rows(1, (1, 2, 3)),
        11: rows(2, (1, 2, 3)),
        13: rows(3, (1, 2, 3)),
    }
    for when, work in plan.items():

        @pl.when(step == when)
        def _():
            for do in work:
                do()

    @pl.when(step == 2 * blocks)
    def _():
        for k in range(7):
            keep_out(k).wait()
        normed.finish(False)
        gather.finish(True)
        for k in range(3):
            for part in range(2):
                gate_to(k, part).wait_send()


def rise(
    tokens, ln_gain, w_up, w_query, w_key, w_value, conv_w, conv_b, gate_own, gate_b, out_gain,
    skip_gain, w_down, cot,
):
    heads, size, _ = w_query.shape
    micro, block, width = cot.shape
    steps = 8
    count = steps * block
    late = lambda g: jnp.clip(g - steps, 0, steps - 1)
    after = lambda g: jnp.clip(g - steps - 1, 0, steps - 1)
    by_row = lambda n, at: pl.BlockSpec((block, n), lambda g: (at(g), 0))
    kept = lambda shape, index: pl.BlockSpec(shape, index, pipeline_mode=pl.Buffered(1))
    lanes = lambda rows: kept((rows, size), lambda g: (0, own_head()))
    anywhere = pl.BlockSpec(memory_space=pl.ANY)
    own = kept(cot.shape, lambda g: (0, 0, 0))
    specs = [
        own, kept(ln_gain.shape, lambda g: (0, 0)), anywhere, anywhere, anywhere, anywhere, lanes(4), lanes(1), kept(gate_own.shape, lambda g: (0, 0)),
        pl.BlockSpec(memory_space=pltpu.SMEM), lanes(1), lanes(1),
        anywhere, anywhere,
    ]
    whole = [((count, width), bf16)] + [((count, size), bf16)] * 5 + [((count, size), f32)]
    outs = [struct(*value) for value in whole]
    out_specs = [anywhere] * 7
    outs += [
        struct((count, width), bf16), struct((count, size), f32),
        struct((steps, size, size), bf16), struct((steps, 8, size), f32),
        struct((count, block), bf16), struct((count, 128), f32), struct((8, count), f32),
        struct((count, width), bf16),
    ]
    out_specs += [
        by_row(width, after), by_row(size, after),
        pl.BlockSpec((1, size, size), lambda g: (late(g), 0, 0)),
        pl.BlockSpec((1, 8, size), lambda g: (late(g), 0, 0)),
        by_row(block, late), by_row(128, after),
        pl.BlockSpec((8, block), lambda g: (0, late(g))), anywhere,
    ]
    scratch = whole + [((micro, block, width), bf16)]
    scratch += [((8, count), f32), ((heads, 8, count), f32), ((8, block), f32)]
    scratch += [((3, 32, size), bf16), ((block, size), f32), ((block, 128), f32)]
    loaded = [((width, size), bf16)] * 2 + [((1, size, size), bf16)] * 3
    loaded += [((size, width), bf16), (cot.shape, bf16)]
    states = [((size, size), f32), ((8, size), f32), ((8, 128), f32)]
    return pl.pallas_call(
        rise_kernel,
        grid=(2 * steps + 1,),
        in_specs=specs,
        out_specs=out_specs,
        out_shape=outs,
        scratch_shapes=[pltpu.VMEM(shape, dtype) for shape, dtype in scratch + loaded]
        + [pltpu.SemaphoreType.DMA((7,))]
        + [pltpu.VMEM(shape, dtype) for shape, dtype in states]
        + [pltpu.SemaphoreType.DMA(shape) for shape in ((3, 2), (4, 2), (7,))]
        + gather_sems(4) * 2,
        compiler_params=pltpu.CompilerParams(
            dimension_semantics=("arbitrary",), collective_id=3, has_side_effects=True,
            vmem_limit_bytes=vmem_bytes,
        ),
        name="rise",
    )(
        tokens, ln_gain, w_up, w_query, w_key, w_value, conv_w, conv_b, gate_own, gate_b,
        out_gain, skip_gain, w_down, cot,
    )


def own_head():
    first, z, y, x, c = where_am_i()
    return 2 * c + y


def settle_kernel(*refs):
    ins, refs = refs[:16], refs[16:]
    part_ref, tokens_ref, *refs = refs
    (dq_out, dk_out, dv_out, dskip_out, dz_out, g_down_out, g_z_out, g_gain_out,
     block_out, gate_out, *refs) = refs
    state, (gate_rows, gate_all, own, from_core, kept, to_row, from_row, to_owner, owned, *sems) = (
        refs[:5], refs[5:],
    )
    own_sem, c_sent, c_landed, y_sent, y_landed, o_sent, o_landed, h_sent, h_landed = sems
    step = pl.program_id(0)
    first, z, y, x, c = where_am_i()
    head = 2 * c + y
    high, low = halves_of(z, 4)
    half = own.shape[1]
    block = ins[1].shape[0]

    def device(zz, yy, cc):
        return (first + 2 * zz + yy, 2 * x + cc)

    around = [turn(z + k, 4) for k in range(1, 4)]
    order = around + [z]
    group = [(1 - y, c), (y, 1 - c), (1 - y, 1 - c)]

    def rows_of(at, cc):
        return part_ref.at[pl.ds(pl.multiple_of((2 * at + cc) * half, half), half)]

    def load(at):
        return pltpu.make_async_copy(rows_of(at, c), own.at[at], own_sem.at[at])

    def to_c(at):
        return remote(
            rows_of(at, 1 - c), from_core.at[at], c_sent.at[at], c_landed.at[at],
            device(z, y, 1 - c),
        )

    def to_y(zz):
        return remote(
            to_row.at[zz], from_row.at[zz], y_sent.at[zz], y_landed.at[zz], device(z, 1 - y, c)
        )

    def to_o(zz):
        return remote(
            to_owner.at[zz], owned.at[low, c], o_sent.at[zz], o_landed.at[low, c],
            device(zz, y, high),
        )

    def core_sum(at):
        load(at).wait()
        to_c(at).wait_recv()
        return (own[at].astype(f32) + from_core[at].astype(f32)).astype(bf16)

    def core_step(zz):
        to_row[zz] = core_sum(2 * zz + 1 - y)
        to_y(zz).start()
        kept[zz] = core_sum(2 * zz + y)

    def row_sum(zz):
        to_y(zz).wait_recv()
        return (kept[zz].astype(f32) + from_row[zz].astype(f32)).astype(bf16)

    enters = high == c

    def row_step(zz):
        to_owner[zz] = row_sum(zz)
        to_o(zz).start()

    def gate_to(k):
        yy, cc = group[k]
        return remote(
            gate_rows, gate_all.at[head], h_sent.at[k], h_landed.at[head], device(z, yy, cc)
        )

    def gate_from(k):
        at = 2 * group[k][1] + group[k][0]
        return remote(
            gate_rows, gate_all.at[at], h_sent.at[k], h_landed.at[at], device(z, *group[k])
        )

    @pl.when(step == 0)
    def _():
        others = [device(z, yy, cc) for yy, cc in group]
        for zz in around:
            others += [device(zz, y, c), device(zz, y, 1 - c)]
        greet(others)
        for zz in order:
            for yy in (1 - y, y):
                to_c(2 * zz + yy).start()
                load(2 * zz + yy).start()

    now = pl.num_programs(0) - 1 - step
    lanes = pl.ds(pl.multiple_of(now * block, block), block)
    cell_backward_kernel(
        False, None, *ins, dq_out, dk_out, dv_out, dskip_out, dz_out, gate_rows.at[:, lanes],
        g_down_out, g_z_out, g_gain_out, *state,
    )

    for k in range(4):
        pl.when(step == k)(lambda: core_step(order[k]))
    for k, when in enumerate((1, 3, 5)):
        pl.when(step == when)(lambda: row_step(order[k]))

    @pl.when(step == pl.num_programs(0) - 1)
    def _():
        for k in range(3):
            gate_to(k).start()
        gate_all[head] = gate_rows[...]

        @pl.when(enters)
        def _():
            owned[low, c] = row_sum(z)

        @pl.when(jnp.logical_not(enters))
        def _():
            row_step(z)

        for m in range(2):
            for cc in range(2):
                own_part = jnp.logical_and(2 * c + m == z, c == cc)
                landed = remote(
                    to_owner.at[0], owned.at[m, cc], o_sent.at[0], o_landed.at[m, cc],
                    device(2 * c + m, y, cc),
                )
                pl.when(jnp.logical_not(own_part))(lambda: landed.wait_recv())
                here = pl.ds(cc * half, half)
                block_out[m, here] = (
                    tokens_ref[m, here].astype(f32) + owned[m, cc].astype(f32)
                ).astype(bf16)
        for k in range(3):
            gate_from(k).wait_recv()
        heads = gate_all.shape[0]
        for h in range(heads):
            gate_out[h : h + 1, :] = gate_all[h, 0:1, :]
            gate_out[heads + h : heads + h + 1, :] = gate_all[h, 1:2, :]
        for k in range(3):
            gate_to(k).wait_send()
            to_o(order[k]).wait_send()
        pl.when(jnp.logical_not(enters))(lambda: to_o(z).wait_send())
        for zz in range(4):
            to_y(zz).wait_send()
        for at in range(8):
            to_c(at).wait_send()


def settle(
    part, tokens, rows, q, k, v, conv, gate_z, normed, states, norms, weights, cols, cot, rows_in,
    out_gain, skip_gain, w_down,
):
    count, size = q.shape
    width = w_down.shape[1]
    micro, block, _ = tokens.shape
    half = block // 2
    length = chunk_len
    end = count // length - 1
    by_row = lambda n: pl.BlockSpec((length, n), lambda g: (end - g, 0))
    gain = pl.BlockSpec((1, size), lambda g: (0, own_head()), pipeline_mode=pl.Buffered(1))
    kept = lambda value: pl.BlockSpec(
        value.shape, lambda g: (0,) * len(value.shape), pipeline_mode=pl.Buffered(1)
    )
    specs = [pl.BlockSpec((8, length), lambda g: (0, end - g))] + [by_row(size)] * 6
    specs += [
        pl.BlockSpec((1, size, size), lambda g: (end - g, 0, 0)),
        pl.BlockSpec((1, 8, size), lambda g: (end - g, 0, 0)),
        by_row(length), by_row(128), by_row(width), by_row(width), gain, gain,
        pl.BlockSpec((size, width), lambda g: (own_head(), 0), pipeline_mode=pl.Buffered(1)),
        pl.BlockSpec(memory_space=pl.ANY), kept(tokens),
    ]
    whole = [
        struct((2, size, width // 2), bf16), struct((width, size), bf16), struct((8, size), f32),
        struct(tokens.shape, bf16), struct((8, count), f32),
    ]
    outs = [struct((count, size), f32)] * 4 + [struct((count, size), bf16)] + whole
    scratch = [
        ((size, size), f32), ((8, size), f32), ((size, width), f32), ((width, size), f32),
        ((8, size), f32), ((8, count), f32), ((4, 8, count), f32),
        ((8, half, width), bf16), ((8, half, width), bf16), ((4, half, width), bf16),
        ((4, half, width), bf16), ((4, half, width), bf16), ((4, half, width), bf16),
        ((2, 2, half, width), bf16),
    ]
    sems = [(8,), (8,), (8,), (4,), (4,), (4,), (2, 2), (3,), (4,)]
    return pl.pallas_call(
        settle_kernel,
        grid=(count // length,),
        in_specs=specs,
        out_specs=[by_row(size)] * 5 + [kept(value) for value in whole],
        out_shape=outs,
        scratch_shapes=[pltpu.VMEM(shape, dtype) for shape, dtype in scratch]
        + [pltpu.SemaphoreType.DMA(shape) for shape in sems],
        compiler_params=pltpu.CompilerParams(
            dimension_semantics=("arbitrary",), collective_id=2, has_side_effects=True,
            vmem_limit_bytes=60 * 2**20,
        ),
        cost_estimate=pl.CostEstimate(
            flops=2 * count * size * (4 * length + 4 * size + 3 * width),
            bytes_accessed=48 * 2**20, transcendentals=0,
        ),
        name="settle",
    )(
        rows, q, k, v, conv, gate_z, normed, states, norms, weights, cols, cot, rows_in,
        out_gain, skip_gain, w_down, part, tokens,
    )


def drain_kernel(
    d_gate, dq, dk, dv, mix_ref, conv, q_ref, k_ref, v_ref,
    dskip, dskip_next, dz, mix_before, mix_next, normed,
    gate_own, g_gain, w_query, w_key, w_value, w_up, conv_w, conv_b,
    down_ref, lifted_ref, rows_ref, cot_ref, gain_ref, *refs
):
    grad_out, up_out, query_out, key_out, value_out, down_out, small_out, *refs = refs
    w_q, w_k, w_v, w_mix, w_gate, taps_w, taps_b, gate_pairs, q_all, k_all, v_all, *refs = refs
    g_q, g_k, g_v, g_small, rows_all, lifted_all, part_all, *refs = refs
    from_core, kept, to_row, from_row, to_owner, owned, *refs = refs
    give_up, give_square, *refs = refs
    cross_go, cross_got, *refs = refs
    from_x, totals, refs = refs[:3], (*refs[3:6], None, refs[6]), refs[7:]
    from_near, pairs, from_far, ends = (refs[k : 20 : 4] for k in range(4))
    refs = refs[20:]
    up_go, up_got, sq_go, sq_got, dn_go, dn_got, small_x, small_sum, small_z, small_all, *refs = refs
    c_sent, c_landed, y_sent, y_landed, o_sent, o_landed, *refs = refs
    x_sent, x_landed, near_sent, near_landed, far_sent, far_landed, *refs = refs
    cross_sem, w_sem, up_sem, sq_sent, sq_landed, dn_sent, dn_landed, sx_sem, sz_sent, sz_landed, *refs = refs
    sh_sent, sh_landed = refs
    step = pl.program_id(0)
    blocks, block, width = part_all.shape
    half = block // 2
    size = g_q.shape[0]
    first, z, y, x, c = where_am_i()
    head = 2 * c + y
    high, low = halves_of(z, 4)

    def device(zz, yy, cc, xx=x):
        return (first + 2 * zz + yy, 2 * xx + cc)

    around = [turn(z + k, 4) for k in range(1, 4)]
    group = [(1 - y, c), (y, 1 - c), (1 - y, 1 - c)]

    def down_rows(q):
        tall = down_ref.shape[1] // 4
        return pl.ds(q * tall, tall)

    def up_rows(q):
        tall = lifted_ref.shape[0] // 4
        return pl.ds(q * tall, tall)

    def to_x(p, q):
        give = (give_up, give_square)[p].at[q] if p < 2 else down_ref.at[1 - x, down_rows(q)]
        return remote(
            give, from_x[p].at[q], x_sent.at[p, q], x_landed.at[p, q], device(z, y, c, 1 - x)
        )

    def before_near(p, q):
        if p == 3:
            return lifted_ref.at[up_rows(q), pl.ds(size // 2, size // 2)]
        return totals[p].at[q]

    def to_near(p, q):
        return remote(
            before_near(p, q), from_near[p].at[q // 2], near_sent.at[p, q], near_landed.at[p, q],
            device(z + 1 - 2 * low, y, c),
        )

    def start_near(p, q):
        pl.when(low != q % 2)(lambda: to_near(p, q).start())

    def to_far(p, q):
        return remote(
            pairs[p].at[q // 2], from_far[p], far_sent.at[p, q], far_landed.at[p, q],
            device(z + 2 - 4 * high, y, c),
        )

    def x_step(p, q):
        to_x(p, q).wait_recv()
        own = totals[p][q] if p < 2 else down_ref[x, down_rows(q)]
        totals[p][q] = (own.astype(f32) + from_x[p][q].astype(f32)).astype(bf16)
        start_near(p, q)

    def near_step(p, q):
        @pl.when(low == q % 2)
        def _():
            to_near(p, q).wait_recv()
            pairs[p][q // 2] = (
                before_near(p, q)[...].astype(f32) + from_near[p][q // 2].astype(f32)
            ).astype(bf16)
            pl.when(high != q // 2)(lambda: to_far(p, q).start())

    def far_step(p, q):
        @pl.when(z == q)
        def _():
            to_far(p, q).wait_recv()
            total = pairs[p][q // 2].astype(f32) + from_far[p][...].astype(f32)
            ends[p][:, : total.shape[1]] = total

    def to_cross():
        return remote(cross_go, cross_got, cross_sem.at[0], cross_sem.at[1], device(z, y, c, 1 - x))

    def cross(p):
        cross_go[...] = ends[p][...].astype(bf16)
        to_cross().start()

    def weight_copies():
        lanes = pl.ds(pl.multiple_of(head * size, size), size)
        gate_lanes = pl.ds(pl.multiple_of((w_query.shape[0] + head) * size, size), size)
        pairs_of = [
            (w_query.at[head], w_q), (w_key.at[head], w_k), (w_value.at[head], w_v),
            (w_up.at[:, lanes], w_mix), (w_up.at[:, gate_lanes], w_gate),
            (conv_w.at[:, lanes], taps_w), (conv_b.at[:, lanes], taps_b),
        ]
        return [
            pltpu.make_async_copy(src, dst, w_sem.at[k]) for k, (src, dst) in enumerate(pairs_of)
        ]

    def to_c(at):
        there = pl.ds(pl.multiple_of((1 - c) * half, half), half)
        return remote(
            part_all.at[at, there], from_core.at[at], c_sent.at[at], c_landed.at[at],
            device(z, y, 1 - c),
        )

    def to_y(zz):
        return remote(
            to_row.at[zz], from_row.at[zz], y_sent.at[zz], y_landed.at[zz], device(z, 1 - y, c)
        )

    def to_o(zz):
        return remote(
            to_owner.at[zz], owned.at[low, c], o_sent.at[zz], o_landed.at[low, c],
            device(zz, y, high),
        )

    def stays(zz):
        return jnp.logical_and(z == zz, high == c)

    def core_step(at):
        zz, yy = halves_of(at, 8)
        to_c(at).wait_recv()
        here = pl.ds(pl.multiple_of(c * half, half), half)
        value = (part_all[at, here].astype(f32) + from_core[at].astype(f32)).astype(bf16)

        @pl.when(yy == y)
        def _():
            kept[zz] = value

        @pl.when(yy != y)
        def _():
            to_row[zz] = value
            to_y(zz).start()

    def row_step(zz):
        to_y(zz).wait_recv()
        to_owner[zz] = (kept[zz].astype(f32) + from_row[zz].astype(f32)).astype(bf16)

        @pl.when(stays(zz))
        def _():
            owned[low, c] = to_owner[zz]

        pl.when(jnp.logical_not(stays(zz)))(lambda: to_o(zz).start())

    def to_group(k, src, dst, sent, landed):
        yy, cc = group[k]
        return remote(src, dst, sent.at[k], landed, device(z, yy, cc))

    def small_to_x():
        return remote(g_small, small_x, sx_sem.at[0], sx_sem.at[1], device(z, y, c, 1 - x))

    def small_to_z(k):
        return remote(
            small_sum, small_z.at[z], sz_sent.at[k], sz_landed.at[z], device(around[k], y, c)
        )

    def small_from_z(k):
        return remote(
            small_sum, small_z.at[around[k]], sz_sent.at[k], sz_landed.at[around[k]],
            device(around[k], y, c),
        )

    def small_to_head(k):
        return to_group(k, small_all.at[head], small_all.at[head], sh_sent, sh_landed.at[head])

    def small_from_head(k):
        at = 2 * group[k][1] + group[k][0]
        return to_group(k, small_all.at[at], small_all.at[at], sh_sent, sh_landed.at[at])

    def up_to_y():
        return remote(up_go, up_got, up_sem.at[0], up_sem.at[1], device(z, 1 - y, c))

    def square_to(k):
        yy, cc = group[k]
        return to_group(k, sq_go.at[yy, cc], sq_got.at[head], sq_sent, sq_landed.at[head])

    def square_from(k):
        at = 2 * group[k][1] + group[k][0]
        return to_group(k, sq_go.at[0, 0], sq_got.at[at], sq_sent, sq_landed.at[at])

    def down_to(cc):
        return remote(
            dn_go.at[cc], dn_got.at[low], dn_sent.at[cc], dn_landed.at[low],
            device(head, high, cc),
        )

    def down_from(k):
        return remote(
            dn_go.at[0], dn_got.at[k], dn_sent.at[0], dn_landed.at[k],
            device(2 * y + k, low, high),
        )

    home = jnp.logical_and(head == z, high == y)

    @pl.when(step == 0)
    def _():
        others = [device(z, yy, cc) for yy, cc in group] + [device(z, y, c, 1 - x)]
        for zz in around:
            others += [device(zz, yy, cc) for yy, cc in [(y, c)] + group]
        greet(others)
        for q in range(4):
            to_x(2, q).start()
        for q in range(4):
            start_near(3, q)
        for p in range(3):
            one, two, three = split_three(gate_own[8 * p : 8 * p + 8, :])
            gate_pairs[:, size * p : size * p + size] = jnp.concatenate(
                [one, one, one, two, two, three], axis=0
            )
        for copy in weight_copies():
            copy.start()
        for ref in (g_q, g_k, g_v, g_small):
            ref[...] = jnp.zeros_like(ref)
        for ref in (q_all, k_all, v_all):
            ref[blocks * block :] = jnp.zeros_like(ref[blocks * block :])

    order = around + [z]
    tall, wide = size // 4, size // 2

    @pl.when(step < blocks)
    def _():
        lows = lower_first(
            d_gate, dq, dk, dv, mix_ref, conv, q_ref, k_ref, v_ref, gate_pairs, g_q, g_k, g_v, g_small
        )
        here = pl.ds(pl.multiple_of(step * block, block), block)
        for ref, value in zip((q_all, k_all, v_all), lows):
            ref[here] = value

    @pl.when(step == blocks - 1)
    def _():
        for q in range(4):
            rows_q = slice(tall * q, tall * q + tall)
            for at, ref in enumerate((g_q, g_k, g_v)):
                lanes = slice(wide * at, wide * at + wide)
                left, right = ref[rows_q, :wide], ref[rows_q, wide:]
                totals[1][q, :, lanes] = jnp.where(x == 0, left, right).astype(bf16)
                give_square[q, :, lanes] = jnp.where(x == 0, right, left).astype(bf16)
            to_x(1, q).start()
        for copy in weight_copies():
            copy.wait()

    @pl.when(step >= blocks)
    def _():
        now = drain_order(step, blocks)
        here = pl.ds(pl.multiple_of(now * block, block), block)
        more = pl.ds(pl.multiple_of(now * block, block), block + mix_next.shape[0])
        rows, d_mix, d_normed = lower_block(
            now == 0, now == blocks - 1, (q_all[more], k_all[more], v_all[here]),
            dskip, dskip_next, dz, mix_ref, mix_before, mix_next, normed,
            w_q, w_k, w_v, w_mix, w_gate, taps_w, taps_b, g_small,
        )
        rows_all[here] = rows
        lifted_all[here] = d_mix
        part_all[now] = d_normed.astype(bf16)
        to_c(now).start()
        pl.when(step > blocks)(lambda: core_step(drain_order(step - 1, blocks)))

    def at_end(when, *work):
        @pl.when(step == blocks + when)
        def _():
            for do in work:
                do()

    def spread_down():
        span = dn_go.shape[2]
        for cc in range(2):
            dn_go[cc] = ends[2][:, span * cc : span * cc + span].astype(bf16)
            left_here = jnp.logical_and(home, c == cc)

            @pl.when(left_here)
            def _():
                dn_got[low] = dn_go[cc]

            pl.when(jnp.logical_not(left_here))(lambda: down_to(cc).start())

    def every(do, p):
        return [partial(do, p, q) for q in range(4)]

    def early_cross():
        pl.when(x == 0)(lambda: cross(3))

    at_end(-3, *every(near_step, 3))
    at_end(-1, *every(x_step, 2))
    at_end(1, *every(far_step, 3), early_cross)
    at_end(2, *every(near_step, 2), partial(x_step, 1, 0))
    at_end(4, partial(x_step, 1, 1), partial(near_step, 1, 0), *every(far_step, 2), spread_down)
    at_end(5, partial(row_step, order[0]))
    at_end(6, partial(x_step, 1, 2), partial(near_step, 1, 1))
    at_end(7, partial(row_step, order[1]), partial(x_step, 1, 3))

    def norm_back(m, cc):
        own_part = jnp.logical_and(2 * c + m == z, c == cc)
        landed = remote(
            to_owner.at[0], owned.at[m, cc], o_sent.at[0], o_landed.at[m, cc],
            device(2 * c + m, y, cc),
        )
        pl.when(jnp.logical_not(own_part))(lambda: landed.wait_recv())
        rows_here = pl.ds(cc * half, half)
        row_hat, rstd = normalize(rows_ref[m, rows_here].astype(f32))
        scaled = owned[m, cc].astype(f32) * gain_ref[...]
        d_row = rstd * (
            scaled
            - jnp.mean(scaled, axis=-1, keepdims=True)
            - row_hat * jnp.mean(scaled * row_hat, axis=-1, keepdims=True)
        )
        grad_out[m, rows_here] = (cot_ref[m, rows_here].astype(f32) + d_row).astype(bf16)

    def small_after_x():
        small_to_x().wait_recv()
        small_sum[...] = g_small[...] + small_x[...]
        small_z[z] = small_sum[...]
        for k in range(3):
            small_to_z(k).start()

    def small_after_z():
        for k in range(3):
            small_from_z(k).wait_recv()
        total = small_z[0]
        for zz in range(1, 4):
            total = total + small_z[zz]
        small_all[head] = total
        for k in range(3):
            small_to_head(k).start()

    def spread_square():
        for yy in range(2):
            for cc in range(2):
                for a in range(3):
                    sq_go[yy, cc, :, tall * a : tall * a + tall] = ends[1][
                        tall // 2 * yy : tall // 2 * yy + tall // 2,
                        (2 * a + cc) * tall : (2 * a + cc) * tall + tall,
                    ].astype(bf16)
        sq_got[head] = sq_go[y, c]
        for k in range(3):
            square_to(k).start()

    @pl.when(step == 2 * blocks - 1)
    def _():
        g_small[29:32, :] = g_gain[0:3, :]
        small_to_x().start()
        for q in range(4):
            got = mm_tn(rows_all[:, block * q : block * q + block], lifted_all[...]).astype(bf16)
            given = lifted_ref[up_rows(q), :wide]
            totals[0][q] = jnp.where(x == 0, got[:, :wide], given)
            give_up[q] = jnp.where(x == 0, given, got[:, :wide])
            totals[4][q] = got[:, wide:]
            to_x(0, q).start()
            start_near(4, q)
            if q == 0:
                core_step(2 * z + y)
        small_after_x()
        row_step(order[2])
        near_step(1, 2)
        near_step(1, 3)
        x_step(0, 0)
        near_step(4, 0)
        near_step(4, 1)
        far_step(1, 0)
        far_step(1, 1)
        row_step(z)
        x_step(0, 1)
        near_step(4, 2)
        near_step(4, 3)
        small_after_z()
        x_step(0, 2)
        near_step(0, 0)
        near_step(0, 1)
        far_step(1, 2)
        far_step(1, 3)
        spread_square()
        x_step(0, 3)
        for q in range(4):
            far_step(4, q)
        pl.when(x == 1)(lambda: cross(4))
        near_step(0, 2)
        for m in range(2):
            for cc in range(2):
                norm_back(m, cc)
        near_step(0, 3)
        for q in range(4):
            far_step(0, q)
        to_cross().wait_recv()
        kept_half = jnp.where(x == 0, ends[4][...], ends[3][...])
        ends[0][:, wide:] = kept_half + cross_got[...].astype(f32)
        value = ends[0][...]
        mine = jnp.where(y == 0, value[:half], value[half:])
        up_go[...] = jnp.where(y == 0, value[half:], value[:half]).astype(bf16)
        up_to_y().start()
        for yy in range(2):

            @pl.when(y == yy)
            def _():
                up_out[:, size * yy : size * yy + size] = mine

        for k in range(3):
            small_from_head(k).wait_recv()
        small_out[...] = small_all[...]
        for k in range(3):
            square_from(k).wait_recv()
        for a, ref in enumerate((query_out, key_out, value_out)):
            ref[...] = sq_got[:, :, tall * a : tall * a + tall].astype(f32)
        for k in range(2):
            mine = jnp.logical_and(home, jnp.logical_and(low == k, high == c))
            pl.when(jnp.logical_not(mine))(lambda: down_from(k).wait_recv())
            deep = dn_got.shape[1]
            down_out[deep * k : deep * k + deep] = dn_got[k].astype(f32)
        up_to_y().wait_recv()
        for yy in range(2):

            @pl.when(y == yy)
            def _():
                up_out[:, size * (1 - yy) : size * (1 - yy) + size] = up_got[...].astype(f32)

        small_to_x().wait_send()
        up_to_y().wait_send()
        to_cross().wait_send()
        for p in range(5):
            for q in range(4):
                if p < 3:
                    to_x(p, q).wait_send()
                pl.when(low != q % 2)(lambda: to_near(p, q).wait_send())
                passes = jnp.logical_and(low == q % 2, high != q // 2)
                pl.when(passes)(lambda: to_far(p, q).wait_send())
        for at in range(blocks):
            to_c(at).wait_send()
        for zz in range(4):
            to_y(zz).wait_send()
            pl.when(jnp.logical_not(stays(zz)))(lambda: to_o(zz).wait_send())
        for k in range(3):
            small_to_z(k).wait_send()
            small_to_head(k).wait_send()
            square_to(k).wait_send()
        for cc in range(2):
            left_here = jnp.logical_and(home, c == cc)
            pl.when(jnp.logical_not(left_here))(lambda: down_to(cc).wait_send())


def drain_order(step, blocks):
    first, z, y, x, c = where_am_i()
    k, odd = halves_of(jnp.maximum(step - blocks, 0), blocks)
    return 2 * turn(z + 1 + k, 4) + jnp.where(odd == 0, 1 - y, y)


def drain(inputs, down, lifted, rows, cot, gain):
    (d_gate, dq, dk, dv, dskip, dz, mix, conv, q, k, v, normed,
     w_query, w_key, w_value, w_up, conv_w, conv_b, gate_own, g_gain) = inputs
    tokens, size = q.shape
    micro, block, width = rows.shape
    half = block // 2
    lines = 40
    steps = tokens // block
    early = lambda g: jnp.minimum(g, steps - 1)
    late = lambda g: drain_order(g, steps)
    both = lambda g: jnp.where(g < steps, g, drain_order(g, steps))
    edge = lambda at: pl.BlockSpec(
        (16, size), lambda g: (jnp.clip(at(g), 0, tokens // 16 - 1), 0)
    )
    before = edge(lambda g: late(g) * (block // 16) - 1)
    behind = edge(lambda g: (late(g) + 1) * (block // 16))
    by_row = lambda n, at: pl.BlockSpec((block, n), lambda g: (at(g), 0))
    kept = lambda value: pl.BlockSpec(
        value.shape, lambda g: (0,) * value.ndim, pipeline_mode=pl.Buffered(1)
    )
    anywhere = pl.BlockSpec(memory_space=pl.ANY)
    arguments = (
        d_gate, dq, dk, dv, mix, conv, q, k, v, dskip, dskip, dz, mix, mix, normed, gate_own, g_gain,
        w_query, w_key, w_value, w_up, conv_w, conv_b, down, lifted, rows, cot, gain,
    )
    specs = [pl.BlockSpec((8, block), lambda g: (0, early(g)))] + [by_row(size, early)] * 3
    specs += [by_row(size, both)] + [by_row(size, early)] * 4
    specs += [by_row(size, late), behind, by_row(size, late), before, behind, by_row(width, late)]
    specs += [kept(gate_own), kept(g_gain)]
    specs += [anywhere] * 6 + [kept(value) for value in (down, lifted, rows, cot, gain)]
    scratch = [((size, size), bf16)] * 3 + [((width, size), bf16)] * 2
    scratch += [((4, size), f32), ((1, size), f32), ((48, 3 * size), bf16)]
    scratch += [((tokens + 16, size), bf16)] * 3
    scratch += [((size, size), f32)] * 3 + [((lines, size), f32)]
    scratch += [((tokens, width), bf16), ((tokens, size), bf16), ((8, block, width), bf16)]
    scratch += [
        ((8, half, width), bf16), ((4, half, width), bf16), ((4, half, width), bf16),
        ((4, half, width), bf16), ((4, half, width), bf16), ((2, 2, half, width), bf16),
    ]
    up = (width // 4, size // 2)
    pieces = [up, (size // 4, 3 * size // 2), (size // 4, width // 2), up, up]
    scratch += [((4, *piece), bf16) for piece in pieces[:2]] + [(up, bf16)] * 2
    scratch += [((4, *piece), bf16) for piece in pieces[:3] + pieces[:3] + pieces[4:]]
    for piece in pieces:
        scratch += [((2, *piece), bf16)] * 2 + [(piece, bf16), (piece, f32)]
    scratch[-17] = ((up[0], size), f32)
    scratch += [
        ((width // 8, size), bf16), ((width // 8, size), bf16),
        ((2, 2, size // 8, 3 * size // 4), bf16), ((4, size // 8, 3 * size // 4), bf16),
        ((2, size // 4, width // 4), bf16), ((2, size // 4, width // 4), bf16),
        ((lines, size), f32), ((lines, size), f32), ((4, lines, size), f32), ((4, lines, size), f32),
    ]
    sems = [(8,), (8,), (4,), (4,), (4,), (2, 2)] + [(5, 4)] * 6
    sems += [(2,), (7,), (2,), (3,), (4,), (2,), (2,), (2,), (3,), (4,), (3,), (4,)]
    square = struct((4, size // 8, size // 4), f32)
    outs = [
        struct(rows.shape, bf16), struct((width // 8, 2 * size), f32), square, square, square,
        struct((size // 2, width // 4), f32), struct((4, lines, size), f32),
    ]
    return pl.pallas_call(
        drain_kernel,
        grid=(2 * steps,),
        in_specs=specs,
        out_specs=[kept(value) for value in outs],
        scratch_shapes=[pltpu.VMEM(shape, dtype) for shape, dtype in scratch]
        + [pltpu.SemaphoreType.DMA(shape) for shape in sems],
        out_shape=outs,
        compiler_params=pltpu.CompilerParams(
            dimension_semantics=("arbitrary",), collective_id=1, has_side_effects=True,
            vmem_limit_bytes=60 * 2**20,
        ),
        cost_estimate=pl.CostEstimate(
            flops=2 * tokens * size * (6 * size + 4 * width), bytes_accessed=48 * 2**20,
            transcendentals=0,
        ),
        name="drain",
    )(*arguments)


def spread_kernel(small, gain, *refs):
    count = (len(refs) - 7) // 2
    for k in range(count):
        refs[count + 7 + k][...] = refs[k][...]
    ln_out, conv_out, bias_out, gate_out, forget_out, out_gain, skip_gain = refs[count : count + 7]
    heads, _, size = small.shape
    total = small[0, 32:34, :]
    for h in range(1, heads):
        total = total + small[h, 32:34, :]
    for k in range(2):
        lanes = slice(size * k, size * k + size)
        ln_out[:, lanes] = total[k : k + 1, :] / gain[:, lanes]
    for h in range(heads):
        lanes = slice(size * h, size * h + size)
        conv_out[:, lanes] = small[h, 24:28, :]
        bias_out[:, lanes] = small[h, 28:29, :]
        out_gain[:, lanes] = small[h, 29:30, :]
        skip_gain[:, lanes] = small[h, 30:31, :]
        forget_out[:, h : h + 1] = small[h, 31:32, 0:1]
        for p in range(3):
            start = (heads * p + h) * size
            gate_out[:, start : start + size] = small[h, 8 * p : 8 * p + 8, :]


def spread(small, gain, *made):
    heads, _, size = small.shape
    inner = heads * size
    shapes = [gain.shape, (4, inner), (1, inner), (8, 3 * inner), (1, heads), (1, inner), (1, inner)]
    return pl.pallas_call(
        spread_kernel,
        out_shape=[struct(shape, f32) for shape in shapes]
        + [struct(value.shape, value.dtype) for value in made],
        name="spread",
        compiler_params=pltpu.CompilerParams(vmem_limit_bytes=62 * 2**20),
    )(small, gain, *made)


def swap(value, axis, mask):
    count = lax.axis_size(axis)
    return lax.ppermute(value, axis, [(s, s ^ mask) for s in range(count)])


def part_of(value, at, count, axis):
    size = value.shape[axis] // count
    return lax.dynamic_slice_in_dim(value, at * size, size, axis)


def halved(value, bit, dim, axis, mask):
    kept = part_of(value, bit, 2, dim).astype(f32)
    return kept + swap(part_of(value, 1 - bit, 2, dim), axis, mask).astype(f32)


def paired(mine, other, bit, dim):
    return jnp.where(
        bit == 0, jnp.concatenate([mine, other], dim), jnp.concatenate([other, mine], dim)
    )


def place():
    at_seq, at_batch = lax.axis_index("seq"), lax.axis_index("batch")
    return (at_seq % 8) // 2, at_seq % 2, at_batch // 2, at_batch % 2


def sent_across(blocks, z):
    got = [lax.dynamic_index_in_dim(blocks, z, 0, keepdims=False)]
    for k in range(1, 4):
        got.append(swap(lax.dynamic_index_in_dim(blocks, z ^ k, 0, keepdims=False), "seq", 2 * k))
    return got


def in_order(got, z):
    got = jnp.stack(got)
    return jnp.stack([lax.dynamic_index_in_dim(got, z ^ k, 0, keepdims=False) for k in range(4)])


def gather_sequence(own):
    z, y, x, c = place()
    micro, rows, width = own.shape
    slots = paired(own, swap(own, "batch", 1), c, 0)
    blocks = in_order(sent_across(part_of(slots, c, 2, 2), z), z)[:, None]
    both = paired(blocks, swap(blocks, "seq", 1), y, 1)
    return paired(both, swap(both, "batch", 1), c, 3).reshape(8 * rows, width)


def scatter_first(parts):
    z, y, x, c = place()
    blocks = parts.reshape(4, 2, -1, parts.shape[1])
    return halved(blocks, c, 2, "batch", 1).astype(bf16)


def scatter_last(slots):
    z, y, x, c = place()
    other = swap(part_of(slots, 1 - c, 2, 0), "batch", 1)
    return paired(part_of(slots, c, 2, 0), other, c, 1).astype(f32)


def scatter_sequence(parts):
    z, y, x, c = place()
    blocks = scatter_first(parts)
    blocks = halved(blocks, y, 1, "seq", 1).astype(bf16)[:, 0]
    return scatter_last(in_order(sent_across(blocks, z), z))


def total_over_heads(value):
    value = value + swap(value, "batch", 1)
    return value + swap(value, "seq", 1)


def over_ranges(value, count):
    size = lax.axis_size("seq")
    groups = [[first + 8 * k for k in range(count)] for first in range(8)]
    return lax.all_gather(value, "seq", axis_index_groups=groups) if size > 8 else value[None]


def state_before(state, norm, level, total, ranges):
    index = lax.axis_index("seq") // 8
    summary = (state, norm[0], level[0, 0], total)
    everything = jax.tree.map(lambda part: over_ranges(part, ranges), summary)
    before = state_identity(summary)
    for k in range(ranges - 1):
        new = combine_states(before, jax.tree.map(lambda part: part[k], everything))
        before = jax.tree.map(lambda a, b: jnp.where(k < index, a, b), new, before)
    return (
        before[0],
        jnp.broadcast_to(before[1], norm.shape),
        jnp.broadcast_to(before[2], level.shape),
    )


def cotangent_after(d_state, d_norm, keep, ranges):
    index = lax.axis_index("seq") // 8
    own = (d_state, d_norm)
    everything = jax.tree.map(lambda part: over_ranges(part, ranges), own)
    keeps = over_ranges(keep, ranges)
    after = jax.tree.map(jnp.zeros_like, own)
    for k in range(ranges - 1, 0, -1):
        new = jax.tree.map(lambda a, b: a[k] + keeps[k] * b, everything, after)
        after = jax.tree.map(lambda a, b: jnp.where(k > index, a, b), new, after)
    return after


def reduce_blocks(at, up, square, down, heads):
    count, batch_count = lax.axis_size("seq"), lax.axis_size("batch")
    g_m, g_z = up
    width, size = g_m.shape
    half = size // 2
    squares = [
        jnp.concatenate([square[0, :, k : k + half], square[1, :, k : k + half]], 1)
        for k in range(0, 3 * half, half)
    ]
    g_down = jnp.concatenate([down[0], down[1]], 1)
    inner = heads * size
    up = jnp.zeros((width, 2 * inner), f32)
    up = lax.dynamic_update_slice_in_dim(up, g_m.astype(f32), at * size, 1)
    up = lax.dynamic_update_slice_in_dim(up, g_z.astype(f32), inner + at * size, 1)
    down = lax.dynamic_update_slice_in_dim(
        jnp.zeros((inner, width), f32), g_down.astype(f32), at * size, 0
    )
    full = [up, down]
    for g in squares:
        full.append(
            lax.dynamic_update_slice_in_dim(
                jnp.zeros((heads, size, size), f32), g.astype(f32)[None], at, 0
            )
        )
    blocks = tuple(to_device_blocks(g, count, batch_count) for g in full)
    pieces = lax.psum_scatter(blocks, ("seq", "batch"), scatter_dimension=0, tiled=True)
    s_up, s_down, s_query, s_key, s_value = tuple(p[0] for p in pieces)
    return s_up, jnp.stack([s_query, s_key, s_value], 1), s_down


def head_device(
    tokens, ln_gain, w_up, conv_w, conv_b, w_query, w_key, w_value, gate_w, gate_b,
    out_gain, skip_gain, w_down, d_out,
):
    z, y, x, c = place()
    at = 2 * c + y
    ranges = lax.axis_size("seq") // 8
    direct = ranges == 1 and lax.axis_size("batch") == 4
    head = jnp.reshape(at, (1,)).astype(jnp.int32)
    heads, size, _ = w_query.shape
    inner = heads * size
    conv_row = conv_b.reshape(1, inner)
    out_row = out_gain.reshape(1, inner)
    skip_row = skip_gain.reshape(1, inner)

    gate_own = lax.dynamic_index_in_dim(
        gate_w.reshape(3, heads, size, 8), at, 1, keepdims=False
    ).transpose(0, 2, 1)
    gate_rows = gate_own.reshape(24, size)
    high = lax.reduce_precision(gate_own, 8, 7)
    middle = lax.reduce_precision(gate_own - high, 8, 7)
    low = lax.reduce_precision(gate_own - high - middle, 8, 7)
    gate_parts = jnp.concatenate([high, middle, low, jnp.zeros_like(high)], 1).astype(bf16)
    gate_pairs = (
        jnp.concatenate([high, high, high, middle, middle, low], 1)
        .astype(bf16)
        .transpose(1, 0, 2)
        .reshape(48, 3 * size)
    )

    if direct:
        (normed, mix, conv, q, k, v, gate_z,
         part, head_normed, states, norms, weights, cols, rows, cot) = rise(
            tokens[:, 0], ln_gain[None], w_up, w_query, w_key, w_value, conv_w, conv_row, gate_rows, gate_b,
            out_row, skip_row, w_down, d_out[:, 0],
        )
    else:
        normed = gather_normed(tokens[:, 0], ln_gain[None])
        cot = gather_sequence(d_out[:, 0])
        first = () if ranges == 1 else (shifted(normed[-16:], "seq", 8),)
        mix, conv, q, k, v, gate_z, gates, *halo = lift(
            head, normed, w_up, w_query, w_key, w_value, conv_w, conv_row, gate_parts, *first
        )
        gates = total_over_heads(gates)
        gates = jnp.concatenate(
            [
                lax.dynamic_slice_in_dim(gates, at, 1, 0),
                lax.dynamic_slice_in_dim(gates, heads + at, 1, 0)
                + lax.dynamic_slice_in_dim(gate_b, at, 1, 0)[:, None],
            ]
        )
        first = ()
        if ranges > 1:
            first = (
                jnp.zeros((size, size), f32),
                jnp.zeros((8, size), f32),
                jnp.full((8, 128), floor_value, f32),
            )
            *_, state, norm, level = cell_forward(
                head, gates, q, k, v, conv, gate_z, out_row, skip_row, w_down, *first
            )
            total = jnp.sum(jax.nn.log_sigmoid(gates[1]))
            first = state_before(state, norm, level, total, ranges)
        part, head_normed, states, norms, weights, cols, rows, *last = cell_forward(
            head, gates, q, k, v, conv, gate_z, out_row, skip_row, w_down, *first
        )
    cell_args = (
        rows, q, k, v, conv, gate_z, head_normed, states, norms, weights, cols, cot, normed,
        out_row, skip_row, w_down,
    )
    if direct:
        dq, dk, dv, dskip, dz, g_down, g_z, g_gain, block_rows, d_gate = settle(
            part, tokens[:, 0], *cell_args
        )
    else:
        block_rows = (tokens[:, 0].astype(f32) + scatter_sequence(part)).astype(bf16)
        after = ()
        if ranges > 1:
            after = (jnp.zeros((size, size), f32), jnp.zeros((8, size), f32))
            *_, d_state, d_norm = cell_backward(head, *cell_args, *after)
            keep = jnp.exp(total + first[2][0, 0] - last[2][0, 0])
            after = cotangent_after(d_state, d_norm, keep, ranges)
        dq, dk, dv, dskip, dz, d_rows, g_down, g_z, g_gain, *_ = cell_backward(
            head, *cell_args, *after
        )
        index = jnp.arange(2 * heads)[:, None]
        d_gate = jnp.where(
            index == at, d_rows[0:1], jnp.where(index == heads + at, d_rows[1:2], 0.0)
        )
        d_gate = total_over_heads(d_gate)
    lower_args = (
        d_gate, dq, dk, dv, dskip, dz, mix, conv, q, k, v, normed,
        w_query, w_key, w_value, w_up, conv_w, conv_row, gate_pairs, g_gain,
    )
    if direct:
        grad_rows, s_up, s_query, s_key, s_value, s_down, small = drain(
            (*lower_args[:18], gate_rows, g_gain), g_down, g_z, tokens[:, 0], d_out[:, 0], ln_gain[None]
        )
    else:
        first = ()
        if ranges > 1:
            *_, later = lower(head, *lower_args, halo[0], jnp.zeros((8, size), f32))
            first = (halo[0], shifted(later, "seq", -8))
        d_part, square, up, small, *_ = lower(head, *lower_args, *first)
    if not direct:
        d_normed = scatter_sequence(d_part)
        row_f = tokens[:, 0].astype(f32)
        centre = row_f - jnp.mean(row_f, axis=-1, keepdims=True)
        rstd = lax.rsqrt(jnp.mean(centre * centre, axis=-1, keepdims=True) + norm_epsilon)
        row_hat = centre * rstd
        scaled = d_normed * ln_gain
        d_row = rstd * (
            scaled
            - jnp.mean(scaled, axis=-1, keepdims=True)
            - row_hat * jnp.mean(scaled * row_hat, axis=-1, keepdims=True)
        )
        grad_rows = (d_out[:, 0].astype(f32) + d_row).astype(bf16)
        s_up, squares, s_down = reduce_blocks(at, up, square, g_down, heads)
        s_query, s_key, s_value = squares[:, 0], squares[:, 1], squares[:, 2]
        small = jnp.where(jnp.arange(heads)[:, None, None] == at, small, 0.0)
        small = lax.psum(small, ("seq", "batch"))
    (s_ln, s_conv_w, s_conv_b, s_gate_w, s_gate_b, s_out_gain, s_skip,
     block_rows, grad_rows, s_up, s_query, s_key, s_value, s_down) = spread(
        small, ln_gain[None], block_rows, grad_rows, s_up, s_query, s_key, s_value, s_down
    )
    return (
        block_rows[:, None],
        grad_rows[:, None],
        s_ln[0],
        s_up,
        s_conv_w,
        s_conv_b[0],
        s_query,
        s_key,
        s_value,
        s_gate_w.T,
        s_gate_b[0],
        s_out_gain[0],
        s_skip[0],
        s_down,
    )


def solution(mesh):
    placed = (P(None, "batch", "seq", None),) + (P(),) * 12 + (P(None, "batch", "seq", None),)
    return jax.shard_map(
        head_device,
        mesh=mesh,
        in_specs=placed,
        out_specs=(
            P(None, "batch", "seq", None),
            P(None, "batch", "seq", None),
            P(),
            P("seq", "batch"),
            P(),
            P(),
            P(None, "seq", "batch"),
            P(None, "seq", "batch"),
            P(None, "seq", "batch"),
            P(),
            P(),
            P(),
            P(),
            P("seq", "batch"),
        ),
        check_vma=False,
    )
```
